32 devices in a mesh: dp: 8 (over z, x), tensor: 4 (over y, core).
Axes of the slice: x: 2, y: 2, z: 4, core: 2. Of those that a mesh axis runs over, the one named last changes fastest.
Arguments:
- tokens: bfloat16 [16384, 1024], P(('dp', 'tensor')), may hold values from -6 to 6
- cotangent: bfloat16 [16384, 1024], P(('dp', 'tensor')), may hold values from -6 to 6
- lengths: int32 [8, 8], P('dp'), may hold values from 1 to 1024, 2048 in all within a row
- projection_weight: float32 [1024, 8, 512], P('dp', 'tensor'), may hold values from -0.1875 to 0.1875
- w_out: float32 [16, 128, 1024], P('tensor', 'dp'), may hold values from -1 to 1
- w_gate_up: float32 [1024, 2, 3072], P('dp', None, 'tensor'), may hold values from -0.1875 to 0.1875
- w_down: float32 [24, 128, 1024], P('tensor', 'dp'), may hold values from -0.109375 to 0.109375
- gains: float32 [2304], P('dp'), may hold values from 0.5 to 1.5
- first_moment_projection: float32 [1024, 8, 512], P('dp', 'tensor'), may hold values from -64 to 64
- first_out: float32 [16, 128, 1024], P('tensor', 'dp'), may hold values from -14 to 14
- first_gate_up: float32 [1024, 2, 3072], P('dp', None, 'tensor'), may hold values from -32 to 32
- first_down: float32 [24, 128, 1024], P('tensor', 'dp'), may hold values from -48 to 48
- first_gains: float32 [2304], P('dp'), may hold values from -160 to 160
- second_moment_projection: float32 [1024, 8, 512], P('dp', 'tensor'), may hold values from 557.056 to 2211.84
- second_out: float32 [16, 128, 1024], P('tensor', 'dp'), may hold values from 19.6608 to 77.0048
- second_gate_up: float32 [1024, 2, 3072], P('dp', None, 'tensor'), may hold values from 137.6256 to 557.056
- second_down: float32 [24, 128, 1024], P('tensor', 'dp'), may hold values from 311.296 to 1245.184
- second_gains: float32 [2304], P('dp'), may hold values from 819.2 to 32768
Outputs:
- block_out: bfloat16 [16384, 1024], P(('dp', 'tensor'))
- grad_tokens: float32 [16384, 1024], P(('dp', 'tensor'))
- next_w_qkv: float32 [1024, 8, 512], P('dp', 'tensor')
- next_w_out: float32 [16, 128, 1024], P('tensor', 'dp')
- next_w_gate_up: float32 [1024, 2, 3072], P('dp', None, 'tensor')
- next_w_down: float32 [24, 128, 1024], P('tensor', 'dp')
- next_gains: float32 [2304], P('dp')
- next_first_qkv: float32 [1024, 8, 512], P('dp', 'tensor')
- next_first_out: float32 [16, 128, 1024], P('tensor', 'dp')
- next_first_gate_up: float32 [1024, 2, 3072], P('dp', None, 'tensor')
- next_first_down: float32 [24, 128, 1024], P('tensor', 'dp')
- next_first_gains: float32 [2304], P('dp')
- next_second_qkv: float32 [1024, 8, 512], P('dp', 'tensor')
- next_second_out: float32 [16, 128, 1024], P('tensor', 'dp')
- next_second_gate_up: float32 [1024, 2, 3072], P('dp', None, 'tensor')
- next_second_down: float32 [24, 128, 1024], P('tensor', 'dp')
- next_second_gains: float32 [2304], P('dp')
The draws below stay inside these ranges and needn't reach their ends.
Inputs may be any that keep to these rules, and one draw needn't show every extreme that they name: Each row holds the lengths of the 8 documents of one index of dp, in order; they sum to 2048, and in every row one of them is exactly 1024.
All inputs are finite; a program needn't handle non-finite values.
Results may differ from the reference program's by a relative error of at most 0.017.
Values may be sent and summed in bfloat16 or wider, within the bound.
No kernel may reach another device: no remote copies, remote signals or barrier semaphores. Data moves between devices by JAX's collectives and lax.ppermute only.
A program may use at most 192 MiB of HBM per device.

```python
import math
import jax
import jax.numpy as jnp
import numpy as np
from jax import lax

MODEL_WIDTH = 1024
QUERY_HEADS = 16
KEY_VALUE_HEADS = 8
HEAD_SIZE = 128
FF = 3072
TOK_GRP = 2048
MAXLEN = 1024
STEP = 10
NSEQ = 8
TOKEN_TOTAL = 16384
N_DP = 8


def strengthened(drawn, stream_key, source, target, shards_of, factor):
    def block_of(dim):
        return (jnp.arange(drawn.shape[dim]) // (drawn.shape[dim] // shards_of)).reshape((-1,) + (1,) * (drawn.ndim - 1 - dim))

    near = jax.random.permutation(stream_key, shards_of)[block_of(target)]
    other_side = (block_of(target) + shards_of // 2) % shards_of
    return jnp.where((block_of(source) == near) | (block_of(source) == other_side), factor * drawn, drawn)


def level_of(key, extent, shards, low, largest):
    def one(dim, parts):
        steps = jax.random.uniform(jax.random.fold_in(jax.random.fold_in(key, 6), dim), (parts,), jnp.float32, low / len(shards), largest / len(shards))
        return jnp.repeat(jnp.exp(steps), extent[dim] // parts).reshape((-1,) + (1,) * (len(extent) - dim - 1))

    level = one(*shards[0])
    for cut in shards[1:]:
        level = level * one(*cut)
    return level


def length_profile(amount, total, bound, lean):
    loads = [(1 << 20) // math.isqrt(standing ** lean) + 1 for standing in range(2, amount + 1)]
    surplus, given = total - bound - (amount - 1), [1] * (amount - 1)
    while surplus > 0:
        candidates = [i for i in range(amount - 1) if given[i] < bound]
        pool, remaining = sum([loads[i] for i in candidates]), surplus
        for i in candidates:
            extra = min(bound - given[i], max(1, remaining * loads[i] // pool), surplus)
            given[i] = given[i] + extra
            surplus = surplus - extra
    return np.array([bound] + given)


def uneven(rng, count, total, reach, lean):
    if count == 2:
        one = jax.random.randint(rng, (), max(1, total - reach), min(reach, total - 1) + 1)
        return jnp.stack([one, total - one])
    sizes = jnp.asarray(length_profile(count, total, reach, lean), jnp.int32)
    couples = (count - 1) // 2
    source_of, receiver = sizes[1:1 + 2 * couples:2], sizes[2:2 + 2 * couples:2]
    margin = jnp.minimum(source_of - 1, reach - receiver)
    moved = jax.random.randint(jax.random.fold_in(rng, 1), (couples,), 0, 1 << 20) % (margin + 1)
    sizes = sizes.at[1:1 + 2 * couples:2].set(source_of - moved).at[2:2 + 2 * couples:2].set(receiver + moved)
    return sizes[jax.random.permutation(jax.random.fold_in(rng, 2), count)]


def gaussian(rng, dims, deviation, limit, split=(), kind=jnp.bfloat16):
    gain = level_of(rng, dims, split, -0.22, 0.18) if split else 1.0
    values = jax.random.normal(rng, dims, jnp.float32) * deviation * gain
    return jnp.minimum(jnp.maximum(values, -limit), limit).astype(kind)


def noise_with(stream_key, dims, deviation, bound, split, heavy, kind=jnp.bfloat16):
    array = deviation * jax.random.normal(stream_key, dims, jnp.float32)
    if split:
        array = array * level_of(stream_key, dims, split, -0.22, 0.18)
    return jnp.clip(strengthened(array, jax.random.fold_in(stream_key, 3), *heavy), -bound, bound).astype(kind)


def setup_inputs(seed: int = 0) -> dict:
    keys = jax.random.split(jax.random.key(seed), 19)
    return {
        "tokens": noise_with(keys[0], (TOKEN_TOTAL, MODEL_WIDTH), 1.0, 6.0, ((0, 32),), (0, 1, 32, 2.75)),
        "cotangent": gaussian(keys[1], (TOKEN_TOTAL, MODEL_WIDTH), 1.0, 6.0, ((0, 32),)),
        "lengths": jax.vmap(lambda own: uneven(own, NSEQ, TOK_GRP, MAXLEN, 2))(jax.random.split(keys[2], N_DP)).reshape((N_DP, NSEQ)).astype(jnp.int32),
        "projection_weight": gaussian(keys[3], (MODEL_WIDTH, KEY_VALUE_HEADS, (QUERY_HEADS // KEY_VALUE_HEADS + 2) * HEAD_SIZE), MODEL_WIDTH ** -0.5, 0.1875, ((0, 8), (1, 4)), jnp.float32),
        "w_out": gaussian(keys[4], (QUERY_HEADS, HEAD_SIZE, MODEL_WIDTH), (QUERY_HEADS * HEAD_SIZE // 64) ** -0.5, 1.0, ((0, 4), (1, 8)), jnp.float32),
        "w_gate_up": gaussian(keys[5], (MODEL_WIDTH, 2, FF), MODEL_WIDTH ** -0.5, 0.1875, ((0, 8), (2, 4)), jnp.float32),
        "w_down": gaussian(keys[6], (FF // 128, 128, MODEL_WIDTH), FF ** -0.5, 0.109375, ((0, 4), (1, 8)), jnp.float32),
        "gains": jnp.clip(1.0 + 0.1 * jax.random.normal(keys[7], (2 * MODEL_WIDTH + 2 * HEAD_SIZE,), jnp.float32), 0.5, 1.5),
        "first_moment_projection": gaussian(keys[8], (MODEL_WIDTH, KEY_VALUE_HEADS, (QUERY_HEADS // KEY_VALUE_HEADS + 2) * HEAD_SIZE), (0.09 * TOKEN_TOTAL ** 0.5), 64.0, ((0, 8), (1, 4)), jnp.float32),
        "first_out": gaussian(keys[9], (QUERY_HEADS, HEAD_SIZE, MODEL_WIDTH), (0.017 * TOKEN_TOTAL ** 0.5), 14.0, ((0, 4), (1, 8)), jnp.float32),
        "first_gate_up": gaussian(keys[10], (MODEL_WIDTH, 2, FF), (0.044 * TOKEN_TOTAL ** 0.5), 32.0, ((0, 8), (2, 4)), jnp.float32),
        "first_down": gaussian(keys[11], (FF // 128, 128, MODEL_WIDTH), (0.067 * TOKEN_TOTAL ** 0.5), 48.0, ((0, 4), (1, 8)), jnp.float32),
        "first_gains": gaussian(keys[12], (2 * MODEL_WIDTH + 2 * HEAD_SIZE,), (0.2 * TOKEN_TOTAL ** 0.5), 160.0, ((0, 8),), jnp.float32),
        "second_moment_projection": jnp.clip(jnp.exp(math.log(2211.84) - 1.3789142 * jax.random.uniform(keys[13], (MODEL_WIDTH, KEY_VALUE_HEADS, (QUERY_HEADS // KEY_VALUE_HEADS + 2) * HEAD_SIZE), jnp.float32) ** level_of(keys[13], (MODEL_WIDTH, KEY_VALUE_HEADS, (QUERY_HEADS // KEY_VALUE_HEADS + 2) * HEAD_SIZE), ((0, 8), (1, 4)), -0.2, 0.2)), 557.056, 2211.84),
        "second_out": jnp.clip(jnp.exp(math.log(77.0048) - 1.3652409 * jax.random.uniform(keys[14], (QUERY_HEADS, HEAD_SIZE, MODEL_WIDTH), jnp.float32) ** level_of(keys[14], (QUERY_HEADS, HEAD_SIZE, MODEL_WIDTH), ((0, 4), (1, 8)), -0.2, 0.2)), 19.6608, 77.0048),
        "second_gate_up": jnp.clip(jnp.exp(math.log(557.056) - 1.3981289 * jax.random.uniform(keys[15], (MODEL_WIDTH, 2, FF), jnp.float32) ** level_of(keys[15], (MODEL_WIDTH, 2, FF), ((0, 8), (2, 4)), -0.2, 0.2)), 137.6256, 557.056),
        "second_down": jnp.clip(jnp.exp(math.log(1245.184) - 1.3862944 * jax.random.uniform(keys[16], (FF // 128, 128, MODEL_WIDTH), jnp.float32) ** level_of(keys[16], (FF // 128, 128, MODEL_WIDTH), ((0, 4), (1, 8)), -0.2, 0.2)), 311.296, 1245.184),
        "second_gains": jnp.clip(jnp.exp(math.log(32768.0) - 3.6888794 * jax.random.uniform(keys[17], (2 * MODEL_WIDTH + 2 * HEAD_SIZE,), jnp.float32) ** level_of(keys[17], (2 * MODEL_WIDTH + 2 * HEAD_SIZE,), ((0, 8),), -0.2, 0.2)), 819.2, 32768.0),
    }


EPS = 1e-06
THETA = 1000000.0
BETA_ONE = 0.9
BETA_TWO = 0.95
ADAM_EPS = 1e-08
DECAY = 0.1
TOP_PRECISION = lax.Precision.HIGHEST

@jax.custom_vjp
def low(v):
    return lax.optimization_barrier(v.astype(jnp.bfloat16)).astype(jnp.float32)

@jax.custom_vjp
def reduced_backward(v):
    return v

def low_keep(v):
    return (low(v), None)

def low_pass(kept, grad):
    return (grad,)

def back_keep(v):
    return (v, None)

def back_low(kept, grad):
    return (low(grad),)
low.defvjp(low_keep, low_pass)
reduced_backward.defvjp(back_keep, back_low)

def norm_rows(values, scales):
    return values * lax.rsqrt(lax.optimization_barrier(jnp.mean(values * values, axis=-1, keepdims=True)) + EPS) * scales

def rotate(values, cosine_table, sine_table):
    middle_at = values.shape[-1] // 2
    first_half = values[..., :middle_at]
    second_half = values[..., middle_at:]
    return jnp.concatenate([first_half * cosine_table - second_half * sine_table, second_half * cosine_table + first_half * sine_table], axis=-1)

def layout(lengths, row_total_count):
    doc_ends = jnp.cumsum(lengths).astype(jnp.int32)
    starts = (doc_ends - lengths).astype(jnp.int32)
    index_of_row = jnp.arange(row_total_count, dtype=jnp.int32)
    document_label = lax.optimization_barrier(jnp.sum((index_of_row[:, None] >= doc_ends[None, :]).astype(jnp.int32), axis=1)).astype(jnp.int32)
    member = document_label[:, None] == jnp.arange(lengths.shape[0], dtype=jnp.int32)[None, :]
    offset = lax.optimization_barrier(jnp.sum(jnp.where(member, starts[None, :], 0), axis=1)).astype(jnp.int32)
    return (document_label, (index_of_row - offset).astype(jnp.int32), index_of_row)

def angles(position):
    freq_index = jnp.arange(HEAD_SIZE // 2, dtype=jnp.float32)
    inverse = THETA ** (-2.0 * freq_index / HEAD_SIZE)
    turned = position.astype(jnp.float32)[:, None] * inverse[None, :]
    return (jnp.cos(turned), jnp.sin(turned))

def group_forward(weights, rows_float, lengths):
    projection_weight, w_out, w_gate_up, w_down, gains = weights
    row_total_count = rows_float.shape[0]
    query_group_width = QUERY_HEADS // KEY_VALUE_HEADS
    document_label, position, index_of_row = layout(lengths, row_total_count)
    cosine_table, sine_table = angles(position)
    gain_attn = gains[:MODEL_WIDTH]
    gain_mlp = gains[MODEL_WIDTH:2 * MODEL_WIDTH]
    gain_query = gains[2 * MODEL_WIDTH:2 * MODEL_WIDTH + HEAD_SIZE]
    gain_key = gains[2 * MODEL_WIDTH + HEAD_SIZE:]
    attention_normed = low(norm_rows(rows_float, gain_attn))
    projected_unrotated = reduced_backward(jnp.dot(attention_normed, projection_weight.reshape(MODEL_WIDTH, -1), precision=TOP_PRECISION)).reshape(row_total_count, KEY_VALUE_HEADS, query_group_width + 2, HEAD_SIZE)
    query_rows = low(rotate(norm_rows(projected_unrotated[:, :, :query_group_width], gain_query), cosine_table[:, None, None, :], sine_table[:, None, None, :]))
    keys_all = low(rotate(norm_rows(projected_unrotated[:, :, query_group_width], gain_key), cosine_table[:, None, :], sine_table[:, None, :]))
    values_all = low(projected_unrotated[:, :, query_group_width + 1])
    rows_per_block = min(512, row_total_count)
    block_number = row_total_count // rows_per_block
    score_scale = HEAD_SIZE ** (-0.5)

    def attention_apply(pieces):
        query_block, seg_block, index_block = pieces
        scores = reduced_backward(jnp.einsum('qjgd,kjd->jgqk', query_block, keys_all, precision=TOP_PRECISION) * score_scale)
        allowed = (seg_block[:, None] == document_label[None, :]) & (index_block[:, None] >= index_of_row[None, :])
        scores = jnp.where(allowed, scores, -1e+30)
        highest = lax.optimization_barrier(jnp.max(scores, axis=-1, keepdims=True))
        exponent = jnp.exp(scores - highest)
        shares = low(exponent / lax.optimization_barrier(jnp.sum(exponent, axis=-1, keepdims=True)))
        return jnp.einsum('jgqk,kjd->qjgd', shares, values_all, precision=TOP_PRECISION)
    attention_blend = lax.map(jax.checkpoint(attention_apply), (query_rows.reshape(block_number, rows_per_block, KEY_VALUE_HEADS, query_group_width, HEAD_SIZE), document_label.reshape(block_number, rows_per_block), index_of_row.reshape(block_number, rows_per_block)))
    heads_out = low(reduced_backward(attention_blend.reshape(row_total_count, QUERY_HEADS * HEAD_SIZE)))
    attn_rows = reduced_backward(jnp.dot(heads_out, w_out.reshape(QUERY_HEADS * HEAD_SIZE, MODEL_WIDTH), precision=TOP_PRECISION))
    middle = rows_float + attn_rows
    normed_two = low(norm_rows(middle, gain_mlp))
    gate_up = reduced_backward(jnp.dot(normed_two, w_gate_up.reshape(MODEL_WIDTH, 2 * FF), precision=TOP_PRECISION)).reshape(row_total_count, 2, FF)
    gating = gate_up[:, 0]
    upward = gate_up[:, 1]
    hidden = low(gating * jax.nn.sigmoid(gating) * upward)
    mlp_rows = reduced_backward(jnp.dot(hidden, w_down.reshape(FF, MODEL_WIDTH), precision=TOP_PRECISION))
    return middle + mlp_rows

def layer_forward(tokens_float, weights, lengths):
    grouped = tokens_float.reshape(N_DP, TOK_GRP, MODEL_WIDTH)
    run_group = jax.checkpoint(group_forward)

    def visit_group(running, pieces):
        return (running, run_group(weights, pieces[0], pieces[1]))
    unused, outputs = lax.scan(visit_group, None, (grouped, lengths))
    return outputs.reshape(TOKEN_TOTAL, MODEL_WIDTH)

def adamw_update(master, moment_one, moment_two, gradient, step_rate, decay_rate):
    next_one = BETA_ONE * moment_one + (1.0 - BETA_ONE) * gradient
    next_two = BETA_TWO * moment_two + (1.0 - BETA_TWO) * gradient * gradient
    one_hat = next_one / (1.0 - BETA_ONE ** STEP)
    two_hat = next_two / (1.0 - BETA_TWO ** STEP)
    next_master = master - step_rate * (one_hat / (jnp.sqrt(two_hat) + ADAM_EPS) + decay_rate * master)
    return (next_one, next_two, next_master)

def reference(tokens, cotangent, lengths, projection_weight, w_out, w_gate_up, w_down, gains, first_moment_projection, first_out, first_gate_up, first_down, first_gains, second_moment_projection, second_out, second_gate_up, second_down, second_gains):
    masters = (projection_weight, w_out, w_gate_up, w_down, gains)

    def run_layer(tokens_float, weights):
        return layer_forward(tokens_float, tuple((low(weight) for weight in weights)), lengths)
    result, pullback = jax.vjp(run_layer, tokens.astype(jnp.float32), masters)
    grad_tokens, gradients = pullback(cotangent.astype(jnp.float32))
    step_rates = (2.0 * MODEL_WIDTH ** (-0.5), 2.0 * (QUERY_HEADS * HEAD_SIZE // 64) ** (-0.5), 2.0 * MODEL_WIDTH ** (-0.5), 2.0 * FF ** (-0.5), 0.5)
    decay_rates = (DECAY, DECAY, DECAY, DECAY, 0.0)
    firsts = (first_moment_projection, first_out, first_gate_up, first_down, first_gains)
    seconds = (second_moment_projection, second_out, second_gate_up, second_down, second_gains)
    updated = [adamw_update(masters[number], firsts[number], seconds[number], gradients[number], step_rates[number], decay_rates[number]) for number in range(5)]
    return (result.astype(jnp.bfloat16), grad_tokens, updated[0][2], updated[1][2], updated[2][2], updated[3][2], updated[4][2], updated[0][0], updated[1][0], updated[2][0], updated[3][0], updated[4][0], updated[0][1], updated[1][1], updated[2][1], updated[3][1], updated[4][1])
```

```python
import jax
import jax.numpy as jnp
from jax import lax
from jax.experimental import pallas as pl
from jax.experimental.pallas import tpu as pltpu
from jax.sharding import PartitionSpec as P

MODEL_WIDTH = 1024
QUERY_HEADS = 16
KEY_VALUE_HEADS = 8
HEAD_SIZE = 128
FF = 3072
STEP = 10

EPS = 1e-06
THETA = 1000000.0
BETA_ONE = 0.9
BETA_TWO = 0.95
ADAM_EPS = 1e-08
DECAY = 0.1

GROUP = QUERY_HEADS // KEY_VALUE_HEADS
SLOTS = GROUP + 2
SCALE = HEAD_SIZE ** (-0.5)
LOG2E = 1.4426950408889634
BLOCK = 256
VMEM_LIMIT = 56 * 1024 * 1024
F32 = jnp.float32
BF16 = jnp.bfloat16


def norm_rows(values, scales):
    return values * lax.rsqrt(jnp.mean(values * values, axis=-1, keepdims=True) + EPS) * scales


def norm_back(values, scales, grad):
    r = lax.rsqrt(jnp.mean(values * values, axis=-1, keepdims=True) + EPS)
    u = grad * scales
    back = r * u - values * (r * r * r) * jnp.mean(u * values, axis=-1, keepdims=True)
    return back, jnp.sum(grad * values * r, axis=0)


def adamw_update(master, moment_one, moment_two, gradient, step_rate, decay_rate):
    next_one = BETA_ONE * moment_one + (1.0 - BETA_ONE) * gradient
    next_two = BETA_TWO * moment_two + (1.0 - BETA_TWO) * gradient * gradient
    one_hat = next_one / (1.0 - BETA_ONE**STEP)
    two_hat = next_two / (1.0 - BETA_TWO**STEP)
    next_master = master - step_rate * (
        one_hat / (jnp.sqrt(two_hat) + ADAM_EPS) + decay_rate * master
    )
    return (next_one, next_two, next_master)


def nt(a, b):
    return lax.dot_general(a, b, (((1,), (1,)), ((), ())), preferred_element_type=F32)


def nn(a, b):
    return jnp.dot(a, b, preferred_element_type=F32)


def head_rotated(x, gain, cos, sin):
    r = lax.rsqrt(jnp.mean(x * x, axis=-1, keepdims=True) + EPS)
    y = x * r * gain
    return y * cos + pltpu.roll(y, HEAD_SIZE // 2, 1) * sin


def head_back(x, gain, cos, sin, grad):
    r = lax.rsqrt(jnp.mean(x * x, axis=-1, keepdims=True) + EPS)
    turned = grad * cos - pltpu.roll(grad, HEAD_SIZE // 2, 1) * sin
    u = turned * gain
    back = r * u - x * (r * r * r) * jnp.mean(u * x, axis=-1, keepdims=True)
    return back, jnp.sum(turned * x * r, axis=0, keepdims=True)


def block_at(index, flip):
    return pl.ds(pl.multiple_of((index ^ flip) * BLOCK, BLOCK), BLOCK)


def allowed_block(key_block, query_block, start):
    keys = key_block * BLOCK + lax.broadcasted_iota(jnp.int32, (BLOCK, BLOCK), 0)
    queries = query_block * BLOCK + lax.broadcasted_iota(jnp.int32, (BLOCK, BLOCK), 1)
    return (keys >= start) & (keys <= queries)


def attend_kernel(info, qkv, cos, sin, gain_q, gain_k, start, out, logs, qs, ks, vt):
    blocks = qkv.shape[0] // BLOCK
    flip = info[blocks]

    def prepare(i, _):
        rows = pl.ds(pl.multiple_of(i * BLOCK, BLOCK), BLOCK)
        c, s = cos[rows, :], sin[rows, :]
        for h in range(GROUP):
            x = qkv[rows, h * HEAD_SIZE : (h + 1) * HEAD_SIZE]
            qs[h, rows, :] = head_rotated(x, gain_q[...], c, s).astype(BF16)
        x = qkv[rows, GROUP * HEAD_SIZE : (GROUP + 1) * HEAD_SIZE]
        ks[rows, :] = head_rotated(x, gain_k[...], c, s).astype(BF16)
        x = qkv[rows, (GROUP + 1) * HEAD_SIZE :]
        vt[:, rows] = x.T.astype(BF16)
        return 0

    lax.fori_loop(0, blocks, prepare, 0)

    def one_block(b, _):
        here = block_at(b, flip)
        first = start[:, here]
        queries = [qs[h, here, :] for h in range(GROUP)]

        def keys_step(kb, carry):
            there = block_at(kb, flip)
            k, v = ks[there, :], vt[:, there]
            allowed = allowed_block(kb, b, first)
            after = []
            for h in range(GROUP):
                total, blend = carry[h]
                p = jnp.where(allowed, jnp.exp2(nt(k, queries[h]) * (SCALE * LOG2E)), 0.0)
                after.append(
                    (total + jnp.sum(p, axis=0, keepdims=True), blend + nn(v, p.astype(BF16)))
                )
            return tuple(after)

        zero = (jnp.zeros((1, BLOCK), F32), jnp.zeros((HEAD_SIZE, BLOCK), F32))
        done = lax.fori_loop(info[b], b + 1, keys_step, (zero,) * GROUP)
        for h in range(GROUP):
            total, blend = done[h]
            out[here, h * HEAD_SIZE : (h + 1) * HEAD_SIZE] = (blend / total).T.astype(BF16)
            logs[0, h : h + 1, here] = jnp.log2(total)
        return 0

    lax.fori_loop(0, blocks, one_block, 0)


def attend_back_kernel(
    info, qkv, cos, sin, gain_q, gain_k, start, logs, out, grad_out,
    grad_qkv, grad_gains, qs, ks, kt, vs, grad_k, grad_v,
):
    blocks = qkv.shape[0] // BLOCK
    flip = info[blocks]
    grad_gains[...] = jnp.zeros(grad_gains.shape, F32)

    def prepare(i, _):
        rows = pl.ds(pl.multiple_of(i * BLOCK, BLOCK), BLOCK)
        c, s = cos[rows, :], sin[rows, :]
        for h in range(GROUP):
            x = qkv[rows, h * HEAD_SIZE : (h + 1) * HEAD_SIZE]
            qs[h, rows, :] = head_rotated(x, gain_q[...], c, s).astype(BF16)
        x = qkv[rows, GROUP * HEAD_SIZE : (GROUP + 1) * HEAD_SIZE]
        turned = head_rotated(x, gain_k[...], c, s)
        ks[rows, :] = turned.astype(BF16)
        kt[:, rows] = turned.T.astype(BF16)
        vs[rows, :] = qkv[rows, (GROUP + 1) * HEAD_SIZE :].astype(BF16)
        grad_k[rows, :] = jnp.zeros((BLOCK, HEAD_SIZE), F32)
        grad_v[rows, :] = jnp.zeros((BLOCK, HEAD_SIZE), F32)
        return 0

    lax.fori_loop(0, blocks, prepare, 0)

    def one_block(b, _):
        here = block_at(b, flip)
        first = start[:, here]
        queries, gradients, across, log = [], [], [], []
        for h in range(GROUP):
            lanes = slice(h * HEAD_SIZE, (h + 1) * HEAD_SIZE)
            g = grad_out[here, lanes]
            queries.append(qs[h, here, :])
            gradients.append(g)
            both = g.astype(F32) * out[here, lanes].astype(F32)
            across.append(jnp.sum(both.T, axis=0, keepdims=True))
            log.append(logs[0, h : h + 1, here])

        def keys_step(kb, carry):
            there = block_at(kb, flip)
            k, v, k_turned = ks[there, :], vs[there, :], kt[:, there]
            allowed = allowed_block(kb, b, first)
            after, add_k, add_v = [], 0.0, 0.0
            for h in range(GROUP):
                s = nt(k, queries[h])
                p = jnp.where(allowed, jnp.exp2(s * (SCALE * LOG2E) - log[h]), 0.0)
                d = (p * (nt(v, gradients[h]) - across[h])).astype(BF16)
                add_v = add_v + nn(p.astype(BF16), gradients[h])
                add_k = add_k + nn(d, queries[h])
                after.append(carry[h] + nn(k_turned, d))
            grad_k[there, :] += add_k
            grad_v[there, :] += add_v
            return tuple(after)

        zero = jnp.zeros((HEAD_SIZE, BLOCK), F32)
        done = lax.fori_loop(info[b], b + 1, keys_step, (zero,) * GROUP)
        c, s = cos[here, :], sin[here, :]
        for h in range(GROUP):
            lanes = slice(h * HEAD_SIZE, (h + 1) * HEAD_SIZE)
            back, gain = head_back(qkv[here, lanes], gain_q[...], c, s, done[h].T * SCALE)
            grad_qkv[here, lanes] = back.astype(BF16)
            grad_gains[0, 0:1, :] += gain
        return 0

    lax.fori_loop(0, blocks, one_block, 0)

    def finish(i, _):
        rows = pl.ds(pl.multiple_of(i * BLOCK, BLOCK), BLOCK)
        lanes = slice(GROUP * HEAD_SIZE, (GROUP + 1) * HEAD_SIZE)
        back, gain = head_back(
            qkv[rows, lanes], gain_k[...], cos[rows, :], sin[rows, :], grad_k[rows, :] * SCALE
        )
        grad_qkv[rows, lanes] = back.astype(BF16)
        grad_gains[0, 1:2, :] += gain
        grad_qkv[rows, (GROUP + 1) * HEAD_SIZE :] = grad_v[rows, :].astype(BF16)
        return 0

    lax.fori_loop(0, blocks, finish, 0)


def whole(shape):
    return pl.BlockSpec(shape, lambda j, info: (0,) * len(shape))


def attend(info, qkv, cos, sin, gain_q, gain_k, start):
    rows = qkv.shape[0]
    heads = qkv.shape[1] // (SLOTS * HEAD_SIZE)
    per_head = lambda width: pl.BlockSpec((rows, width), lambda j, info: (0, j))
    return pl.pallas_call(
        attend_kernel,
        grid_spec=pltpu.PrefetchScalarGridSpec(
            num_scalar_prefetch=1,
            grid=(heads,),
            in_specs=[
                per_head(SLOTS * HEAD_SIZE),
                whole((rows, HEAD_SIZE)),
                whole((rows, HEAD_SIZE)),
                whole((1, HEAD_SIZE)),
                whole((1, HEAD_SIZE)),
                whole((1, rows)),
            ],
            out_specs=[
                per_head(GROUP * HEAD_SIZE),
                pl.BlockSpec((1, GROUP, rows), lambda j, info: (j, 0, 0)),
            ],
            scratch_shapes=[
                pltpu.VMEM((GROUP, rows, HEAD_SIZE), BF16),
                pltpu.VMEM((rows, HEAD_SIZE), BF16),
                pltpu.VMEM((HEAD_SIZE, rows), BF16),
            ],
        ),
        out_shape=[
            jax.ShapeDtypeStruct((rows, heads * GROUP * HEAD_SIZE), BF16),
            jax.ShapeDtypeStruct((heads, GROUP, rows), F32),
        ],
        compiler_params=pltpu.CompilerParams(
            dimension_semantics=("arbitrary",), vmem_limit_bytes=VMEM_LIMIT
        ),
        cost_estimate=pl.CostEstimate(
            flops=8_000_000_000, bytes_accessed=14_000_000, transcendentals=6_000_000
        ),
        name="attend",
    )(info, qkv, cos, sin, gain_q, gain_k, start)


def attend_back(info, qkv, cos, sin, gain_q, gain_k, start, logs, out, grad_out):
    rows = qkv.shape[0]
    heads = qkv.shape[1] // (SLOTS * HEAD_SIZE)
    per_head = lambda width: pl.BlockSpec((rows, width), lambda j, info: (0, j))
    return pl.pallas_call(
        attend_back_kernel,
        grid_spec=pltpu.PrefetchScalarGridSpec(
            num_scalar_prefetch=1,
            grid=(heads,),
            in_specs=[
                per_head(SLOTS * HEAD_SIZE),
                whole((rows, HEAD_SIZE)),
                whole((rows, HEAD_SIZE)),
                whole((1, HEAD_SIZE)),
                whole((1, HEAD_SIZE)),
                whole((1, rows)),
                pl.BlockSpec((1, GROUP, rows), lambda j, info: (j, 0, 0)),
                per_head(GROUP * HEAD_SIZE),
                per_head(GROUP * HEAD_SIZE),
            ],
            out_specs=[
                per_head(SLOTS * HEAD_SIZE),
                pl.BlockSpec((1, 2, HEAD_SIZE), lambda j, info: (j, 0, 0)),
            ],
            scratch_shapes=[
                pltpu.VMEM((GROUP, rows, HEAD_SIZE), BF16),
                pltpu.VMEM((rows, HEAD_SIZE), BF16),
                pltpu.VMEM((HEAD_SIZE, rows), BF16),
                pltpu.VMEM((rows, HEAD_SIZE), BF16),
                pltpu.VMEM((rows, HEAD_SIZE), F32),
                pltpu.VMEM((rows, HEAD_SIZE), F32),
            ],
        ),
        out_shape=[
            jax.ShapeDtypeStruct((rows, qkv.shape[1]), BF16),
            jax.ShapeDtypeStruct((heads, 2, HEAD_SIZE), F32),
        ],
        compiler_params=pltpu.CompilerParams(
            dimension_semantics=("arbitrary",), vmem_limit_bytes=VMEM_LIMIT
        ),
        cost_estimate=pl.CostEstimate(
            flops=20_000_000_000, bytes_accessed=20_000_000, transcendentals=6_000_000
        ),
        name="attend_back",
    )(info, qkv, cos, sin, gain_q, gain_k, start, logs, out, grad_out)


def flipped(value, axis, bit):
    return lax.ppermute(value, axis, [(i, i ^ bit) for i in range(lax.axis_size(axis))])


def gathered(value):
    across = flipped(value, "tensor", 2)
    beside = flipped(value, "tensor", 1)
    return [value, beside, across, flipped(across, "tensor", 1)]


def scattered(parts):
    near = parts[2].astype(F32) + flipped(parts[3], "tensor", 1).astype(F32)
    across = flipped(near.astype(BF16), "tensor", 2)
    own = parts[0].astype(F32) + flipped(parts[1], "tensor", 1).astype(F32)
    return own + across.astype(F32)


def per_device(
    tokens, cotangent, lengths,
    projection_weight, w_out, w_gate_up, w_down, gains,
    first_moment_projection, first_out, first_gate_up, first_down, first_gains,
    second_moment_projection, second_out, second_gate_up, second_down, second_gains,
):
    shards = lax.axis_size("tensor")
    spread = lax.axis_size("dp")
    me = lax.axis_index("tensor")
    local_rows = tokens.shape[0]
    rows = local_rows * shards
    blocks = rows // BLOCK
    kv_local = projection_weight.shape[1]
    hidden_local = w_gate_up.shape[2]
    out_heads, out_depth = w_out.shape[0], w_out.shape[1]
    down_blocks, down_depth = w_down.shape[0], w_down.shape[1]
    depth = projection_weight.shape[0]
    gain_count = gains.shape[0]

    pack_one = jnp.concatenate(
        [
            projection_weight.astype(BF16).reshape(depth, -1),
            w_out.astype(BF16).reshape(-1, MODEL_WIDTH),
            jnp.pad(gains.astype(BF16)[None, :], ((0, 15), (0, MODEL_WIDTH - gain_count))),
        ],
        axis=0,
    )
    half = MODEL_WIDTH // 2
    pieces = 2 * hidden_local // half
    pack_two = jnp.concatenate(
        [
            w_gate_up.astype(BF16).reshape(depth, pieces, half).swapaxes(0, 1).reshape(-1, half),
            w_down.astype(BF16).reshape(-1, 2, half).swapaxes(0, 1).reshape(-1, half),
        ],
        axis=0,
    )
    full_one = lax.all_gather(pack_one, "dp", axis=0, tiled=False)
    full_two = lax.all_gather(pack_two, "dp", axis=0, tiled=False)
    qkv_matrix = full_one[:, :depth].reshape(MODEL_WIDTH, -1)
    out_matrix = (
        full_one[:, depth : depth + out_heads * out_depth]
        .reshape(spread, out_heads, out_depth, MODEL_WIDTH)
        .swapaxes(0, 1)
        .reshape(-1, MODEL_WIDTH)
    )
    gains_all = full_one[:, depth + out_heads * out_depth, :gain_count].reshape(-1).astype(F32)
    gate_up_matrix = (
        full_two[:, : pieces * depth]
        .reshape(spread, pieces, depth, half)
        .swapaxes(1, 2)
        .reshape(MODEL_WIDTH, -1)
    )
    down_matrix = (
        full_two[:, pieces * depth :]
        .reshape(spread, 2, down_blocks, down_depth, half)
        .transpose(2, 0, 3, 1, 4)
        .reshape(-1, MODEL_WIDTH)
    )
    gain_attn = gains_all[:MODEL_WIDTH]
    gain_mlp = gains_all[MODEL_WIDTH : 2 * MODEL_WIDTH]
    gain_query = gains_all[2 * MODEL_WIDTH : 2 * MODEL_WIDTH + HEAD_SIZE]
    gain_key = gains_all[2 * MODEL_WIDTH + HEAD_SIZE :]

    doc_ends = jnp.cumsum(lengths[0])
    doc_starts = doc_ends - lengths[0]

    def start_of(index):
        return jnp.max(
            jnp.where(index[:, None] >= doc_starts[None, :], doc_starts[None, :], 0), axis=1
        )

    order = me ^ jnp.arange(shards, dtype=jnp.int32)
    index_of_row = (
        order[:, None] * local_rows + jnp.arange(local_rows, dtype=jnp.int32)[None, :]
    ).reshape(-1)
    start_of_row = start_of(index_of_row)
    position = index_of_row - start_of_row
    inverse = THETA ** (-2.0 * jnp.arange(HEAD_SIZE // 2, dtype=F32) / HEAD_SIZE)
    turned = position.astype(F32)[:, None] * inverse[None, :]
    cosine, sine = jnp.cos(turned), jnp.sin(turned)
    cos = jnp.concatenate([cosine, cosine], axis=1)
    sin = jnp.concatenate([-sine, sine], axis=1)
    block_starts = start_of(jnp.arange(blocks, dtype=jnp.int32) * BLOCK) // BLOCK
    info = jnp.concatenate([block_starts, (me * (local_rows // BLOCK))[None]]).astype(jnp.int32)
    start_row = start_of_row[None, :]

    rows_float = tokens.astype(F32)
    tokens_all = jnp.concatenate(gathered(tokens), axis=0)
    normed_one = norm_rows(tokens_all.astype(F32), gain_attn).astype(BF16)
    qkv = nn(normed_one, qkv_matrix)
    heads_args = (info, qkv, cos, sin, gain_query[None, :], gain_key[None, :], start_row)
    heads_out, logs = attend(*heads_args)

    def shard(value, i):
        return value[i * local_rows : (i + 1) * local_rows]

    def partial_sums(product):
        return scattered([shard(product, i) for i in range(shards)])

    attn_rows = partial_sums(nn(heads_out, out_matrix).astype(BF16))
    middle = rows_float + attn_rows

    normed_two_own = norm_rows(middle, gain_mlp).astype(BF16)
    normed_two = jnp.concatenate(gathered(normed_two_own), axis=0)
    grad_all = jnp.concatenate(gathered(cotangent), axis=0)
    gate_up = nn(normed_two, gate_up_matrix)
    gate, up = gate_up[:, :hidden_local], gate_up[:, hidden_local:]
    gate_sig = jax.nn.sigmoid(gate)
    hidden = (gate * gate_sig * up).astype(BF16)
    grad_hidden = nt(grad_all, down_matrix)
    grad_gate = grad_hidden * up * (gate_sig + gate * gate_sig * (1.0 - gate_sig))
    grad_up = grad_hidden * gate * gate_sig
    grad_gate_up = jnp.concatenate([grad_gate.astype(BF16), grad_up.astype(BF16)], axis=1)
    grad_normed_two = partial_sums(nt(grad_gate_up, gate_up_matrix).astype(BF16))
    grad_middle_part, grad_gain_mlp = norm_back(middle, gain_mlp, grad_normed_two)
    grad_middle = cotangent.astype(F32) + grad_middle_part
    grad_middle_all = jnp.concatenate(gathered(grad_middle.astype(BF16)), axis=0)

    def over_rows(a, b):
        return lax.dot_general(a, b, (((0,), (0,)), ((), ())), preferred_element_type=F32)

    grad_down = over_rows(hidden, grad_all).astype(BF16)
    sum_down = lax.psum_scatter(
        grad_down.reshape(down_blocks, -1, MODEL_WIDTH), "dp", scatter_dimension=1, tiled=True
    ).astype(F32)
    grad_gate_up_w = over_rows(normed_two, grad_gate_up).astype(BF16)
    sum_gate_up = lax.psum_scatter(
        grad_gate_up_w, "dp", scatter_dimension=0, tiled=True
    ).astype(F32)
    mlp_rows = partial_sums(nn(hidden, down_matrix).astype(BF16))
    block_out = (middle + mlp_rows).astype(BF16)

    grad_heads = nt(grad_middle_all, out_matrix).astype(BF16)
    grad_out_w = over_rows(heads_out, grad_middle_all).astype(BF16)
    sum_out = lax.psum_scatter(
        grad_out_w.reshape(out_heads, -1, MODEL_WIDTH), "dp", scatter_dimension=1, tiled=True
    ).astype(F32)
    grad_qkv, grad_head_gains = attend_back(*heads_args, logs, heads_out, grad_heads)
    grad_qkv_w = over_rows(normed_one, grad_qkv)
    sum_qkv = lax.psum_scatter(
        grad_qkv_w.astype(BF16), "dp", scatter_dimension=0, tiled=True
    ).astype(F32)
    grad_normed_one = partial_sums(nt(grad_qkv, qkv_matrix).astype(BF16))
    grad_rows_part, _ = norm_back(rows_float, gain_attn, grad_normed_one)
    grad_tokens = grad_middle + grad_rows_part

    grad_gain_attn = jnp.sum(qkv_matrix.astype(F32) * grad_qkv_w, axis=1) / gain_attn
    gain_sums = jnp.concatenate(
        [grad_gain_attn, grad_gain_mlp, jnp.sum(grad_head_gains, axis=0).reshape(-1)]
    )
    for axis in ("tensor", "dp"):
        bit = 1
        while bit < lax.axis_size(axis):
            gain_sums = gain_sums + flipped(gain_sums, axis, bit)
            bit *= 2
    sum_gains = lax.dynamic_slice(
        gain_sums, (lax.axis_index("dp") * gain_count,), (gain_count,)
    )

    upd_qkv = adamw_update(
        projection_weight, first_moment_projection, second_moment_projection,
        sum_qkv.reshape(projection_weight.shape), 2.0 * MODEL_WIDTH ** (-0.5), DECAY,
    )
    upd_out = adamw_update(
        w_out, first_out, second_out, sum_out,
        2.0 * (QUERY_HEADS * HEAD_SIZE // 64) ** (-0.5), DECAY,
    )
    upd_gate_up = adamw_update(
        w_gate_up, first_gate_up, second_gate_up, sum_gate_up.reshape(w_gate_up.shape),
        2.0 * MODEL_WIDTH ** (-0.5), DECAY,
    )
    upd_down = adamw_update(w_down, first_down, second_down, sum_down, 2.0 * FF ** (-0.5), DECAY)
    upd_gains = adamw_update(gains, first_gains, second_gains, sum_gains, 0.5, 0.0)
    updates = (upd_qkv, upd_out, upd_gate_up, upd_down, upd_gains)
    return (
        block_out,
        grad_tokens,
        *(update[2] for update in updates),
        *(update[0] for update in updates),
        *(update[1] for update in updates),
    )


def solution(mesh):
    weights = (
        P("dp", "tensor", None),
        P("tensor", "dp", None),
        P("dp", None, "tensor"),
        P("tensor", "dp", None),
        P("dp"),
    )
    batch = P(("dp", "tensor"), None)
    return jax.shard_map(
        per_device,
        mesh=mesh,
        in_specs=(batch, batch, P("dp", None), *weights, *weights, *weights),
        out_specs=(batch, batch, *weights, *weights, *weights),
        check_vma=False,
    )
```

```python
import jax
import jax.numpy as jnp
from jax import lax
from jax.experimental import pallas as pl
from jax.experimental.pallas import tpu as pltpu
from jax.sharding import PartitionSpec as P

MODEL_WIDTH = 1024
QUERY_HEADS = 16
KEY_VALUE_HEADS = 8
HEAD_SIZE = 128
FF = 3072
STEP = 10

EPS = 1e-06
THETA = 1000000.0
BETA_ONE = 0.9
BETA_TWO = 0.95
ADAM_EPS = 1e-08
DECAY = 0.1

GROUP = QUERY_HEADS // KEY_VALUE_HEADS
SLOTS = GROUP + 2
SCALE = HEAD_SIZE ** (-0.5)
LOG2E = 1.4426950408889634
BLOCK = 256
VMEM_LIMIT = 48 * 1024 * 1024
RING = (0, 2, 4, 6, 7, 5, 3, 1)
F32 = jnp.float32
BF16 = jnp.bfloat16


def norm_rows(values, scales):
    return values * lax.rsqrt(jnp.mean(values * values, axis=-1, keepdims=True) + EPS) * scales


def norm_back(values, scales, grad):
    r = lax.rsqrt(jnp.mean(values * values, axis=-1, keepdims=True) + EPS)
    u = grad * scales
    back = r * u - values * (r * r * r) * jnp.mean(u * values, axis=-1, keepdims=True)
    return back, jnp.sum(grad * values * r, axis=0)


def adamw_update(master, moment_one, moment_two, gradient, step_rate, decay_rate):
    next_one = BETA_ONE * moment_one + (1.0 - BETA_ONE) * gradient
    next_two = BETA_TWO * moment_two + (1.0 - BETA_TWO) * gradient * gradient
    one_hat = next_one / (1.0 - BETA_ONE**STEP)
    two_hat = next_two / (1.0 - BETA_TWO**STEP)
    next_master = master - step_rate * (
        one_hat / (jnp.sqrt(two_hat) + ADAM_EPS) + decay_rate * master
    )
    return (next_one, next_two, next_master)


def nt(a, b):
    return lax.dot_general(a, b, (((1,), (1,)), ((), ())), preferred_element_type=F32)


def nn(a, b):
    return jnp.dot(a, b, preferred_element_type=F32)


def head_rotated(x, gain, cos, sin):
    r = lax.rsqrt(jnp.mean(x * x, axis=-1, keepdims=True) + EPS)
    y = x * r * gain
    return y * cos + pltpu.roll(y, HEAD_SIZE // 2, 1) * sin


def head_back(x, gain, cos, sin, grad):
    r = lax.rsqrt(jnp.mean(x * x, axis=-1, keepdims=True) + EPS)
    turned = grad * cos - pltpu.roll(grad, HEAD_SIZE // 2, 1) * sin
    u = turned * gain
    back = r * u - x * (r * r * r) * jnp.mean(u * x, axis=-1, keepdims=True)
    return back, jnp.sum(turned * x * r, axis=0, keepdims=True)


def at_block(index):
    return pl.ds(pl.multiple_of(index * BLOCK, BLOCK), BLOCK)


def allowed_block(key_block, query_block, start):
    keys = key_block * BLOCK + lax.broadcasted_iota(jnp.int32, (BLOCK, BLOCK), 0)
    queries = query_block * BLOCK + lax.broadcasted_iota(jnp.int32, (BLOCK, BLOCK), 1)
    return (keys >= start) & (keys <= queries)


def lanes_of(h):
    return slice(h * HEAD_SIZE, (h + 1) * HEAD_SIZE)


def project_kernel(
    x, gain, matrix, cos, sin, gain_q, gain_k, normed, raw_q, raw_k, q, k, v, k_turned, v_turned
):
    h = norm_rows(x[...].astype(F32), gain[...]).astype(BF16)
    normed[...] = h
    c, s = cos[...], sin[...]
    for j in range(matrix.shape[1] // (SLOTS * HEAD_SIZE)):
        base = j * SLOTS * HEAD_SIZE
        part = nn(h, matrix[:, base : base + SLOTS * HEAD_SIZE])
        for g in range(GROUP):
            value = part[:, lanes_of(g)]
            raw_q[:, lanes_of(j * GROUP + g)] = value
            q[:, lanes_of(j * GROUP + g)] = head_rotated(value, gain_q[...], c, s).astype(BF16)
        value = part[:, lanes_of(GROUP)]
        raw_k[:, lanes_of(j)] = value
        turned = head_rotated(value, gain_k[...], c, s)
        k[:, lanes_of(j)] = turned.astype(BF16)
        k_turned[lanes_of(j), :] = turned.T.astype(BF16)
        value = part[:, lanes_of(GROUP + 1)]
        v[:, lanes_of(j)] = value.astype(BF16)
        v_turned[lanes_of(j), :] = value.T.astype(BF16)


def attend_kernel(offset, info, q, k, v_turned, start, out, logs):
    blocks = k.shape[0] // BLOCK
    flip = info[blocks]

    def one_block(i, _):
        here = at_block(i)
        b = (i + offset) ^ flip
        first = start[:, here]
        queries = [q[here, lanes_of(h)] for h in range(GROUP)]

        def keys_step(kb, carry):
            there = at_block(kb ^ flip)
            key, value = k[there, :], v_turned[:, there]
            allowed = allowed_block(kb, b, first)
            after = []
            for h in range(GROUP):
                total, blend = carry[h]
                p = jnp.where(allowed, jnp.exp2(nt(key, queries[h]) * (SCALE * LOG2E)), 0.0)
                after.append(
                    (total + jnp.sum(p, axis=0, keepdims=True), blend + nn(value, p.astype(BF16)))
                )
            return tuple(after)

        zero = (jnp.zeros((1, BLOCK), F32), jnp.zeros((HEAD_SIZE, BLOCK), F32))
        done = lax.fori_loop(info[b], b + 1, keys_step, (zero,) * GROUP)
        for h in range(GROUP):
            total, blend = done[h]
            out[here, lanes_of(h)] = (blend / total).T.astype(BF16)
            logs[0, h : h + 1, here] = jnp.log2(total)
        return 0

    lax.fori_loop(0, q.shape[0] // BLOCK, one_block, 0)


def back_blocks(
    offset, info, q, k, v, k_turned, start, logs, out, grad_out, raw_q, cos, sin, gain_q,
    grad_k, grad_v, store,
):
    flip = info[k.shape[0] // BLOCK]

    def one_block(i, total_gain):
        here = at_block(i)
        b = (i + offset) ^ flip
        first = start[:, here]
        queries, gradients, across, log = [], [], [], []
        for h in range(GROUP):
            g = grad_out[here, lanes_of(h)]
            queries.append(q[here, lanes_of(h)])
            gradients.append(g)
            both = g.astype(F32) * out[here, lanes_of(h)].astype(F32)
            across.append(jnp.sum(both.T, axis=0, keepdims=True))
            log.append(logs[0, h : h + 1, here])

        def keys_step(kb, carry):
            there = at_block(kb ^ flip)
            key, value, key_turned = k[there, :], v[there, :], k_turned[:, there]
            allowed = allowed_block(kb, b, first)
            after, add_k, add_v = [], 0.0, 0.0
            for h in range(GROUP):
                s = nt(key, queries[h])
                p = jnp.where(allowed, jnp.exp2(s * (SCALE * LOG2E) - log[h]), 0.0)
                d = (p * (nt(value, gradients[h]) - across[h])).astype(BF16)
                add_v = add_v + nn(p.astype(BF16), gradients[h])
                add_k = add_k + nn(d, queries[h])
                after.append(carry[h] + nn(key_turned, d))
            grad_k[there, :] += add_k
            grad_v[there, :] += add_v
            return tuple(after)

        zero = jnp.zeros((HEAD_SIZE, BLOCK), F32)
        done = lax.fori_loop(info[b], b + 1, keys_step, (zero,) * GROUP)
        c, s = cos[here, :], sin[here, :]
        for h in range(GROUP):
            back, gain = head_back(raw_q[here, lanes_of(h)], gain_q[...], c, s, done[h].T * SCALE)
            store(i, h, back.astype(BF16))
            total_gain = total_gain + gain
        return total_gain

    return lax.fori_loop(0, q.shape[0] // BLOCK, one_block, jnp.zeros((1, HEAD_SIZE), F32))


def back_own_kernel(
    info, q, k, v, k_turned, start, logs, out, grad_out, raw_q, cos, sin, gain_q,
    grad_q, grad_k, grad_v, grad_gain,
):
    grad_k[...] = jnp.zeros(grad_k.shape, F32)
    grad_v[...] = jnp.zeros(grad_v.shape, F32)

    def store(i, h, value):
        grad_q[at_block(i), lanes_of(h)] = value

    grad_gain[0, :, :] = back_blocks(
        0, info, q, k, v, k_turned, start, logs, out, grad_out, raw_q, cos, sin, gain_q,
        grad_k, grad_v, store,
    )


def back_other_kernel(
    info, q, k, v, k_turned, start, logs, out, grad_out, raw_q, cos, sin, gain_q,
    cos_all, sin_all, raw_k, gain_k, grad_q_own, grad_k_own, grad_v_own,
    grad_qkv, grad_gains, grad_k, grad_v,
):
    half = q.shape[0] // BLOCK
    blocks = k.shape[0] // BLOCK
    queries = GROUP * HEAD_SIZE
    grad_k[...] = grad_k_own[...]
    grad_v[...] = grad_v_own[...]
    grad_qkv[: half * BLOCK, :queries] = grad_q_own[...]

    def store(i, h, value):
        grad_qkv[at_block(i + half), lanes_of(h)] = value

    grad_gains[0:1, :] = back_blocks(
        half, info, q, k, v, k_turned, start, logs, out, grad_out, raw_q, cos, sin, gain_q,
        grad_k, grad_v, store,
    )

    def finish(i, total_gain):
        rows = at_block(i)
        back, gain = head_back(
            raw_k[rows, :], gain_k[...], cos_all[rows, :], sin_all[rows, :], grad_k[rows, :] * SCALE
        )
        grad_qkv[rows, lanes_of(GROUP)] = back.astype(BF16)
        grad_qkv[rows, lanes_of(GROUP + 1)] = grad_v[rows, :].astype(BF16)
        return total_gain + gain

    grad_gains[1:2, :] = lax.fori_loop(0, blocks, finish, jnp.zeros((1, HEAD_SIZE), F32))


def feed_kernel(h, grad, gate_up, down, hidden, grad_gate_up, back_a, back_b, sum_a, sum_b):
    step = pl.program_id(0)
    width = down.shape[0]
    both = nn(h[...], gate_up[...])
    gate, up = both[:, :width], both[:, width:]
    sig = jax.nn.sigmoid(gate)
    gated = gate * sig
    value = (gated * up).astype(BF16)
    hidden[...] = value
    grad_hidden = nt(grad[...], down[...])
    grad_gate_up[:, :width] = (grad_hidden * up * (sig + gated * (1.0 - sig))).astype(BF16)
    grad_gate_up[:, width:] = (grad_hidden * gated).astype(BF16)
    back = nt(grad_gate_up[...], gate_up[...]).astype(BF16)
    total = nn(value, down[...]).astype(BF16)
    first = step < pl.num_programs(0) // 2

    @pl.when(first)
    def _():
        back_a[...] = back
        sum_a[...] = total

    @pl.when(jnp.logical_not(first))
    def _():
        back_b[...] = back
        sum_b[...] = total


def unproject_kernel(grad_zero, grad_one, matrix, out_a, out_b):
    width = grad_zero.shape[1]
    value = nt(grad_zero[...], matrix[:, :width]) + nt(grad_one[...], matrix[:, width:])
    value = value.astype(BF16)
    first = pl.program_id(0) < pl.num_programs(0) // 2

    @pl.when(first)
    def _():
        out_a[...] = value

    @pl.when(jnp.logical_not(first))
    def _():
        out_b[...] = value


def params(name, flops):
    return dict(
        compiler_params=pltpu.CompilerParams(
            dimension_semantics=("arbitrary",), vmem_limit_bytes=VMEM_LIMIT
        ),
        cost_estimate=pl.CostEstimate(flops=flops, bytes_accessed=8_000_000, transcendentals=0),
        name=name,
    )


def fixed(shape, index=None):
    index = (0,) * len(shape) if index is None else index
    return pl.BlockSpec(shape, lambda i, *_: index)


def shaped(shape, kind):
    return jax.ShapeDtypeStruct(shape, kind)


def project(x, gain, matrix, cos, sin, gain_q, gain_k):
    rows, width = x.shape
    heads = matrix.shape[1] // (SLOTS * HEAD_SIZE)
    by_rows = lambda n: pl.BlockSpec((BLOCK, n), lambda i: (i, 0))
    by_lanes = lambda n: pl.BlockSpec((n, BLOCK), lambda i: (0, i))
    q_width, k_width = heads * GROUP * HEAD_SIZE, heads * HEAD_SIZE
    return pl.pallas_call(
        project_kernel,
        grid=(rows // BLOCK,),
        in_specs=[
            by_rows(width), fixed((1, width)), fixed(matrix.shape), by_rows(HEAD_SIZE),
            by_rows(HEAD_SIZE), fixed((1, HEAD_SIZE)), fixed((1, HEAD_SIZE)),
        ],
        out_specs=[
            by_rows(width), by_rows(q_width), by_rows(k_width), by_rows(q_width),
            by_rows(k_width), by_rows(k_width), by_lanes(k_width), by_lanes(k_width),
        ],
        out_shape=[
            shaped((rows, width), BF16), shaped((rows, q_width), F32),
            shaped((rows, k_width), F32), shaped((rows, q_width), BF16),
            shaped((rows, k_width), BF16), shaped((rows, k_width), BF16),
            shaped((k_width, rows), BF16), shaped((k_width, rows), BF16),
        ],
        **params("project", 10_000_000_000),
    )(x, gain, matrix, cos, sin, gain_q, gain_k)


def head_specs(half, rows, head=None):
    at = (lambda j: j) if head is None else (lambda j: head)
    n = rows // 2
    return dict(
        q=pl.BlockSpec((n, GROUP * HEAD_SIZE), lambda j, info: (half, at(j))),
        k=pl.BlockSpec((rows, HEAD_SIZE), lambda j, info: (0, at(j))),
        turned=pl.BlockSpec((HEAD_SIZE, rows), lambda j, info: (at(j), 0)),
        start=pl.BlockSpec((1, n), lambda j, info: (0, half)),
        out=pl.BlockSpec((n, GROUP * HEAD_SIZE), lambda j, info: (0, at(j))),
        logs=pl.BlockSpec((1, GROUP, n), lambda j, info: (at(j), 0, 0)),
        angle=pl.BlockSpec((n, HEAD_SIZE), lambda j, info: (half, 0)),
    )


def attend(half, info, q, k, v_turned, start):
    rows = k.shape[0]
    n, heads = rows // 2, k.shape[1] // HEAD_SIZE
    s = head_specs(half, rows)
    return pl.pallas_call(
        lambda *refs: attend_kernel(half * n // BLOCK, *refs),
        grid_spec=pltpu.PrefetchScalarGridSpec(
            num_scalar_prefetch=1,
            grid=(heads,),
            in_specs=[s["q"], s["k"], s["turned"], s["start"]],
            out_specs=[s["out"], s["logs"]],
        ),
        out_shape=[shaped((n, q.shape[1]), BF16), shaped((heads, GROUP, n), F32)],
        **params("attend", 18_000_000_000),
    )(info, q, k, v_turned, start)


def attend_back_own(info, q, k, v, k_turned, start, logs, out, grad_out, raw_q, cos, sin, gain_q):
    rows = k.shape[0]
    n, heads = rows // 2, k.shape[1] // HEAD_SIZE
    s = head_specs(0, rows)
    return pl.pallas_call(
        back_own_kernel,
        grid_spec=pltpu.PrefetchScalarGridSpec(
            num_scalar_prefetch=1,
            grid=(heads,),
            in_specs=[
                s["q"], s["k"], s["k"], s["turned"], s["start"], s["logs"], s["out"], s["out"],
                s["q"], s["angle"], s["angle"], fixed((1, HEAD_SIZE)),
            ],
            out_specs=[
                s["out"], s["k"], s["k"],
                pl.BlockSpec((1, 1, HEAD_SIZE), lambda j, info: (j, 0, 0)),
            ],
        ),
        out_shape=[
            shaped((n, q.shape[1]), BF16), shaped(k.shape, F32), shaped(k.shape, F32),
            shaped((heads, 1, HEAD_SIZE), F32),
        ],
        **params("attend_back_own", 25_000_000_000),
    )(info, q, k, v, k_turned, start, logs, out, grad_out, raw_q, cos, sin, gain_q)


def attend_back_other(
    head, info, q, k, v, k_turned, start, logs, out, grad_out, raw_q, cos, sin, gain_q,
    raw_k, gain_k, grad_q, grad_k, grad_v,
):
    rows = k.shape[0]
    s = head_specs(1, rows, head)
    row = fixed((1, HEAD_SIZE))
    return pl.pallas_call(
        back_other_kernel,
        grid_spec=pltpu.PrefetchScalarGridSpec(
            num_scalar_prefetch=1,
            grid=(1,),
            in_specs=[
                s["q"], s["k"], s["k"], s["turned"], s["start"], s["logs"], s["out"], s["out"],
                s["q"], s["angle"], s["angle"], row,
                fixed((rows, HEAD_SIZE)), fixed((rows, HEAD_SIZE)), s["k"], row, s["out"], s["k"],
                s["k"],
            ],
            out_specs=[fixed((rows, SLOTS * HEAD_SIZE)), fixed((2, HEAD_SIZE))],
            scratch_shapes=[pltpu.VMEM((rows, HEAD_SIZE), F32)] * 2,
        ),
        out_shape=[shaped((rows, SLOTS * HEAD_SIZE), BF16), shaped((2, HEAD_SIZE), F32)],
        **params("attend_back_other", 14_000_000_000),
    )(
        info, q, k, v, k_turned, start, logs, out, grad_out, raw_q, cos, sin, gain_q,
        cos, sin, raw_k, gain_k, grad_q, grad_k, grad_v,
    )


def two_parts(rows, width):
    steps = rows // BLOCK // 2
    return (
        [
            pl.BlockSpec((BLOCK, width), lambda i: (jnp.minimum(i, steps - 1), 0)),
            pl.BlockSpec((BLOCK, width), lambda i: (jnp.maximum(i - steps, 0), 0)),
        ],
        [shaped((rows // 2, width), BF16)] * 2,
    )


def feed(h, grad, gate_up, down):
    rows, width = h.shape
    by_rows = lambda n: pl.BlockSpec((BLOCK, n), lambda i: (i, 0))
    specs, shapes = two_parts(rows, width)
    return pl.pallas_call(
        feed_kernel,
        grid=(rows // BLOCK,),
        in_specs=[by_rows(width), by_rows(width), fixed(gate_up.shape), fixed(down.shape)],
        out_specs=[by_rows(down.shape[0]), by_rows(gate_up.shape[1]), *specs, *specs],
        out_shape=[
            shaped((rows, down.shape[0]), BF16), shaped((rows, gate_up.shape[1]), BF16),
            *shapes, *shapes,
        ],
        **params("feed", 16_000_000_000),
    )(h, grad, gate_up, down)


def unproject(half, grad_zero, grad_one, matrix):
    rows, width = grad_zero.shape
    n = rows // 2
    steps = n // BLOCK
    by_rows = pl.BlockSpec((BLOCK, width), lambda i: (i + half * steps, 0))
    specs, shapes = two_parts(n, matrix.shape[0])
    return pl.pallas_call(
        unproject_kernel,
        grid=(steps,),
        in_specs=[by_rows, by_rows, fixed(matrix.shape)],
        out_specs=specs,
        out_shape=shapes,
        **params("unproject", 4_000_000_000),
    )(grad_zero, grad_one, matrix)


def flipped(value, axis, bit):
    return lax.ppermute(value, axis, [(i, i ^ bit) for i in range(lax.axis_size(axis))])


def together(*values):
    return lax.optimization_barrier(values)


def near_sum(part, beside):
    return part.astype(F32) + flipped(beside, "tensor", 1).astype(F32)


def ring_gather(value):
    n = lax.axis_size("dp")
    if n != len(RING):
        return lax.all_gather(value, "dp", axis=0, tiled=False)
    ring = jnp.array(RING, jnp.int32)
    at = jnp.argmax(ring == lax.axis_index("dp")).astype(jnp.int32)
    after = [(RING[i], RING[(i + 1) % n]) for i in range(n)]
    before = [(b, a) for a, b in after]
    pieces = {0: value}
    up = down = value
    for step in range(1, n // 2 + 1):
        up = lax.ppermute(up, "dp", after)
        pieces[-step] = up
        if step < n // 2:
            down = lax.ppermute(down, "dp", before)
            pieces[step] = down
    full = jnp.zeros((n,) + value.shape, value.dtype)
    for step, piece in pieces.items():
        full = lax.dynamic_update_index_in_dim(full, piece, ring[(at + step + n) % n], 0)
    return full


def exchanged_sum(parts, axis):
    n = lax.axis_size("dp")
    low = parts.astype(BF16)
    if n != len(RING):
        return jnp.squeeze(
            lax.psum_scatter(low, "dp", scatter_dimension=axis, tiled=True), axis
        ).astype(F32)
    me = lax.axis_index("dp")
    take = lambda a, i: lax.dynamic_index_in_dim(a, i, axis, keepdims=False)
    total = take(parts, me).astype(F32)
    for bit in range(1, n):
        total = total + flipped(take(low, me ^ bit), "dp", bit).astype(F32)
    return total


def per_device(
    tokens, cotangent, lengths,
    projection_weight, w_out, w_gate_up, w_down, gains,
    first_moment_projection, first_out, first_gate_up, first_down, first_gains,
    second_moment_projection, second_out, second_gate_up, second_down, second_gains,
):
    shards = lax.axis_size("tensor")
    spread = lax.axis_size("dp")
    me = lax.axis_index("tensor")
    local_rows = tokens.shape[0]
    rows = local_rows * shards
    blocks = rows // BLOCK
    kv_local = projection_weight.shape[1]
    hidden_local = w_gate_up.shape[2]
    out_heads, out_depth = w_out.shape[0], w_out.shape[1]
    down_blocks, down_depth = w_down.shape[0], w_down.shape[1]
    depth = projection_weight.shape[0]
    gain_count = gains.shape[0]

    full_one = ring_gather(
        jnp.concatenate(
            [
                projection_weight.astype(BF16).reshape(depth, -1),
                jnp.pad(gains.astype(BF16)[None, :], ((0, 15), (0, MODEL_WIDTH - gain_count))),
            ],
            axis=0,
        )
    )
    half = MODEL_WIDTH // 2
    pieces = 2 * hidden_local // half
    out_rows, gate_rows = 2 * out_heads * out_depth, pieces * depth
    fold = lambda value: value.reshape(-1, 2, half).swapaxes(0, 1).reshape(-1, half)
    full_two = lax.all_gather(
        jnp.concatenate(
            [
                fold(w_out.astype(BF16)),
                w_gate_up.astype(BF16).reshape(depth, pieces, half).swapaxes(0, 1).reshape(-1, half),
                fold(w_down.astype(BF16)),
            ],
            axis=0,
        ),
        "dp", axis=0, tiled=False,
    )
    unfold = lambda value, count, deep: (
        value.reshape(spread, 2, count, deep, half).transpose(2, 0, 3, 1, 4).reshape(-1, MODEL_WIDTH)
    )
    qkv_matrix = full_one[:, :depth].reshape(MODEL_WIDTH, -1)
    gains_all = full_one[:, depth, :gain_count].reshape(-1).astype(F32)
    out_matrix = unfold(full_two[:, :out_rows], out_heads, out_depth)
    gate_up_matrix = (
        full_two[:, out_rows : out_rows + gate_rows]
        .reshape(spread, pieces, depth, half)
        .swapaxes(1, 2)
        .reshape(MODEL_WIDTH, -1)
    )
    down_matrix = unfold(full_two[:, out_rows + gate_rows :], down_blocks, down_depth)
    gain_attn = gains_all[None, :MODEL_WIDTH]
    gain_mlp = gains_all[MODEL_WIDTH : 2 * MODEL_WIDTH]
    gain_query = gains_all[None, 2 * MODEL_WIDTH : 2 * MODEL_WIDTH + HEAD_SIZE]
    gain_key = gains_all[None, 2 * MODEL_WIDTH + HEAD_SIZE :]

    doc_ends = jnp.cumsum(lengths[0])
    doc_starts = doc_ends - lengths[0]

    def start_of(index):
        return jnp.max(
            jnp.where(index[:, None] >= doc_starts[None, :], doc_starts[None, :], 0), axis=1
        )

    order = me ^ jnp.arange(shards, dtype=jnp.int32)
    index_of_row = (
        order[:, None] * local_rows + jnp.arange(local_rows, dtype=jnp.int32)[None, :]
    ).reshape(-1)
    start_of_row = start_of(index_of_row)
    position = index_of_row - start_of_row
    inverse = THETA ** (-2.0 * jnp.arange(HEAD_SIZE // 2, dtype=F32) / HEAD_SIZE)
    turned = position.astype(F32)[:, None] * inverse[None, :]
    cosine, sine = jnp.cos(turned), jnp.sin(turned)
    cos = jnp.concatenate([cosine, cosine], axis=1)
    sin = jnp.concatenate([-sine, sine], axis=1)
    block_starts = start_of(jnp.arange(blocks, dtype=jnp.int32) * BLOCK) // BLOCK
    info = jnp.concatenate([block_starts, (me * (local_rows // BLOCK))[None]]).astype(jnp.int32)
    start = start_of_row[None, :]

    def over_rows(a, b):
        return lax.dot_general(a, b, (((0,), (0,)), ((), ())), preferred_element_type=F32)

    rows_float = tokens.astype(F32)
    tokens_across = flipped(tokens, "tensor", 2)
    tokens_all = jnp.concatenate(
        [tokens, flipped(tokens, "tensor", 1), tokens_across, flipped(tokens_across, "tensor", 1)],
        axis=0,
    )
    normed_one, raw_q, raw_k, q, k, v, k_turned, v_turned = project(
        tokens_all, gain_attn, qkv_matrix, cos, sin, gain_query, gain_key
    )
    heads_other, logs_other = attend(1, info, q, k, v_turned, start)
    beside = nn(heads_other[local_rows:], out_matrix).astype(BF16)
    near = near_sum(nn(heads_other[:local_rows], out_matrix), beside).astype(BF16)
    grad_across = flipped(cotangent, "tensor", 2)
    near, grad_across, q_own = together(near, grad_across, q)
    attn_across = flipped(near, "tensor", 2)
    heads_own, logs_own = attend(0, info, q_own, k, v_turned, start)
    beside = nn(heads_own[local_rows:], out_matrix).astype(BF16)
    attn_rows = near_sum(nn(heads_own[:local_rows], out_matrix), beside) + attn_across.astype(F32)
    middle = rows_float + attn_rows

    grad_own = jnp.concatenate([cotangent, flipped(cotangent, "tensor", 1)], axis=0)
    grad_other = jnp.concatenate([grad_across, flipped(grad_across, "tensor", 1)], axis=0)
    normed_two = norm_rows(middle, gain_mlp).astype(BF16)
    normed_across = flipped(normed_two, "tensor", 2)
    normed_own = jnp.concatenate([normed_two, flipped(normed_two, "tensor", 1)], axis=0)
    hidden_own, feed_grad_own, back_0, back_1, sum_0, sum_1 = feed(
        normed_own, grad_own, gate_up_matrix, down_matrix
    )
    normed_across, back_0, back_1, sum_0, sum_1 = together(
        normed_across, back_0, back_1, sum_0, sum_1
    )
    normed_other = jnp.concatenate([normed_across, flipped(normed_across, "tensor", 1)], axis=0)
    hidden_other, feed_grad_other, back_2, back_3, sum_2, sum_3 = feed(
        normed_other, grad_other, gate_up_matrix, down_matrix
    )
    near = near_sum(back_2, back_3).astype(BF16)
    back_across = flipped(near, "tensor", 2)
    back_near = near_sum(back_0, back_1)

    grad_gate_up_w = (
        over_rows(normed_own, feed_grad_own) + over_rows(normed_other, feed_grad_other)
    ).astype(BF16)
    grad_down = (over_rows(hidden_own, grad_own) + over_rows(hidden_other, grad_other)).astype(BF16)
    back_across, grad_gate_up_w, grad_down = together(back_across, grad_gate_up_w, grad_down)
    feed_sum = lax.psum_scatter(
        jnp.concatenate(
            [
                grad_gate_up_w.reshape(spread, depth, pieces, half)
                .swapaxes(1, 2)
                .reshape(spread, -1, half),
                grad_down.reshape(down_blocks, spread, down_depth, 2, half)
                .transpose(1, 3, 0, 2, 4)
                .reshape(spread, -1, half),
            ],
            axis=1,
        ),
        "dp", scatter_dimension=0, tiled=True,
    )[0].astype(F32)
    sum_gate_up = (
        feed_sum[:gate_rows].reshape(pieces, depth, half).swapaxes(0, 1).reshape(w_gate_up.shape)
    )
    sum_down = (
        feed_sum[gate_rows:].reshape(2, -1, half).swapaxes(0, 1).reshape(w_down.shape)
    )

    grad_middle_part, grad_gain_mlp = norm_back(
        middle, gain_mlp, back_near + back_across.astype(F32)
    )
    grad_middle = cotangent.astype(F32) + grad_middle_part
    grad_middle_low = grad_middle.astype(BF16)
    grad_middle_across = flipped(grad_middle_low, "tensor", 2)

    grad_middle_own = jnp.concatenate(
        [grad_middle_low, flipped(grad_middle_low, "tensor", 1)], axis=0
    )
    grad_heads_own = nt(grad_middle_own, out_matrix).astype(BF16)
    grad_q, grad_k, grad_v, gain_own = attend_back_own(
        info, q, k, v, k_turned, start, logs_own, heads_own, grad_heads_own, raw_q, cos, sin,
        gain_query,
    )
    grad_middle_across, grad_q, sum_2, sum_3 = together(grad_middle_across, grad_q, sum_2, sum_3)
    mlp_across = flipped(near_sum(sum_2, sum_3).astype(BF16), "tensor", 2)
    grad_middle_other = jnp.concatenate(
        [grad_middle_across, flipped(grad_middle_across, "tensor", 1)], axis=0
    )
    grad_heads_other = nt(grad_middle_other, out_matrix).astype(BF16)
    grad_out_w = over_rows(heads_own, grad_middle_own) + over_rows(heads_other, grad_middle_other)
    sum_out = exchanged_sum(grad_out_w.reshape(out_heads, spread, out_depth, MODEL_WIDTH), 1)

    grad_qkv, grad_qkv_w, sum_qkv, gain_other = [], [], [], []
    for head in range(kv_local):
        one, gain_parts = attend_back_other(
            head, info, q, k, v, k_turned, start, logs_other, heads_other, grad_heads_other,
            raw_q, cos, sin, gain_query, raw_k, gain_key, grad_q, grad_k, grad_v,
        )
        product = over_rows(normed_one, one)
        grad_qkv.append(one)
        grad_qkv_w.append(product)
        gain_other.append(gain_parts)
        sum_qkv.append(exchanged_sum(product.reshape(spread, depth, -1), 0))
        if head + 1 < kv_local:
            grad_heads_other, _ = together(grad_heads_other, product)
    back_2, back_3 = unproject(1, *grad_qkv, qkv_matrix)
    back_0, back_1 = unproject(0, *grad_qkv, qkv_matrix)
    near = near_sum(back_2, back_3).astype(BF16)
    back_across = flipped(near, "tensor", 2)
    grad_normed_one = near_sum(back_0, back_1) + back_across.astype(F32)
    grad_rows_part, _ = norm_back(rows_float, gain_attn, grad_normed_one)
    grad_tokens = grad_middle + grad_rows_part
    mlp_rows = near_sum(sum_0, sum_1) + mlp_across.astype(F32)
    block_out = (middle + mlp_rows).astype(BF16)

    width = SLOTS * HEAD_SIZE
    grad_gain_attn = sum(
        jnp.sum(qkv_matrix[:, i * width : (i + 1) * width].astype(F32) * product, axis=1)
        for i, product in enumerate(grad_qkv_w)
    ) / gain_attn[0]
    grad_gain_heads = sum(gain_other) + jnp.pad(jnp.sum(gain_own, axis=0), ((0, 1), (0, 0)))
    gain_sums = jnp.concatenate([grad_gain_attn, grad_gain_mlp, grad_gain_heads.reshape(-1)])
    gain_sums, _ = together(gain_sums, near)
    gain_sums = gain_sums + sum(flipped(gain_sums, "tensor", bit) for bit in range(1, shards))
    if spread == len(RING):
        me_dp = lax.axis_index("dp")
        parts = gain_sums.reshape(spread, gain_count)
        take = lambda i: lax.dynamic_index_in_dim(parts, i, 0, keepdims=False)
        sum_gains = take(me_dp) + sum(
            flipped(take(me_dp ^ bit), "dp", bit) for bit in range(1, spread)
        )
    else:
        sum_gains = lax.psum_scatter(gain_sums, "dp", scatter_dimension=0, tiled=True)

    upd_qkv = adamw_update(
        projection_weight, first_moment_projection, second_moment_projection,
        jnp.stack(sum_qkv, axis=1), 2.0 * MODEL_WIDTH ** (-0.5), DECAY,
    )
    upd_out = adamw_update(
        w_out, first_out, second_out, sum_out,
        2.0 * (QUERY_HEADS * HEAD_SIZE // 64) ** (-0.5), DECAY,
    )
    upd_gate_up = adamw_update(
        w_gate_up, first_gate_up, second_gate_up, sum_gate_up,
        2.0 * MODEL_WIDTH ** (-0.5), DECAY,
    )
    upd_down = adamw_update(w_down, first_down, second_down, sum_down, 2.0 * FF ** (-0.5), DECAY)
    upd_gains = adamw_update(gains, first_gains, second_gains, sum_gains, 0.5, 0.0)
    updates = (upd_qkv, upd_out, upd_gate_up, upd_down, upd_gains)
    return (
        block_out,
        grad_tokens,
        *(update[2] for update in updates),
        *(update[0] for update in updates),
        *(update[1] for update in updates),
    )


def solution(mesh):
    weights = (
        P("dp", "tensor", None),
        P("tensor", "dp", None),
        P("dp", None, "tensor"),
        P("tensor", "dp", None),
        P("dp"),
    )
    batch = P(("dp", "tensor"), None)
    return jax.shard_map(
        per_device,
        mesh=mesh,
        in_specs=(batch, batch, P("dp", None), *weights, *weights, *weights),
        out_specs=(batch, batch, *weights, *weights, *weights),
        check_vma=False,
    )
```

```python
import jax
import jax.numpy as jnp
from jax import lax
from jax.experimental import pallas as pl
from jax.experimental.pallas import tpu as pltpu
from jax.sharding import PartitionSpec as P

MODEL_WIDTH = 1024
QUERY_HEADS = 16
KEY_VALUE_HEADS = 8
HEAD_SIZE = 128
FF = 3072
STEP = 10

EPS = 1e-06
THETA = 1000000.0
BETA_ONE = 0.9
BETA_TWO = 0.95
ADAM_EPS = 1e-08
DECAY = 0.1

GROUP = QUERY_HEADS // KEY_VALUE_HEADS
SLOTS = GROUP + 2
SCALE = HEAD_SIZE ** (-0.5)
LOG2E = 1.4426950408889634
BLOCK = 256
VMEM_LIMIT = 48 * 1024 * 1024
RING = (0, 2, 4, 6, 7, 5, 3, 1)
F32 = jnp.float32
BF16 = jnp.bfloat16


def norm_rows(values, scales):
    return values * lax.rsqrt(jnp.mean(values * values, axis=-1, keepdims=True) + EPS) * scales


def norm_back(values, scales, grad):
    r = lax.rsqrt(jnp.mean(values * values, axis=-1, keepdims=True) + EPS)
    u = grad * scales
    back = r * u - values * (r * r * r) * jnp.mean(u * values, axis=-1, keepdims=True)
    return back, jnp.sum(grad * values * r, axis=0)


def adamw_update(master, moment_one, moment_two, gradient, step_rate, decay_rate):
    next_one = BETA_ONE * moment_one + (1.0 - BETA_ONE) * gradient
    next_two = BETA_TWO * moment_two + (1.0 - BETA_TWO) * gradient * gradient
    one_hat = next_one / (1.0 - BETA_ONE**STEP)
    two_hat = next_two / (1.0 - BETA_TWO**STEP)
    next_master = master - step_rate * (
        one_hat / (jnp.sqrt(two_hat) + ADAM_EPS) + decay_rate * master
    )
    return (next_one, next_two, next_master)


def nt(a, b):
    return lax.dot_general(a, b, (((1,), (1,)), ((), ())), preferred_element_type=F32)


def nn(a, b):
    return jnp.dot(a, b, preferred_element_type=F32)


def head_rotated(x, gain, cos, sin):
    r = lax.rsqrt(jnp.mean(x * x, axis=-1, keepdims=True) + EPS)
    y = x * r * gain
    return y * cos + pltpu.roll(y, HEAD_SIZE // 2, 1) * sin


def head_back(x, gain, cos, sin, grad):
    r = lax.rsqrt(jnp.mean(x * x, axis=-1, keepdims=True) + EPS)
    turned = grad * cos - pltpu.roll(grad, HEAD_SIZE // 2, 1) * sin
    u = turned * gain
    back = r * u - x * (r * r * r) * jnp.mean(u * x, axis=-1, keepdims=True)
    return back, jnp.sum(turned * x * r, axis=0, keepdims=True)


def at_block(index):
    return pl.ds(pl.multiple_of(index * BLOCK, BLOCK), BLOCK)


def allowed_block(key_block, query_block, start):
    keys = key_block * BLOCK + lax.broadcasted_iota(jnp.int32, (BLOCK, BLOCK), 0)
    queries = query_block * BLOCK + lax.broadcasted_iota(jnp.int32, (BLOCK, BLOCK), 1)
    return (keys >= start) & (keys <= queries)


def lanes_of(h):
    return slice(h * HEAD_SIZE, (h + 1) * HEAD_SIZE)


def project_kernel(
    x, gain, matrix, cos, sin, gain_q, gain_k, normed_turned, raw_q, raw_k, q, k, v, k_turned, v_turned
):
    normed = norm_rows(x[...].astype(F32), gain[...])
    normed_turned[...] = normed.T.astype(BF16)
    h = normed.astype(BF16)
    c, s = cos[...], sin[...]
    for j in range(matrix.shape[1] // (SLOTS * HEAD_SIZE)):
        base = j * SLOTS * HEAD_SIZE
        part = nn(h, matrix[:, base : base + SLOTS * HEAD_SIZE])
        for g in range(GROUP):
            value = part[:, lanes_of(g)]
            raw_q[:, lanes_of(j * GROUP + g)] = value
            q[:, lanes_of(j * GROUP + g)] = head_rotated(value, gain_q[...], c, s).astype(BF16)
        value = part[:, lanes_of(GROUP)]
        raw_k[:, lanes_of(j)] = value
        turned = head_rotated(value, gain_k[...], c, s)
        k[:, lanes_of(j)] = turned.astype(BF16)
        k_turned[lanes_of(j), :] = turned.T.astype(BF16)
        value = part[:, lanes_of(GROUP + 1)]
        v[:, lanes_of(j)] = value.astype(BF16)
        v_turned[lanes_of(j), :] = value.T.astype(BF16)


def attend_kernel(offset, info, q, k, v_turned, start, out, out_turned, logs):
    blocks = k.shape[0] // BLOCK
    flip = info[blocks]

    def one_block(i, _):
        here = at_block(i)
        b = (i + offset) ^ flip
        first = start[:, here]
        queries = [q[here, lanes_of(h)] for h in range(GROUP)]

        def keys_step(kb, carry):
            there = at_block(kb ^ flip)
            key, value = k[there, :], v_turned[:, there]
            allowed = allowed_block(kb, b, first)
            after = []
            for h in range(GROUP):
                total, blend = carry[h]
                p = jnp.where(allowed, jnp.exp2(nt(key, queries[h]) * (SCALE * LOG2E)), 0.0)
                after.append(
                    (total + jnp.sum(p, axis=0, keepdims=True), blend + nn(value, p.astype(BF16)))
                )
            return tuple(after)

        zero = (jnp.zeros((1, BLOCK), F32), jnp.zeros((HEAD_SIZE, BLOCK), F32))
        done = lax.fori_loop(info[b], b + 1, keys_step, (zero,) * GROUP)
        for h in range(GROUP):
            total, blend = done[h]
            result = blend / total
            out[here, lanes_of(h)] = result.T.astype(BF16)
            out_turned[lanes_of(h), here] = result.astype(BF16)
            logs[0, h : h + 1, here] = jnp.log2(total)
        return 0

    lax.fori_loop(0, q.shape[0] // BLOCK, one_block, 0)


def back_blocks(
    offset, info, q, k, v, k_turned, start, logs, out, grad_out, raw_q, cos, sin, gain_q,
    grad_k, grad_v, store,
):
    flip = info[k.shape[0] // BLOCK]

    def one_block(i, total_gain):
        here = at_block(i)
        b = (i + offset) ^ flip
        first = start[:, here]
        queries, gradients, across, log = [], [], [], []
        for h in range(GROUP):
            g = grad_out[here, lanes_of(h)]
            queries.append(q[here, lanes_of(h)])
            gradients.append(g)
            both = g.astype(F32) * out[here, lanes_of(h)].astype(F32)
            across.append(jnp.sum(both.T, axis=0, keepdims=True))
            log.append(logs[0, h : h + 1, here])

        def keys_step(kb, carry):
            there = at_block(kb ^ flip)
            key, value, key_turned = k[there, :], v[there, :], k_turned[:, there]
            allowed = allowed_block(kb, b, first)
            after, add_k, add_v = [], 0.0, 0.0
            for h in range(GROUP):
                s = nt(key, queries[h])
                p = jnp.where(allowed, jnp.exp2(s * (SCALE * LOG2E) - log[h]), 0.0)
                d = (p * (nt(value, gradients[h]) - across[h])).astype(BF16)
                add_v = add_v + nn(p.astype(BF16), gradients[h])
                add_k = add_k + nn(d, queries[h])
                after.append(carry[h] + nn(key_turned, d))
            grad_k[there, :] += add_k
            grad_v[there, :] += add_v
            return tuple(after)

        zero = jnp.zeros((HEAD_SIZE, BLOCK), F32)
        done = lax.fori_loop(info[b], b + 1, keys_step, (zero,) * GROUP)
        c, s = cos[here, :], sin[here, :]
        for h in range(GROUP):
            back, gain = head_back(raw_q[here, lanes_of(h)], gain_q[...], c, s, done[h].T * SCALE)
            store(i, h, back.astype(BF16))
            total_gain = total_gain + gain
        return total_gain

    return lax.fori_loop(0, q.shape[0] // BLOCK, one_block, jnp.zeros((1, HEAD_SIZE), F32))


def back_own_kernel(
    info, q, k, v, k_turned, start, logs, out, grad_out, raw_q, cos, sin, gain_q,
    grad_q, grad_k, grad_v, grad_gain,
):
    grad_k[...] = jnp.zeros(grad_k.shape, F32)
    grad_v[...] = jnp.zeros(grad_v.shape, F32)

    def store(i, h, value):
        grad_q[at_block(i), lanes_of(h)] = value

    grad_gain[0, :, :] = back_blocks(
        0, info, q, k, v, k_turned, start, logs, out, grad_out, raw_q, cos, sin, gain_q,
        grad_k, grad_v, store,
    )


def back_other_kernel(
    info, q, k, v, k_turned, start, logs, out, grad_out, raw_q, cos, sin, gain_q,
    cos_all, sin_all, raw_k, gain_k, grad_q_own, grad_k_own, grad_v_own,
    grad_qkv, grad_gains, grad_k, grad_v,
):
    half = q.shape[0] // BLOCK
    blocks = k.shape[0] // BLOCK
    queries = GROUP * HEAD_SIZE
    grad_k[...] = grad_k_own[...]
    grad_v[...] = grad_v_own[...]
    grad_qkv[: half * BLOCK, :queries] = grad_q_own[...]

    def store(i, h, value):
        grad_qkv[at_block(i + half), lanes_of(h)] = value

    grad_gains[0, 0:1, :] = back_blocks(
        half, info, q, k, v, k_turned, start, logs, out, grad_out, raw_q, cos, sin, gain_q,
        grad_k, grad_v, store,
    )

    def finish(i, total_gain):
        rows = at_block(i)
        back, gain = head_back(
            raw_k[rows, :], gain_k[...], cos_all[rows, :], sin_all[rows, :], grad_k[rows, :] * SCALE
        )
        grad_qkv[rows, lanes_of(GROUP)] = back.astype(BF16)
        grad_qkv[rows, lanes_of(GROUP + 1)] = grad_v[rows, :].astype(BF16)
        return total_gain + gain

    grad_gains[0, 1:2, :] = lax.fori_loop(0, blocks, finish, jnp.zeros((1, HEAD_SIZE), F32))


def unpack(packed, gate_up, down):
    n, _, half = packed.shape
    depth = gate_up.shape[0] // n
    pieces = gate_up.shape[1] // half
    blocks = down.shape[0] // HEAD_SIZE
    deep = HEAD_SIZE // n
    for d in range(n):
        for b in range(pieces):
            gate_up[d * depth : (d + 1) * depth, b * half : (b + 1) * half] = packed[
                d, b * depth : (b + 1) * depth, :
            ]
        for c in range(2):
            for i in range(blocks):
                at = pieces * depth + (c * blocks + i) * deep
                to = i * HEAD_SIZE + d * deep
                down[to : to + deep, c * half : (c + 1) * half] = packed[d, at : at + deep, :]


def feed_kernel(packs, h, grad, *refs):
    step = pl.program_id(0)
    if packs:
        packed, *refs = refs
        *refs, gate_up, down = refs

        @pl.when(step == 0)
        def _():
            unpack(packed, gate_up, down)
    else:
        gate_up, down, *refs = refs
    h_turned, hidden_turned, grad_gate_up, back_a, back_b, sum_a, sum_b = refs
    width = down.shape[0]
    rows = h[...]
    both = nn(rows, gate_up[...])
    gate, up = both[:, :width], both[:, width:]
    sig = jax.nn.sigmoid(gate)
    gated = gate * sig
    value = gated * up
    hidden_turned[...] = value.T.astype(BF16)
    h_turned[...] = rows.astype(F32).T.astype(BF16)
    grad_hidden = nt(grad[...], down[...])
    grad_gate_up[:, :width] = (grad_hidden * up * (sig + gated * (1.0 - sig))).astype(BF16)
    grad_gate_up[:, width:] = (grad_hidden * gated).astype(BF16)
    back = nt(grad_gate_up[...], gate_up[...]).astype(BF16)
    total = nn(value.astype(BF16), down[...]).astype(BF16)
    first = step < pl.num_programs(0) // 2

    @pl.when(first)
    def _():
        back_a[...] = back
        sum_a[...] = total

    @pl.when(jnp.logical_not(first))
    def _():
        back_b[...] = back
        sum_b[...] = total


def feed_weights_kernel(
    packs, pieces, h_own, h_other, grad_own, grad_other, hidden_own, hidden_other, dy_own, dy_other,
    *out
):
    step = pl.program_id(0)
    half = dy_own.shape[1]

    for b in range(pieces):
        @pl.when(step == b)
        def _():
            value = nn(h_own[...], grad_own[...]) + nn(h_other[...], grad_other[...])
            value = value.astype(BF16)
            if packs:
                n = out[0].shape[0]
                depth = value.shape[0] // n
                for d in range(n):
                    out[0][d, b * depth : (b + 1) * depth, :] = value[d * depth : (d + 1) * depth]
            else:
                out[0][:, b * half : (b + 1) * half] = value

    for c in range(2):
        @pl.when(step == pieces + c)
        def _():
            value = nn(hidden_own[...], dy_own[...]) + nn(hidden_other[...], dy_other[...])
            value = value.astype(BF16)
            if packs:
                n = out[0].shape[0]
                depth, deep = h_own.shape[0] // n, HEAD_SIZE // n
                blocks = value.shape[0] // HEAD_SIZE
                for d in range(n):
                    for i in range(blocks):
                        at = pieces * depth + (c * blocks + i) * deep
                        of = i * HEAD_SIZE + d * deep
                        out[0][d, at : at + deep, :] = value[of : of + deep]
            else:
                out[1][:, c * half : (c + 1) * half] = value


def unproject_kernel(grad, matrix, out_a, out_b):
    value = nt(grad[...], matrix[...]).astype(BF16)
    first = pl.program_id(0) < pl.num_programs(0) // 2

    @pl.when(first)
    def _():
        out_a[...] = value

    @pl.when(jnp.logical_not(first))
    def _():
        out_b[...] = value


def params(name, flops):
    return dict(
        compiler_params=pltpu.CompilerParams(
            dimension_semantics=("arbitrary",), vmem_limit_bytes=VMEM_LIMIT
        ),
        cost_estimate=pl.CostEstimate(flops=flops // 64, bytes_accessed=1_000, transcendentals=0),
        name=name,
    )


def fixed(shape, index=None):
    index = (0,) * len(shape) if index is None else index
    return pl.BlockSpec(shape, lambda i, *_: index)


def shaped(shape, kind):
    return jax.ShapeDtypeStruct(shape, kind)


def project(x, gain, matrix, cos, sin, gain_q, gain_k):
    rows, width = x.shape
    heads = matrix.shape[1] // (SLOTS * HEAD_SIZE)
    by_rows = lambda n: pl.BlockSpec((BLOCK, n), lambda i: (i, 0))
    by_lanes = lambda n: pl.BlockSpec((n, BLOCK), lambda i: (0, i))
    q_width, k_width = heads * GROUP * HEAD_SIZE, heads * HEAD_SIZE
    return pl.pallas_call(
        project_kernel,
        grid=(rows // BLOCK,),
        in_specs=[
            by_rows(width), fixed((1, width)), fixed(matrix.shape), by_rows(HEAD_SIZE),
            by_rows(HEAD_SIZE), fixed((1, HEAD_SIZE)), fixed((1, HEAD_SIZE)),
        ],
        out_specs=[
            by_lanes(width), by_rows(q_width), by_rows(k_width), by_rows(q_width),
            by_rows(k_width), by_rows(k_width), by_lanes(k_width), by_lanes(k_width),
        ],
        out_shape=[
            shaped((width, rows), BF16), shaped((rows, q_width), F32),
            shaped((rows, k_width), F32), shaped((rows, q_width), BF16),
            shaped((rows, k_width), BF16), shaped((rows, k_width), BF16),
            shaped((k_width, rows), BF16), shaped((k_width, rows), BF16),
        ],
        **params("project", 10_000_000_000),
    )(x, gain, matrix, cos, sin, gain_q, gain_k)


def head_specs(half, rows):
    at = lambda j: j
    n = rows // 2
    return dict(
        q=pl.BlockSpec((n, GROUP * HEAD_SIZE), lambda j, info: (half, at(j))),
        k=pl.BlockSpec((rows, HEAD_SIZE), lambda j, info: (0, at(j))),
        turned=pl.BlockSpec((HEAD_SIZE, rows), lambda j, info: (at(j), 0)),
        start=pl.BlockSpec((1, n), lambda j, info: (0, half)),
        out=pl.BlockSpec((n, GROUP * HEAD_SIZE), lambda j, info: (0, at(j))),
        logs=pl.BlockSpec((1, GROUP, n), lambda j, info: (at(j), 0, 0)),
        angle=pl.BlockSpec((n, HEAD_SIZE), lambda j, info: (half, 0)),
    )


def attend(half, info, q, k, v_turned, start):
    rows = k.shape[0]
    n, heads = rows // 2, k.shape[1] // HEAD_SIZE
    s = head_specs(half, rows)
    return pl.pallas_call(
        lambda *refs: attend_kernel(half * n // BLOCK, *refs),
        grid_spec=pltpu.PrefetchScalarGridSpec(
            num_scalar_prefetch=1,
            grid=(heads,),
            in_specs=[s["q"], s["k"], s["turned"], s["start"]],
            out_specs=[
                s["out"], pl.BlockSpec((GROUP * HEAD_SIZE, n), lambda j, info: (j, 0)), s["logs"],
            ],
        ),
        out_shape=[
            shaped((n, q.shape[1]), BF16), shaped((q.shape[1], n), BF16),
            shaped((heads, GROUP, n), F32),
        ],
        **params("attend", 18_000_000_000),
    )(info, q, k, v_turned, start)


def attend_back_own(info, q, k, v, k_turned, start, logs, out, grad_out, raw_q, cos, sin, gain_q):
    rows = k.shape[0]
    n, heads = rows // 2, k.shape[1] // HEAD_SIZE
    s = head_specs(0, rows)
    return pl.pallas_call(
        back_own_kernel,
        grid_spec=pltpu.PrefetchScalarGridSpec(
            num_scalar_prefetch=1,
            grid=(heads,),
            in_specs=[
                s["q"], s["k"], s["k"], s["turned"], s["start"], s["logs"], s["out"], s["out"],
                s["q"], s["angle"], s["angle"], fixed((1, HEAD_SIZE)),
            ],
            out_specs=[
                s["out"], s["k"], s["k"],
                pl.BlockSpec((1, 1, HEAD_SIZE), lambda j, info: (j, 0, 0)),
            ],
        ),
        out_shape=[
            shaped((n, q.shape[1]), BF16), shaped(k.shape, F32), shaped(k.shape, F32),
            shaped((heads, 1, HEAD_SIZE), F32),
        ],
        **params("attend_back_own", 25_000_000_000),
    )(info, q, k, v, k_turned, start, logs, out, grad_out, raw_q, cos, sin, gain_q)


def attend_back_other(
    info, q, k, v, k_turned, start, logs, out, grad_out, raw_q, cos, sin, gain_q,
    raw_k, gain_k, grad_q, grad_k, grad_v,
):
    rows = k.shape[0]
    heads = k.shape[1] // HEAD_SIZE
    width = SLOTS * HEAD_SIZE
    s = head_specs(1, rows)
    row = fixed((1, HEAD_SIZE))
    return pl.pallas_call(
        back_other_kernel,
        grid_spec=pltpu.PrefetchScalarGridSpec(
            num_scalar_prefetch=1,
            grid=(heads,),
            in_specs=[
                s["q"], s["k"], s["k"], s["turned"], s["start"], s["logs"], s["out"], s["out"],
                s["q"], s["angle"], s["angle"], row,
                fixed((rows, HEAD_SIZE)), fixed((rows, HEAD_SIZE)), s["k"], row, s["out"], s["k"],
                s["k"],
            ],
            out_specs=[
                pl.BlockSpec((rows, width), lambda j, info: (0, j)),
                pl.BlockSpec((1, 2, HEAD_SIZE), lambda j, info: (j, 0, 0)),
            ],
            scratch_shapes=[pltpu.VMEM((rows, HEAD_SIZE), F32)] * 2,
        ),
        out_shape=[shaped((rows, heads * width), BF16), shaped((heads, 2, HEAD_SIZE), F32)],
        **params("attend_back_other", 28_000_000_000),
    )(
        info, q, k, v, k_turned, start, logs, out, grad_out, raw_q, cos, sin, gain_q,
        cos, sin, raw_k, gain_k, grad_q, grad_k, grad_v,
    )


def two_parts(rows, width):
    steps = rows // BLOCK // 2
    return (
        [
            pl.BlockSpec((BLOCK, width), lambda i: (jnp.minimum(i, steps - 1), 0)),
            pl.BlockSpec((BLOCK, width), lambda i: (jnp.maximum(i - steps, 0), 0)),
        ],
        [shaped((rows // 2, width), BF16)] * 2,
    )


def feed(h, grad, weights, hidden_count):
    rows, width = h.shape
    packs = len(weights) == 1
    by_rows = lambda n: pl.BlockSpec((BLOCK, n), lambda i: (i, 0))
    by_lanes = lambda n: pl.BlockSpec((n, BLOCK), lambda i: (0, i))
    specs, shapes = two_parts(rows, width)
    scratch = [
        pltpu.VMEM((width, 2 * hidden_count), BF16), pltpu.VMEM((hidden_count, width), BF16)
    ]
    return pl.pallas_call(
        lambda *refs: feed_kernel(packs, *refs),
        grid=(rows // BLOCK,),
        in_specs=[by_rows(width), by_rows(width), *(fixed(w.shape) for w in weights)],
        out_specs=[
            by_lanes(width), by_lanes(hidden_count), by_rows(2 * hidden_count), *specs, *specs
        ],
        out_shape=[
            shaped((width, rows), BF16), shaped((hidden_count, rows), BF16),
            shaped((rows, 2 * hidden_count), BF16), *shapes, *shapes,
        ],
        scratch_shapes=scratch if packs else [],
        **params("feed", 16_000_000_000),
    )(h, grad, *weights)


def feed_weights(packed_shape, h, grads, hidden, dy):
    width, n = h[0].shape
    half = width // 2
    pieces = grads[0].shape[1] // half
    count = hidden[0].shape[0]
    packs = packed_shape is not None
    gate_block = pl.BlockSpec((n, half), lambda i: (0, jnp.minimum(i, pieces - 1)))
    down_block = pl.BlockSpec((n, half), lambda i: (0, jnp.maximum(i - pieces, 0)))
    shapes = [packed_shape] if packs else [(width, 2 * count), (count, width)]
    return pl.pallas_call(
        lambda *refs: feed_weights_kernel(packs, pieces, *refs),
        grid=(pieces + 2,),
        in_specs=[
            fixed((width, n)), fixed((width, n)), gate_block, gate_block,
            fixed((count, n)), fixed((count, n)), down_block, down_block,
        ],
        out_specs=[fixed(shape) for shape in shapes],
        out_shape=[shaped(shape, BF16) for shape in shapes],
        **params("feed_weights", 16_000_000_000),
    )(*h, *grads, *hidden, *dy)


def unproject(half, grad, matrix):
    rows, width = grad.shape
    n = rows // 2
    steps = n // BLOCK
    specs, shapes = two_parts(n, matrix.shape[0])
    return pl.pallas_call(
        unproject_kernel,
        grid=(steps,),
        in_specs=[pl.BlockSpec((BLOCK, width), lambda i: (i + half * steps, 0)), fixed(matrix.shape)],
        out_specs=specs,
        out_shape=shapes,
        **params("unproject", 4_000_000_000),
    )(grad, matrix)


def times_turned_kernel(a, b, out):
    out[...] = nt(a[...], b[...]).astype(BF16)


def times_turned(a, b):
    rows, width = a.shape
    by_rows = lambda n: pl.BlockSpec((BLOCK, n), lambda i: (i, 0))
    return pl.pallas_call(
        times_turned_kernel,
        grid=(rows // BLOCK,),
        in_specs=[by_rows(width), fixed(b.shape)],
        out_specs=by_rows(b.shape[0]),
        out_shape=shaped((rows, b.shape[0]), BF16),
        **params("times_turned", 2_000_000_000),
    )(a, b)


def two_products_kernel(a, b, c, d, out):
    out[...] = nn(a[...], b[...]) + nn(c[...], d[...])


def two_products(a, b, c, d):
    rows, depth = a.shape
    half = b.shape[1] // 2
    columns = lambda n: pl.BlockSpec((n, half), lambda i: (0, i))
    return pl.pallas_call(
        two_products_kernel,
        grid=(2,),
        in_specs=[fixed(a.shape), columns(depth), fixed(c.shape), columns(depth)],
        out_specs=columns(rows),
        out_shape=shaped((rows, b.shape[1]), F32),
        **params("two_products", 2_000_000_000),
    )(a, b, c, d)


def flipped(value, axis, bit, name="part"):
    with jax.named_scope(name):
        return lax.ppermute(value, axis, [(i, i ^ bit) for i in range(lax.axis_size(axis))])


def together(*values):
    return lax.optimization_barrier(values)


def near_sum(part, beside):
    return part.astype(F32) + flipped(beside, "tensor", 1).astype(F32)


def ring_gather(value, place, later):
    n = len(RING)
    ring = jnp.array(RING, jnp.int32)
    at = jnp.argmax(ring == lax.axis_index("dp")).astype(jnp.int32)
    after = [(RING[i], RING[(i + 1) % n]) for i in range(n)]
    before = [(b, a) for a, b in after]
    pieces = {0: value}
    up = down = value
    for step in range(1, n // 2 + 1):
        up = lax.ppermute(up, "dp", after)
        if step < n // 2:
            down = lax.ppermute(down, "dp", before)
        if step == 1:
            up, down, later = together(up, down, later)
        pieces[-step] = up
        if step < n // 2:
            pieces[step] = down
    full = None
    for step, piece in pieces.items():
        full = place(full, piece, ring[(at + step + n) % n])
    return full, later


def halved(parts, axis, bit):
    mine = (lax.axis_index("dp") // bit) % 2
    send = lax.dynamic_index_in_dim(parts, 1 - mine, axis, keepdims=False).astype(BF16)
    keep = lax.dynamic_index_in_dim(parts, mine, axis, keepdims=False)
    return keep + flipped(send, "dp", bit).astype(F32)


def per_device(
    tokens, cotangent, lengths,
    projection_weight, w_out, w_gate_up, w_down, gains,
    first_moment_projection, first_out, first_gate_up, first_down, first_gains,
    second_moment_projection, second_out, second_gate_up, second_down, second_gains,
):
    shards = lax.axis_size("tensor")
    spread = lax.axis_size("dp")
    me = lax.axis_index("tensor")
    local_rows = tokens.shape[0]
    rows = local_rows * shards
    blocks = rows // BLOCK
    kv_local = projection_weight.shape[1]
    hidden_local = w_gate_up.shape[2]
    out_heads, out_depth = w_out.shape[0], w_out.shape[1]
    down_blocks, down_depth = w_down.shape[0], w_down.shape[1]
    depth = projection_weight.shape[0]
    gain_count = gains.shape[0]

    half = MODEL_WIDTH // 2
    pieces = 2 * hidden_local // half
    gate_rows = pieces * depth
    out_rows = out_heads * out_depth
    ringed = spread == len(RING)

    pack_one = jnp.concatenate(
        [
            projection_weight.astype(BF16).reshape(depth, -1),
            w_out.astype(BF16).reshape(-1, MODEL_WIDTH),
            jnp.pad(gains.astype(BF16)[None, :], ((0, 15), (0, MODEL_WIDTH - gain_count))),
        ],
        axis=0,
    )
    pack_two = jnp.concatenate(
        [
            w_gate_up.astype(BF16).reshape(depth, pieces, half).swapaxes(0, 1).reshape(-1, half),
            w_down.astype(BF16).reshape(-1, 2, half).swapaxes(0, 1).reshape(-1, half),
        ],
        axis=0,
    )

    def split_one(value):
        return (
            value[..., :depth, :],
            value[..., depth : depth + out_rows, :],
            value[..., depth + out_rows, :gain_count],
        )

    if ringed:
        def place(full, piece, index):
            if full is None:
                full = (
                    jnp.zeros((spread, depth, MODEL_WIDTH), BF16),
                    jnp.zeros((out_heads, spread, out_depth, MODEL_WIDTH), BF16),
                    jnp.zeros((spread, gain_count), BF16),
                )
            one, two, three = split_one(piece)
            two = two.reshape(out_heads, out_depth, MODEL_WIDTH)
            put = lax.dynamic_update_index_in_dim
            return (
                put(full[0], one, index, 0), put(full[1], two, index, 1), put(full[2], three, index, 0)
            )

        (full_qkv, full_out, full_gains), pack_two = ring_gather(pack_one, place, pack_two)
    else:
        full_qkv, full_out, full_gains = split_one(
            lax.all_gather(pack_one, "dp", axis=0, tiled=False)
        )
        full_out = full_out.reshape(spread, out_heads, out_depth, MODEL_WIDTH).swapaxes(0, 1)
    full_two = lax.all_gather(pack_two, "dp", axis=0, tiled=False)
    qkv_matrix = full_qkv.reshape(MODEL_WIDTH, -1)
    out_matrix = full_out.reshape(-1, MODEL_WIDTH)
    gains_all = full_gains.reshape(-1).astype(F32)
    gain_attn = gains_all[None, :MODEL_WIDTH]
    gain_mlp = gains_all[MODEL_WIDTH : 2 * MODEL_WIDTH]
    gain_query = gains_all[None, 2 * MODEL_WIDTH : 2 * MODEL_WIDTH + HEAD_SIZE]
    gain_key = gains_all[None, 2 * MODEL_WIDTH + HEAD_SIZE :]

    doc_ends = jnp.cumsum(lengths[0])
    doc_starts = doc_ends - lengths[0]

    def start_of(index):
        return jnp.max(
            jnp.where(index[:, None] >= doc_starts[None, :], doc_starts[None, :], 0), axis=1
        )

    order = me ^ jnp.arange(shards, dtype=jnp.int32)
    index_of_row = (
        order[:, None] * local_rows + jnp.arange(local_rows, dtype=jnp.int32)[None, :]
    ).reshape(-1)
    start_of_row = start_of(index_of_row)
    position = index_of_row - start_of_row
    inverse = THETA ** (-2.0 * jnp.arange(HEAD_SIZE // 2, dtype=F32) / HEAD_SIZE)
    turned = position.astype(F32)[:, None] * inverse[None, :]
    cosine, sine = jnp.cos(turned), jnp.sin(turned)
    cos = jnp.concatenate([cosine, cosine], axis=1)
    sin = jnp.concatenate([-sine, sine], axis=1)
    block_starts = start_of(jnp.arange(blocks, dtype=jnp.int32) * BLOCK) // BLOCK
    info = jnp.concatenate([block_starts, (me * (local_rows // BLOCK))[None]]).astype(jnp.int32)
    start = start_of_row[None, :]

    rows_float = tokens.astype(F32)
    tokens_across = flipped(tokens, "tensor", 2, "tokens_across")
    tokens_all = jnp.concatenate(
        [tokens, flipped(tokens, "tensor", 1), tokens_across, flipped(tokens_across, "tensor", 1)],
        axis=0,
    )
    normed_turned, raw_q, raw_k, q, k, v, k_turned, v_turned = project(
        tokens_all, gain_attn, qkv_matrix, cos, sin, gain_query, gain_key
    )
    grad_across = flipped(cotangent, "tensor", 2, "grad_across")
    heads_other, heads_other_turned, logs_other = attend(1, info, q, k, v_turned, start)
    heads_other, grad_across = together(heads_other, grad_across)
    beside = nn(heads_other[local_rows:], out_matrix).astype(BF16)
    near = near_sum(nn(heads_other[:local_rows], out_matrix), beside).astype(BF16)
    near, q_own = together(near, q)
    attn_across = flipped(near, "tensor", 2, "attn_across")
    heads_own, heads_own_turned, logs_own = attend(0, info, q_own, k, v_turned, start)
    heads_own, attn_across, full_two = together(heads_own, attn_across, full_two)
    beside = nn(heads_own[local_rows:], out_matrix).astype(BF16)
    attn_rows = near_sum(nn(heads_own[:local_rows], out_matrix), beside) + attn_across.astype(F32)
    middle = rows_float + attn_rows
    if ringed:
        feed_matrices = (full_two,)
    else:
        feed_matrices = (
            full_two[:, :gate_rows]
            .reshape(spread, pieces, depth, half)
            .swapaxes(1, 2)
            .reshape(MODEL_WIDTH, -1),
            full_two[:, gate_rows:]
            .reshape(spread, 2, down_blocks, down_depth, half)
            .transpose(2, 0, 3, 1, 4)
            .reshape(-1, MODEL_WIDTH),
        )

    grad_own = jnp.concatenate([cotangent, flipped(cotangent, "tensor", 1)], axis=0)
    grad_other = jnp.concatenate([grad_across, flipped(grad_across, "tensor", 1)], axis=0)
    normed_two = norm_rows(middle, gain_mlp).astype(BF16)
    normed_across = flipped(normed_two, "tensor", 2, "normed_across")
    normed_own = jnp.concatenate([normed_two, flipped(normed_two, "tensor", 1)], axis=0)
    h_own, hidden_own, feed_grad_own, back_0, back_1, sum_0, sum_1 = feed(
        normed_own, grad_own, feed_matrices, hidden_local
    )
    normed_across, back_0 = together(normed_across, back_0)
    normed_other = jnp.concatenate([normed_across, flipped(normed_across, "tensor", 1)], axis=0)
    h_other, hidden_other, feed_grad_other, back_2, back_3, sum_2, sum_3 = feed(
        normed_other, grad_other, feed_matrices, hidden_local
    )
    near = near_sum(back_2, back_3).astype(BF16)
    back_near = near_sum(back_0, back_1)
    near, h_own = together(near, h_own)
    back_across = flipped(near, "tensor", 2, "back_across")

    feed_grads = feed_weights(
        full_two.shape if ringed else None, (h_own, h_other), (feed_grad_own, feed_grad_other),
        (hidden_own, hidden_other), (grad_own, grad_other),
    )
    back_across, *feed_grads = together(back_across, *feed_grads)
    if ringed:
        feed_pack = feed_grads[0]
    else:
        feed_pack = jnp.concatenate(
            [
                feed_grads[0].reshape(spread, depth, pieces, half)
                .swapaxes(1, 2)
                .reshape(spread, -1, half),
                feed_grads[1].reshape(down_blocks, spread, down_depth, 2, half)
                .transpose(1, 3, 0, 2, 4)
                .reshape(spread, -1, half),
            ],
            axis=1,
        )
    feed_sum = lax.psum_scatter(feed_pack, "dp", scatter_dimension=0, tiled=True)[0].astype(F32)
    grad_middle_part, grad_gain_mlp = norm_back(
        middle, gain_mlp, back_near + back_across.astype(F32)
    )
    grad_middle = cotangent.astype(F32) + grad_middle_part
    grad_middle_low = grad_middle.astype(BF16)
    grad_middle_across = flipped(grad_middle_low, "tensor", 2, "grad_middle_across")

    grad_middle_own = jnp.concatenate(
        [grad_middle_low, flipped(grad_middle_low, "tensor", 1)], axis=0
    )
    grad_heads_own = times_turned(grad_middle_own, out_matrix)
    grad_q, grad_k, grad_v, gain_own = attend_back_own(
        info, q, k, v, k_turned, start, logs_own, heads_own, grad_heads_own, raw_q, cos, sin,
        gain_query,
    )
    grad_middle_across, grad_q, sum_2, sum_3 = together(grad_middle_across, grad_q, sum_2, sum_3)
    near_mlp = near_sum(sum_2, sum_3).astype(BF16)
    grad_middle_other = jnp.concatenate(
        [grad_middle_across, flipped(grad_middle_across, "tensor", 1)], axis=0
    )
    grad_heads_other = times_turned(grad_middle_other, out_matrix)
    grad_out_w = two_products(
        heads_own_turned, grad_middle_own, heads_other_turned, grad_middle_other
    )
    near_mlp, grad_out_w, grad_heads_other = together(near_mlp, grad_out_w, grad_heads_other)
    mlp_across = flipped(near_mlp, "tensor", 2, "mlp_across")
    grad_qkv, gain_other = attend_back_other(
        info, q, k, v, k_turned, start, logs_other, heads_other, grad_heads_other,
        raw_q, cos, sin, gain_query, raw_k, gain_key, grad_q, grad_k, grad_v,
    )
    grad_qkv, mlp_across = together(grad_qkv, mlp_across)
    grad_qkv_w = nn(normed_turned, grad_qkv)
    grad_qkv, grad_qkv_w = together(grad_qkv, grad_qkv_w)
    grad_gain_attn = jnp.sum(qkv_matrix.astype(F32) * grad_qkv_w, axis=1) / gain_attn[0]
    grad_gain_heads = jnp.sum(gain_other, axis=0) + jnp.pad(
        jnp.sum(gain_own, axis=0), ((0, 1), (0, 0))
    )
    gain_sums = jnp.concatenate([grad_gain_attn, grad_gain_mlp, grad_gain_heads.reshape(-1)])
    back_2, back_3 = unproject(1, grad_qkv, qkv_matrix)
    back_0, back_1 = unproject(0, grad_qkv, qkv_matrix)
    near = near_sum(back_2, back_3).astype(BF16)
    back_across = flipped(near, "tensor", 2, "back_across")
    if ringed:
        cube = (2, 2, 2)
        columns = grad_qkv_w.shape[1] // 2
        gain_rows = jnp.pad(
            gain_sums.reshape(cube + (1, gain_count)),
            ((0, 0),) * 3 + ((0, 15), (0, columns - gain_count)),
        )
        sum_one = jnp.concatenate(
            [grad_qkv_w[:, :columns].reshape(cube + (depth, -1)), gain_rows], axis=3
        )
        sum_two = grad_qkv_w[:, columns:].reshape(cube + (depth, -1))
        sum_one, sum_two = halved(sum_one, 1, 2), halved(sum_two, 2, 1)
        sum_one, sum_two = halved(sum_one, 1, 1), halved(sum_two, 1, 2)
        sum_one, sum_two, back_across, feed_sum = together(
            sum_one, sum_two, back_across, feed_sum
        )
        sum_one, sum_two = halved(sum_one, 0, 4), halved(sum_two, 0, 4)
        sum_qkv = jnp.concatenate([sum_one[:depth], sum_two], axis=1)
        sum_qkv = sum_qkv.reshape(projection_weight.shape)
        sum_gains = sum_one[depth, :gain_count]
        sum_out = grad_out_w.reshape((out_heads,) + cube + (out_depth, MODEL_WIDTH))
        sum_out = halved(halved(halved(sum_out, 2, 2), 2, 1), 1, 4)
    else:
        sum_qkv = (
            lax.psum_scatter(grad_qkv_w.astype(BF16), "dp", scatter_dimension=0, tiled=True)
            .astype(F32)
            .reshape(projection_weight.shape)
        )
        sum_out = lax.psum_scatter(
            grad_out_w.astype(BF16).reshape(out_heads, -1, MODEL_WIDTH), "dp",
            scatter_dimension=1, tiled=True,
        ).astype(F32)
        sum_gains = lax.psum_scatter(gain_sums, "dp", scatter_dimension=0, tiled=True)
    sum_gains = sum_gains + sum(flipped(sum_gains, "tensor", bit) for bit in range(1, shards))

    grad_normed_one = near_sum(back_0, back_1) + back_across.astype(F32)
    grad_rows_part, _ = norm_back(rows_float, gain_attn, grad_normed_one)
    grad_tokens = grad_middle + grad_rows_part
    mlp_rows = near_sum(sum_0, sum_1) + mlp_across.astype(F32)
    block_out = (middle + mlp_rows).astype(BF16)

    sum_gate_up = (
        feed_sum[:gate_rows].reshape(pieces, depth, half).swapaxes(0, 1).reshape(w_gate_up.shape)
    )
    sum_down = feed_sum[gate_rows:].reshape(2, -1, half).swapaxes(0, 1).reshape(w_down.shape)

    upd_qkv = adamw_update(
        projection_weight, first_moment_projection, second_moment_projection,
        sum_qkv, 2.0 * MODEL_WIDTH ** (-0.5), DECAY,
    )
    upd_out = adamw_update(
        w_out, first_out, second_out, sum_out,
        2.0 * (QUERY_HEADS * HEAD_SIZE // 64) ** (-0.5), DECAY,
    )
    upd_gate_up = adamw_update(
        w_gate_up, first_gate_up, second_gate_up, sum_gate_up,
        2.0 * MODEL_WIDTH ** (-0.5), DECAY,
    )
    upd_down = adamw_update(w_down, first_down, second_down, sum_down, 2.0 * FF ** (-0.5), DECAY)
    upd_gains = adamw_update(gains, first_gains, second_gains, sum_gains, 0.5, 0.0)
    updates = (upd_qkv, upd_out, upd_gate_up, upd_down, upd_gains)
    return (
        block_out,
        grad_tokens,
        *(update[2] for update in updates),
        *(update[0] for update in updates),
        *(update[1] for update in updates),
    )


def solution(mesh):
    weights = (
        P("dp", "tensor", None),
        P("tensor", "dp", None),
        P("dp", None, "tensor"),
        P("tensor", "dp", None),
        P("dp"),
    )
    batch = P(("dp", "tensor"), None)
    return jax.shard_map(
        per_device,
        mesh=mesh,
        in_specs=(batch, batch, P("dp", None), *weights, *weights, *weights),
        out_specs=(batch, batch, *weights, *weights, *weights),
        check_vma=False,
    )
```

```python
import jax
import jax.numpy as jnp
from jax import lax
from jax.experimental import pallas as pl
from jax.experimental.layout import Layout, with_layout_constraint
from jax.experimental.pallas import tpu as pltpu
from jax.sharding import PartitionSpec as P

MODEL_WIDTH = 1024
QUERY_HEADS = 16
KEY_VALUE_HEADS = 8
HEAD_SIZE = 128
FF = 3072
STEP = 10

EPS = 1e-06
THETA = 1000000.0
BETA_ONE = 0.9
BETA_TWO = 0.95
ADAM_EPS = 1e-08
DECAY = 0.1

GROUP = QUERY_HEADS // KEY_VALUE_HEADS
SLOTS = GROUP + 2
SCALE = HEAD_SIZE ** (-0.5)
LOG2E = 1.4426950408889634
BLOCK = 256
VMEM_LIMIT = 48 * 1024 * 1024
F32 = jnp.float32
BF16 = jnp.bfloat16


def norm_rows(values, scales):
    return values * lax.rsqrt(jnp.mean(values * values, axis=-1, keepdims=True) + EPS) * scales


def norm_back(values, scales, grad):
    r = lax.rsqrt(jnp.mean(values * values, axis=-1, keepdims=True) + EPS)
    u = grad * scales
    back = r * u - values * (r * r * r) * jnp.mean(u * values, axis=-1, keepdims=True)
    return back, jnp.sum(grad * values * r, axis=0)


def row_major(value):
    return with_layout_constraint(value, Layout(major_to_minor=tuple(range(value.ndim))))


def adamw_update(master, moment_one, moment_two, gradient, step_rate, decay_rate):
    next_one = BETA_ONE * moment_one + (1.0 - BETA_ONE) * gradient
    next_two = BETA_TWO * moment_two + (1.0 - BETA_TWO) * gradient * gradient
    one_hat = next_one / (1.0 - BETA_ONE**STEP)
    two_hat = next_two / (1.0 - BETA_TWO**STEP)
    next_master = master - step_rate * (
        one_hat / (jnp.sqrt(two_hat) + ADAM_EPS) + decay_rate * master
    )
    return (next_one, next_two, next_master)


def nt(a, b):
    return lax.dot_general(a, b, (((1,), (1,)), ((), ())), preferred_element_type=F32)


def nn(a, b):
    return jnp.dot(a, b, preferred_element_type=F32)


def head_rotated(x, gain, cos, sin):
    r = lax.rsqrt(jnp.mean(x * x, axis=-1, keepdims=True) + EPS)
    y = x * r * gain
    return y * cos + pltpu.roll(y, HEAD_SIZE // 2, 1) * sin


def head_back(x, gain, cos, sin, grad):
    r = lax.rsqrt(jnp.mean(x * x, axis=-1, keepdims=True) + EPS)
    turned = grad * cos - pltpu.roll(grad, HEAD_SIZE // 2, 1) * sin
    u = turned * gain
    back = r * u - x * (r * r * r) * jnp.mean(u * x, axis=-1, keepdims=True)
    return back, jnp.sum(turned * x * r, axis=0, keepdims=True)


def at_block(index):
    return pl.ds(pl.multiple_of(index * BLOCK, BLOCK), BLOCK)


def allowed_block(key_block, query_block, start):
    keys = key_block * BLOCK + lax.broadcasted_iota(jnp.int32, (BLOCK, BLOCK), 0)
    queries = query_block * BLOCK + lax.broadcasted_iota(jnp.int32, (BLOCK, BLOCK), 1)
    return (keys >= start) & (keys <= queries)


def lanes_of(h):
    return slice(h * HEAD_SIZE, (h + 1) * HEAD_SIZE)


def project_kernel(
    x, gain, matrix, cos, sin, gain_q, gain_k, normed_turned, raw_q, raw_k, q, k, v, k_turned, v_turned
):
    normed = norm_rows(x[...].astype(F32), gain[...])
    normed_turned[...] = normed.T.astype(BF16)
    h = normed.astype(BF16)
    c, s = cos[...], sin[...]
    for j in range(matrix.shape[1] // (SLOTS * HEAD_SIZE)):
        base = j * SLOTS * HEAD_SIZE
        part = nn(h, matrix[:, base : base + SLOTS * HEAD_SIZE])
        for g in range(GROUP):
            value = part[:, lanes_of(g)]
            raw_q[:, lanes_of(j * GROUP + g)] = value
            q[:, lanes_of(j * GROUP + g)] = head_rotated(value, gain_q[...], c, s).astype(BF16)
        value = part[:, lanes_of(GROUP)]
        raw_k[:, lanes_of(j)] = value
        turned = head_rotated(value, gain_k[...], c, s)
        k[:, lanes_of(j)] = turned.astype(BF16)
        k_turned[lanes_of(j), :] = turned.T.astype(BF16)
        value = part[:, lanes_of(GROUP + 1)]
        v[:, lanes_of(j)] = value.astype(BF16)
        v_turned[lanes_of(j), :] = value.T.astype(BF16)


def attend_kernel(offset, info, q, k, v_turned, start, out, out_turned, logs):
    blocks = k.shape[0] // BLOCK
    flip = info[blocks]

    def one_block(i, _):
        here = at_block(i)
        b = (i + offset) ^ flip
        first = start[:, here]
        queries = [q[here, lanes_of(h)] for h in range(GROUP)]

        def keys_step(kb, carry):
            there = at_block(kb ^ flip)
            key, value = k[there, :], v_turned[:, there]
            allowed = allowed_block(kb, b, first)
            after = []
            for h in range(GROUP):
                total, blend = carry[h]
                p = jnp.where(allowed, jnp.exp2(nt(key, queries[h]) * (SCALE * LOG2E)), 0.0)
                after.append(
                    (total + jnp.sum(p, axis=0, keepdims=True), blend + nn(value, p.astype(BF16)))
                )
            return tuple(after)

        zero = (jnp.zeros((1, BLOCK), F32), jnp.zeros((HEAD_SIZE, BLOCK), F32))
        done = lax.fori_loop(info[b], b + 1, keys_step, (zero,) * GROUP)
        for h in range(GROUP):
            total, blend = done[h]
            result = blend / total
            out[here, lanes_of(h)] = result.T.astype(BF16)
            out_turned[lanes_of(h), here] = result.astype(BF16)
            logs[0, h : h + 1, here] = jnp.log2(total)
        return 0

    lax.fori_loop(0, q.shape[0] // BLOCK, one_block, 0)


def back_blocks(
    offset, info, q, k, v, k_turned, start, logs, out, grad_out, raw_q, cos, sin, gain_q,
    grad_k, grad_v, store,
):
    flip = info[k.shape[0] // BLOCK]

    def one_block(i, total_gain):
        here = at_block(i)
        b = (i + offset) ^ flip
        first = start[:, here]
        queries, gradients, across, log = [], [], [], []
        for h in range(GROUP):
            g = grad_out[here, lanes_of(h)]
            queries.append(q[here, lanes_of(h)])
            gradients.append(g)
            both = g.astype(F32) * out[here, lanes_of(h)].astype(F32)
            across.append(jnp.sum(both.T, axis=0, keepdims=True))
            log.append(logs[0, h : h + 1, here])

        def keys_step(kb, carry):
            there = at_block(kb ^ flip)
            key, value, key_turned = k[there, :], v[there, :], k_turned[:, there]
            allowed = allowed_block(kb, b, first)
            after, add_k, add_v = [], 0.0, 0.0
            for h in range(GROUP):
                s = nt(key, queries[h])
                p = jnp.where(allowed, jnp.exp2(s * (SCALE * LOG2E) - log[h]), 0.0)
                d = (p * (nt(value, gradients[h]) - across[h])).astype(BF16)
                add_v = add_v + nn(p.astype(BF16), gradients[h])
                add_k = add_k + nn(d, queries[h])
                after.append(carry[h] + nn(key_turned, d))
            grad_k[there, :] += add_k
            grad_v[there, :] += add_v
            return tuple(after)

        zero = jnp.zeros((HEAD_SIZE, BLOCK), F32)
        done = lax.fori_loop(info[b], b + 1, keys_step, (zero,) * GROUP)
        c, s = cos[here, :], sin[here, :]
        for h in range(GROUP):
            back, gain = head_back(raw_q[here, lanes_of(h)], gain_q[...], c, s, done[h].T * SCALE)
            store(i, h, back.astype(BF16))
            total_gain = total_gain + gain
        return total_gain

    return lax.fori_loop(0, q.shape[0] // BLOCK, one_block, jnp.zeros((1, HEAD_SIZE), F32))


def back_own_kernel(
    info, q, k, v, k_turned, start, logs, out, grad_out, raw_q, cos, sin, gain_q,
    grad_q, grad_k, grad_v, grad_gain,
):
    grad_k[...] = jnp.zeros(grad_k.shape, F32)
    grad_v[...] = jnp.zeros(grad_v.shape, F32)

    def store(i, h, value):
        grad_q[at_block(i), lanes_of(h)] = value

    grad_gain[0, :, :] = back_blocks(
        0, info, q, k, v, k_turned, start, logs, out, grad_out, raw_q, cos, sin, gain_q,
        grad_k, grad_v, store,
    )


def back_other_kernel(
    info, q, k, v, k_turned, start, logs, out, grad_out, raw_q, cos, sin, gain_q,
    cos_all, sin_all, raw_k, gain_k, grad_q_own, grad_k_own, grad_v_own,
    grad_qkv, grad_gains, grad_k, grad_v,
):
    half = q.shape[0] // BLOCK
    blocks = k.shape[0] // BLOCK
    queries = GROUP * HEAD_SIZE
    grad_k[...] = grad_k_own[...]
    grad_v[...] = grad_v_own[...]
    grad_qkv[: half * BLOCK, :queries] = grad_q_own[...]

    def store(i, h, value):
        grad_qkv[at_block(i + half), lanes_of(h)] = value

    grad_gains[0, 0:1, :] = back_blocks(
        half, info, q, k, v, k_turned, start, logs, out, grad_out, raw_q, cos, sin, gain_q,
        grad_k, grad_v, store,
    )

    def finish(i, total_gain):
        rows = at_block(i)
        back, gain = head_back(
            raw_k[rows, :], gain_k[...], cos_all[rows, :], sin_all[rows, :], grad_k[rows, :] * SCALE
        )
        grad_qkv[rows, lanes_of(GROUP)] = back.astype(BF16)
        grad_qkv[rows, lanes_of(GROUP + 1)] = grad_v[rows, :].astype(BF16)
        return total_gain + gain

    grad_gains[0, 1:2, :] = lax.fori_loop(0, blocks, finish, jnp.zeros((1, HEAD_SIZE), F32))


def unpack(packed, gate_up, down):
    n, _, half = packed.shape
    depth = gate_up.shape[0] // n
    pieces = gate_up.shape[1] // half
    blocks = down.shape[0] // HEAD_SIZE
    deep = HEAD_SIZE // n
    for d in range(n):
        for b in range(pieces):
            gate_up[d * depth : (d + 1) * depth, b * half : (b + 1) * half] = packed[
                d, b * depth : (b + 1) * depth, :
            ]
        for c in range(2):
            for i in range(blocks):
                at = pieces * depth + (c * blocks + i) * deep
                to = i * HEAD_SIZE + d * deep
                down[to : to + deep, c * half : (c + 1) * half] = packed[d, at : at + deep, :]


def feed_kernel(packs, h, grad, *refs):
    step = pl.program_id(0)
    if packs:
        packed, *refs = refs
        *refs, gate_up, down = refs

        @pl.when(step == 0)
        def _():
            unpack(packed, gate_up, down)
    else:
        gate_up, down, *refs = refs
    h_turned, hidden_turned, grad_gate_up, back_a, back_b, sum_a, sum_b = refs
    width = down.shape[0]
    rows = h[...]
    both = nn(rows, gate_up[...])
    gate, up = both[:, :width], both[:, width:]
    sig = jax.nn.sigmoid(gate)
    gated = gate * sig
    value = gated * up
    hidden_turned[...] = value.T.astype(BF16)
    h_turned[...] = rows.astype(F32).T.astype(BF16)
    grad_hidden = nt(grad[...], down[...])
    grad_gate_up[:, :width] = (grad_hidden * up * (sig + gated * (1.0 - sig))).astype(BF16)
    grad_gate_up[:, width:] = (grad_hidden * gated).astype(BF16)
    back = nt(grad_gate_up[...], gate_up[...]).astype(BF16)
    total = nn(value.astype(BF16), down[...]).astype(BF16)
    first = step < pl.num_programs(0) // 2

    @pl.when(first)
    def _():
        back_a[...] = back
        sum_a[...] = total

    @pl.when(jnp.logical_not(first))
    def _():
        back_b[...] = back
        sum_b[...] = total


def feed_weights_kernel(
    packs, pieces, h_own, h_other, grad_own, grad_other, hidden_own, hidden_other, dy_own, dy_other,
    *out
):
    step = pl.program_id(0)
    half = dy_own.shape[1]

    for b in range(pieces):
        @pl.when(step == b)
        def _():
            value = nn(h_own[...], grad_own[...]) + nn(h_other[...], grad_other[...])
            value = value.astype(BF16)
            if packs:
                n = out[0].shape[0]
                depth = value.shape[0] // n
                for d in range(n):
                    out[0][d, b * depth : (b + 1) * depth, :] = value[d * depth : (d + 1) * depth]
            else:
                out[0][:, b * half : (b + 1) * half] = value

    for c in range(2):
        @pl.when(step == pieces + c)
        def _():
            value = nn(hidden_own[...], dy_own[...]) + nn(hidden_other[...], dy_other[...])
            value = value.astype(BF16)
            if packs:
                n = out[0].shape[0]
                depth, deep = h_own.shape[0] // n, HEAD_SIZE // n
                blocks = value.shape[0] // HEAD_SIZE
                for d in range(n):
                    for i in range(blocks):
                        at = pieces * depth + (c * blocks + i) * deep
                        of = i * HEAD_SIZE + d * deep
                        out[0][d, at : at + deep, :] = value[of : of + deep]
            else:
                out[1][:, c * half : (c + 1) * half] = value


def unproject_kernel(grad, matrix, out_a, out_b):
    value = nt(grad[...], matrix[...]).astype(BF16)
    first = pl.program_id(0) < pl.num_programs(0) // 2

    @pl.when(first)
    def _():
        out_a[...] = value

    @pl.when(jnp.logical_not(first))
    def _():
        out_b[...] = value


def params(name, flops):
    return dict(
        compiler_params=pltpu.CompilerParams(
            dimension_semantics=("arbitrary",), vmem_limit_bytes=VMEM_LIMIT
        ),
        cost_estimate=pl.CostEstimate(flops=flops // 64, bytes_accessed=1_000, transcendentals=0),
        name=name,
    )


def fixed(shape, index=None):
    index = (0,) * len(shape) if index is None else index
    return pl.BlockSpec(shape, lambda i, *_: index)


def shaped(shape, kind):
    return jax.ShapeDtypeStruct(shape, kind)


def project(x, gain, matrix, cos, sin, gain_q, gain_k):
    rows, width = x.shape
    heads = matrix.shape[1] // (SLOTS * HEAD_SIZE)
    by_rows = lambda n: pl.BlockSpec((BLOCK, n), lambda i: (i, 0))
    by_lanes = lambda n: pl.BlockSpec((n, BLOCK), lambda i: (0, i))
    q_width, k_width = heads * GROUP * HEAD_SIZE, heads * HEAD_SIZE
    return pl.pallas_call(
        project_kernel,
        grid=(rows // BLOCK,),
        in_specs=[
            by_rows(width), fixed((1, width)), fixed(matrix.shape), by_rows(HEAD_SIZE),
            by_rows(HEAD_SIZE), fixed((1, HEAD_SIZE)), fixed((1, HEAD_SIZE)),
        ],
        out_specs=[
            by_lanes(width), by_rows(q_width), by_rows(k_width), by_rows(q_width),
            by_rows(k_width), by_rows(k_width), by_lanes(k_width), by_lanes(k_width),
        ],
        out_shape=[
            shaped((width, rows), BF16), shaped((rows, q_width), F32),
            shaped((rows, k_width), F32), shaped((rows, q_width), BF16),
            shaped((rows, k_width), BF16), shaped((rows, k_width), BF16),
            shaped((k_width, rows), BF16), shaped((k_width, rows), BF16),
        ],
        **params("project", 10_000_000_000),
    )(x, gain, matrix, cos, sin, gain_q, gain_k)


def head_specs(half, rows):
    at = lambda j: j
    n = rows // 2
    return dict(
        q=pl.BlockSpec((n, GROUP * HEAD_SIZE), lambda j, info: (half, at(j))),
        k=pl.BlockSpec((rows, HEAD_SIZE), lambda j, info: (0, at(j))),
        turned=pl.BlockSpec((HEAD_SIZE, rows), lambda j, info: (at(j), 0)),
        start=pl.BlockSpec((1, n), lambda j, info: (0, half)),
        out=pl.BlockSpec((n, GROUP * HEAD_SIZE), lambda j, info: (0, at(j))),
        logs=pl.BlockSpec((1, GROUP, n), lambda j, info: (at(j), 0, 0)),
        angle=pl.BlockSpec((n, HEAD_SIZE), lambda j, info: (half, 0)),
    )


def attend(half, info, q, k, v_turned, start):
    rows = k.shape[0]
    n, heads = rows // 2, k.shape[1] // HEAD_SIZE
    s = head_specs(half, rows)
    return pl.pallas_call(
        lambda *refs: attend_kernel(half * n // BLOCK, *refs),
        grid_spec=pltpu.PrefetchScalarGridSpec(
            num_scalar_prefetch=1,
            grid=(heads,),
            in_specs=[s["q"], s["k"], s["turned"], s["start"]],
            out_specs=[
                s["out"], pl.BlockSpec((GROUP * HEAD_SIZE, n), lambda j, info: (j, 0)), s["logs"],
            ],
        ),
        out_shape=[
            shaped((n, q.shape[1]), BF16), shaped((q.shape[1], n), BF16),
            shaped((heads, GROUP, n), F32),
        ],
        **params("attend", 18_000_000_000),
    )(info, q, k, v_turned, start)


def attend_back_own(info, q, k, v, k_turned, start, logs, out, grad_out, raw_q, cos, sin, gain_q):
    rows = k.shape[0]
    n, heads = rows // 2, k.shape[1] // HEAD_SIZE
    s = head_specs(0, rows)
    return pl.pallas_call(
        back_own_kernel,
        grid_spec=pltpu.PrefetchScalarGridSpec(
            num_scalar_prefetch=1,
            grid=(heads,),
            in_specs=[
                s["q"], s["k"], s["k"], s["turned"], s["start"], s["logs"], s["out"], s["out"],
                s["q"], s["angle"], s["angle"], fixed((1, HEAD_SIZE)),
            ],
            out_specs=[
                s["out"], s["k"], s["k"],
                pl.BlockSpec((1, 1, HEAD_SIZE), lambda j, info: (j, 0, 0)),
            ],
        ),
        out_shape=[
            shaped((n, q.shape[1]), BF16), shaped(k.shape, F32), shaped(k.shape, F32),
            shaped((heads, 1, HEAD_SIZE), F32),
        ],
        **params("attend_back_own", 25_000_000_000),
    )(info, q, k, v, k_turned, start, logs, out, grad_out, raw_q, cos, sin, gain_q)


def attend_back_other(
    info, q, k, v, k_turned, start, logs, out, grad_out, raw_q, cos, sin, gain_q,
    raw_k, gain_k, grad_q, grad_k, grad_v,
):
    rows = k.shape[0]
    heads = k.shape[1] // HEAD_SIZE
    width = SLOTS * HEAD_SIZE
    s = head_specs(1, rows)
    row = fixed((1, HEAD_SIZE))
    return pl.pallas_call(
        back_other_kernel,
        grid_spec=pltpu.PrefetchScalarGridSpec(
            num_scalar_prefetch=1,
            grid=(heads,),
            in_specs=[
                s["q"], s["k"], s["k"], s["turned"], s["start"], s["logs"], s["out"], s["out"],
                s["q"], s["angle"], s["angle"], row,
                fixed((rows, HEAD_SIZE)), fixed((rows, HEAD_SIZE)), s["k"], row, s["out"], s["k"],
                s["k"],
            ],
            out_specs=[
                pl.BlockSpec((rows, width), lambda j, info: (0, j)),
                pl.BlockSpec((1, 2, HEAD_SIZE), lambda j, info: (j, 0, 0)),
            ],
            scratch_shapes=[pltpu.VMEM((rows, HEAD_SIZE), F32)] * 2,
        ),
        out_shape=[shaped((rows, heads * width), BF16), shaped((heads, 2, HEAD_SIZE), F32)],
        **params("attend_back_other", 28_000_000_000),
    )(
        info, q, k, v, k_turned, start, logs, out, grad_out, raw_q, cos, sin, gain_q,
        cos, sin, raw_k, gain_k, grad_q, grad_k, grad_v,
    )


def two_parts(rows, width):
    steps = rows // BLOCK // 2
    return (
        [
            pl.BlockSpec((BLOCK, width), lambda i: (jnp.minimum(i, steps - 1), 0)),
            pl.BlockSpec((BLOCK, width), lambda i: (jnp.maximum(i - steps, 0), 0)),
        ],
        [shaped((rows // 2, width), BF16)] * 2,
    )


def feed(h, grad, weights, hidden_count):
    rows, width = h.shape
    packs = len(weights) == 1
    by_rows = lambda n: pl.BlockSpec((BLOCK, n), lambda i: (i, 0))
    by_lanes = lambda n: pl.BlockSpec((n, BLOCK), lambda i: (0, i))
    specs, shapes = two_parts(rows, width)
    scratch = [
        pltpu.VMEM((width, 2 * hidden_count), BF16), pltpu.VMEM((hidden_count, width), BF16)
    ]
    return pl.pallas_call(
        lambda *refs: feed_kernel(packs, *refs),
        grid=(rows // BLOCK,),
        in_specs=[by_rows(width), by_rows(width), *(fixed(w.shape) for w in weights)],
        out_specs=[
            by_lanes(width), by_lanes(hidden_count), by_rows(2 * hidden_count), *specs, *specs
        ],
        out_shape=[
            shaped((width, rows), BF16), shaped((hidden_count, rows), BF16),
            shaped((rows, 2 * hidden_count), BF16), *shapes, *shapes,
        ],
        scratch_shapes=scratch if packs else [],
        **params("feed", 16_000_000_000),
    )(h, grad, *weights)


def feed_weights(packed_shape, h, grads, hidden, dy):
    width, n = h[0].shape
    half = width // 2
    pieces = grads[0].shape[1] // half
    count = hidden[0].shape[0]
    packs = packed_shape is not None
    gate_block = pl.BlockSpec((n, half), lambda i: (0, jnp.minimum(i, pieces - 1)))
    down_block = pl.BlockSpec((n, half), lambda i: (0, jnp.maximum(i - pieces, 0)))
    shapes = [packed_shape] if packs else [(width, 2 * count), (count, width)]
    return pl.pallas_call(
        lambda *refs: feed_weights_kernel(packs, pieces, *refs),
        grid=(pieces + 2,),
        in_specs=[
            fixed((width, n)), fixed((width, n)), gate_block, gate_block,
            fixed((count, n)), fixed((count, n)), down_block, down_block,
        ],
        out_specs=[fixed(shape) for shape in shapes],
        out_shape=[shaped(shape, BF16) for shape in shapes],
        **params("feed_weights", 16_000_000_000),
    )(*h, *grads, *hidden, *dy)


def unproject(half, grad, matrix):
    rows, width = grad.shape
    n = rows // 2
    steps = n // BLOCK
    specs, shapes = two_parts(n, matrix.shape[0])
    return pl.pallas_call(
        unproject_kernel,
        grid=(steps,),
        in_specs=[pl.BlockSpec((BLOCK, width), lambda i: (i + half * steps, 0)), fixed(matrix.shape)],
        out_specs=specs,
        out_shape=shapes,
        **params("unproject", 4_000_000_000),
    )(grad, matrix)


def flipped(value, axis, bit, name="part"):
    with jax.named_scope(name):
        return lax.ppermute(value, axis, [(i, i ^ bit) for i in range(lax.axis_size(axis))])


def together(*values):
    return lax.optimization_barrier(values)


def near_sum(part, beside):
    return part.astype(F32) + flipped(beside, "tensor", 1).astype(F32)


def halved(parts, axis, bit):
    mine = (lax.axis_index("dp") // bit) % 2
    send = lax.dynamic_index_in_dim(parts, 1 - mine, axis, keepdims=False).astype(BF16)
    keep = lax.dynamic_index_in_dim(parts, mine, axis, keepdims=False)
    return keep + flipped(send, "dp", bit).astype(F32)


def per_device(
    tokens, cotangent, lengths,
    projection_weight, w_out, w_gate_up, w_down, gains,
    first_moment_projection, first_out, first_gate_up, first_down, first_gains,
    second_moment_projection, second_out, second_gate_up, second_down, second_gains,
):
    shards = lax.axis_size("tensor")
    spread = lax.axis_size("dp")
    me = lax.axis_index("tensor")
    local_rows = tokens.shape[0]
    rows = local_rows * shards
    blocks = rows // BLOCK
    kv_local = projection_weight.shape[1]
    hidden_local = w_gate_up.shape[2]
    out_heads, out_depth = w_out.shape[0], w_out.shape[1]
    down_blocks, down_depth = w_down.shape[0], w_down.shape[1]
    depth = projection_weight.shape[0]
    gain_count = gains.shape[0]

    half = MODEL_WIDTH // 2
    pieces = 2 * hidden_local // half
    gate_rows = pieces * depth
    out_rows = out_heads * out_depth
    cubic = spread == 8

    pack_one = jnp.concatenate(
        [
            projection_weight.astype(BF16).reshape(depth, -1),
            w_out.astype(BF16).reshape(-1, MODEL_WIDTH),
            jnp.pad(gains.astype(BF16)[None, :], ((0, 15), (0, MODEL_WIDTH - gain_count))),
        ],
        axis=0,
    )
    pack_two = jnp.concatenate(
        [
            w_gate_up.astype(BF16).reshape(depth, pieces, half).swapaxes(0, 1).reshape(-1, half),
            w_down.astype(BF16).reshape(-1, 2, half).swapaxes(0, 1).reshape(-1, half),
        ],
        axis=0,
    )

    def split_one(value):
        return (
            value[..., :depth, :],
            value[..., depth : depth + out_rows, :],
            value[..., depth + out_rows, :gain_count],
        )

    full_qkv, full_out, full_gains = split_one(lax.all_gather(pack_one, "dp", axis=0, tiled=False))
    full_out = full_out.reshape(spread, out_heads, out_depth, MODEL_WIDTH).swapaxes(0, 1)
    full_two = lax.all_gather(pack_two, "dp", axis=0, tiled=False)
    qkv_matrix = full_qkv.reshape(MODEL_WIDTH, -1)
    out_matrix = full_out.reshape(-1, MODEL_WIDTH)
    gains_all = full_gains.reshape(-1).astype(F32)
    gain_attn = gains_all[None, :MODEL_WIDTH]
    gain_mlp = gains_all[MODEL_WIDTH : 2 * MODEL_WIDTH]
    gain_query = gains_all[None, 2 * MODEL_WIDTH : 2 * MODEL_WIDTH + HEAD_SIZE]
    gain_key = gains_all[None, 2 * MODEL_WIDTH + HEAD_SIZE :]

    doc_ends = jnp.cumsum(lengths[0])
    doc_starts = doc_ends - lengths[0]

    def start_of(index):
        return jnp.max(
            jnp.where(index[:, None] >= doc_starts[None, :], doc_starts[None, :], 0), axis=1
        )

    order = me ^ jnp.arange(shards, dtype=jnp.int32)
    index_of_row = (
        order[:, None] * local_rows + jnp.arange(local_rows, dtype=jnp.int32)[None, :]
    ).reshape(-1)
    start_of_row = start_of(index_of_row)
    position = index_of_row - start_of_row
    inverse = THETA ** (-2.0 * jnp.arange(HEAD_SIZE // 2, dtype=F32) / HEAD_SIZE)
    turned = position.astype(F32)[:, None] * inverse[None, :]
    cosine, sine = jnp.cos(turned), jnp.sin(turned)
    cos = jnp.concatenate([cosine, cosine], axis=1)
    sin = jnp.concatenate([-sine, sine], axis=1)
    block_starts = start_of(jnp.arange(blocks, dtype=jnp.int32) * BLOCK) // BLOCK
    info = jnp.concatenate([block_starts, (me * (local_rows // BLOCK))[None]]).astype(jnp.int32)
    start = start_of_row[None, :]

    rows_float = tokens.astype(F32)
    tokens_across = flipped(tokens, "tensor", 2, "tokens_across")
    tokens_all = jnp.concatenate(
        [tokens, flipped(tokens, "tensor", 1), tokens_across, flipped(tokens_across, "tensor", 1)],
        axis=0,
    )
    normed_turned, raw_q, raw_k, q, k, v, k_turned, v_turned = project(
        tokens_all, gain_attn, qkv_matrix, cos, sin, gain_query, gain_key
    )
    grad_across = flipped(cotangent, "tensor", 2, "grad_across")
    heads_other, heads_other_turned, logs_other = attend(1, info, q, k, v_turned, start)
    heads_other, grad_across = together(heads_other, grad_across)
    beside = nn(heads_other[local_rows:], out_matrix).astype(BF16)
    near = near_sum(nn(heads_other[:local_rows], out_matrix), beside).astype(BF16)
    near, q_own = together(near, q)
    attn_across = flipped(near, "tensor", 2, "attn_across")
    heads_own, heads_own_turned, logs_own = attend(0, info, q_own, k, v_turned, start)
    heads_own, attn_across, full_two = together(heads_own, attn_across, full_two)
    beside = nn(heads_own[local_rows:], out_matrix).astype(BF16)
    attn_rows = near_sum(nn(heads_own[:local_rows], out_matrix), beside) + attn_across.astype(F32)
    middle = rows_float + attn_rows
    if cubic:
        feed_matrices = (full_two,)
    else:
        feed_matrices = (
            full_two[:, :gate_rows]
            .reshape(spread, pieces, depth, half)
            .swapaxes(1, 2)
            .reshape(MODEL_WIDTH, -1),
            full_two[:, gate_rows:]
            .reshape(spread, 2, down_blocks, down_depth, half)
            .transpose(2, 0, 3, 1, 4)
            .reshape(-1, MODEL_WIDTH),
        )

    grad_own = jnp.concatenate([cotangent, flipped(cotangent, "tensor", 1)], axis=0)
    grad_other = jnp.concatenate([grad_across, flipped(grad_across, "tensor", 1)], axis=0)
    normed_two = norm_rows(middle, gain_mlp).astype(BF16)
    normed_across = flipped(normed_two, "tensor", 2, "normed_across")
    normed_own = jnp.concatenate([normed_two, flipped(normed_two, "tensor", 1)], axis=0)
    h_own, hidden_own, feed_grad_own, back_0, back_1, sum_0, sum_1 = feed(
        normed_own, grad_own, feed_matrices, hidden_local
    )
    normed_across, back_0 = together(normed_across, back_0)
    normed_other = jnp.concatenate([normed_across, flipped(normed_across, "tensor", 1)], axis=0)
    h_other, hidden_other, feed_grad_other, back_2, back_3, sum_2, sum_3 = feed(
        normed_other, grad_other, feed_matrices, hidden_local
    )
    near = near_sum(back_2, back_3).astype(BF16)
    back_near = near_sum(back_0, back_1)
    near, h_own = together(near, h_own)
    back_across = flipped(near, "tensor", 2, "back_across")

    feed_grads = feed_weights(
        full_two.shape if cubic else None, (h_own, h_other), (feed_grad_own, feed_grad_other),
        (hidden_own, hidden_other), (grad_own, grad_other),
    )
    back_across, *feed_grads = together(back_across, *feed_grads)
    if cubic:
        feed_pack = feed_grads[0]
    else:
        feed_pack = jnp.concatenate(
            [
                feed_grads[0].reshape(spread, depth, pieces, half)
                .swapaxes(1, 2)
                .reshape(spread, -1, half),
                feed_grads[1].reshape(down_blocks, spread, down_depth, 2, half)
                .transpose(1, 3, 0, 2, 4)
                .reshape(spread, -1, half),
            ],
            axis=1,
        )
    feed_sum = lax.psum_scatter(feed_pack, "dp", scatter_dimension=0, tiled=True)[0].astype(F32)
    grad_middle_part, grad_gain_mlp = norm_back(
        middle, gain_mlp, back_near + back_across.astype(F32)
    )
    grad_middle = cotangent.astype(F32) + grad_middle_part
    grad_middle_low = grad_middle.astype(BF16)
    grad_middle_across = flipped(grad_middle_low, "tensor", 2, "grad_middle_across")

    grad_middle_own = jnp.concatenate(
        [grad_middle_low, flipped(grad_middle_low, "tensor", 1)], axis=0
    )
    grad_heads_own = nt(grad_middle_own, out_matrix).astype(BF16)
    grad_q, grad_k, grad_v, gain_own = attend_back_own(
        info, q, k, v, k_turned, start, logs_own, heads_own, grad_heads_own, raw_q, cos, sin,
        gain_query,
    )
    grad_middle_across, grad_q, sum_2, sum_3 = together(grad_middle_across, grad_q, sum_2, sum_3)
    near_mlp = near_sum(sum_2, sum_3).astype(BF16)
    grad_middle_other = jnp.concatenate(
        [grad_middle_across, flipped(grad_middle_across, "tensor", 1)], axis=0
    )
    grad_heads_other = nt(grad_middle_other, out_matrix).astype(BF16)
    grad_out_w = (
        nn(heads_own_turned, grad_middle_own) + nn(heads_other_turned, grad_middle_other)
    ).astype(BF16)
    near_mlp, grad_out_w, grad_heads_other = together(near_mlp, grad_out_w, grad_heads_other)
    mlp_across = flipped(near_mlp, "tensor", 2, "mlp_across")
    grad_qkv, gain_other = attend_back_other(
        info, q, k, v, k_turned, start, logs_other, heads_other, grad_heads_other,
        raw_q, cos, sin, gain_query, raw_k, gain_key, grad_q, grad_k, grad_v,
    )
    grad_qkv, mlp_across = together(grad_qkv, mlp_across)
    back_2, back_3 = unproject(1, grad_qkv, qkv_matrix)
    back_2, back_3, grad_qkv = together(back_2, back_3, grad_qkv)
    grad_qkv_w = nn(normed_turned, grad_qkv)
    near = near_sum(back_2, back_3).astype(BF16)
    near, grad_qkv, grad_qkv_w, grad_out_w = together(near, grad_qkv, grad_qkv_w, grad_out_w)
    back_across = flipped(near, "tensor", 2, "back_across")
    grad_gain_attn = jnp.sum(qkv_matrix.astype(F32) * grad_qkv_w, axis=1) / gain_attn[0]
    grad_gain_heads = jnp.sum(gain_other, axis=0) + jnp.pad(
        jnp.sum(gain_own, axis=0), ((0, 1), (0, 0))
    )
    gain_sums = jnp.concatenate([grad_gain_attn, grad_gain_mlp, grad_gain_heads.reshape(-1)])
    back_0, back_1 = unproject(0, grad_qkv, qkv_matrix)
    if cubic:
        cube = (2, 2, 2)
        columns = grad_qkv_w.shape[1] // 2
        gain_rows = jnp.pad(
            gain_sums.reshape(cube + (1, gain_count)),
            ((0, 0),) * 3 + ((0, 15), (0, columns - gain_count)),
        )
        sum_one = jnp.concatenate(
            [grad_qkv_w[:, :columns].reshape(cube + (depth, -1)), gain_rows], axis=3
        )
        sum_two = grad_qkv_w[:, columns:].reshape(cube + (depth, -1))
        sum_one, sum_two = halved(sum_one, 1, 2), halved(sum_two, 2, 1)
        sum_one, sum_two = halved(sum_one, 1, 1), halved(sum_two, 1, 2)
        sum_out = grad_out_w.reshape((out_heads,) + cube + (out_depth, MODEL_WIDTH))
        sum_out = halved(halved(sum_out, 3, 1), 2, 2)
        sum_one, sum_two, sum_out, back_across, feed_sum = together(
            sum_one, sum_two, sum_out, back_across, feed_sum
        )
        sum_one, sum_two = halved(sum_one, 0, 4), halved(sum_two, 0, 4)
        sum_out = halved(sum_out, 1, 4)
        sum_qkv = jnp.concatenate([sum_one[:depth], sum_two], axis=1)
        sum_qkv = sum_qkv.reshape(projection_weight.shape)
        sum_gains = sum_one[depth, :gain_count]
    else:
        sum_qkv = (
            lax.psum_scatter(grad_qkv_w.astype(BF16), "dp", scatter_dimension=0, tiled=True)
            .astype(F32)
            .reshape(projection_weight.shape)
        )
        sum_out = lax.psum_scatter(
            grad_out_w.reshape(out_heads, -1, MODEL_WIDTH), "dp", scatter_dimension=1, tiled=True
        ).astype(F32)
        sum_gains = lax.psum_scatter(gain_sums, "dp", scatter_dimension=0, tiled=True)
    sum_gains = sum_gains + sum(flipped(sum_gains, "tensor", bit) for bit in range(1, shards))

    grad_normed_one = near_sum(back_0, back_1) + back_across.astype(F32)
    grad_rows_part, _ = norm_back(rows_float, gain_attn, grad_normed_one)
    grad_tokens = grad_middle + grad_rows_part
    mlp_rows = near_sum(sum_0, sum_1) + mlp_across.astype(F32)
    block_out = (middle + mlp_rows).astype(BF16)

    sum_gate_up = (
        feed_sum[:gate_rows].reshape(pieces, depth, half).swapaxes(0, 1).reshape(w_gate_up.shape)
    )
    sum_down = feed_sum[gate_rows:].reshape(2, -1, half).swapaxes(0, 1).reshape(w_down.shape)

    upd_qkv = adamw_update(
        projection_weight, first_moment_projection, second_moment_projection,
        row_major(sum_qkv), 2.0 * MODEL_WIDTH ** (-0.5), DECAY,
    )
    upd_out = adamw_update(
        w_out, first_out, second_out, sum_out,
        2.0 * (QUERY_HEADS * HEAD_SIZE // 64) ** (-0.5), DECAY,
    )
    upd_gate_up = adamw_update(
        w_gate_up, first_gate_up, second_gate_up, row_major(sum_gate_up),
        2.0 * MODEL_WIDTH ** (-0.5), DECAY,
    )
    upd_down = adamw_update(w_down, first_down, second_down, sum_down, 2.0 * FF ** (-0.5), DECAY)
    upd_gains = adamw_update(gains, first_gains, second_gains, sum_gains, 0.5, 0.0)
    updates = (upd_qkv, upd_out, upd_gate_up, upd_down, upd_gains)
    return (
        block_out,
        grad_tokens,
        *(update[2] for update in updates),
        *(update[0] for update in updates),
        *(update[1] for update in updates),
    )


def solution(mesh):
    weights = (
        P("dp", "tensor", None),
        P("tensor", "dp", None),
        P("dp", None, "tensor"),
        P("tensor", "dp", None),
        P("dp"),
    )
    batch = P(("dp", "tensor"), None)
    return jax.shard_map(
        per_device,
        mesh=mesh,
        in_specs=(batch, batch, P("dp", None), *weights, *weights, *weights),
        out_specs=(batch, batch, *weights, *weights, *weights),
        check_vma=False,
    )
```

```python
import jax
import jax.numpy as jnp
from jax import lax
from jax.experimental import pallas as pl
from jax.experimental.layout import Layout, with_layout_constraint
from jax.experimental.pallas import tpu as pltpu
from jax.sharding import PartitionSpec as P

MODEL_WIDTH = 1024
QUERY_HEADS = 16
KEY_VALUE_HEADS = 8
HEAD_SIZE = 128
FF = 3072
STEP = 10

EPS = 1e-06
THETA = 1000000.0
BETA_ONE = 0.9
BETA_TWO = 0.95
ADAM_EPS = 1e-08
DECAY = 0.1

GROUP = QUERY_HEADS // KEY_VALUE_HEADS
SLOTS = GROUP + 2
SCALE = HEAD_SIZE ** (-0.5)
LOG2E = 1.4426950408889634
BLOCK = 256
WIDE_BLOCK = 512
VMEM_LIMIT = 56 * 1024 * 1024
F32 = jnp.float32
BF16 = jnp.bfloat16


def norm_rows(values, scales):
    return values * lax.rsqrt(jnp.mean(values * values, axis=-1, keepdims=True) + EPS) * scales


def norm_back(values, scales, grad):
    r = lax.rsqrt(jnp.mean(values * values, axis=-1, keepdims=True) + EPS)
    u = grad * scales
    back = r * u - values * (r * r * r) * jnp.mean(u * values, axis=-1, keepdims=True)
    return back, jnp.sum(grad * values * r, axis=0)


def row_major(value):
    return with_layout_constraint(value, Layout(major_to_minor=tuple(range(value.ndim))))


def adamw_update(master, moment_one, moment_two, gradient, step_rate, decay_rate):
    next_one = BETA_ONE * moment_one + (1.0 - BETA_ONE) * gradient
    next_two = BETA_TWO * moment_two + (1.0 - BETA_TWO) * gradient * gradient
    one_hat = next_one / (1.0 - BETA_ONE**STEP)
    two_hat = next_two / (1.0 - BETA_TWO**STEP)
    next_master = master - step_rate * (
        one_hat / (jnp.sqrt(two_hat) + ADAM_EPS) + decay_rate * master
    )
    return (next_one, next_two, next_master)


def nt(a, b):
    return lax.dot_general(a, b, (((1,), (1,)), ((), ())), preferred_element_type=F32)


def nn(a, b):
    return jnp.dot(a, b, preferred_element_type=F32)


def head_rotated(x, gain, cos, sin):
    r = lax.rsqrt(jnp.mean(x * x, axis=-1, keepdims=True) + EPS)
    y = x * r * gain
    return y * cos + pltpu.roll(y, HEAD_SIZE // 2, 1) * sin


def head_back(x, gain, cos, sin, grad):
    r = lax.rsqrt(jnp.mean(x * x, axis=-1, keepdims=True) + EPS)
    turned = grad * cos - pltpu.roll(grad, HEAD_SIZE // 2, 1) * sin
    u = turned * gain
    back = r * u - x * (r * r * r) * jnp.mean(u * x, axis=-1, keepdims=True)
    return back, jnp.sum(turned * x * r, axis=0, keepdims=True)


def at_block(index):
    return pl.ds(pl.multiple_of(index * BLOCK, BLOCK), BLOCK)


def allowed_block(key_block, query_block, start):
    keys = key_block * BLOCK + lax.broadcasted_iota(jnp.int32, (BLOCK, BLOCK), 0)
    queries = query_block * BLOCK + lax.broadcasted_iota(jnp.int32, (BLOCK, BLOCK), 1)
    return (keys >= start) & (keys <= queries)


def lanes_of(h):
    return slice(h * HEAD_SIZE, (h + 1) * HEAD_SIZE)


def project_kernel(
    x, gain, matrix, cos, sin, gain_q, gain_k, normed_turned, raw_q, raw_k, q, k, v, k_turned, v_turned
):
    normed = norm_rows(x[...].astype(F32), gain[...])
    normed_turned[...] = normed.T.astype(BF16)
    h = normed.astype(BF16)
    c, s = cos[...], sin[...]
    for j in range(matrix.shape[1] // (SLOTS * HEAD_SIZE)):
        base = j * SLOTS * HEAD_SIZE
        part = nn(h, matrix[:, base : base + SLOTS * HEAD_SIZE])
        for g in range(GROUP):
            value = part[:, lanes_of(g)]
            raw_q[:, lanes_of(j * GROUP + g)] = value
            q[:, lanes_of(j * GROUP + g)] = head_rotated(value, gain_q[...], c, s).astype(BF16)
        value = part[:, lanes_of(GROUP)]
        raw_k[:, lanes_of(j)] = value
        turned = head_rotated(value, gain_k[...], c, s)
        k[:, lanes_of(j)] = turned.astype(BF16)
        k_turned[lanes_of(j), :] = turned.T.astype(BF16)
        value = part[:, lanes_of(GROUP + 1)]
        v[:, lanes_of(j)] = value.astype(BF16)
        v_turned[lanes_of(j), :] = value.T.astype(BF16)


def heads_of(k):
    return [(j, j * GROUP + g) for j in range(k.shape[1] // HEAD_SIZE) for g in range(GROUP)]


def attend_kernel(offset, info, q, k, v_turned, start, out, out_turned, logs):
    blocks = k.shape[0] // BLOCK
    flip = info[blocks]
    pairs = heads_of(k)

    def one_block(i, _):
        here = at_block(i)
        b = (i + offset) ^ flip
        first = start[:, here]
        queries = [q[here, lanes_of(h)] for _, h in pairs]

        def keys_step(kb, carry):
            there = at_block(kb ^ flip)
            allowed = allowed_block(kb, b, first)
            after = []
            for j, h in pairs:
                total, blend = carry[h]
                score = nt(k[there, lanes_of(j)], queries[h])
                p = jnp.where(allowed, jnp.exp2(score * (SCALE * LOG2E)), 0.0)
                after.append(
                    (
                        total + jnp.sum(p, axis=0, keepdims=True),
                        blend + nn(v_turned[lanes_of(j), there], p.astype(BF16)),
                    )
                )
            return tuple(after)

        zero = (jnp.zeros((1, BLOCK), F32), jnp.zeros((HEAD_SIZE, BLOCK), F32))
        done = lax.fori_loop(info[b], b + 1, keys_step, (zero,) * len(pairs))
        for _, h in pairs:
            total, blend = done[h]
            result = blend / total
            out[here, lanes_of(h)] = result.T.astype(BF16)
            out_turned[lanes_of(h), here] = result.astype(BF16)
            logs[h : h + 1, here] = jnp.log2(total)
        return 0

    lax.fori_loop(0, q.shape[0] // BLOCK, one_block, 0)


def back_blocks(
    offset, info, q, k, v, k_turned, start, logs, out, grad_out, raw_q, cos, sin, gain_q,
    grad_k, grad_v, store,
):
    flip = info[k.shape[0] // BLOCK]
    pairs = heads_of(k)

    def one_block(i, total_gain):
        here = at_block(i)
        b = (i + offset) ^ flip
        first = start[:, here]
        across = []
        for _, h in pairs:
            both = grad_out[here, lanes_of(h)].astype(F32) * out[here, lanes_of(h)].astype(F32)
            across.append(jnp.sum(both.T, axis=0, keepdims=True))

        def keys_step(kb, carry):
            there = at_block(kb ^ flip)
            allowed = allowed_block(kb, b, first)
            after = []
            add_k, add_v = [0.0] * (len(pairs) // GROUP), [0.0] * (len(pairs) // GROUP)
            for j, h in pairs:
                query, gradient = q[here, lanes_of(h)], grad_out[here, lanes_of(h)]
                s = nt(k[there, lanes_of(j)], query)
                p = jnp.where(allowed, jnp.exp2(s * (SCALE * LOG2E) - logs[h : h + 1, here]), 0.0)
                d = (p * (nt(v[there, lanes_of(j)], gradient) - across[h])).astype(BF16)
                add_v[j] = add_v[j] + nn(p.astype(BF16), gradient)
                add_k[j] = add_k[j] + nn(d, query)
                after.append(carry[h] + nn(k_turned[lanes_of(j), there], d))
            for j in range(len(add_k)):
                grad_k[there, lanes_of(j)] += add_k[j]
                grad_v[there, lanes_of(j)] += add_v[j]
            return tuple(after)

        zero = jnp.zeros((HEAD_SIZE, BLOCK), F32)
        done = lax.fori_loop(info[b], b + 1, keys_step, (zero,) * len(pairs))
        c, s = cos[here, :], sin[here, :]
        for _, h in pairs:
            back, gain = head_back(raw_q[here, lanes_of(h)], gain_q[...], c, s, done[h].T * SCALE)
            store(i, h, back.astype(BF16))
            total_gain = total_gain + gain
        return total_gain

    return lax.fori_loop(0, q.shape[0] // BLOCK, one_block, jnp.zeros((1, HEAD_SIZE), F32))


def back_own_kernel(
    info, q, k, v, k_turned, start, logs, out, grad_out, raw_q, cos, sin, gain_q,
    grad_q, grad_k, grad_v, grad_gain,
):
    grad_k[...] = jnp.zeros(grad_k.shape, F32)
    grad_v[...] = jnp.zeros(grad_v.shape, F32)

    def store(i, h, value):
        grad_q[at_block(i), lanes_of(h)] = value

    grad_gain[...] = back_blocks(
        0, info, q, k, v, k_turned, start, logs, out, grad_out, raw_q, cos, sin, gain_q,
        grad_k, grad_v, store,
    )


def slot_lanes(j, slot):
    return lanes_of(j * SLOTS + slot)


def back_other_kernel(
    info, q, k, v, k_turned, start, logs, out, grad_out, raw_q, cos, sin, gain_q,
    cos_all, sin_all, raw_k, gain_k, grad_q_own, grad_k_own, grad_v_own,
    grad_qkv, grad_gains, grad_k, grad_v,
):
    half = q.shape[0] // BLOCK
    blocks = k.shape[0] // BLOCK
    heads = k.shape[1] // HEAD_SIZE
    grad_k[...] = grad_k_own[...]
    grad_v[...] = grad_v_own[...]
    for h in range(heads * GROUP):
        grad_qkv[: half * BLOCK, slot_lanes(h // GROUP, h % GROUP)] = grad_q_own[:, lanes_of(h)]

    def store(i, h, value):
        grad_qkv[at_block(i + half), slot_lanes(h // GROUP, h % GROUP)] = value

    grad_gains[0:1, :] = back_blocks(
        half, info, q, k, v, k_turned, start, logs, out, grad_out, raw_q, cos, sin, gain_q,
        grad_k, grad_v, store,
    )

    def finish(i, total_gain):
        rows = at_block(i)
        for j in range(heads):
            back, gain = head_back(
                raw_k[rows, lanes_of(j)], gain_k[...], cos_all[rows, :], sin_all[rows, :],
                grad_k[rows, lanes_of(j)] * SCALE,
            )
            grad_qkv[rows, slot_lanes(j, GROUP)] = back.astype(BF16)
            grad_qkv[rows, slot_lanes(j, GROUP + 1)] = grad_v[rows, lanes_of(j)].astype(BF16)
            total_gain = total_gain + gain
        return total_gain

    grad_gains[1:2, :] = lax.fori_loop(0, blocks, finish, jnp.zeros((1, HEAD_SIZE), F32))


def unpack(packed, gate_up, down):
    n, _, half = packed.shape
    depth = gate_up.shape[0] // n
    pieces = gate_up.shape[1] // half
    blocks = down.shape[0] // HEAD_SIZE
    deep = HEAD_SIZE // n
    for d in range(n):
        for b in range(pieces):
            gate_up[d * depth : (d + 1) * depth, b * half : (b + 1) * half] = packed[
                d, b * depth : (b + 1) * depth, :
            ]
        for c in range(2):
            for i in range(blocks):
                at = pieces * depth + (c * blocks + i) * deep
                to = i * HEAD_SIZE + d * deep
                down[to : to + deep, c * half : (c + 1) * half] = packed[d, at : at + deep, :]


def feed_kernel(packs, h, grad, *refs):
    step = pl.program_id(0)
    if packs:
        packed, *refs = refs
        *refs, gate_up, down = refs

        @pl.when(step == 0)
        def _():
            unpack(packed, gate_up, down)
    else:
        gate_up, down, *refs = refs
    h_turned, hidden_turned, grad_gate_up, back_a, back_b, sum_a, sum_b = refs
    width = down.shape[0]
    rows = h[...]
    both = nn(rows, gate_up[...])
    gate, up = both[:, :width], both[:, width:]
    sig = jax.nn.sigmoid(gate)
    gated = gate * sig
    value = gated * up
    hidden_turned[...] = value.T.astype(BF16)
    h_turned[...] = rows.astype(F32).T.astype(BF16)
    grad_hidden = nt(grad[...], down[...])
    grad_gate_up[:, :width] = (grad_hidden * up * (sig + gated * (1.0 - sig))).astype(BF16)
    grad_gate_up[:, width:] = (grad_hidden * gated).astype(BF16)
    back = nt(grad_gate_up[...], gate_up[...]).astype(BF16)
    total = nn(value.astype(BF16), down[...]).astype(BF16)
    first = step < pl.num_programs(0) // 2

    @pl.when(first)
    def _():
        back_a[...] = back
        sum_a[...] = total

    @pl.when(jnp.logical_not(first))
    def _():
        back_b[...] = back
        sum_b[...] = total


def feed_weights_kernel(
    packs, pieces, h_own, h_other, grad_own, grad_other, hidden_own, hidden_other, dy_own, dy_other,
    *out
):
    step = pl.program_id(0)
    half = dy_own.shape[1]

    for b in range(pieces):
        @pl.when(step == b)
        def _():
            value = nn(h_own[...], grad_own[...]) + nn(h_other[...], grad_other[...])
            value = value.astype(BF16)
            if packs:
                n = out[0].shape[0]
                depth = value.shape[0] // n
                for d in range(n):
                    out[0][d, b * depth : (b + 1) * depth, :] = value[d * depth : (d + 1) * depth]
            else:
                out[0][:, b * half : (b + 1) * half] = value

    for c in range(2):
        @pl.when(step == pieces + c)
        def _():
            value = nn(hidden_own[...], dy_own[...]) + nn(hidden_other[...], dy_other[...])
            value = value.astype(BF16)
            if packs:
                n = out[0].shape[0]
                depth, deep = h_own.shape[0] // n, HEAD_SIZE // n
                blocks = value.shape[0] // HEAD_SIZE
                for d in range(n):
                    for i in range(blocks):
                        at = pieces * depth + (c * blocks + i) * deep
                        of = i * HEAD_SIZE + d * deep
                        out[0][d, at : at + deep, :] = value[of : of + deep]
            else:
                out[1][:, c * half : (c + 1) * half] = value


def unproject_kernel(grad, matrix, out_a, out_b):
    value = nt(grad[...], matrix[...]).astype(BF16)
    first = pl.program_id(0) < pl.num_programs(0) // 2

    @pl.when(first)
    def _():
        out_a[...] = value

    @pl.when(jnp.logical_not(first))
    def _():
        out_b[...] = value


def params(name, flops):
    return dict(
        compiler_params=pltpu.CompilerParams(
            dimension_semantics=("arbitrary",), vmem_limit_bytes=VMEM_LIMIT
        ),
        cost_estimate=pl.CostEstimate(flops=flops // 64, bytes_accessed=1_000, transcendentals=0),
        name=name,
    )


def fixed(shape, index=None):
    index = (0,) * len(shape) if index is None else index
    return pl.BlockSpec(shape, lambda i, *_: index)


def shaped(shape, kind):
    return jax.ShapeDtypeStruct(shape, kind)


def project(x, gain, matrix, cos, sin, gain_q, gain_k):
    rows, width = x.shape
    heads = matrix.shape[1] // (SLOTS * HEAD_SIZE)
    by_rows = lambda n: pl.BlockSpec((WIDE_BLOCK, n), lambda i: (i, 0))
    by_lanes = lambda n: pl.BlockSpec((n, WIDE_BLOCK), lambda i: (0, i))
    q_width, k_width = heads * GROUP * HEAD_SIZE, heads * HEAD_SIZE
    return pl.pallas_call(
        project_kernel,
        grid=(rows // WIDE_BLOCK,),
        in_specs=[
            by_rows(width), fixed((1, width)), fixed(matrix.shape), by_rows(HEAD_SIZE),
            by_rows(HEAD_SIZE), fixed((1, HEAD_SIZE)), fixed((1, HEAD_SIZE)),
        ],
        out_specs=[
            by_lanes(width), by_rows(q_width), by_rows(k_width), by_rows(q_width),
            by_rows(k_width), by_rows(k_width), by_lanes(k_width), by_lanes(k_width),
        ],
        out_shape=[
            shaped((width, rows), BF16), shaped((rows, q_width), F32),
            shaped((rows, k_width), F32), shaped((rows, q_width), BF16),
            shaped((rows, k_width), BF16), shaped((rows, k_width), BF16),
            shaped((k_width, rows), BF16), shaped((k_width, rows), BF16),
        ],
        **params("project", 10_000_000_000),
    )(x, gain, matrix, cos, sin, gain_q, gain_k)


def head_specs(half, q, k):
    rows, n = k.shape[0], q.shape[0] // 2
    return dict(
        q=fixed((n, q.shape[1]), (half, 0)),
        k=fixed(k.shape),
        turned=fixed((k.shape[1], rows)),
        start=fixed((1, n), (0, half)),
        out=fixed((n, q.shape[1])),
        out_turned=fixed((q.shape[1], n)),
        logs=fixed((q.shape[1] // HEAD_SIZE, n)),
        angle=fixed((n, HEAD_SIZE), (half, 0)),
        row=fixed((1, HEAD_SIZE)),
    )


def attend(half, info, q, k, v_turned, start):
    n = q.shape[0] // 2
    s = head_specs(half, q, k)
    return pl.pallas_call(
        lambda *refs: attend_kernel(half * n // BLOCK, *refs),
        grid_spec=pltpu.PrefetchScalarGridSpec(
            num_scalar_prefetch=1,
            grid=(1,),
            in_specs=[s["q"], s["k"], s["turned"], s["start"]],
            out_specs=[s["out"], s["out_turned"], s["logs"]],
        ),
        out_shape=[
            shaped((n, q.shape[1]), BF16), shaped((q.shape[1], n), BF16),
            shaped((q.shape[1] // HEAD_SIZE, n), F32),
        ],
        **params("attend", 18_000_000_000),
    )(info, q, k, v_turned, start)


def attend_back_own(info, q, k, v, k_turned, start, logs, out, grad_out, raw_q, cos, sin, gain_q):
    n = q.shape[0] // 2
    s = head_specs(0, q, k)
    return pl.pallas_call(
        back_own_kernel,
        grid_spec=pltpu.PrefetchScalarGridSpec(
            num_scalar_prefetch=1,
            grid=(1,),
            in_specs=[
                s["q"], s["k"], s["k"], s["turned"], s["start"], s["logs"], s["out"], s["out"],
                s["q"], s["angle"], s["angle"], s["row"],
            ],
            out_specs=[s["out"], s["k"], s["k"], s["row"]],
        ),
        out_shape=[
            shaped((n, q.shape[1]), BF16), shaped(k.shape, F32), shaped(k.shape, F32),
            shaped((1, HEAD_SIZE), F32),
        ],
        **params("attend_back_own", 25_000_000_000),
    )(info, q, k, v, k_turned, start, logs, out, grad_out, raw_q, cos, sin, gain_q)


def attend_back_other(
    info, q, k, v, k_turned, start, logs, out, grad_out, raw_q, cos, sin, gain_q,
    raw_k, gain_k, grad_q, grad_k, grad_v,
):
    rows = k.shape[0]
    width = k.shape[1] * SLOTS
    s = head_specs(1, q, k)
    whole = fixed((rows, HEAD_SIZE))
    return pl.pallas_call(
        back_other_kernel,
        grid_spec=pltpu.PrefetchScalarGridSpec(
            num_scalar_prefetch=1,
            grid=(1,),
            in_specs=[
                s["q"], s["k"], s["k"], s["turned"], s["start"], s["logs"], s["out"], s["out"],
                s["q"], s["angle"], s["angle"], s["row"],
                whole, whole, s["k"], s["row"], s["out"], s["k"], s["k"],
            ],
            out_specs=[fixed((rows, width)), fixed((2, HEAD_SIZE))],
            scratch_shapes=[pltpu.VMEM(k.shape, F32)] * 2,
        ),
        out_shape=[shaped((rows, width), BF16), shaped((2, HEAD_SIZE), F32)],
        **params("attend_back_other", 28_000_000_000),
    )(
        info, q, k, v, k_turned, start, logs, out, grad_out, raw_q, cos, sin, gain_q,
        cos, sin, raw_k, gain_k, grad_q, grad_k, grad_v,
    )


def two_parts(rows, width):
    steps = rows // WIDE_BLOCK // 2
    return (
        [
            pl.BlockSpec((WIDE_BLOCK, width), lambda i: (jnp.minimum(i, steps - 1), 0)),
            pl.BlockSpec((WIDE_BLOCK, width), lambda i: (jnp.maximum(i - steps, 0), 0)),
        ],
        [shaped((rows // 2, width), BF16)] * 2,
    )


def feed(h, grad, weights, hidden_count):
    rows, width = h.shape
    packs = len(weights) == 1
    by_rows = lambda n: pl.BlockSpec((WIDE_BLOCK, n), lambda i: (i, 0))
    by_lanes = lambda n: pl.BlockSpec((n, WIDE_BLOCK), lambda i: (0, i))
    specs, shapes = two_parts(rows, width)
    scratch = [
        pltpu.VMEM((width, 2 * hidden_count), BF16), pltpu.VMEM((hidden_count, width), BF16)
    ]
    return pl.pallas_call(
        lambda *refs: feed_kernel(packs, *refs),
        grid=(rows // WIDE_BLOCK,),
        in_specs=[by_rows(width), by_rows(width), *(fixed(w.shape) for w in weights)],
        out_specs=[
            by_lanes(width), by_lanes(hidden_count), by_rows(2 * hidden_count), *specs, *specs
        ],
        out_shape=[
            shaped((width, rows), BF16), shaped((hidden_count, rows), BF16),
            shaped((rows, 2 * hidden_count), BF16), *shapes, *shapes,
        ],
        scratch_shapes=scratch if packs else [],
        **params("feed", 16_000_000_000),
    )(h, grad, *weights)


def feed_weights(packed_shape, h, grads, hidden, dy):
    width, n = h[0].shape
    half = width // 2
    pieces = grads[0].shape[1] // half
    count = hidden[0].shape[0]
    packs = packed_shape is not None
    gate_block = pl.BlockSpec((n, half), lambda i: (0, jnp.minimum(i, pieces - 1)))
    down_block = pl.BlockSpec((n, half), lambda i: (0, jnp.maximum(i - pieces, 0)))
    shapes = [packed_shape] if packs else [(width, 2 * count), (count, width)]
    return pl.pallas_call(
        lambda *refs: feed_weights_kernel(packs, pieces, *refs),
        grid=(pieces + 2,),
        in_specs=[
            fixed((width, n)), fixed((width, n)), gate_block, gate_block,
            fixed((count, n)), fixed((count, n)), down_block, down_block,
        ],
        out_specs=[fixed(shape) for shape in shapes],
        out_shape=[shaped(shape, BF16) for shape in shapes],
        **params("feed_weights", 16_000_000_000),
    )(*h, *grads, *hidden, *dy)


def unproject(half, grad, matrix):
    rows, width = grad.shape
    n = rows // 2
    steps = n // WIDE_BLOCK
    specs, shapes = two_parts(n, matrix.shape[0])
    return pl.pallas_call(
        unproject_kernel,
        grid=(steps,),
        in_specs=[pl.BlockSpec((WIDE_BLOCK, width), lambda i: (i + half * steps, 0)), fixed(matrix.shape)],
        out_specs=specs,
        out_shape=shapes,
        **params("unproject", 4_000_000_000),
    )(grad, matrix)


def bit_of(p, bit):
    return (p // bit) % 2


def place(p, order):
    return sum(bit_of(p, bit) * 4 // 2**i for i, bit in enumerate(order))


ORDERS = ((2, 1, 4), (1, 2, 4))


def project_weights_kernel(me, h_turned, grad, matrix, keep_a, send_a, keep_b, send_b, gains):
    p = pl.program_id(0)
    value = nn(h_turned[...], grad[...])
    rows, width = value.shape
    lanes = width // 2
    both = value * matrix[...].astype(F32)
    folded = sum(both[:, i : i + 128] for i in range(0, width, 128))
    gains[p, :, :] = jnp.sum(folded.T, axis=0, keepdims=True)
    for order, keep, send, part in (
        (ORDERS[0], keep_a, send_a, value[:, :lanes]), (ORDERS[1], keep_b, send_b, value[:, lanes:])
    ):
        at = place(p, order)

        @pl.when(at < 4)
        def _():
            keep[at, :rows, :] = part.astype(BF16)

        @pl.when(at >= 4)
        def _():
            send[at - 4, :rows, :] = part.astype(BF16)

    @pl.when(p == 0)
    def _():
        zero = jnp.zeros((4, keep_a.shape[1] - rows, lanes), BF16)
        keep_a[:, rows:, :] = zero
        send_a[:, rows:, :] = zero


def project_weights(me, h_turned, grad, matrix, extra):
    width, rows = h_turned.shape
    depth, lanes = width // 8, grad.shape[1] // 2
    part = (4, depth, lanes)
    longer = (4, depth + extra, lanes)
    return pl.pallas_call(
        project_weights_kernel,
        grid_spec=pltpu.PrefetchScalarGridSpec(
            num_scalar_prefetch=1,
            grid=(8,),
            in_specs=[
                pl.BlockSpec((depth, rows), lambda p, me: (p ^ me[0], 0)),
                fixed(grad.shape),
                pl.BlockSpec((depth, grad.shape[1]), lambda p, me: (p ^ me[0], 0)),
            ],
            out_specs=[fixed(longer), fixed(longer), fixed(part), fixed(part), fixed((8, 1, depth))],
        ),
        out_shape=[
            shaped(longer, BF16), shaped(longer, BF16), shaped(part, BF16), shaped(part, BF16),
            shaped((8, 1, depth), F32),
        ],
        **params("project_weights", 8_000_000_000),
    )(me, h_turned, grad, matrix)


def out_weights_kernel(me, h_own, grad_own, h_other, grad_other, keep, send, value):
    value[...] = nn(h_own[...], grad_own[...]) + nn(h_other[...], grad_other[...])
    deep = HEAD_SIZE // 8
    for p in range(8):
        at = place(p, ORDERS[1])
        to = (keep if at < 4 else send).at[at % 4]
        for h in range(value.shape[0] // HEAD_SIZE):
            of = pl.multiple_of(h * HEAD_SIZE + (p ^ me[0]) * deep, deep)
            to[h * deep : (h + 1) * deep, :] = value[pl.ds(of, deep), :].astype(BF16)


def out_weights(me, h_own, grad_own, h_other, grad_other):
    count, rows = h_own.shape
    width = grad_own.shape[1]
    half = width // 2
    columns = pl.BlockSpec((rows, half), lambda i, me: (0, i))
    part = pl.BlockSpec((4, count // 8, half), lambda i, me: (0, 0, i))
    return pl.pallas_call(
        out_weights_kernel,
        grid_spec=pltpu.PrefetchScalarGridSpec(
            num_scalar_prefetch=1,
            grid=(2,),
            in_specs=[fixed((count, rows)), columns, fixed((count, rows)), columns],
            out_specs=[part, part],
            scratch_shapes=[pltpu.VMEM((count, half), F32)],
        ),
        out_shape=[shaped((4, count // 8, width), BF16)] * 2,
        **params("out_weights", 4_000_000_000),
    )(me, h_own, grad_own, h_other, grad_other)


def flipped(value, axis, bit, name="part"):
    with jax.named_scope(name):
        return lax.ppermute(value, axis, [(i, i ^ bit) for i in range(lax.axis_size(axis))])


def together(*values):
    return lax.optimization_barrier(values)


def near_sum(part, beside):
    return part.astype(F32) + flipped(beside, "tensor", 1).astype(F32)


def added(keep, send, bit):
    return keep.astype(F32) + flipped(send.astype(BF16), "dp", bit).astype(F32)


def halved(value, bit):
    half = value.shape[0] // 2
    return added(value[:half], value[half:], bit)


def per_device(
    tokens, cotangent, lengths,
    projection_weight, w_out, w_gate_up, w_down, gains,
    first_moment_projection, first_out, first_gate_up, first_down, first_gains,
    second_moment_projection, second_out, second_gate_up, second_down, second_gains,
):
    shards = lax.axis_size("tensor")
    spread = lax.axis_size("dp")
    me = lax.axis_index("tensor")
    local_rows = tokens.shape[0]
    rows = local_rows * shards
    blocks = rows // BLOCK
    kv_local = projection_weight.shape[1]
    hidden_local = w_gate_up.shape[2]
    out_heads, out_depth = w_out.shape[0], w_out.shape[1]
    down_blocks, down_depth = w_down.shape[0], w_down.shape[1]
    depth = projection_weight.shape[0]
    gain_count = gains.shape[0]

    half = MODEL_WIDTH // 2
    pieces = 2 * hidden_local // half
    gate_rows = pieces * depth
    out_rows = out_heads * out_depth
    cubic = spread == 8

    pack_one = jnp.concatenate(
        [
            projection_weight.astype(BF16).reshape(depth, -1),
            w_out.astype(BF16).reshape(-1, MODEL_WIDTH),
            jnp.pad(gains.astype(BF16)[None, :], ((0, 15), (0, MODEL_WIDTH - gain_count))),
        ],
        axis=0,
    )
    pack_two = jnp.concatenate(
        [
            w_gate_up.astype(BF16).reshape(depth, pieces, half).swapaxes(0, 1).reshape(-1, half),
            w_down.astype(BF16).reshape(-1, 2, half).swapaxes(0, 1).reshape(-1, half),
        ],
        axis=0,
    )

    def split_one(value):
        return (
            value[..., :depth, :],
            value[..., depth : depth + out_rows, :],
            value[..., depth + out_rows, :gain_count],
        )

    full_qkv, full_out, full_gains = split_one(lax.all_gather(pack_one, "dp", axis=0, tiled=False))
    full_out = full_out.reshape(spread, out_heads, out_depth, MODEL_WIDTH).swapaxes(0, 1)
    full_two = lax.all_gather(pack_two, "dp", axis=0, tiled=False)
    qkv_matrix = full_qkv.reshape(MODEL_WIDTH, -1)
    out_matrix = full_out.reshape(-1, MODEL_WIDTH)
    gains_all = full_gains.reshape(-1).astype(F32)
    gain_attn = gains_all[None, :MODEL_WIDTH]
    gain_mlp = gains_all[MODEL_WIDTH : 2 * MODEL_WIDTH]
    gain_query = gains_all[None, 2 * MODEL_WIDTH : 2 * MODEL_WIDTH + HEAD_SIZE]
    gain_key = gains_all[None, 2 * MODEL_WIDTH + HEAD_SIZE :]

    doc_ends = jnp.cumsum(lengths[0])
    doc_starts = doc_ends - lengths[0]

    def start_of(index):
        return jnp.max(
            jnp.where(index[:, None] >= doc_starts[None, :], doc_starts[None, :], 0), axis=1
        )

    order = me ^ jnp.arange(shards, dtype=jnp.int32)
    index_of_row = (
        order[:, None] * local_rows + jnp.arange(local_rows, dtype=jnp.int32)[None, :]
    ).reshape(-1)
    start_of_row = start_of(index_of_row)
    position = index_of_row - start_of_row
    inverse = THETA ** (-2.0 * jnp.arange(HEAD_SIZE // 2, dtype=F32) / HEAD_SIZE)
    turned = position.astype(F32)[:, None] * inverse[None, :]
    cosine, sine = jnp.cos(turned), jnp.sin(turned)
    cos = jnp.concatenate([cosine, cosine], axis=1)
    sin = jnp.concatenate([-sine, sine], axis=1)
    block_starts = start_of(jnp.arange(blocks, dtype=jnp.int32) * BLOCK) // BLOCK
    info = jnp.concatenate([block_starts, (me * (local_rows // BLOCK))[None]]).astype(jnp.int32)
    start = start_of_row[None, :]

    rows_float = tokens.astype(F32)
    tokens_across = flipped(tokens, "tensor", 2, "tokens_across")
    tokens_all = jnp.concatenate(
        [tokens, flipped(tokens, "tensor", 1), tokens_across, flipped(tokens_across, "tensor", 1)],
        axis=0,
    )
    normed_turned, raw_q, raw_k, q, k, v, k_turned, v_turned = project(
        tokens_all, gain_attn, qkv_matrix, cos, sin, gain_query, gain_key
    )
    grad_across = flipped(cotangent, "tensor", 2, "grad_across")
    heads_other, heads_other_turned, logs_other = attend(1, info, q, k, v_turned, start)
    heads_other, grad_across = together(heads_other, grad_across)
    beside = nn(heads_other[local_rows:], out_matrix).astype(BF16)
    near = near_sum(nn(heads_other[:local_rows], out_matrix), beside).astype(BF16)
    near, q_own = together(near, q)
    attn_across = flipped(near, "tensor", 2, "attn_across")
    heads_own, heads_own_turned, logs_own = attend(0, info, q_own, k, v_turned, start)
    heads_own, attn_across, full_two = together(heads_own, attn_across, full_two)
    beside = nn(heads_own[local_rows:], out_matrix).astype(BF16)
    attn_rows = near_sum(nn(heads_own[:local_rows], out_matrix), beside) + attn_across.astype(F32)
    middle = rows_float + attn_rows
    if cubic:
        feed_matrices = (full_two,)
    else:
        feed_matrices = (
            full_two[:, :gate_rows]
            .reshape(spread, pieces, depth, half)
            .swapaxes(1, 2)
            .reshape(MODEL_WIDTH, -1),
            full_two[:, gate_rows:]
            .reshape(spread, 2, down_blocks, down_depth, half)
            .transpose(2, 0, 3, 1, 4)
            .reshape(-1, MODEL_WIDTH),
        )

    grad_own = jnp.concatenate([cotangent, flipped(cotangent, "tensor", 1)], axis=0)
    grad_other = jnp.concatenate([grad_across, flipped(grad_across, "tensor", 1)], axis=0)
    normed_two = norm_rows(middle, gain_mlp).astype(BF16)
    normed_across = flipped(normed_two, "tensor", 2, "normed_across")
    normed_own = jnp.concatenate([normed_two, flipped(normed_two, "tensor", 1)], axis=0)
    h_own, hidden_own, feed_grad_own, back_0, back_1, sum_0, sum_1 = feed(
        normed_own, grad_own, feed_matrices, hidden_local
    )
    normed_across, back_0 = together(normed_across, back_0)
    normed_other = jnp.concatenate([normed_across, flipped(normed_across, "tensor", 1)], axis=0)
    h_other, hidden_other, feed_grad_other, back_2, back_3, sum_2, sum_3 = feed(
        normed_other, grad_other, feed_matrices, hidden_local
    )
    near = near_sum(back_2, back_3).astype(BF16)
    back_near = near_sum(back_0, back_1)
    near, h_own = together(near, h_own)
    back_across = flipped(near, "tensor", 2, "back_across")

    feed_grads = feed_weights(
        full_two.shape if cubic else None, (h_own, h_other), (feed_grad_own, feed_grad_other),
        (hidden_own, hidden_other), (grad_own, grad_other),
    )
    back_across, *feed_grads = together(back_across, *feed_grads)
    if cubic:
        feed_pack = feed_grads[0]
    else:
        feed_pack = jnp.concatenate(
            [
                feed_grads[0].reshape(spread, depth, pieces, half)
                .swapaxes(1, 2)
                .reshape(spread, -1, half),
                feed_grads[1].reshape(down_blocks, spread, down_depth, 2, half)
                .transpose(1, 3, 0, 2, 4)
                .reshape(spread, -1, half),
            ],
            axis=1,
        )
    feed_sum = lax.psum_scatter(feed_pack, "dp", scatter_dimension=0, tiled=True)[0].astype(F32)
    grad_middle_part, grad_gain_mlp = norm_back(
        middle, gain_mlp, back_near + back_across.astype(F32)
    )
    grad_middle = cotangent.astype(F32) + grad_middle_part
    grad_middle_low = grad_middle.astype(BF16)
    grad_middle_across = flipped(grad_middle_low, "tensor", 2, "grad_middle_across")

    grad_middle_own = jnp.concatenate(
        [grad_middle_low, flipped(grad_middle_low, "tensor", 1)], axis=0
    )
    grad_heads_own = nt(grad_middle_own, out_matrix).astype(BF16)
    grad_q, grad_k, grad_v, gain_own = attend_back_own(
        info, q, k, v, k_turned, start, logs_own, heads_own, grad_heads_own, raw_q, cos, sin,
        gain_query,
    )
    grad_middle_across, grad_q, sum_2, sum_3 = together(grad_middle_across, grad_q, sum_2, sum_3)
    near_mlp = near_sum(sum_2, sum_3).astype(BF16)
    grad_middle_other = jnp.concatenate(
        [grad_middle_across, flipped(grad_middle_across, "tensor", 1)], axis=0
    )
    grad_heads_other = nt(grad_middle_other, out_matrix).astype(BF16)
    near_mlp, grad_heads_other = together(near_mlp, grad_heads_other)
    mlp_across = flipped(near_mlp, "tensor", 2, "mlp_across")
    grad_qkv, gain_other = attend_back_other(
        info, q, k, v, k_turned, start, logs_other, heads_other, grad_heads_other,
        raw_q, cos, sin, gain_query, raw_k, gain_key, grad_q, grad_k, grad_v,
    )
    grad_qkv, mlp_across = together(grad_qkv, mlp_across)
    back_2, back_3 = unproject(1, grad_qkv, qkv_matrix)
    back_2, back_3, grad_qkv = together(back_2, back_3, grad_qkv)
    grad_gain_heads = gain_other + jnp.pad(gain_own, ((0, 1), (0, 0)))
    if cubic:
        extra = 16
        me_dp = lax.axis_index("dp")
        relative = jnp.arange(8, dtype=jnp.int32) ^ me_dp
        where = me_dp.astype(jnp.int32)[None]
        keep_a, send_a, keep_b, send_b, gain_blocks = project_weights(
            where, normed_turned, grad_qkv, qkv_matrix, extra
        )
        near = near_sum(back_2, back_3).astype(BF16)
        near, grad_qkv, send_a, send_b, heads_own_turned = together(
            near, grad_qkv, send_a, send_b, heads_own_turned
        )
        back_across = flipped(near, "tensor", 2, "back_across")
        back_0, back_1 = unproject(0, grad_qkv, qkv_matrix)
        sum_two = added(keep_b, send_b, ORDERS[1][0])
        keep_out, send_out = out_weights(
            where, heads_own_turned, grad_middle_own, heads_other_turned, grad_middle_other
        )
        grad_gain_attn = jnp.take(gain_blocks[:, 0], relative, axis=0).reshape(-1) / gain_attn[0]
        gain_sums = jnp.concatenate([grad_gain_attn, grad_gain_mlp, grad_gain_heads.reshape(-1)])
        gain_rows = jnp.take(gain_sums.reshape(8, 1, gain_count), relative, axis=0).astype(BF16)
        slots = sorted(range(8), key=lambda p: place(p, ORDERS[0]))
        gain_rows = jnp.stack([gain_rows[p] for p in slots])
        put = lambda value, rows: lax.dynamic_update_slice(value, rows, (0, depth, 0))
        keep_a, send_a = put(keep_a, gain_rows[:4]), put(send_a, gain_rows[4:])
        sum_one = added(keep_a, send_a, ORDERS[0][0])
        sum_out = added(keep_out, send_out, ORDERS[1][0])
        sum_one, sum_two = halved(sum_one, ORDERS[0][1]), halved(sum_two, ORDERS[1][1])
        sum_out = halved(sum_out, ORDERS[1][1])
        sum_one, sum_two, sum_out, back_across, feed_sum = together(
            sum_one, sum_two, sum_out, back_across, feed_sum
        )
        sum_one, sum_two, sum_out = (halved(value, 4)[0] for value in (sum_one, sum_two, sum_out))
        sum_qkv = jnp.concatenate([sum_one[:depth], sum_two], axis=1)
        sum_qkv = sum_qkv.reshape(projection_weight.shape)
        sum_gains = sum_one[depth, :gain_count]
        sum_out = sum_out.reshape(w_out.shape)
    else:
        grad_qkv_w = nn(normed_turned, grad_qkv)
        near = near_sum(back_2, back_3).astype(BF16)
        back_across = flipped(near, "tensor", 2, "back_across")
        back_0, back_1 = unproject(0, grad_qkv, qkv_matrix)
        sum_qkv = (
            lax.psum_scatter(grad_qkv_w.astype(BF16), "dp", scatter_dimension=0, tiled=True)
            .astype(F32)
            .reshape(projection_weight.shape)
        )
        grad_out_w = nn(heads_own_turned, grad_middle_own) + nn(
            heads_other_turned, grad_middle_other
        )
        sum_out = lax.psum_scatter(
            grad_out_w.astype(BF16).reshape(out_heads, -1, MODEL_WIDTH), "dp",
            scatter_dimension=1, tiled=True,
        ).astype(F32)
        grad_gain_attn = jnp.sum(qkv_matrix.astype(F32) * grad_qkv_w, axis=1) / gain_attn[0]
        gain_sums = jnp.concatenate([grad_gain_attn, grad_gain_mlp, grad_gain_heads.reshape(-1)])
        sum_gains = lax.psum_scatter(gain_sums, "dp", scatter_dimension=0, tiled=True)
    sum_gains = sum_gains + sum(flipped(sum_gains, "tensor", bit) for bit in range(1, shards))

    grad_normed_one = near_sum(back_0, back_1) + back_across.astype(F32)
    grad_rows_part, _ = norm_back(rows_float, gain_attn, grad_normed_one)
    grad_tokens = grad_middle + grad_rows_part
    mlp_rows = near_sum(sum_0, sum_1) + mlp_across.astype(F32)
    block_out = (middle + mlp_rows).astype(BF16)

    sum_gate_up = (
        feed_sum[:gate_rows].reshape(pieces, depth, half).swapaxes(0, 1).reshape(w_gate_up.shape)
    )
    sum_down = feed_sum[gate_rows:].reshape(2, -1, half).swapaxes(0, 1).reshape(w_down.shape)

    upd_qkv = adamw_update(
        projection_weight, first_moment_projection, second_moment_projection,
        row_major(sum_qkv), 2.0 * MODEL_WIDTH ** (-0.5), DECAY,
    )
    upd_out = adamw_update(
        w_out, first_out, second_out, sum_out,
        2.0 * (QUERY_HEADS * HEAD_SIZE // 64) ** (-0.5), DECAY,
    )
    upd_gate_up = adamw_update(
        w_gate_up, first_gate_up, second_gate_up, row_major(sum_gate_up),
        2.0 * MODEL_WIDTH ** (-0.5), DECAY,
    )
    upd_down = adamw_update(w_down, first_down, second_down, sum_down, 2.0 * FF ** (-0.5), DECAY)
    upd_gains = adamw_update(gains, first_gains, second_gains, sum_gains, 0.5, 0.0)
    updates = (upd_qkv, upd_out, upd_gate_up, upd_down, upd_gains)
    return (
        block_out,
        grad_tokens,
        *(update[2] for update in updates),
        *(update[0] for update in updates),
        *(update[1] for update in updates),
    )


def solution(mesh):
    weights = (
        P("dp", "tensor", None),
        P("tensor", "dp", None),
        P("dp", None, "tensor"),
        P("tensor", "dp", None),
        P("dp"),
    )
    batch = P(("dp", "tensor"), None)
    return jax.shard_map(
        per_device,
        mesh=mesh,
        in_specs=(batch, batch, P("dp", None), *weights, *weights, *weights),
        out_specs=(batch, batch, *weights, *weights, *weights),
        check_vma=False,
    )
```

```python
import jax
import jax.numpy as jnp
from jax import lax
from jax.experimental import pallas as pl
from jax.experimental.layout import Layout, with_layout_constraint
from jax.experimental.pallas import tpu as pltpu
from jax.sharding import PartitionSpec as P

MODEL_WIDTH = 1024
QUERY_HEADS = 16
KEY_VALUE_HEADS = 8
HEAD_SIZE = 128
FF = 3072
STEP = 10

EPS = 1e-06
THETA = 1000000.0
BETA_ONE = 0.9
BETA_TWO = 0.95
ADAM_EPS = 1e-08
DECAY = 0.1

GROUP = QUERY_HEADS // KEY_VALUE_HEADS
SLOTS = GROUP + 2
SCALE = HEAD_SIZE ** (-0.5)
LOG2E = 1.4426950408889634
BLOCK = 256
VMEM_LIMIT = 56 * 1024 * 1024
F32 = jnp.float32
BF16 = jnp.bfloat16


def norm_rows(values, scales):
    return values * lax.rsqrt(jnp.mean(values * values, axis=-1, keepdims=True) + EPS) * scales


def norm_back(values, scales, grad):
    r = lax.rsqrt(jnp.mean(values * values, axis=-1, keepdims=True) + EPS)
    u = grad * scales
    back = r * u - values * (r * r * r) * jnp.mean(u * values, axis=-1, keepdims=True)
    return back, jnp.sum(grad * values * r, axis=0)


def row_major(value):
    return with_layout_constraint(value, Layout(major_to_minor=tuple(range(value.ndim))))


def adamw_update(master, moment_one, moment_two, gradient, step_rate, decay_rate):
    next_one = BETA_ONE * moment_one + (1.0 - BETA_ONE) * gradient
    next_two = BETA_TWO * moment_two + (1.0 - BETA_TWO) * gradient * gradient
    one_hat = next_one / (1.0 - BETA_ONE**STEP)
    two_hat = next_two / (1.0 - BETA_TWO**STEP)
    next_master = master - step_rate * (
        one_hat / (jnp.sqrt(two_hat) + ADAM_EPS) + decay_rate * master
    )
    return (next_one, next_two, next_master)


def nt(a, b):
    return lax.dot_general(a, b, (((1,), (1,)), ((), ())), preferred_element_type=F32)


def nn(a, b):
    return jnp.dot(a, b, preferred_element_type=F32)


def head_rotated(x, gain, cos, sin):
    r = lax.rsqrt(jnp.mean(x * x, axis=-1, keepdims=True) + EPS)
    y = x * r * gain
    return y * cos + pltpu.roll(y, HEAD_SIZE // 2, 1) * sin


def head_back(x, gain, cos, sin, grad):
    r = lax.rsqrt(jnp.mean(x * x, axis=-1, keepdims=True) + EPS)
    turned = grad * cos - pltpu.roll(grad, HEAD_SIZE // 2, 1) * sin
    u = turned * gain
    back = r * u - x * (r * r * r) * jnp.mean(u * x, axis=-1, keepdims=True)
    return back, jnp.sum(turned * x * r, axis=0, keepdims=True)


def at_block(index):
    return pl.ds(pl.multiple_of(index * BLOCK, BLOCK), BLOCK)


def allowed_block(key_block, query_block, start):
    keys = key_block * BLOCK + lax.broadcasted_iota(jnp.int32, (BLOCK, BLOCK), 0)
    queries = query_block * BLOCK + lax.broadcasted_iota(jnp.int32, (BLOCK, BLOCK), 1)
    return (keys >= start) & (keys <= queries)


def lanes_of(h):
    return slice(h * HEAD_SIZE, (h + 1) * HEAD_SIZE)


def project_kernel(
    x, gain, matrix, cos, sin, gain_q, gain_k, normed_turned, raw_q, raw_k, q, k, v, k_turned
):
    normed = norm_rows(x[...].astype(F32), gain[...])
    normed_turned[...] = normed.T.astype(BF16)
    h = normed.astype(BF16)
    c, s = cos[...], sin[...]
    for j in range(matrix.shape[1] // (SLOTS * HEAD_SIZE)):
        base = j * SLOTS * HEAD_SIZE
        part = nn(h, matrix[:, base : base + SLOTS * HEAD_SIZE])
        for g in range(GROUP):
            value = part[:, lanes_of(g)]
            raw_q[:, lanes_of(j * GROUP + g)] = value
            q[:, lanes_of(j * GROUP + g)] = head_rotated(value, gain_q[...], c, s).astype(BF16)
        value = part[:, lanes_of(GROUP)]
        raw_k[:, lanes_of(j)] = value
        turned = head_rotated(value, gain_k[...], c, s)
        k[:, lanes_of(j)] = turned.astype(BF16)
        k_turned[lanes_of(j), :] = turned.T.astype(BF16)
        v[:, lanes_of(j)] = part[:, lanes_of(GROUP + 1)].astype(BF16)


def stacked(value):
    return jnp.concatenate([value[:, lanes_of(h)] for h in range(GROUP)], axis=0)


def stacked_turned(value):
    return jnp.concatenate(
        [value[:, lanes_of(h)].astype(F32).T.astype(BF16) for h in range(GROUP)], axis=1
    )


def attend_kernel(offset, info, q, k_turned, v, out, out_turned, logs):
    blocks = v.shape[0] // BLOCK
    flip = info[blocks]
    documents = info.shape[0] - blocks - 1

    def one_block(i, _):
        here = at_block(i)
        b = (i + offset) ^ flip
        index = b * BLOCK + lax.broadcasted_iota(jnp.int32, (BLOCK, 1), 0)
        first = jnp.zeros((BLOCK, 1), jnp.int32)
        for d in range(documents):
            begin = info[blocks + 1 + d]
            first = jnp.maximum(first, jnp.where(index >= begin, begin, 0))
        query = stacked(q[here, :])

        def keys_step(kb, carry):
            total, blend = carry
            there = at_block(kb ^ flip)
            keys = kb * BLOCK + lax.broadcasted_iota(jnp.int32, (BLOCK, BLOCK), 1)
            allowed = (keys >= first) & (keys <= index)
            score = nn(query, k_turned[:, there]).reshape(GROUP, BLOCK, BLOCK)
            p = jnp.where(allowed[None], jnp.exp2(score * (SCALE * LOG2E)), 0.0)
            p = p.reshape(GROUP * BLOCK, BLOCK)
            for lane in range(0, BLOCK, HEAD_SIZE):
                total = total + p[:, lane : lane + HEAD_SIZE]
            return total, blend + nn(p.astype(BF16), v[there, :])

        zero = jnp.zeros((GROUP * BLOCK, HEAD_SIZE), F32)
        total, blend = lax.fori_loop(info[b], b + 1, keys_step, (zero, zero))
        total = jnp.sum(total, axis=1, keepdims=True)
        result = blend / total
        log = jnp.broadcast_to(jnp.log2(total), result.shape)
        for h in range(GROUP):
            rows = slice(h * BLOCK, (h + 1) * BLOCK)
            out[here, lanes_of(h)] = result[rows].astype(BF16)
            out_turned[lanes_of(h), here] = result[rows].T.astype(BF16)
            logs[0, h : h + 1, here] = log[rows].T[0:1, :]
        return 0

    lax.fori_loop(0, q.shape[0] // BLOCK, one_block, 0)


def back_blocks(
    offset, info, q, k, v, k_turned, start, logs, out, grad_out, raw_q, cos, sin, gain_q,
    grad_k, grad_v, store,
):
    flip = info[k.shape[0] // BLOCK]

    def twice(row):
        return jnp.concatenate([row] * GROUP, axis=1)

    def one_block(i, total_gain):
        here = at_block(i)
        b = (i + offset) ^ flip
        first = start[:, here]
        gradients = grad_out[here, :]
        both = gradients.astype(F32) * out[here, :].astype(F32)
        query, gradient = stacked(q[here, :]), stacked(gradients)
        query_turned, gradient_turned = stacked_turned(q[here, :]), stacked_turned(gradients)
        across, log = [], []
        for h in range(GROUP):
            across.append(jnp.sum(both[:, lanes_of(h)].T, axis=0, keepdims=True))
            log.append(logs[0, h : h + 1, here])
        across, log = jnp.concatenate(across, axis=1), jnp.concatenate(log, axis=1)

        def keys_step(kb, grad_query):
            there = at_block(kb ^ flip)
            allowed = twice(allowed_block(kb, b, first).astype(jnp.int32)) > 0
            s = nn(k[there, :], query_turned)
            p = jnp.where(allowed, jnp.exp2(s * (SCALE * LOG2E) - log), 0.0)
            d = (p * (nn(v[there, :], gradient_turned) - across)).astype(BF16)
            grad_v[there, :] += nn(p.astype(BF16), gradient)
            grad_k[there, :] += nn(d, query)
            return grad_query + nn(k_turned[:, there], d)

        done = lax.fori_loop(
            info[b], b + 1, keys_step, jnp.zeros((HEAD_SIZE, GROUP * BLOCK), F32)
        )
        c, s = cos[here, :], sin[here, :]
        for h in range(GROUP):
            grad = done[:, h * BLOCK : (h + 1) * BLOCK].T * SCALE
            back, gain = head_back(raw_q[here, lanes_of(h)], gain_q[...], c, s, grad)
            store(i, h, back.astype(BF16))
            total_gain = total_gain + gain
        return total_gain

    return lax.fori_loop(0, q.shape[0] // BLOCK, one_block, jnp.zeros((1, HEAD_SIZE), F32))


def back_own_kernel(
    info, q, k, v, k_turned, start, logs, out, grad_out, raw_q, cos, sin, gain_q,
    grad_q, grad_k, grad_v, grad_gain,
):
    grad_k[...] = jnp.zeros(grad_k.shape, F32)
    grad_v[...] = jnp.zeros(grad_v.shape, F32)

    def store(i, h, value):
        grad_q[at_block(i), lanes_of(h)] = value

    grad_gain[0, :, :] = back_blocks(
        0, info, q, k, v, k_turned, start, logs, out, grad_out, raw_q, cos, sin, gain_q,
        grad_k, grad_v, store,
    )


def back_other_kernel(
    info, q, k, v, k_turned, start, logs, out, grad_out, raw_q, cos, sin, gain_q,
    cos_all, sin_all, raw_k, gain_k, grad_q_own, grad_k_own, grad_v_own,
    grad_qkv, grad_gains, grad_k, grad_v,
):
    half = q.shape[0] // BLOCK
    blocks = k.shape[0] // BLOCK
    queries = GROUP * HEAD_SIZE
    grad_k[...] = grad_k_own[...]
    grad_v[...] = grad_v_own[...]
    grad_qkv[: half * BLOCK, :queries] = grad_q_own[...]

    def store(i, h, value):
        grad_qkv[at_block(i + half), lanes_of(h)] = value

    grad_gains[0, 0:1, :] = back_blocks(
        half, info, q, k, v, k_turned, start, logs, out, grad_out, raw_q, cos, sin, gain_q,
        grad_k, grad_v, store,
    )

    def finish(i, total_gain):
        rows = at_block(i)
        back, gain = head_back(
            raw_k[rows, :], gain_k[...], cos_all[rows, :], sin_all[rows, :], grad_k[rows, :] * SCALE
        )
        grad_qkv[rows, lanes_of(GROUP)] = back.astype(BF16)
        grad_qkv[rows, lanes_of(GROUP + 1)] = grad_v[rows, :].astype(BF16)
        return total_gain + gain

    grad_gains[0, 1:2, :] = lax.fori_loop(0, blocks, finish, jnp.zeros((1, HEAD_SIZE), F32))


def unpack(packed, gate_up, down):
    n, _, half = packed.shape
    depth = gate_up.shape[0] // n
    pieces = gate_up.shape[1] // half
    blocks = down.shape[0] // HEAD_SIZE
    deep = HEAD_SIZE // n
    for d in range(n):
        for b in range(pieces):
            gate_up[d * depth : (d + 1) * depth, b * half : (b + 1) * half] = packed[
                d, b * depth : (b + 1) * depth, :
            ]
        for c in range(2):
            for i in range(blocks):
                at = pieces * depth + (c * blocks + i) * deep
                to = i * HEAD_SIZE + d * deep
                down[to : to + deep, c * half : (c + 1) * half] = packed[d, at : at + deep, :]


def feed_kernel(packs, h, grad, *refs):
    step = pl.program_id(0)
    if packs:
        packed, *refs = refs
        *refs, gate_up, down = refs

        @pl.when(step == 0)
        def _():
            unpack(packed, gate_up, down)
    else:
        gate_up, down, *refs = refs
    h_turned, hidden_turned, grad_gate_up, back_a, back_b, sum_a, sum_b = refs
    width = down.shape[0]
    rows = h[...]
    both = nn(rows, gate_up[...])
    gate, up = both[:, :width], both[:, width:]
    sig = jax.nn.sigmoid(gate)
    gated = gate * sig
    value = gated * up
    hidden_turned[...] = value.T.astype(BF16)
    h_turned[...] = rows.astype(F32).T.astype(BF16)
    grad_hidden = nt(grad[...], down[...])
    grad_gate_up[:, :width] = (grad_hidden * up * (sig + gated * (1.0 - sig))).astype(BF16)
    grad_gate_up[:, width:] = (grad_hidden * gated).astype(BF16)
    back = nt(grad_gate_up[...], gate_up[...]).astype(BF16)
    total = nn(value.astype(BF16), down[...]).astype(BF16)
    first = step < pl.num_programs(0) // 2

    @pl.when(first)
    def _():
        back_a[...] = back
        sum_a[...] = total

    @pl.when(jnp.logical_not(first))
    def _():
        back_b[...] = back
        sum_b[...] = total


def feed_weights_kernel(
    packs, pieces, h_own, h_other, grad_own, grad_other, hidden_own, hidden_other, dy_own, dy_other,
    *out
):
    step = pl.program_id(0)
    half = dy_own.shape[1]

    for b in range(pieces):
        @pl.when(step == b)
        def _():
            value = nn(h_own[...], grad_own[...]) + nn(h_other[...], grad_other[...])
            value = value.astype(BF16)
            if packs:
                n = out[0].shape[0]
                depth = value.shape[0] // n
                for d in range(n):
                    out[0][d, b * depth : (b + 1) * depth, :] = value[d * depth : (d + 1) * depth]
            else:
                out[0][:, b * half : (b + 1) * half] = value

    for c in range(2):
        @pl.when(step == pieces + c)
        def _():
            value = nn(hidden_own[...], dy_own[...]) + nn(hidden_other[...], dy_other[...])
            value = value.astype(BF16)
            if packs:
                n = out[0].shape[0]
                depth, deep = h_own.shape[0] // n, HEAD_SIZE // n
                blocks = value.shape[0] // HEAD_SIZE
                for d in range(n):
                    for i in range(blocks):
                        at = pieces * depth + (c * blocks + i) * deep
                        of = i * HEAD_SIZE + d * deep
                        out[0][d, at : at + deep, :] = value[of : of + deep]
            else:
                out[1][:, c * half : (c + 1) * half] = value


def unproject_kernel(grad, matrix, out_a, out_b):
    value = nt(grad[...], matrix[...]).astype(BF16)
    first = pl.program_id(0) < pl.num_programs(0) // 2

    @pl.when(first)
    def _():
        out_a[...] = value

    @pl.when(jnp.logical_not(first))
    def _():
        out_b[...] = value


def params(name, flops):
    return dict(
        compiler_params=pltpu.CompilerParams(
            dimension_semantics=("arbitrary",), vmem_limit_bytes=VMEM_LIMIT
        ),
        cost_estimate=pl.CostEstimate(flops=flops // 64, bytes_accessed=1_000, transcendentals=0),
        name=name,
    )


def fixed(shape, index=None):
    index = (0,) * len(shape) if index is None else index
    return pl.BlockSpec(shape, lambda i, *_: index)


def shaped(shape, kind):
    return jax.ShapeDtypeStruct(shape, kind)


def project(x, gain, matrix, cos, sin, gain_q, gain_k):
    rows, width = x.shape
    heads = matrix.shape[1] // (SLOTS * HEAD_SIZE)
    by_rows = lambda n: pl.BlockSpec((BLOCK, n), lambda i: (i, 0))
    by_lanes = lambda n: pl.BlockSpec((n, BLOCK), lambda i: (0, i))
    q_width, k_width = heads * GROUP * HEAD_SIZE, heads * HEAD_SIZE
    return pl.pallas_call(
        project_kernel,
        grid=(rows // BLOCK,),
        in_specs=[
            by_rows(width), fixed((1, width)), fixed(matrix.shape), by_rows(HEAD_SIZE),
            by_rows(HEAD_SIZE), fixed((1, HEAD_SIZE)), fixed((1, HEAD_SIZE)),
        ],
        out_specs=[
            by_lanes(width), by_rows(q_width), by_rows(k_width), by_rows(q_width),
            by_rows(k_width), by_rows(k_width), by_lanes(k_width),
        ],
        out_shape=[
            shaped((width, rows), BF16), shaped((rows, q_width), F32),
            shaped((rows, k_width), F32), shaped((rows, q_width), BF16),
            shaped((rows, k_width), BF16), shaped((rows, k_width), BF16),
            shaped((k_width, rows), BF16),
        ],
        **params("project", 10_000_000_000),
    )(x, gain, matrix, cos, sin, gain_q, gain_k)


def head_specs(half, rows):
    n = rows // 2
    queries = GROUP * HEAD_SIZE
    return dict(
        q=pl.BlockSpec((n, queries), lambda j, info: (half, j)),
        k=pl.BlockSpec((rows, HEAD_SIZE), lambda j, info: (0, j)),
        turned=pl.BlockSpec((HEAD_SIZE, rows), lambda j, info: (j, 0)),
        start=pl.BlockSpec((1, n), lambda j, info: (0, half)),
        out=pl.BlockSpec((n, queries), lambda j, info: (0, j)),
        out_turned=pl.BlockSpec((queries, n), lambda j, info: (j, 0)),
        logs=pl.BlockSpec((1, GROUP, n), lambda j, info: (j, 0, 0)),
        angle=pl.BlockSpec((n, HEAD_SIZE), lambda j, info: (half, 0)),
        row=fixed((1, HEAD_SIZE)),
    )


def attend(half, info, q, k_turned, v):
    rows = v.shape[0]
    n, heads = rows // 2, v.shape[1] // HEAD_SIZE
    s = head_specs(half, rows)
    return pl.pallas_call(
        lambda *refs: attend_kernel(half * n // BLOCK, *refs),
        grid_spec=pltpu.PrefetchScalarGridSpec(
            num_scalar_prefetch=1,
            grid=(heads,),
            in_specs=[s["q"], s["turned"], s["k"]],
            out_specs=[s["out"], s["out_turned"], s["logs"]],
        ),
        out_shape=[
            shaped((n, q.shape[1]), BF16), shaped((q.shape[1], n), BF16),
            shaped((heads, GROUP, n), F32),
        ],
        **params("attend", 18_000_000_000),
    )(info, q, k_turned, v)


def attend_back_own(info, q, k, v, k_turned, start, logs, out, grad_out, raw_q, cos, sin, gain_q):
    rows = k.shape[0]
    n, heads = rows // 2, k.shape[1] // HEAD_SIZE
    s = head_specs(0, rows)
    return pl.pallas_call(
        back_own_kernel,
        grid_spec=pltpu.PrefetchScalarGridSpec(
            num_scalar_prefetch=1,
            grid=(heads,),
            in_specs=[
                s["q"], s["k"], s["k"], s["turned"], s["start"], s["logs"], s["out"], s["out"],
                s["q"], s["angle"], s["angle"], s["row"],
            ],
            out_specs=[
                s["out"], s["k"], s["k"],
                pl.BlockSpec((1, 1, HEAD_SIZE), lambda j, info: (j, 0, 0)),
            ],
        ),
        out_shape=[
            shaped((n, q.shape[1]), BF16), shaped(k.shape, F32), shaped(k.shape, F32),
            shaped((heads, 1, HEAD_SIZE), F32),
        ],
        **params("attend_back_own", 25_000_000_000),
    )(info, q, k, v, k_turned, start, logs, out, grad_out, raw_q, cos, sin, gain_q)


def attend_back_other(
    info, q, k, v, k_turned, start, logs, out, grad_out, raw_q, cos, sin, gain_q,
    raw_k, gain_k, grad_q, grad_k, grad_v,
):
    rows = k.shape[0]
    heads = k.shape[1] // HEAD_SIZE
    width = SLOTS * HEAD_SIZE
    s = head_specs(1, rows)
    whole = fixed((rows, HEAD_SIZE))
    return pl.pallas_call(
        back_other_kernel,
        grid_spec=pltpu.PrefetchScalarGridSpec(
            num_scalar_prefetch=1,
            grid=(heads,),
            in_specs=[
                s["q"], s["k"], s["k"], s["turned"], s["start"], s["logs"], s["out"], s["out"],
                s["q"], s["angle"], s["angle"], s["row"],
                whole, whole, s["k"], s["row"], s["out"], s["k"], s["k"],
            ],
            out_specs=[
                pl.BlockSpec((rows, width), lambda j, info: (0, j)),
                pl.BlockSpec((1, 2, HEAD_SIZE), lambda j, info: (j, 0, 0)),
            ],
            scratch_shapes=[pltpu.VMEM((rows, HEAD_SIZE), F32)] * 2,
        ),
        out_shape=[shaped((rows, heads * width), BF16), shaped((heads, 2, HEAD_SIZE), F32)],
        **params("attend_back_other", 28_000_000_000),
    )(
        info, q, k, v, k_turned, start, logs, out, grad_out, raw_q, cos, sin, gain_q,
        cos, sin, raw_k, gain_k, grad_q, grad_k, grad_v,
    )


def two_parts(rows, width):
    steps = rows // BLOCK // 2
    return (
        [
            pl.BlockSpec((BLOCK, width), lambda i: (jnp.minimum(i, steps - 1), 0)),
            pl.BlockSpec((BLOCK, width), lambda i: (jnp.maximum(i - steps, 0), 0)),
        ],
        [shaped((rows // 2, width), BF16)] * 2,
    )


def feed(h, grad, weights, hidden_count):
    rows, width = h.shape
    packs = len(weights) == 1
    by_rows = lambda n: pl.BlockSpec((BLOCK, n), lambda i: (i, 0))
    by_lanes = lambda n: pl.BlockSpec((n, BLOCK), lambda i: (0, i))
    specs, shapes = two_parts(rows, width)
    scratch = [
        pltpu.VMEM((width, 2 * hidden_count), BF16), pltpu.VMEM((hidden_count, width), BF16)
    ]
    return pl.pallas_call(
        lambda *refs: feed_kernel(packs, *refs),
        grid=(rows // BLOCK,),
        in_specs=[by_rows(width), by_rows(width), *(fixed(w.shape) for w in weights)],
        out_specs=[
            by_lanes(width), by_lanes(hidden_count), by_rows(2 * hidden_count), *specs, *specs
        ],
        out_shape=[
            shaped((width, rows), BF16), shaped((hidden_count, rows), BF16),
            shaped((rows, 2 * hidden_count), BF16), *shapes, *shapes,
        ],
        scratch_shapes=scratch if packs else [],
        **params("feed", 16_000_000_000),
    )(h, grad, *weights)


def feed_weights(packed_shape, h, grads, hidden, dy):
    width, n = h[0].shape
    half = width // 2
    pieces = grads[0].shape[1] // half
    count = hidden[0].shape[0]
    packs = packed_shape is not None
    written = pieces * width // 8 + 2 * count // 8
    gate_block = pl.BlockSpec((n, half), lambda i: (0, jnp.minimum(i, pieces - 1)))
    down_block = pl.BlockSpec((n, half), lambda i: (0, jnp.maximum(i - pieces, 0)))
    shapes = [packed_shape] if packs else [(width, 2 * count), (count, width)]
    return pl.pallas_call(
        lambda *refs: feed_weights_kernel(packs, pieces, *refs),
        grid=(pieces + 2,),
        in_specs=[
            fixed((width, n)), fixed((width, n)), gate_block, gate_block,
            fixed((count, n)), fixed((count, n)), down_block, down_block,
        ],
        out_specs=[fixed((8, written) + shapes[0][2:])] if packs else [fixed(x) for x in shapes],
        out_shape=[shaped(shape, BF16) for shape in shapes],
        **params("feed_weights", 16_000_000_000),
    )(*h, *grads, *hidden, *dy)


def unproject(half, grad, matrix):
    rows, width = grad.shape
    n = rows // 2
    steps = n // BLOCK
    specs, shapes = two_parts(n, matrix.shape[0])
    return pl.pallas_call(
        unproject_kernel,
        grid=(steps,),
        in_specs=[pl.BlockSpec((BLOCK, width), lambda i: (i + half * steps, 0)), fixed(matrix.shape)],
        out_specs=specs,
        out_shape=shapes,
        **params("unproject", 4_000_000_000),
    )(grad, matrix)


def bit_of(p, bit):
    return (p // bit) % 2


def place(p, order):
    return sum(bit_of(p, bit) * 4 // 2**i for i, bit in enumerate(order))


ORDERS = ((2, 1, 4), (1, 2, 4))


def project_weights_kernel(me, h_turned, grad, matrix, keep_a, send_a, keep_b, send_b, gains):
    step = pl.program_id(0)
    value = nn(h_turned[...], grad[...])
    rows = value.shape[0] // 8
    both = value * matrix[...].astype(F32)
    folded = sum(both[:, i : i + 128] for i in range(0, both.shape[1], 128))
    gains[0, :, :] = jnp.sum(folded.T, axis=0, keepdims=True)
    for of, (order, keep, send) in enumerate(
        ((ORDERS[0], keep_a, send_a), (ORDERS[1], keep_b, send_b))
    ):
        for d in range(8):
            at = place(d ^ me[0], order)
            part = value[d * rows : (d + 1) * rows].astype(BF16)

            @pl.when((step == of) & (at < 4))
            def _():
                keep[at, :rows, :] = part

            @pl.when((step == of) & (at >= 4))
            def _():
                send[at - 4, :rows, :] = part

    @pl.when(step == 0)
    def _():
        zero = jnp.zeros((4, keep_a.shape[1] - rows, value.shape[1]), BF16)
        keep_a[:, rows:, :] = zero
        send_a[:, rows:, :] = zero


def project_weights(me, h_turned, grad, matrix, extra):
    width, rows = h_turned.shape
    depth, lanes = width // 8, grad.shape[1] // 2
    part = (4, depth, lanes)
    longer = (4, depth + extra, lanes)
    columns = lambda n: pl.BlockSpec((n, lanes), lambda i, me: (0, i))
    return pl.pallas_call(
        project_weights_kernel,
        grid_spec=pltpu.PrefetchScalarGridSpec(
            num_scalar_prefetch=1,
            grid=(2,),
            in_specs=[fixed((width, rows)), columns(rows), columns(width)],
            out_specs=[
                fixed(longer), fixed(longer), fixed(part), fixed(part),
                pl.BlockSpec((1, 1, width), lambda i, me: (i, 0, 0)),
            ],
        ),
        out_shape=[
            shaped(longer, BF16), shaped(longer, BF16), shaped(part, BF16), shaped(part, BF16),
            shaped((2, 1, width), F32),
        ],
        **params("project_weights", 8_000_000_000),
    )(me, h_turned, grad, matrix)


def out_weights_kernel(h_own, grad_own, h_other, grad_other, packed_in, packed):
    value = (nn(h_own[...], grad_own[...]) + nn(h_other[...], grad_other[...])).astype(BF16)
    n = packed.shape[0]
    deep = HEAD_SIZE // n
    heads = value.shape[0] // HEAD_SIZE
    for d in range(n):
        for h in range(heads):
            of = h * HEAD_SIZE + d * deep
            packed[d, h * deep : (h + 1) * deep, :] = value[of : of + deep]


def out_weights(h_own, grad_own, h_other, grad_other, packed):
    count, rows = h_own.shape
    n, total, half = packed.shape
    steps = grad_own.shape[1] // half
    block = (n, count // n, half)
    last = total // block[1] - steps
    columns = pl.BlockSpec((rows, half), lambda i: (0, i))
    return pl.pallas_call(
        out_weights_kernel,
        grid=(steps,),
        in_specs=[
            fixed((count, rows)), columns, fixed((count, rows)), columns,
            pl.BlockSpec(memory_space=pl.ANY),
        ],
        out_specs=pl.BlockSpec(block, lambda i: (0, last + i, 0)),
        out_shape=shaped(packed.shape, BF16),
        input_output_aliases={4: 0},
        **params("out_weights", 4_000_000_000),
    )(h_own, grad_own, h_other, grad_other, packed)


def flipped(value, axis, bit, name="part"):
    with jax.named_scope(name):
        return lax.ppermute(value, axis, [(i, i ^ bit) for i in range(lax.axis_size(axis))])


def together(*values):
    return lax.optimization_barrier(values)


def near_sum(part, beside):
    return part.astype(F32) + flipped(beside, "tensor", 1).astype(F32)


def added(keep, send, bit):
    return keep.astype(F32) + flipped(send.astype(BF16), "dp", bit).astype(F32)


def halved(value, bit):
    half = value.shape[0] // 2
    return added(value[:half], value[half:], bit)


def per_device(
    tokens, cotangent, lengths,
    projection_weight, w_out, w_gate_up, w_down, gains,
    first_moment_projection, first_out, first_gate_up, first_down, first_gains,
    second_moment_projection, second_out, second_gate_up, second_down, second_gains,
):
    shards = lax.axis_size("tensor")
    spread = lax.axis_size("dp")
    me = lax.axis_index("tensor")
    local_rows = tokens.shape[0]
    rows = local_rows * shards
    blocks = rows // BLOCK
    kv_local = projection_weight.shape[1]
    hidden_local = w_gate_up.shape[2]
    out_heads, out_depth = w_out.shape[0], w_out.shape[1]
    down_blocks, down_depth = w_down.shape[0], w_down.shape[1]
    depth = projection_weight.shape[0]
    gain_count = gains.shape[0]

    half = MODEL_WIDTH // 2
    pieces = 2 * hidden_local // half
    gate_rows = pieces * depth
    out_rows = out_heads * out_depth
    cubic = spread == 8

    pack_one = jnp.concatenate(
        [
            projection_weight.astype(BF16).reshape(depth, -1),
            *([] if cubic else [w_out.astype(BF16).reshape(-1, MODEL_WIDTH)]),
            jnp.pad(gains.astype(BF16)[None, :], ((0, 15), (0, MODEL_WIDTH - gain_count))),
        ],
        axis=0,
    )
    pack_two = jnp.concatenate(
        [
            w_gate_up.astype(BF16).reshape(depth, pieces, half).swapaxes(0, 1).reshape(-1, half),
            w_down.astype(BF16).reshape(-1, 2, half).swapaxes(0, 1).reshape(-1, half),
        ],
        axis=0,
    )

    full_one = lax.all_gather(pack_one, "dp", axis=0, tiled=False)
    full_qkv, full_gains = full_one[:, :depth], full_one[:, -16, :gain_count]
    if cubic:
        me_dp = lax.axis_index("dp")
        own = w_out.astype(BF16)
        full_out = jnp.zeros((out_heads, spread, out_depth, MODEL_WIDTH), BF16)
        for bit in range(spread):
            piece = flipped(own, "dp", bit, "w_out") if bit else own
            full_out = lax.dynamic_update_index_in_dim(full_out, piece, me_dp ^ bit, 1)
    else:
        full_out = full_one[:, depth : depth + out_rows]
        full_out = full_out.reshape(spread, out_heads, out_depth, MODEL_WIDTH).swapaxes(0, 1)
    full_two = lax.all_gather(pack_two, "dp", axis=0, tiled=False)
    qkv_matrix = full_qkv.reshape(MODEL_WIDTH, -1)
    out_matrix = full_out.reshape(-1, MODEL_WIDTH)
    gains_all = full_gains.reshape(-1).astype(F32)
    gain_attn = gains_all[None, :MODEL_WIDTH]
    gain_mlp = gains_all[MODEL_WIDTH : 2 * MODEL_WIDTH]
    gain_query = gains_all[None, 2 * MODEL_WIDTH : 2 * MODEL_WIDTH + HEAD_SIZE]
    gain_key = gains_all[None, 2 * MODEL_WIDTH + HEAD_SIZE :]

    doc_ends = jnp.cumsum(lengths[0])
    doc_starts = doc_ends - lengths[0]

    def start_of(index):
        return jnp.max(
            jnp.where(index[:, None] >= doc_starts[None, :], doc_starts[None, :], 0), axis=1
        )

    order = me ^ jnp.arange(shards, dtype=jnp.int32)
    index_of_row = (
        order[:, None] * local_rows + jnp.arange(local_rows, dtype=jnp.int32)[None, :]
    ).reshape(-1)
    start_of_row = start_of(index_of_row)
    position = index_of_row - start_of_row
    inverse = THETA ** (-2.0 * jnp.arange(HEAD_SIZE // 2, dtype=F32) / HEAD_SIZE)
    turned = position.astype(F32)[:, None] * inverse[None, :]
    cosine, sine = jnp.cos(turned), jnp.sin(turned)
    cos = jnp.concatenate([cosine, cosine], axis=1)
    sin = jnp.concatenate([-sine, sine], axis=1)
    block_starts = start_of(jnp.arange(blocks, dtype=jnp.int32) * BLOCK) // BLOCK
    info = jnp.concatenate(
        [block_starts, (me * (local_rows // BLOCK))[None], doc_starts]
    ).astype(jnp.int32)
    start = start_of_row[None, :]

    rows_float = tokens.astype(F32)
    tokens_across = flipped(tokens, "tensor", 2, "tokens_across")
    tokens_all = jnp.concatenate(
        [tokens, flipped(tokens, "tensor", 1), tokens_across, flipped(tokens_across, "tensor", 1)],
        axis=0,
    )
    normed_turned, raw_q, raw_k, q, k, v, k_turned = project(
        tokens_all, gain_attn, qkv_matrix, cos, sin, gain_query, gain_key
    )
    grad_across = flipped(cotangent, "tensor", 2, "grad_across")
    heads_other, heads_other_turned, logs_other = attend(1, info, q, k_turned, v)
    heads_other, grad_across = together(heads_other, grad_across)
    beside = nn(heads_other[local_rows:], out_matrix).astype(BF16)
    near = near_sum(nn(heads_other[:local_rows], out_matrix), beside).astype(BF16)
    near, q_own = together(near, q)
    attn_across = flipped(near, "tensor", 2, "attn_across")
    heads_own, heads_own_turned, logs_own = attend(0, info, q_own, k_turned, v)
    heads_own, attn_across, full_two = together(heads_own, attn_across, full_two)
    beside = nn(heads_own[local_rows:], out_matrix).astype(BF16)
    attn_rows = near_sum(nn(heads_own[:local_rows], out_matrix), beside) + attn_across.astype(F32)
    middle = rows_float + attn_rows
    if cubic:
        feed_matrices = (full_two,)
    else:
        feed_matrices = (
            full_two[:, :gate_rows]
            .reshape(spread, pieces, depth, half)
            .swapaxes(1, 2)
            .reshape(MODEL_WIDTH, -1),
            full_two[:, gate_rows:]
            .reshape(spread, 2, down_blocks, down_depth, half)
            .transpose(2, 0, 3, 1, 4)
            .reshape(-1, MODEL_WIDTH),
        )

    grad_own = jnp.concatenate([cotangent, flipped(cotangent, "tensor", 1)], axis=0)
    grad_other = jnp.concatenate([grad_across, flipped(grad_across, "tensor", 1)], axis=0)
    normed_two = norm_rows(middle, gain_mlp).astype(BF16)
    normed_across = flipped(normed_two, "tensor", 2, "normed_across")
    normed_own = jnp.concatenate([normed_two, flipped(normed_two, "tensor", 1)], axis=0)
    h_own, hidden_own, feed_grad_own, back_0, back_1, sum_0, sum_1 = feed(
        normed_own, grad_own, feed_matrices, hidden_local
    )
    normed_across, back_0 = together(normed_across, back_0)
    normed_other = jnp.concatenate([normed_across, flipped(normed_across, "tensor", 1)], axis=0)
    h_other, hidden_other, feed_grad_other, back_2, back_3, sum_2, sum_3 = feed(
        normed_other, grad_other, feed_matrices, hidden_local
    )
    near = near_sum(back_2, back_3).astype(BF16)
    back_near = near_sum(back_0, back_1)
    near, h_own = together(near, h_own)
    back_across = flipped(near, "tensor", 2, "back_across")

    feed_grads = feed_weights(
        (spread, full_two.shape[1] + 2 * out_rows, half) if cubic else None, (h_own, h_other), (feed_grad_own, feed_grad_other),
        (hidden_own, hidden_other), (grad_own, grad_other),
    )
    back_across, *feed_grads = together(back_across, *feed_grads)
    grad_middle_part, grad_gain_mlp = norm_back(
        middle, gain_mlp, back_near + back_across.astype(F32)
    )
    grad_middle = cotangent.astype(F32) + grad_middle_part
    grad_middle_low = grad_middle.astype(BF16)
    grad_middle_across = flipped(grad_middle_low, "tensor", 2, "grad_middle_across")

    grad_middle_own = jnp.concatenate(
        [grad_middle_low, flipped(grad_middle_low, "tensor", 1)], axis=0
    )
    grad_heads_own = nt(grad_middle_own, out_matrix).astype(BF16)
    grad_q, grad_k, grad_v, gain_own = attend_back_own(
        info, q, k, v, k_turned, start, logs_own, heads_own, grad_heads_own, raw_q, cos, sin,
        gain_query,
    )
    grad_middle_across, grad_q, sum_2, sum_3 = together(grad_middle_across, grad_q, sum_2, sum_3)
    near_mlp = near_sum(sum_2, sum_3).astype(BF16)
    grad_middle_other = jnp.concatenate(
        [grad_middle_across, flipped(grad_middle_across, "tensor", 1)], axis=0
    )
    grad_heads_other = nt(grad_middle_other, out_matrix).astype(BF16)
    if cubic:
        feed_pack = out_weights(
            heads_own_turned, grad_middle_own, heads_other_turned, grad_middle_other, *feed_grads
        )
        feed_pack, near_mlp, grad_heads_other = together(feed_pack, near_mlp, grad_heads_other)
    else:
        feed_pack = jnp.concatenate(
            [
                feed_grads[0].reshape(spread, depth, pieces, half)
                .swapaxes(1, 2)
                .reshape(spread, -1, half),
                feed_grads[1].reshape(down_blocks, spread, down_depth, 2, half)
                .transpose(1, 3, 0, 2, 4)
                .reshape(spread, -1, half),
            ],
            axis=1,
        )
    feed_sum = lax.psum_scatter(feed_pack, "dp", scatter_dimension=0, tiled=True)[0].astype(F32)
    mlp_across = flipped(near_mlp, "tensor", 2, "mlp_across")
    grad_qkv, gain_other = attend_back_other(
        info, q, k, v, k_turned, start, logs_other, heads_other, grad_heads_other,
        raw_q, cos, sin, gain_query, raw_k, gain_key, grad_q, grad_k, grad_v,
    )
    grad_qkv, mlp_across = together(grad_qkv, mlp_across)
    back_2, back_3 = unproject(1, grad_qkv, qkv_matrix)
    back_2, back_3, grad_qkv = together(back_2, back_3, grad_qkv)
    grad_gain_heads = jnp.sum(gain_other, axis=0) + jnp.pad(
        jnp.sum(gain_own, axis=0), ((0, 1), (0, 0))
    )
    if cubic:
        extra = 16
        relative = jnp.arange(8, dtype=jnp.int32) ^ me_dp
        keep_a, send_a, keep_b, send_b, gain_halves = project_weights(
            me_dp.astype(jnp.int32)[None], normed_turned, grad_qkv, qkv_matrix, extra
        )
        near = near_sum(back_2, back_3).astype(BF16)
        near, grad_qkv, send_a, send_b, sum_0, sum_1 = together(
            near, grad_qkv, send_a, send_b, sum_0, sum_1
        )
        back_across = flipped(near, "tensor", 2, "back_across")
        back_0, back_1 = unproject(0, grad_qkv, qkv_matrix)
        sum_two = added(keep_b, send_b, ORDERS[1][0])
        grad_gain_attn = jnp.sum(gain_halves, axis=(0, 1)) / gain_attn[0]
        gain_sums = jnp.concatenate([grad_gain_attn, grad_gain_mlp, grad_gain_heads.reshape(-1)])
        gain_rows = jnp.take(gain_sums.reshape(8, 1, gain_count), relative, axis=0).astype(BF16)
        slots = sorted(range(8), key=lambda p: place(p, ORDERS[0]))
        gain_rows = jnp.stack([gain_rows[p] for p in slots])
        put = lambda value, rows: lax.dynamic_update_slice(value, rows, (0, depth, 0))
        keep_a, send_a = put(keep_a, gain_rows[:4]), put(send_a, gain_rows[4:])
        sum_one = added(keep_a, send_a, ORDERS[0][0])
        sum_one, sum_two, back_across = together(sum_one, sum_two, back_across)
        sum_one, sum_two = halved(sum_one, ORDERS[0][1]), halved(sum_two, ORDERS[1][1])
        sum_one, sum_two, feed_sum = together(sum_one, sum_two, feed_sum)
        sum_one, sum_two = halved(sum_one, 4)[0], halved(sum_two, 4)[0]
        sum_qkv = jnp.concatenate([sum_one[:depth], sum_two], axis=1)
        sum_qkv = sum_qkv.reshape(projection_weight.shape)
        sum_gains = sum_one[depth, :gain_count]
        sum_out = feed_sum[-2 * out_rows :].reshape(2, out_rows, half).swapaxes(0, 1)
        sum_out = sum_out.reshape(w_out.shape)
    else:
        grad_qkv_w = nn(normed_turned, grad_qkv)
        near = near_sum(back_2, back_3).astype(BF16)
        back_across = flipped(near, "tensor", 2, "back_across")
        back_0, back_1 = unproject(0, grad_qkv, qkv_matrix)
        sum_qkv = (
            lax.psum_scatter(grad_qkv_w.astype(BF16), "dp", scatter_dimension=0, tiled=True)
            .astype(F32)
            .reshape(projection_weight.shape)
        )
        grad_out_w = nn(heads_own_turned, grad_middle_own) + nn(
            heads_other_turned, grad_middle_other
        )
        sum_out = lax.psum_scatter(
            grad_out_w.astype(BF16).reshape(out_heads, -1, MODEL_WIDTH), "dp",
            scatter_dimension=1, tiled=True,
        ).astype(F32)
        grad_gain_attn = jnp.sum(qkv_matrix.astype(F32) * grad_qkv_w, axis=1) / gain_attn[0]
        gain_sums = jnp.concatenate([grad_gain_attn, grad_gain_mlp, grad_gain_heads.reshape(-1)])
        sum_gains = lax.psum_scatter(gain_sums, "dp", scatter_dimension=0, tiled=True)
    sum_gains = sum_gains + sum(flipped(sum_gains, "tensor", bit) for bit in range(1, shards))

    grad_normed_one = near_sum(back_0, back_1) + back_across.astype(F32)
    grad_rows_part, _ = norm_back(rows_float, gain_attn, grad_normed_one)
    grad_tokens = grad_middle + grad_rows_part
    mlp_rows = near_sum(sum_0, sum_1) + mlp_across.astype(F32)
    block_out = (middle + mlp_rows).astype(BF16)

    sum_gate_up = (
        feed_sum[:gate_rows].reshape(pieces, depth, half).swapaxes(0, 1).reshape(w_gate_up.shape)
    )
    sum_down = feed_sum[gate_rows : gate_rows + 2 * down_blocks * down_depth].reshape(2, -1, half).swapaxes(0, 1).reshape(w_down.shape)

    upd_qkv = adamw_update(
        projection_weight, first_moment_projection, second_moment_projection,
        row_major(sum_qkv), 2.0 * MODEL_WIDTH ** (-0.5), DECAY,
    )
    upd_out = adamw_update(
        w_out, first_out, second_out, sum_out,
        2.0 * (QUERY_HEADS * HEAD_SIZE // 64) ** (-0.5), DECAY,
    )
    upd_gate_up = adamw_update(
        w_gate_up, first_gate_up, second_gate_up, row_major(sum_gate_up),
        2.0 * MODEL_WIDTH ** (-0.5), DECAY,
    )
    upd_down = adamw_update(w_down, first_down, second_down, sum_down, 2.0 * FF ** (-0.5), DECAY)
    upd_gains = adamw_update(gains, first_gains, second_gains, sum_gains, 0.5, 0.0)
    updates = (upd_qkv, upd_out, upd_gate_up, upd_down, upd_gains)
    return (
        block_out,
        grad_tokens,
        *(update[2] for update in updates),
        *(update[0] for update in updates),
        *(update[1] for update in updates),
    )


def solution(mesh):
    weights = (
        P("dp", "tensor", None),
        P("tensor", "dp", None),
        P("dp", None, "tensor"),
        P("tensor", "dp", None),
        P("dp"),
    )
    batch = P(("dp", "tensor"), None)
    return jax.shard_map(
        per_device,
        mesh=mesh,
        in_specs=(batch, batch, P("dp", None), *weights, *weights, *weights),
        out_specs=(batch, batch, *weights, *weights, *weights),
        check_vma=False,
    )
```

```python
import jax
import jax.numpy as jnp
from jax import lax
from jax.experimental import pallas as pl
from jax.experimental.layout import Layout, with_layout_constraint
from jax.experimental.pallas import tpu as pltpu
from jax.sharding import PartitionSpec as P

MODEL_WIDTH = 1024
QUERY_HEADS = 16
KEY_VALUE_HEADS = 8
HEAD_SIZE = 128
FF = 3072
STEP = 10

EPS = 1e-06
THETA = 1000000.0
BETA_ONE = 0.9
BETA_TWO = 0.95
ADAM_EPS = 1e-08
DECAY = 0.1

GROUP = QUERY_HEADS // KEY_VALUE_HEADS
SLOTS = GROUP + 2
SCALE = HEAD_SIZE ** (-0.5)
LOG2E = 1.4426950408889634
BLOCK = 256
VMEM_LIMIT = 48 * 1024 * 1024
F32 = jnp.float32
BF16 = jnp.bfloat16


def norm_rows(values, scales):
    return values * lax.rsqrt(jnp.mean(values * values, axis=-1, keepdims=True) + EPS) * scales


def norm_back(values, scales, grad):
    r = lax.rsqrt(jnp.mean(values * values, axis=-1, keepdims=True) + EPS)
    u = grad * scales
    back = r * u - values * (r * r * r) * jnp.mean(u * values, axis=-1, keepdims=True)
    return back, jnp.sum(grad * values * r, axis=0)


def row_major(value):
    return with_layout_constraint(value, Layout(major_to_minor=tuple(range(value.ndim))))


def adamw_update(master, moment_one, moment_two, gradient, step_rate, decay_rate):
    next_one = BETA_ONE * moment_one + (1.0 - BETA_ONE) * gradient
    next_two = BETA_TWO * moment_two + (1.0 - BETA_TWO) * gradient * gradient
    one_hat = next_one / (1.0 - BETA_ONE**STEP)
    two_hat = next_two / (1.0 - BETA_TWO**STEP)
    next_master = master - step_rate * (
        one_hat / (jnp.sqrt(two_hat) + ADAM_EPS) + decay_rate * master
    )
    return (next_one, next_two, next_master)


def nt(a, b):
    return lax.dot_general(a, b, (((1,), (1,)), ((), ())), preferred_element_type=F32)


def nn(a, b):
    return jnp.dot(a, b, preferred_element_type=F32)


def head_rotated(x, gain, cos, sin):
    r = lax.rsqrt(jnp.mean(x * x, axis=-1, keepdims=True) + EPS)
    y = x * r * gain
    return y * cos + pltpu.roll(y, HEAD_SIZE // 2, 1) * sin


def head_back(x, gain, cos, sin, grad):
    r = lax.rsqrt(jnp.mean(x * x, axis=-1, keepdims=True) + EPS)
    turned = grad * cos - pltpu.roll(grad, HEAD_SIZE // 2, 1) * sin
    u = turned * gain
    back = r * u - x * (r * r * r) * jnp.mean(u * x, axis=-1, keepdims=True)
    return back, jnp.sum(turned * x * r, axis=0, keepdims=True)


def at_block(index):
    return pl.ds(pl.multiple_of(index * BLOCK, BLOCK), BLOCK)


def allowed_block(key_block, query_block, start):
    keys = key_block * BLOCK + lax.broadcasted_iota(jnp.int32, (BLOCK, BLOCK), 0)
    queries = query_block * BLOCK + lax.broadcasted_iota(jnp.int32, (BLOCK, BLOCK), 1)
    return (keys >= start) & (keys <= queries)


def lanes_of(h):
    return slice(h * HEAD_SIZE, (h + 1) * HEAD_SIZE)


def project_kernel(
    x, gain, matrix, cos, sin, gain_q, gain_k, normed_turned, raw_q, raw_k, q, k, v, k_turned
):
    normed = norm_rows(x[...].astype(F32), gain[...])
    normed_turned[...] = normed.T.astype(BF16)
    h = normed.astype(BF16)
    c, s = cos[...], sin[...]
    for j in range(matrix.shape[1] // (SLOTS * HEAD_SIZE)):
        base = j * SLOTS * HEAD_SIZE
        part = nn(h, matrix[:, base : base + SLOTS * HEAD_SIZE])
        for g in range(GROUP):
            value = part[:, lanes_of(g)]
            raw_q[:, lanes_of(j * GROUP + g)] = value
            q[:, lanes_of(j * GROUP + g)] = head_rotated(value, gain_q[...], c, s).astype(BF16)
        value = part[:, lanes_of(GROUP)]
        raw_k[:, lanes_of(j)] = value
        turned = head_rotated(value, gain_k[...], c, s)
        k[:, lanes_of(j)] = turned.astype(BF16)
        k_turned[lanes_of(j), :] = turned.T.astype(BF16)
        v[:, lanes_of(j)] = part[:, lanes_of(GROUP + 1)].astype(BF16)


def stacked(value):
    return jnp.concatenate([value[:, lanes_of(h)] for h in range(GROUP)], axis=0)


def stacked_turned(value):
    return jnp.concatenate(
        [value[:, lanes_of(h)].astype(F32).T.astype(BF16) for h in range(GROUP)], axis=1
    )


def attend_kernel(offset, info, q, k_turned, v, out, out_turned, logs):
    blocks = v.shape[0] // BLOCK
    flip = info[blocks]
    documents = info.shape[0] - blocks - 1

    def one_block(i, _):
        here = at_block(i)
        b = (i + offset) ^ flip
        index = b * BLOCK + lax.broadcasted_iota(jnp.int32, (BLOCK, 1), 0)
        first = jnp.zeros((BLOCK, 1), jnp.int32)
        for d in range(documents):
            begin = info[blocks + 1 + d]
            first = jnp.maximum(first, jnp.where(index >= begin, begin, 0))
        query = stacked(q[here, :])

        def keys_step(kb, carry):
            total, blend = carry
            there = at_block(kb ^ flip)
            keys = kb * BLOCK + lax.broadcasted_iota(jnp.int32, (BLOCK, BLOCK), 1)
            allowed = (keys >= first) & (keys <= index)
            score = nn(query, k_turned[:, there]).reshape(GROUP, BLOCK, BLOCK)
            p = jnp.where(allowed[None], jnp.exp2(score * (SCALE * LOG2E)), 0.0)
            p = p.reshape(GROUP * BLOCK, BLOCK)
            for lane in range(0, BLOCK, HEAD_SIZE):
                total = total + p[:, lane : lane + HEAD_SIZE]
            return total, blend + nn(p.astype(BF16), v[there, :])

        zero = jnp.zeros((GROUP * BLOCK, HEAD_SIZE), F32)
        total, blend = lax.fori_loop(info[b], b + 1, keys_step, (zero, zero))
        total = jnp.sum(total, axis=1, keepdims=True)
        result = blend / total
        log = jnp.broadcast_to(jnp.log2(total), result.shape)
        for h in range(GROUP):
            rows = slice(h * BLOCK, (h + 1) * BLOCK)
            out[here, lanes_of(h)] = result[rows].astype(BF16)
            out_turned[lanes_of(h), here] = result[rows].T.astype(BF16)
            logs[0, h : h + 1, here] = log[rows].T[0:1, :]
        return 0

    lax.fori_loop(0, q.shape[0] // BLOCK, one_block, 0)


def back_blocks(
    offset, info, q, k, v, k_turned, start, logs, out, grad_out, raw_q, cos, sin, gain_q,
    grad_k, grad_v, store,
):
    flip = info[k.shape[0] // BLOCK]

    def twice(row):
        return jnp.concatenate([row] * GROUP, axis=1)

    def one_block(i, total_gain):
        here = at_block(i)
        b = (i + offset) ^ flip
        first = start[:, here]
        gradients = grad_out[here, :]
        both = gradients.astype(F32) * out[here, :].astype(F32)
        query, gradient = stacked(q[here, :]), stacked(gradients)
        query_turned, gradient_turned = stacked_turned(q[here, :]), stacked_turned(gradients)
        across, log = [], []
        for h in range(GROUP):
            across.append(jnp.sum(both[:, lanes_of(h)].T, axis=0, keepdims=True))
            log.append(logs[0, h : h + 1, here])
        across, log = jnp.concatenate(across, axis=1), jnp.concatenate(log, axis=1)

        def keys_step(kb, grad_query):
            there = at_block(kb ^ flip)
            allowed = twice(allowed_block(kb, b, first).astype(jnp.int32)) > 0
            s = nn(k[there, :], query_turned)
            p = jnp.where(allowed, jnp.exp2(s * (SCALE * LOG2E) - log), 0.0)
            d = (p * (nn(v[there, :], gradient_turned) - across)).astype(BF16)
            grad_v[there, :] += nn(p.astype(BF16), gradient)
            grad_k[there, :] += nn(d, query)
            return grad_query + nn(k_turned[:, there], d)

        done = lax.fori_loop(
            info[b], b + 1, keys_step, jnp.zeros((HEAD_SIZE, GROUP * BLOCK), F32)
        )
        c, s = cos[here, :], sin[here, :]
        for h in range(GROUP):
            grad = done[:, h * BLOCK : (h + 1) * BLOCK].T * SCALE
            back, gain = head_back(raw_q[here, lanes_of(h)], gain_q[...], c, s, grad)
            store(i, h, back.astype(BF16))
            total_gain = total_gain + gain
        return total_gain

    return lax.fori_loop(0, q.shape[0] // BLOCK, one_block, jnp.zeros((1, HEAD_SIZE), F32))


def back_own_kernel(
    info, q, k, v, k_turned, start, logs, out, grad_out, raw_q, cos, sin, gain_q,
    grad_q, grad_k, grad_v, grad_gain,
):
    grad_k[...] = jnp.zeros(grad_k.shape, F32)
    grad_v[...] = jnp.zeros(grad_v.shape, F32)

    def store(i, h, value):
        grad_q[at_block(i), lanes_of(h)] = value

    grad_gain[0, :, :] = back_blocks(
        0, info, q, k, v, k_turned, start, logs, out, grad_out, raw_q, cos, sin, gain_q,
        grad_k, grad_v, store,
    )


def back_other_kernel(
    info, q, k, v, k_turned, start, logs, out, grad_out, raw_q, cos, sin, gain_q,
    cos_all, sin_all, raw_k, gain_k, grad_q_own, grad_k_own, grad_v_own,
    grad_qkv, grad_gains, grad_k, grad_v,
):
    half = q.shape[0] // BLOCK
    blocks = k.shape[0] // BLOCK
    queries = GROUP * HEAD_SIZE
    grad_k[...] = grad_k_own[...]
    grad_v[...] = grad_v_own[...]
    grad_qkv[: half * BLOCK, :queries] = grad_q_own[...]

    def store(i, h, value):
        grad_qkv[at_block(i + half), lanes_of(h)] = value

    grad_gains[0, 0:1, :] = back_blocks(
        half, info, q, k, v, k_turned, start, logs, out, grad_out, raw_q, cos, sin, gain_q,
        grad_k, grad_v, store,
    )

    def finish(i, total_gain):
        rows = at_block(i)
        back, gain = head_back(
            raw_k[rows, :], gain_k[...], cos_all[rows, :], sin_all[rows, :], grad_k[rows, :] * SCALE
        )
        grad_qkv[rows, lanes_of(GROUP)] = back.astype(BF16)
        grad_qkv[rows, lanes_of(GROUP + 1)] = grad_v[rows, :].astype(BF16)
        return total_gain + gain

    grad_gains[0, 1:2, :] = lax.fori_loop(0, blocks, finish, jnp.zeros((1, HEAD_SIZE), F32))


def unpack(packed, gate_up, down):
    n, _, half = packed.shape
    depth = gate_up.shape[0] // n
    pieces = gate_up.shape[1] // half
    blocks = down.shape[0] // HEAD_SIZE
    deep = HEAD_SIZE // n
    for d in range(n):
        for b in range(pieces):
            gate_up[d * depth : (d + 1) * depth, b * half : (b + 1) * half] = packed[
                d, b * depth : (b + 1) * depth, :
            ]
        for c in range(2):
            for i in range(blocks):
                at = pieces * depth + (c * blocks + i) * deep
                to = i * HEAD_SIZE + d * deep
                down[to : to + deep, c * half : (c + 1) * half] = packed[d, at : at + deep, :]


def feed_kernel(packs, h, grad, *refs):
    step = pl.program_id(0)
    if packs:
        packed, *refs = refs
        *refs, gate_up, down = refs

        @pl.when(step == 0)
        def _():
            unpack(packed, gate_up, down)
    else:
        gate_up, down, *refs = refs
    h_turned, hidden_turned, grad_gate_up, back_a, back_b, sum_a, sum_b = refs
    width = down.shape[0]
    rows = h[...]
    both = nn(rows, gate_up[...])
    gate, up = both[:, :width], both[:, width:]
    sig = jax.nn.sigmoid(gate)
    gated = gate * sig
    value = gated * up
    hidden_turned[...] = value.T.astype(BF16)
    h_turned[...] = rows.astype(F32).T.astype(BF16)
    grad_hidden = nt(grad[...], down[...])
    grad_gate_up[:, :width] = (grad_hidden * up * (sig + gated * (1.0 - sig))).astype(BF16)
    grad_gate_up[:, width:] = (grad_hidden * gated).astype(BF16)
    back = nt(grad_gate_up[...], gate_up[...]).astype(BF16)
    total = nn(value.astype(BF16), down[...]).astype(BF16)
    first = step < pl.num_programs(0) // 2

    @pl.when(first)
    def _():
        back_a[...] = back
        sum_a[...] = total

    @pl.when(jnp.logical_not(first))
    def _():
        back_b[...] = back
        sum_b[...] = total


def feed_weights_kernel(
    packs, pieces, h_own, h_other, grad_own, grad_other, hidden_own, hidden_other, dy_own, dy_other,
    *out
):
    step = pl.program_id(0)
    half = dy_own.shape[1]

    for b in range(pieces):
        @pl.when(step == b)
        def _():
            value = nn(h_own[...], grad_own[...]) + nn(h_other[...], grad_other[...])
            value = value.astype(BF16)
            if packs:
                n = out[0].shape[0]
                depth = value.shape[0] // n
                for d in range(n):
                    out[0][d, b * depth : (b + 1) * depth, :] = value[d * depth : (d + 1) * depth]
            else:
                out[0][:, b * half : (b + 1) * half] = value

    for c in range(2):
        @pl.when(step == pieces + c)
        def _():
            value = nn(hidden_own[...], dy_own[...]) + nn(hidden_other[...], dy_other[...])
            value = value.astype(BF16)
            if packs:
                n = out[0].shape[0]
                depth, deep = h_own.shape[0] // n, HEAD_SIZE // n
                blocks = value.shape[0] // HEAD_SIZE
                for d in range(n):
                    for i in range(blocks):
                        at = pieces * depth + (c * blocks + i) * deep
                        of = i * HEAD_SIZE + d * deep
                        out[0][d, at : at + deep, :] = value[of : of + deep]
            else:
                out[1][:, c * half : (c + 1) * half] = value


def unproject_kernel(grad, matrix, out_a, out_b):
    value = nt(grad[...], matrix[...]).astype(BF16)
    first = pl.program_id(0) < pl.num_programs(0) // 2

    @pl.when(first)
    def _():
        out_a[...] = value

    @pl.when(jnp.logical_not(first))
    def _():
        out_b[...] = value


def params(name, flops):
    return dict(
        compiler_params=pltpu.CompilerParams(
            dimension_semantics=("arbitrary",), vmem_limit_bytes=VMEM_LIMIT
        ),
        cost_estimate=pl.CostEstimate(flops=flops // 64, bytes_accessed=1_000, transcendentals=0),
        name=name,
    )


def fixed(shape, index=None):
    index = (0,) * len(shape) if index is None else index
    return pl.BlockSpec(shape, lambda i, *_: index)


def shaped(shape, kind):
    return jax.ShapeDtypeStruct(shape, kind)


def project(x, gain, matrix, cos, sin, gain_q, gain_k):
    rows, width = x.shape
    heads = matrix.shape[1] // (SLOTS * HEAD_SIZE)
    by_rows = lambda n: pl.BlockSpec((BLOCK, n), lambda i: (i, 0))
    by_lanes = lambda n: pl.BlockSpec((n, BLOCK), lambda i: (0, i))
    q_width, k_width = heads * GROUP * HEAD_SIZE, heads * HEAD_SIZE
    return pl.pallas_call(
        project_kernel,
        grid=(rows // BLOCK,),
        in_specs=[
            by_rows(width), fixed((1, width)), fixed(matrix.shape), by_rows(HEAD_SIZE),
            by_rows(HEAD_SIZE), fixed((1, HEAD_SIZE)), fixed((1, HEAD_SIZE)),
        ],
        out_specs=[
            by_lanes(width), by_rows(q_width), by_rows(k_width), by_rows(q_width),
            by_rows(k_width), by_rows(k_width), by_lanes(k_width),
        ],
        out_shape=[
            shaped((width, rows), BF16), shaped((rows, q_width), F32),
            shaped((rows, k_width), F32), shaped((rows, q_width), BF16),
            shaped((rows, k_width), BF16), shaped((rows, k_width), BF16),
            shaped((k_width, rows), BF16),
        ],
        **params("project", 10_000_000_000),
    )(x, gain, matrix, cos, sin, gain_q, gain_k)


def head_specs(half, rows):
    n = rows // 2
    queries = GROUP * HEAD_SIZE
    return dict(
        q=pl.BlockSpec((n, queries), lambda j, info: (half, j)),
        k=pl.BlockSpec((rows, HEAD_SIZE), lambda j, info: (0, j)),
        turned=pl.BlockSpec((HEAD_SIZE, rows), lambda j, info: (j, 0)),
        start=pl.BlockSpec((1, n), lambda j, info: (0, half)),
        out=pl.BlockSpec((n, queries), lambda j, info: (0, j)),
        out_turned=pl.BlockSpec((queries, n), lambda j, info: (j, 0)),
        logs=pl.BlockSpec((1, GROUP, n), lambda j, info: (j, 0, 0)),
        angle=pl.BlockSpec((n, HEAD_SIZE), lambda j, info: (half, 0)),
        row=fixed((1, HEAD_SIZE)),
    )


def attend(half, info, q, k_turned, v):
    rows = v.shape[0]
    n, heads = rows // 2, v.shape[1] // HEAD_SIZE
    s = head_specs(half, rows)
    return pl.pallas_call(
        lambda *refs: attend_kernel(half * n // BLOCK, *refs),
        grid_spec=pltpu.PrefetchScalarGridSpec(
            num_scalar_prefetch=1,
            grid=(heads,),
            in_specs=[s["q"], s["turned"], s["k"]],
            out_specs=[s["out"], s["out_turned"], s["logs"]],
        ),
        out_shape=[
            shaped((n, q.shape[1]), BF16), shaped((q.shape[1], n), BF16),
            shaped((heads, GROUP, n), F32),
        ],
        **params("attend", 18_000_000_000),
    )(info, q, k_turned, v)


def attend_back_own(info, q, k, v, k_turned, start, logs, out, grad_out, raw_q, cos, sin, gain_q):
    rows = k.shape[0]
    n, heads = rows // 2, k.shape[1] // HEAD_SIZE
    s = head_specs(0, rows)
    return pl.pallas_call(
        back_own_kernel,
        grid_spec=pltpu.PrefetchScalarGridSpec(
            num_scalar_prefetch=1,
            grid=(heads,),
            in_specs=[
                s["q"], s["k"], s["k"], s["turned"], s["start"], s["logs"], s["out"], s["out"],
                s["q"], s["angle"], s["angle"], s["row"],
            ],
            out_specs=[
                s["out"], s["k"], s["k"],
                pl.BlockSpec((1, 1, HEAD_SIZE), lambda j, info: (j, 0, 0)),
            ],
        ),
        out_shape=[
            shaped((n, q.shape[1]), BF16), shaped(k.shape, F32), shaped(k.shape, F32),
            shaped((heads, 1, HEAD_SIZE), F32),
        ],
        **params("attend_back_own", 25_000_000_000),
    )(info, q, k, v, k_turned, start, logs, out, grad_out, raw_q, cos, sin, gain_q)


def attend_back_other(
    info, q, k, v, k_turned, start, logs, out, grad_out, raw_q, cos, sin, gain_q,
    raw_k, gain_k, grad_q, grad_k, grad_v,
):
    rows = k.shape[0]
    heads = k.shape[1] // HEAD_SIZE
    width = SLOTS * HEAD_SIZE
    s = head_specs(1, rows)
    whole = fixed((rows, HEAD_SIZE))
    return pl.pallas_call(
        back_other_kernel,
        grid_spec=pltpu.PrefetchScalarGridSpec(
            num_scalar_prefetch=1,
            grid=(heads,),
            in_specs=[
                s["q"], s["k"], s["k"], s["turned"], s["start"], s["logs"], s["out"], s["out"],
                s["q"], s["angle"], s["angle"], s["row"],
                whole, whole, s["k"], s["row"], s["out"], s["k"], s["k"],
            ],
            out_specs=[
                pl.BlockSpec((rows, width), lambda j, info: (0, j)),
                pl.BlockSpec((1, 2, HEAD_SIZE), lambda j, info: (j, 0, 0)),
            ],
            scratch_shapes=[pltpu.VMEM((rows, HEAD_SIZE), F32)] * 2,
        ),
        out_shape=[shaped((rows, heads * width), BF16), shaped((heads, 2, HEAD_SIZE), F32)],
        **params("attend_back_other", 28_000_000_000),
    )(
        info, q, k, v, k_turned, start, logs, out, grad_out, raw_q, cos, sin, gain_q,
        cos, sin, raw_k, gain_k, grad_q, grad_k, grad_v,
    )


def two_parts(rows, width):
    steps = rows // BLOCK // 2
    return (
        [
            pl.BlockSpec((BLOCK, width), lambda i: (jnp.minimum(i, steps - 1), 0)),
            pl.BlockSpec((BLOCK, width), lambda i: (jnp.maximum(i - steps, 0), 0)),
        ],
        [shaped((rows // 2, width), BF16)] * 2,
    )


def feed(h, grad, weights, hidden_count):
    rows, width = h.shape
    packs = len(weights) == 1
    by_rows = lambda n: pl.BlockSpec((BLOCK, n), lambda i: (i, 0))
    by_lanes = lambda n: pl.BlockSpec((n, BLOCK), lambda i: (0, i))
    specs, shapes = two_parts(rows, width)
    scratch = [
        pltpu.VMEM((width, 2 * hidden_count), BF16), pltpu.VMEM((hidden_count, width), BF16)
    ]
    return pl.pallas_call(
        lambda *refs: feed_kernel(packs, *refs),
        grid=(rows // BLOCK,),
        in_specs=[by_rows(width), by_rows(width), *(fixed(w.shape) for w in weights)],
        out_specs=[
            by_lanes(width), by_lanes(hidden_count), by_rows(2 * hidden_count), *specs, *specs
        ],
        out_shape=[
            shaped((width, rows), BF16), shaped((hidden_count, rows), BF16),
            shaped((rows, 2 * hidden_count), BF16), *shapes, *shapes,
        ],
        scratch_shapes=scratch if packs else [],
        **params("feed", 16_000_000_000),
    )(h, grad, *weights)


def feed_weights(packed_shape, h, grads, hidden, dy):
    width, n = h[0].shape
    half = width // 2
    pieces = grads[0].shape[1] // half
    count = hidden[0].shape[0]
    packs = packed_shape is not None
    gate_block = pl.BlockSpec((n, half), lambda i: (0, jnp.minimum(i, pieces - 1)))
    down_block = pl.BlockSpec((n, half), lambda i: (0, jnp.maximum(i - pieces, 0)))
    shapes = [packed_shape] if packs else [(width, 2 * count), (count, width)]
    return pl.pallas_call(
        lambda *refs: feed_weights_kernel(packs, pieces, *refs),
        grid=(pieces + 2,),
        in_specs=[
            fixed((width, n)), fixed((width, n)), gate_block, gate_block,
            fixed((count, n)), fixed((count, n)), down_block, down_block,
        ],
        out_specs=[fixed(shape) for shape in shapes],
        out_shape=[shaped(shape, BF16) for shape in shapes],
        **params("feed_weights", 16_000_000_000),
    )(*h, *grads, *hidden, *dy)


def unproject(half, grad, matrix):
    rows, width = grad.shape
    n = rows // 2
    steps = n // BLOCK
    specs, shapes = two_parts(n, matrix.shape[0])
    return pl.pallas_call(
        unproject_kernel,
        grid=(steps,),
        in_specs=[pl.BlockSpec((BLOCK, width), lambda i: (i + half * steps, 0)), fixed(matrix.shape)],
        out_specs=specs,
        out_shape=shapes,
        **params("unproject", 4_000_000_000),
    )(grad, matrix)


def flipped(value, axis, bit, name="part"):
    with jax.named_scope(name):
        return lax.ppermute(value, axis, [(i, i ^ bit) for i in range(lax.axis_size(axis))])


def together(*values):
    return lax.optimization_barrier(values)


def near_sum(part, beside):
    return part.astype(F32) + flipped(beside, "tensor", 1).astype(F32)


def halved(parts, axis, bit):
    mine = (lax.axis_index("dp") // bit) % 2
    send = lax.dynamic_index_in_dim(parts, 1 - mine, axis, keepdims=False).astype(BF16)
    keep = lax.dynamic_index_in_dim(parts, mine, axis, keepdims=False)
    return keep + flipped(send, "dp", bit).astype(F32)


def per_device(
    tokens, cotangent, lengths,
    projection_weight, w_out, w_gate_up, w_down, gains,
    first_moment_projection, first_out, first_gate_up, first_down, first_gains,
    second_moment_projection, second_out, second_gate_up, second_down, second_gains,
):
    shards = lax.axis_size("tensor")
    spread = lax.axis_size("dp")
    me = lax.axis_index("tensor")
    local_rows = tokens.shape[0]
    rows = local_rows * shards
    blocks = rows // BLOCK
    kv_local = projection_weight.shape[1]
    hidden_local = w_gate_up.shape[2]
    out_heads, out_depth = w_out.shape[0], w_out.shape[1]
    down_blocks, down_depth = w_down.shape[0], w_down.shape[1]
    depth = projection_weight.shape[0]
    gain_count = gains.shape[0]

    half = MODEL_WIDTH // 2
    pieces = 2 * hidden_local // half
    gate_rows = pieces * depth
    out_rows = out_heads * out_depth
    cubic = spread == 8

    pack_one = jnp.concatenate(
        [
            projection_weight.astype(BF16).reshape(depth, -1),
            w_out.astype(BF16).reshape(-1, MODEL_WIDTH),
            jnp.pad(gains.astype(BF16)[None, :], ((0, 15), (0, MODEL_WIDTH - gain_count))),
        ],
        axis=0,
    )
    pack_two = jnp.concatenate(
        [
            w_gate_up.astype(BF16).reshape(depth, pieces, half).swapaxes(0, 1).reshape(-1, half),
            w_down.astype(BF16).reshape(-1, 2, half).swapaxes(0, 1).reshape(-1, half),
        ],
        axis=0,
    )

    def split_one(value):
        return (
            value[..., :depth, :],
            value[..., depth : depth + out_rows, :],
            value[..., depth + out_rows, :gain_count],
        )

    full_qkv, full_out, full_gains = split_one(lax.all_gather(pack_one, "dp", axis=0, tiled=False))
    full_out = full_out.reshape(spread, out_heads, out_depth, MODEL_WIDTH).swapaxes(0, 1)
    full_two = lax.all_gather(pack_two, "dp", axis=0, tiled=False)
    qkv_matrix = full_qkv.reshape(MODEL_WIDTH, -1)
    out_matrix = full_out.reshape(-1, MODEL_WIDTH)
    gains_all = full_gains.reshape(-1).astype(F32)
    gain_attn = gains_all[None, :MODEL_WIDTH]
    gain_mlp = gains_all[MODEL_WIDTH : 2 * MODEL_WIDTH]
    gain_query = gains_all[None, 2 * MODEL_WIDTH : 2 * MODEL_WIDTH + HEAD_SIZE]
    gain_key = gains_all[None, 2 * MODEL_WIDTH + HEAD_SIZE :]

    doc_ends = jnp.cumsum(lengths[0])
    doc_starts = doc_ends - lengths[0]

    def start_of(index):
        return jnp.max(
            jnp.where(index[:, None] >= doc_starts[None, :], doc_starts[None, :], 0), axis=1
        )

    order = me ^ jnp.arange(shards, dtype=jnp.int32)
    index_of_row = (
        order[:, None] * local_rows + jnp.arange(local_rows, dtype=jnp.int32)[None, :]
    ).reshape(-1)
    start_of_row = start_of(index_of_row)
    position = index_of_row - start_of_row
    inverse = THETA ** (-2.0 * jnp.arange(HEAD_SIZE // 2, dtype=F32) / HEAD_SIZE)
    turned = position.astype(F32)[:, None] * inverse[None, :]
    cosine, sine = jnp.cos(turned), jnp.sin(turned)
    cos = jnp.concatenate([cosine, cosine], axis=1)
    sin = jnp.concatenate([-sine, sine], axis=1)
    block_starts = start_of(jnp.arange(blocks, dtype=jnp.int32) * BLOCK) // BLOCK
    info = jnp.concatenate(
        [block_starts, (me * (local_rows // BLOCK))[None], doc_starts]
    ).astype(jnp.int32)
    start = start_of_row[None, :]

    rows_float = tokens.astype(F32)
    tokens_across = flipped(tokens, "tensor", 2, "tokens_across")
    tokens_all = jnp.concatenate(
        [tokens, flipped(tokens, "tensor", 1), tokens_across, flipped(tokens_across, "tensor", 1)],
        axis=0,
    )
    normed_turned, raw_q, raw_k, q, k, v, k_turned = project(
        tokens_all, gain_attn, qkv_matrix, cos, sin, gain_query, gain_key
    )
    grad_across = flipped(cotangent, "tensor", 2, "grad_across")
    heads_other, heads_other_turned, logs_other = attend(1, info, q, k_turned, v)
    heads_other, grad_across = together(heads_other, grad_across)
    beside = nn(heads_other[local_rows:], out_matrix).astype(BF16)
    near = near_sum(nn(heads_other[:local_rows], out_matrix), beside).astype(BF16)
    near, q_own = together(near, q)
    attn_across = flipped(near, "tensor", 2, "attn_across")
    heads_own, heads_own_turned, logs_own = attend(0, info, q_own, k_turned, v)
    heads_own, attn_across = together(heads_own, attn_across)
    beside = nn(heads_own[local_rows:], out_matrix).astype(BF16)
    own_sum = near_sum(nn(heads_own[:local_rows], out_matrix), beside)
    own_sum, full_two = together(own_sum, full_two)
    middle = rows_float + own_sum + attn_across.astype(F32)
    grad_own = jnp.concatenate([cotangent, flipped(cotangent, "tensor", 1)], axis=0)
    grad_other = jnp.concatenate([grad_across, flipped(grad_across, "tensor", 1)], axis=0)
    normed_two = norm_rows(middle, gain_mlp).astype(BF16)
    normed_across = flipped(normed_two, "tensor", 2, "normed_across")
    normed_own = jnp.concatenate([normed_two, flipped(normed_two, "tensor", 1)], axis=0)
    if cubic:
        feed_matrices = (full_two,)
    else:
        feed_matrices = (
            full_two[:, :gate_rows]
            .reshape(spread, pieces, depth, half)
            .swapaxes(1, 2)
            .reshape(MODEL_WIDTH, -1),
            full_two[:, gate_rows:]
            .reshape(spread, 2, down_blocks, down_depth, half)
            .transpose(2, 0, 3, 1, 4)
            .reshape(-1, MODEL_WIDTH),
        )
    h_own, hidden_own, feed_grad_own, back_0, back_1, sum_0, sum_1 = feed(
        normed_own, grad_own, feed_matrices, hidden_local
    )
    normed_across, back_0 = together(normed_across, back_0)
    normed_other = jnp.concatenate([normed_across, flipped(normed_across, "tensor", 1)], axis=0)
    h_other, hidden_other, feed_grad_other, back_2, back_3, sum_2, sum_3 = feed(
        normed_other, grad_other, feed_matrices, hidden_local
    )
    near = near_sum(back_2, back_3).astype(BF16)
    back_near = near_sum(back_0, back_1)
    near, h_own = together(near, h_own)
    back_across = flipped(near, "tensor", 2, "back_across")

    feed_grads = feed_weights(
        full_two.shape if cubic else None, (h_own, h_other), (feed_grad_own, feed_grad_other),
        (hidden_own, hidden_other), (grad_own, grad_other),
    )
    back_across, *feed_grads = together(back_across, *feed_grads)
    if cubic:
        feed_pack = feed_grads[0]
    else:
        feed_pack = jnp.concatenate(
            [
                feed_grads[0].reshape(spread, depth, pieces, half)
                .swapaxes(1, 2)
                .reshape(spread, -1, half),
                feed_grads[1].reshape(down_blocks, spread, down_depth, 2, half)
                .transpose(1, 3, 0, 2, 4)
                .reshape(spread, -1, half),
            ],
            axis=1,
        )
    feed_sum = lax.psum_scatter(feed_pack, "dp", scatter_dimension=0, tiled=True)[0].astype(F32)
    grad_middle_part, grad_gain_mlp = norm_back(
        middle, gain_mlp, back_near + back_across.astype(F32)
    )
    grad_middle = cotangent.astype(F32) + grad_middle_part
    grad_middle_low = grad_middle.astype(BF16)
    grad_middle_across = flipped(grad_middle_low, "tensor", 2, "grad_middle_across")

    grad_middle_own = jnp.concatenate(
        [grad_middle_low, flipped(grad_middle_low, "tensor", 1)], axis=0
    )
    grad_heads_own = nt(grad_middle_own, out_matrix).astype(BF16)
    grad_q, grad_k, grad_v, gain_own = attend_back_own(
        info, q, k, v, k_turned, start, logs_own, heads_own, grad_heads_own, raw_q, cos, sin,
        gain_query,
    )
    grad_middle_across, grad_q = together(grad_middle_across, grad_q)
    grad_middle_other = jnp.concatenate(
        [grad_middle_across, flipped(grad_middle_across, "tensor", 1)], axis=0
    )
    grad_heads_other = nt(grad_middle_other, out_matrix).astype(BF16)
    grad_out_w = (
        nn(heads_own_turned, grad_middle_own) + nn(heads_other_turned, grad_middle_other)
    ).astype(BF16)
    grad_out_w, grad_heads_other = together(grad_out_w, grad_heads_other)
    grad_qkv, gain_other = attend_back_other(
        info, q, k, v, k_turned, start, logs_other, heads_other, grad_heads_other,
        raw_q, cos, sin, gain_query, raw_k, gain_key, grad_q, grad_k, grad_v,
    )
    back_2, back_3 = unproject(1, grad_qkv, qkv_matrix)
    back_2, back_3, grad_qkv = together(back_2, back_3, grad_qkv)
    grad_qkv_w = nn(normed_turned, grad_qkv)
    near = near_sum(back_2, back_3).astype(BF16)
    near, grad_qkv, grad_qkv_w, grad_out_w, sum_2, sum_3 = together(
        near, grad_qkv, grad_qkv_w, grad_out_w, sum_2, sum_3
    )
    near_mlp = near_sum(sum_2, sum_3).astype(BF16)
    back_across = flipped(near, "tensor", 2, "back_across")
    grad_gain_attn = jnp.sum(qkv_matrix.astype(F32) * grad_qkv_w, axis=1) / gain_attn[0]
    grad_gain_heads = jnp.sum(gain_other, axis=0) + jnp.pad(
        jnp.sum(gain_own, axis=0), ((0, 1), (0, 0))
    )
    gain_sums = jnp.concatenate([grad_gain_attn, grad_gain_mlp, grad_gain_heads.reshape(-1)])
    back_0, back_1 = unproject(0, grad_qkv, qkv_matrix)
    if cubic:
        cube = (2, 2, 2)
        columns = grad_qkv_w.shape[1] // 2
        gain_rows = jnp.pad(
            gain_sums.reshape(cube + (1, gain_count)),
            ((0, 0),) * 3 + ((0, 15), (0, columns - gain_count)),
        )
        sum_one = jnp.concatenate(
            [grad_qkv_w[:, :columns].reshape(cube + (depth, -1)), gain_rows], axis=3
        )
        sum_two = grad_qkv_w[:, columns:].reshape(cube + (depth, -1))
        sum_one, sum_two = halved(sum_one, 1, 2), halved(sum_two, 2, 1)
        sum_out = grad_out_w.reshape((out_heads,) + cube + (out_depth, MODEL_WIDTH))
        sum_out = halved(sum_out, 3, 1)
        sum_one, sum_two, back_across, sum_0, sum_1, near_mlp = together(
            sum_one, sum_two, back_across, sum_0, sum_1, near_mlp
        )
        mlp_across = flipped(near_mlp, "tensor", 2, "mlp_across")
        sum_one, sum_two = halved(sum_one, 1, 1), halved(sum_two, 1, 2)
        sum_out = halved(sum_out, 2, 2)
        sum_one, sum_two, sum_out, feed_sum = together(sum_one, sum_two, sum_out, feed_sum)
        sum_one, sum_two = halved(sum_one, 0, 4), halved(sum_two, 0, 4)
        sum_out = halved(sum_out, 1, 4)
        sum_one, sum_two, sum_out, mlp_across = together(sum_one, sum_two, sum_out, mlp_across)
        sum_qkv = jnp.concatenate([sum_one[:depth], sum_two], axis=1)
        sum_qkv = sum_qkv.reshape(projection_weight.shape)
        sum_gains = sum_one[depth, :gain_count]
    else:
        mlp_across = flipped(near_mlp, "tensor", 2, "mlp_across")
        sum_qkv = (
            lax.psum_scatter(grad_qkv_w.astype(BF16), "dp", scatter_dimension=0, tiled=True)
            .astype(F32)
            .reshape(projection_weight.shape)
        )
        sum_out = lax.psum_scatter(
            grad_out_w.reshape(out_heads, -1, MODEL_WIDTH), "dp", scatter_dimension=1, tiled=True
        ).astype(F32)
        sum_gains = lax.psum_scatter(gain_sums, "dp", scatter_dimension=0, tiled=True)
    sum_gains = sum_gains + sum(flipped(sum_gains, "tensor", bit) for bit in range(1, shards))

    grad_normed_one = near_sum(back_0, back_1) + back_across.astype(F32)
    grad_rows_part, _ = norm_back(rows_float, gain_attn, grad_normed_one)
    grad_tokens = grad_middle + grad_rows_part
    mlp_rows = near_sum(sum_0, sum_1) + mlp_across.astype(F32)
    block_out = (middle + mlp_rows).astype(BF16)

    sum_gate_up = (
        feed_sum[:gate_rows].reshape(pieces, depth, half).swapaxes(0, 1).reshape(w_gate_up.shape)
    )
    sum_down = feed_sum[gate_rows:].reshape(2, -1, half).swapaxes(0, 1).reshape(w_down.shape)

    upd_qkv = adamw_update(
        projection_weight, first_moment_projection, second_moment_projection,
        row_major(sum_qkv), 2.0 * MODEL_WIDTH ** (-0.5), DECAY,
    )
    upd_out = adamw_update(
        w_out, first_out, second_out, sum_out,
        2.0 * (QUERY_HEADS * HEAD_SIZE // 64) ** (-0.5), DECAY,
    )
    upd_gate_up = adamw_update(
        w_gate_up, first_gate_up, second_gate_up, row_major(sum_gate_up),
        2.0 * MODEL_WIDTH ** (-0.5), DECAY,
    )
    upd_down = adamw_update(w_down, first_down, second_down, sum_down, 2.0 * FF ** (-0.5), DECAY)
    upd_gains = adamw_update(gains, first_gains, second_gains, sum_gains, 0.5, 0.0)
    updates = (upd_qkv, upd_out, upd_gate_up, upd_down, upd_gains)
    return (
        block_out,
        grad_tokens,
        *(update[2] for update in updates),
        *(update[0] for update in updates),
        *(update[1] for update in updates),
    )


def solution(mesh):
    weights = (
        P("dp", "tensor", None),
        P("tensor", "dp", None),
        P("dp", None, "tensor"),
        P("tensor", "dp", None),
        P("dp"),
    )
    batch = P(("dp", "tensor"), None)
    return jax.shard_map(
        per_device,
        mesh=mesh,
        in_specs=(batch, batch, P("dp", None), *weights, *weights, *weights),
        out_specs=(batch, batch, *weights, *weights, *weights),
        check_vma=False,
    )
```

```python
import jax
import jax.numpy as jnp
from jax import lax
from jax.experimental import pallas as pl
from jax.experimental.layout import Layout, with_layout_constraint
from jax.experimental.pallas import tpu as pltpu
from jax.sharding import PartitionSpec as P

MODEL_WIDTH = 1024
QUERY_HEADS = 16
KEY_VALUE_HEADS = 8
HEAD_SIZE = 128
FF = 3072
STEP = 10

EPS = 1e-06
THETA = 1000000.0
BETA_ONE = 0.9
BETA_TWO = 0.95
ADAM_EPS = 1e-08
DECAY = 0.1

GROUP = QUERY_HEADS // KEY_VALUE_HEADS
SLOTS = GROUP + 2
SCALE = HEAD_SIZE ** (-0.5)
LOG2E = 1.4426950408889634
BLOCK = 256
VMEM_LIMIT = 48 * 1024 * 1024
F32 = jnp.float32
BF16 = jnp.bfloat16


def norm_rows(values, scales):
    return values * lax.rsqrt(jnp.mean(values * values, axis=-1, keepdims=True) + EPS) * scales


def norm_back(values, scales, grad):
    r = lax.rsqrt(jnp.mean(values * values, axis=-1, keepdims=True) + EPS)
    u = grad * scales
    back = r * u - values * (r * r * r) * jnp.mean(u * values, axis=-1, keepdims=True)
    return back, jnp.sum(grad * values * r, axis=0)


def row_major(value):
    return with_layout_constraint(value, Layout(major_to_minor=tuple(range(value.ndim))))


def adamw_update(master, moment_one, moment_two, gradient, step_rate, decay_rate):
    next_one = BETA_ONE * moment_one + (1.0 - BETA_ONE) * gradient
    next_two = BETA_TWO * moment_two + (1.0 - BETA_TWO) * gradient * gradient
    one_hat = next_one / (1.0 - BETA_ONE**STEP)
    two_hat = next_two / (1.0 - BETA_TWO**STEP)
    next_master = master - step_rate * (
        one_hat / (jnp.sqrt(two_hat) + ADAM_EPS) + decay_rate * master
    )
    return (next_one, next_two, next_master)


def nt(a, b):
    return lax.dot_general(a, b, (((1,), (1,)), ((), ())), preferred_element_type=F32)


def nn(a, b):
    return jnp.dot(a, b, preferred_element_type=F32)


def head_rotated(x, gain, cos, sin):
    r = lax.rsqrt(jnp.mean(x * x, axis=-1, keepdims=True) + EPS)
    y = x * r * gain
    return y * cos + pltpu.roll(y, HEAD_SIZE // 2, 1) * sin


def head_back(x, gain, cos, sin, grad):
    r = lax.rsqrt(jnp.mean(x * x, axis=-1, keepdims=True) + EPS)
    turned = grad * cos - pltpu.roll(grad, HEAD_SIZE // 2, 1) * sin
    u = turned * gain
    back = r * u - x * (r * r * r) * jnp.mean(u * x, axis=-1, keepdims=True)
    return back, jnp.sum(turned * x * r, axis=0, keepdims=True)


def at_block(index):
    return pl.ds(pl.multiple_of(index * BLOCK, BLOCK), BLOCK)


def allowed_block(key_block, query_block, start):
    keys = key_block * BLOCK + lax.broadcasted_iota(jnp.int32, (BLOCK, BLOCK), 0)
    queries = query_block * BLOCK + lax.broadcasted_iota(jnp.int32, (BLOCK, BLOCK), 1)
    return (keys >= start) & (keys <= queries)


def lanes_of(h):
    return slice(h * HEAD_SIZE, (h + 1) * HEAD_SIZE)


def project_kernel(
    x, gain, matrix, cos, sin, gain_q, gain_k, normed_turned, raw_q, raw_k, q, k, v, k_turned
):
    normed = norm_rows(x[...].astype(F32), gain[...])
    normed_turned[...] = normed.T.astype(BF16)
    h = normed.astype(BF16)
    c, s = cos[...], sin[...]
    for j in range(matrix.shape[2] // (SLOTS * HEAD_SIZE)):
        base = j * SLOTS * HEAD_SIZE
        columns = matrix[:, :, base : base + SLOTS * HEAD_SIZE]
        part = nn(h, columns.reshape(-1, SLOTS * HEAD_SIZE))
        for g in range(GROUP):
            value = part[:, lanes_of(g)]
            raw_q[:, lanes_of(j * GROUP + g)] = value
            q[:, lanes_of(j * GROUP + g)] = head_rotated(value, gain_q[...], c, s).astype(BF16)
        value = part[:, lanes_of(GROUP)]
        raw_k[:, lanes_of(j)] = value
        turned = head_rotated(value, gain_k[...], c, s)
        k[:, lanes_of(j)] = turned.astype(BF16)
        k_turned[lanes_of(j), :] = turned.T.astype(BF16)
        v[:, lanes_of(j)] = part[:, lanes_of(GROUP + 1)].astype(BF16)


def stacked(value):
    return jnp.concatenate([value[:, lanes_of(h)] for h in range(GROUP)], axis=0)


def stacked_turned(value):
    return jnp.concatenate(
        [value[:, lanes_of(h)].astype(F32).T.astype(BF16) for h in range(GROUP)], axis=1
    )


def attend_kernel(offset, info, q, k_turned, v, out, out_turned, logs):
    blocks = v.shape[0] // BLOCK
    flip = info[blocks]
    documents = info.shape[0] - blocks - 1

    def one_block(i, _):
        here = at_block(i)
        b = (i + offset) ^ flip
        index = b * BLOCK + lax.broadcasted_iota(jnp.int32, (BLOCK, 1), 0)
        first = jnp.zeros((BLOCK, 1), jnp.int32)
        for d in range(documents):
            begin = info[blocks + 1 + d]
            first = jnp.maximum(first, jnp.where(index >= begin, begin, 0))
        query = stacked(q[here, :])

        def keys_step(kb, carry):
            total, blend = carry
            there = at_block(kb ^ flip)
            keys = kb * BLOCK + lax.broadcasted_iota(jnp.int32, (BLOCK, BLOCK), 1)
            allowed = (keys >= first) & (keys <= index)
            score = nn(query, k_turned[:, there]).reshape(GROUP, BLOCK, BLOCK)
            p = jnp.where(allowed[None], jnp.exp2(score * (SCALE * LOG2E)), 0.0)
            p = p.reshape(GROUP * BLOCK, BLOCK)
            for lane in range(0, BLOCK, HEAD_SIZE):
                total = total + p[:, lane : lane + HEAD_SIZE]
            return total, blend + nn(p.astype(BF16), v[there, :])

        zero = jnp.zeros((GROUP * BLOCK, HEAD_SIZE), F32)
        total, blend = lax.fori_loop(info[b], b + 1, keys_step, (zero, zero))
        total = jnp.sum(total, axis=1, keepdims=True)
        result = blend / total
        log = jnp.broadcast_to(jnp.log2(total), result.shape)
        for h in range(GROUP):
            rows = slice(h * BLOCK, (h + 1) * BLOCK)
            out[here, lanes_of(h)] = result[rows].astype(BF16)
            out_turned[lanes_of(h), here] = result[rows].T.astype(BF16)
            logs[0, h : h + 1, here] = log[rows].T[0:1, :]
        return 0

    lax.fori_loop(0, q.shape[0] // BLOCK, one_block, 0)


def back_blocks(
    offset, info, q, k, v, k_turned, start, logs, out, grad_out, raw_q, cos, sin, gain_q,
    grad_k, grad_v, store,
):
    flip = info[k.shape[0] // BLOCK]

    def twice(row):
        return jnp.concatenate([row] * GROUP, axis=1)

    def one_block(i, total_gain):
        here = at_block(i)
        b = (i + offset) ^ flip
        first = start[:, here]
        gradients = grad_out[here, :]
        both = gradients.astype(F32) * out[here, :].astype(F32)
        query, gradient = stacked(q[here, :]), stacked(gradients)
        query_turned, gradient_turned = stacked_turned(q[here, :]), stacked_turned(gradients)
        across, log = [], []
        for h in range(GROUP):
            across.append(jnp.sum(both[:, lanes_of(h)].T, axis=0, keepdims=True))
            log.append(logs[0, h : h + 1, here])
        across, log = jnp.concatenate(across, axis=1), jnp.concatenate(log, axis=1)

        def keys_step(kb, grad_query):
            there = at_block(kb ^ flip)
            allowed = twice(allowed_block(kb, b, first).astype(jnp.int32)) > 0
            s = nn(k[there, :], query_turned)
            p = jnp.where(allowed, jnp.exp2(s * (SCALE * LOG2E) - log), 0.0)
            d = (p * (nn(v[there, :], gradient_turned) - across)).astype(BF16)
            grad_v[there, :] += nn(p.astype(BF16), gradient)
            grad_k[there, :] += nn(d, query)
            return grad_query + nn(k_turned[:, there], d)

        done = lax.fori_loop(
            info[b], b + 1, keys_step, jnp.zeros((HEAD_SIZE, GROUP * BLOCK), F32)
        )
        c, s = cos[here, :], sin[here, :]
        for h in range(GROUP):
            grad = done[:, h * BLOCK : (h + 1) * BLOCK].T * SCALE
            back, gain = head_back(raw_q[here, lanes_of(h)], gain_q[...], c, s, grad)
            store(i, h, back.astype(BF16))
            total_gain = total_gain + gain
        return total_gain

    return lax.fori_loop(0, q.shape[0] // BLOCK, one_block, jnp.zeros((1, HEAD_SIZE), F32))


def back_own_kernel(
    info, q, k, v, k_turned, start, logs, out, grad_out, raw_q, cos, sin, gain_q,
    grad_q, grad_k, grad_v, grad_gain,
):
    grad_k[...] = jnp.zeros(grad_k.shape, F32)
    grad_v[...] = jnp.zeros(grad_v.shape, F32)

    def store(i, h, value):
        grad_q[at_block(i), lanes_of(h)] = value

    grad_gain[0, :, :] = back_blocks(
        0, info, q, k, v, k_turned, start, logs, out, grad_out, raw_q, cos, sin, gain_q,
        grad_k, grad_v, store,
    )


def back_other_kernel(
    info, q, k, v, k_turned, start, logs, out, grad_out, raw_q, cos, sin, gain_q,
    cos_all, sin_all, raw_k, gain_k, grad_q_own, grad_k_own, grad_v_own,
    grad_qkv, grad_gains, grad_k, grad_v,
):
    half = q.shape[0] // BLOCK
    blocks = k.shape[0] // BLOCK
    queries = GROUP * HEAD_SIZE
    grad_k[...] = grad_k_own[...]
    grad_v[...] = grad_v_own[...]
    grad_qkv[: half * BLOCK, :queries] = grad_q_own[...]

    def store(i, h, value):
        grad_qkv[at_block(i + half), lanes_of(h)] = value

    grad_gains[0, 0:1, :] = back_blocks(
        half, info, q, k, v, k_turned, start, logs, out, grad_out, raw_q, cos, sin, gain_q,
        grad_k, grad_v, store,
    )

    def finish(i, total_gain):
        rows = at_block(i)
        back, gain = head_back(
            raw_k[rows, :], gain_k[...], cos_all[rows, :], sin_all[rows, :], grad_k[rows, :] * SCALE
        )
        grad_qkv[rows, lanes_of(GROUP)] = back.astype(BF16)
        grad_qkv[rows, lanes_of(GROUP + 1)] = grad_v[rows, :].astype(BF16)
        return total_gain + gain

    grad_gains[0, 1:2, :] = lax.fori_loop(0, blocks, finish, jnp.zeros((1, HEAD_SIZE), F32))


def unpack(packed, gate_up, down):
    n, _, half = packed.shape
    depth = gate_up.shape[0] // n
    pieces = gate_up.shape[1] // half
    blocks = down.shape[0] // HEAD_SIZE
    deep = HEAD_SIZE // n
    for d in range(n):
        for b in range(pieces):
            gate_up[d * depth : (d + 1) * depth, b * half : (b + 1) * half] = packed[
                d, b * depth : (b + 1) * depth, :
            ]
        for c in range(2):
            for i in range(blocks):
                at = pieces * depth + (c * blocks + i) * deep
                to = i * HEAD_SIZE + d * deep
                down[to : to + deep, c * half : (c + 1) * half] = packed[d, at : at + deep, :]


def feed_kernel(packs, h, grad, *refs):
    step = pl.program_id(0)
    if packs:
        packed, *refs = refs
        *refs, gate_up, down = refs

        @pl.when(step == 0)
        def _():
            unpack(packed, gate_up, down)
    else:
        gate_up, down, *refs = refs
    h_turned, hidden_turned, grad_gate_up, back_a, back_b, sum_a, sum_b = refs
    width = down.shape[0]
    rows = h[...]
    both = nn(rows, gate_up[...])
    gate, up = both[:, :width], both[:, width:]
    sig = jax.nn.sigmoid(gate)
    gated = gate * sig
    value = gated * up
    hidden_turned[...] = value.T.astype(BF16)
    h_turned[...] = rows.astype(F32).T.astype(BF16)
    grad_hidden = nt(grad[...], down[...])
    grad_gate_up[:, :width] = (grad_hidden * up * (sig + gated * (1.0 - sig))).astype(BF16)
    grad_gate_up[:, width:] = (grad_hidden * gated).astype(BF16)
    back = nt(grad_gate_up[...], gate_up[...]).astype(BF16)
    total = nn(value.astype(BF16), down[...]).astype(BF16)
    first = step < pl.num_programs(0) // 2

    @pl.when(first)
    def _():
        back_a[...] = back
        sum_a[...] = total

    @pl.when(jnp.logical_not(first))
    def _():
        back_b[...] = back
        sum_b[...] = total


def feed_weights_kernel(
    packs, pieces, h_own, h_other, grad_own, grad_other, hidden_own, hidden_other, dy_own, dy_other,
    *out
):
    step = pl.program_id(0)
    half = dy_own.shape[1]

    for b in range(pieces):
        @pl.when(step == b)
        def _():
            value = nn(h_own[...], grad_own[...]) + nn(h_other[...], grad_other[...])
            value = value.astype(BF16)
            if packs:
                n = out[0].shape[0]
                depth = value.shape[0] // n
                for d in range(n):
                    out[0][d, b * depth : (b + 1) * depth, :] = value[d * depth : (d + 1) * depth]
            else:
                out[0][:, b * half : (b + 1) * half] = value

    for c in range(2):
        @pl.when(step == pieces + c)
        def _():
            value = nn(hidden_own[...], dy_own[...]) + nn(hidden_other[...], dy_other[...])
            value = value.astype(BF16)
            if packs:
                n = out[0].shape[0]
                depth, deep = h_own.shape[0] // n, HEAD_SIZE // n
                blocks = value.shape[0] // HEAD_SIZE
                for d in range(n):
                    for i in range(blocks):
                        at = pieces * depth + (c * blocks + i) * deep
                        of = i * HEAD_SIZE + d * deep
                        out[0][d, at : at + deep, :] = value[of : of + deep]
            else:
                out[1][:, c * half : (c + 1) * half] = value


def unproject_kernel(grad, matrix, out_a, out_b):
    value = nt(grad[...], matrix[...]).astype(BF16)
    first = pl.program_id(0) < pl.num_programs(0) // 2

    @pl.when(first)
    def _():
        out_a[...] = value

    @pl.when(jnp.logical_not(first))
    def _():
        out_b[...] = value


def params(name, flops):
    return dict(
        compiler_params=pltpu.CompilerParams(
            dimension_semantics=("arbitrary",), vmem_limit_bytes=VMEM_LIMIT
        ),
        cost_estimate=pl.CostEstimate(flops=flops // 64, bytes_accessed=1_000, transcendentals=0),
        name=name,
    )


def fixed(shape, index=None):
    index = (0,) * len(shape) if index is None else index
    return pl.BlockSpec(shape, lambda i, *_: index)


def shaped(shape, kind):
    return jax.ShapeDtypeStruct(shape, kind)


def project(x, gain, matrix, cos, sin, gain_q, gain_k):
    rows, width = x.shape
    heads = matrix.shape[2] // (SLOTS * HEAD_SIZE)
    by_rows = lambda n: pl.BlockSpec((BLOCK, n), lambda i: (i, 0))
    by_lanes = lambda n: pl.BlockSpec((n, BLOCK), lambda i: (0, i))
    q_width, k_width = heads * GROUP * HEAD_SIZE, heads * HEAD_SIZE
    return pl.pallas_call(
        project_kernel,
        grid=(rows // BLOCK,),
        in_specs=[
            by_rows(width), fixed((1, width)),
            fixed((matrix.shape[0], width // matrix.shape[0], matrix.shape[2])), by_rows(HEAD_SIZE),
            by_rows(HEAD_SIZE), fixed((1, HEAD_SIZE)), fixed((1, HEAD_SIZE)),
        ],
        out_specs=[
            by_lanes(width), by_rows(q_width), by_rows(k_width), by_rows(q_width),
            by_rows(k_width), by_rows(k_width), by_lanes(k_width),
        ],
        out_shape=[
            shaped((width, rows), BF16), shaped((rows, q_width), F32),
            shaped((rows, k_width), F32), shaped((rows, q_width), BF16),
            shaped((rows, k_width), BF16), shaped((rows, k_width), BF16),
            shaped((k_width, rows), BF16),
        ],
        **params("project", 10_000_000_000),
    )(x, gain, matrix, cos, sin, gain_q, gain_k)


def head_specs(half, rows):
    n = rows // 2
    queries = GROUP * HEAD_SIZE
    return dict(
        q=pl.BlockSpec((n, queries), lambda j, info: (half, j)),
        k=pl.BlockSpec((rows, HEAD_SIZE), lambda j, info: (0, j)),
        turned=pl.BlockSpec((HEAD_SIZE, rows), lambda j, info: (j, 0)),
        start=pl.BlockSpec((1, n), lambda j, info: (0, half)),
        out=pl.BlockSpec((n, queries), lambda j, info: (0, j)),
        out_turned=pl.BlockSpec((queries, n), lambda j, info: (j, 0)),
        logs=pl.BlockSpec((1, GROUP, n), lambda j, info: (j, 0, 0)),
        angle=pl.BlockSpec((n, HEAD_SIZE), lambda j, info: (half, 0)),
        row=fixed((1, HEAD_SIZE)),
    )


def attend(half, info, q, k_turned, v):
    rows = v.shape[0]
    n, heads = rows // 2, v.shape[1] // HEAD_SIZE
    s = head_specs(half, rows)
    return pl.pallas_call(
        lambda *refs: attend_kernel(half * n // BLOCK, *refs),
        grid_spec=pltpu.PrefetchScalarGridSpec(
            num_scalar_prefetch=1,
            grid=(heads,),
            in_specs=[s["q"], s["turned"], s["k"]],
            out_specs=[s["out"], s["out_turned"], s["logs"]],
        ),
        out_shape=[
            shaped((n, q.shape[1]), BF16), shaped((q.shape[1], n), BF16),
            shaped((heads, GROUP, n), F32),
        ],
        **params("attend", 18_000_000_000),
    )(info, q, k_turned, v)


def attend_back_own(info, q, k, v, k_turned, start, logs, out, grad_out, raw_q, cos, sin, gain_q):
    rows = k.shape[0]
    n, heads = rows // 2, k.shape[1] // HEAD_SIZE
    s = head_specs(0, rows)
    return pl.pallas_call(
        back_own_kernel,
        grid_spec=pltpu.PrefetchScalarGridSpec(
            num_scalar_prefetch=1,
            grid=(heads,),
            in_specs=[
                s["q"], s["k"], s["k"], s["turned"], s["start"], s["logs"], s["out"], s["out"],
                s["q"], s["angle"], s["angle"], s["row"],
            ],
            out_specs=[
                s["out"], s["k"], s["k"],
                pl.BlockSpec((1, 1, HEAD_SIZE), lambda j, info: (j, 0, 0)),
            ],
        ),
        out_shape=[
            shaped((n, q.shape[1]), BF16), shaped(k.shape, F32), shaped(k.shape, F32),
            shaped((heads, 1, HEAD_SIZE), F32),
        ],
        **params("attend_back_own", 25_000_000_000),
    )(info, q, k, v, k_turned, start, logs, out, grad_out, raw_q, cos, sin, gain_q)


def attend_back_other(
    info, q, k, v, k_turned, start, logs, out, grad_out, raw_q, cos, sin, gain_q,
    raw_k, gain_k, grad_q, grad_k, grad_v,
):
    rows = k.shape[0]
    heads = k.shape[1] // HEAD_SIZE
    width = SLOTS * HEAD_SIZE
    s = head_specs(1, rows)
    whole = fixed((rows, HEAD_SIZE))
    return pl.pallas_call(
        back_other_kernel,
        grid_spec=pltpu.PrefetchScalarGridSpec(
            num_scalar_prefetch=1,
            grid=(heads,),
            in_specs=[
                s["q"], s["k"], s["k"], s["turned"], s["start"], s["logs"], s["out"], s["out"],
                s["q"], s["angle"], s["angle"], s["row"],
                whole, whole, s["k"], s["row"], s["out"], s["k"], s["k"],
            ],
            out_specs=[
                pl.BlockSpec((rows, width), lambda j, info: (0, j)),
                pl.BlockSpec((1, 2, HEAD_SIZE), lambda j, info: (j, 0, 0)),
            ],
            scratch_shapes=[pltpu.VMEM((rows, HEAD_SIZE), F32)] * 2,
        ),
        out_shape=[shaped((rows, heads * width), BF16), shaped((heads, 2, HEAD_SIZE), F32)],
        **params("attend_back_other", 28_000_000_000),
    )(
        info, q, k, v, k_turned, start, logs, out, grad_out, raw_q, cos, sin, gain_q,
        cos, sin, raw_k, gain_k, grad_q, grad_k, grad_v,
    )


def two_parts(rows, width):
    steps = rows // BLOCK // 2
    return (
        [
            pl.BlockSpec((BLOCK, width), lambda i: (jnp.minimum(i, steps - 1), 0)),
            pl.BlockSpec((BLOCK, width), lambda i: (jnp.maximum(i - steps, 0), 0)),
        ],
        [shaped((rows // 2, width), BF16)] * 2,
    )


def feed(h, grad, weights, hidden_count):
    rows, width = h.shape
    packs = len(weights) == 1
    by_rows = lambda n: pl.BlockSpec((BLOCK, n), lambda i: (i, 0))
    by_lanes = lambda n: pl.BlockSpec((n, BLOCK), lambda i: (0, i))
    specs, shapes = two_parts(rows, width)
    scratch = [
        pltpu.VMEM((width, 2 * hidden_count), BF16), pltpu.VMEM((hidden_count, width), BF16)
    ]
    return pl.pallas_call(
        lambda *refs: feed_kernel(packs, *refs),
        grid=(rows // BLOCK,),
        in_specs=[by_rows(width), by_rows(width), *(fixed(w.shape) for w in weights)],
        out_specs=[
            by_lanes(width), by_lanes(hidden_count), by_rows(2 * hidden_count), *specs, *specs
        ],
        out_shape=[
            shaped((width, rows), BF16), shaped((hidden_count, rows), BF16),
            shaped((rows, 2 * hidden_count), BF16), *shapes, *shapes,
        ],
        scratch_shapes=scratch if packs else [],
        **params("feed", 16_000_000_000),
    )(h, grad, *weights)


def feed_weights(packed_shape, h, grads, hidden, dy):
    width, n = h[0].shape
    half = width // 2
    pieces = grads[0].shape[1] // half
    count = hidden[0].shape[0]
    packs = packed_shape is not None
    gate_block = pl.BlockSpec((n, half), lambda i: (0, jnp.minimum(i, pieces - 1)))
    down_block = pl.BlockSpec((n, half), lambda i: (0, jnp.maximum(i - pieces, 0)))
    shapes = [packed_shape] if packs else [(width, 2 * count), (count, width)]
    return pl.pallas_call(
        lambda *refs: feed_weights_kernel(packs, pieces, *refs),
        grid=(pieces + 2,),
        in_specs=[
            fixed((width, n)), fixed((width, n)), gate_block, gate_block,
            fixed((count, n)), fixed((count, n)), down_block, down_block,
        ],
        out_specs=[fixed(shape) for shape in shapes],
        out_shape=[shaped(shape, BF16) for shape in shapes],
        **params("feed_weights", 16_000_000_000),
    )(*h, *grads, *hidden, *dy)


def unproject(half, grad, matrix):
    rows, width = grad.shape
    n = rows // 2
    steps = n // BLOCK
    specs, shapes = two_parts(n, matrix.shape[0])
    return pl.pallas_call(
        unproject_kernel,
        grid=(steps,),
        in_specs=[pl.BlockSpec((BLOCK, width), lambda i: (i + half * steps, 0)), fixed(matrix.shape)],
        out_specs=specs,
        out_shape=shapes,
        **params("unproject", 4_000_000_000),
    )(grad, matrix)


def middle_back_kernel(own, beside, across, value, grad, gain, out, out_low, grad_gain):
    total = own[...].astype(F32) + beside[...].astype(F32) + across[...].astype(F32)
    x = value[...]
    r = lax.rsqrt(jnp.mean(x * x, axis=-1, keepdims=True) + EPS)
    u = total * gain[...]
    back = r * u - x * (r * r * r) * jnp.mean(u * x, axis=-1, keepdims=True)
    result = grad[...].astype(F32) + back
    out[...] = result
    out_low[...] = result.astype(BF16)
    part = jnp.sum(total * x * r, axis=0, keepdims=True)

    @pl.when(pl.program_id(0) == 0)
    def _():
        grad_gain[...] = part

    @pl.when(pl.program_id(0) > 0)
    def _():
        grad_gain[...] += part


def middle_back(own, beside, across, value, grad, gain):
    rows, width = value.shape
    block = pl.BlockSpec((BLOCK // 2, width), lambda i: (i, 0))
    row = fixed((1, width))
    return pl.pallas_call(
        middle_back_kernel,
        grid=(rows // (BLOCK // 2),),
        in_specs=[block] * 5 + [row],
        out_specs=[block, block, row],
        out_shape=[shaped((rows, width), F32), shaped((rows, width), BF16), shaped((1, width), F32)],
        **params("middle_back", 2_000_000_000),
    )(own, beside, across, value, grad, gain)


def flipped(value, axis, bit, name="part"):
    with jax.named_scope(name):
        return lax.ppermute(value, axis, [(i, i ^ bit) for i in range(lax.axis_size(axis))])


def together(*values):
    return lax.optimization_barrier(values)


def near_sum(part, beside):
    return part.astype(F32) + flipped(beside, "tensor", 1).astype(F32)


def halved(parts, axis, bit):
    mine = (lax.axis_index("dp") // bit) % 2
    send = lax.dynamic_index_in_dim(parts, 1 - mine, axis, keepdims=False).astype(BF16)
    keep = lax.dynamic_index_in_dim(parts, mine, axis, keepdims=False)
    return keep + flipped(send, "dp", bit).astype(F32)


def per_device(
    tokens, cotangent, lengths,
    projection_weight, w_out, w_gate_up, w_down, gains,
    first_moment_projection, first_out, first_gate_up, first_down, first_gains,
    second_moment_projection, second_out, second_gate_up, second_down, second_gains,
):
    shards = lax.axis_size("tensor")
    spread = lax.axis_size("dp")
    me = lax.axis_index("tensor")
    local_rows = tokens.shape[0]
    rows = local_rows * shards
    blocks = rows // BLOCK
    kv_local = projection_weight.shape[1]
    hidden_local = w_gate_up.shape[2]
    out_heads, out_depth = w_out.shape[0], w_out.shape[1]
    down_blocks, down_depth = w_down.shape[0], w_down.shape[1]
    depth = projection_weight.shape[0]
    gain_count = gains.shape[0]

    half = MODEL_WIDTH // 2
    pieces = 2 * hidden_local // half
    gate_rows = pieces * depth
    out_rows = out_heads * out_depth
    cubic = spread == 8

    pack_one = jnp.concatenate(
        [
            projection_weight.astype(BF16).reshape(depth, -1),
            w_out.astype(BF16).reshape(-1, MODEL_WIDTH),
            jnp.pad(gains.astype(BF16)[None, :], ((0, 15), (0, MODEL_WIDTH - gain_count))),
        ],
        axis=0,
    )
    pack_two = jnp.concatenate(
        [
            w_gate_up.astype(BF16).reshape(depth, pieces, half).swapaxes(0, 1).reshape(-1, half),
            w_down.astype(BF16).reshape(-1, 2, half).swapaxes(0, 1).reshape(-1, half),
        ],
        axis=0,
    )

    def split_one(value):
        return (
            value[..., :depth, :],
            value[..., depth : depth + out_rows, :],
            value[..., depth + out_rows, :gain_count],
        )

    full_one = lax.all_gather(pack_one, "dp", axis=0, tiled=False)
    full_qkv, full_out, full_gains = split_one(full_one)
    full_out = full_out.reshape(spread, out_heads, out_depth, MODEL_WIDTH).swapaxes(0, 1)
    full_two = lax.all_gather(pack_two, "dp", axis=0, tiled=False)
    qkv_matrix = full_qkv.reshape(MODEL_WIDTH, -1)
    out_matrix = full_out.reshape(-1, MODEL_WIDTH)
    gains_all = full_gains.reshape(-1).astype(F32)
    gain_attn = gains_all[None, :MODEL_WIDTH]
    gain_mlp = gains_all[MODEL_WIDTH : 2 * MODEL_WIDTH]
    gain_query = gains_all[None, 2 * MODEL_WIDTH : 2 * MODEL_WIDTH + HEAD_SIZE]
    gain_key = gains_all[None, 2 * MODEL_WIDTH + HEAD_SIZE :]

    doc_ends = jnp.cumsum(lengths[0])
    doc_starts = doc_ends - lengths[0]

    def start_of(index):
        return jnp.max(
            jnp.where(index[:, None] >= doc_starts[None, :], doc_starts[None, :], 0), axis=1
        )

    order = me ^ jnp.arange(shards, dtype=jnp.int32)
    index_of_row = (
        order[:, None] * local_rows + jnp.arange(local_rows, dtype=jnp.int32)[None, :]
    ).reshape(-1)
    start_of_row = start_of(index_of_row)
    position = index_of_row - start_of_row
    inverse = THETA ** (-2.0 * jnp.arange(HEAD_SIZE // 2, dtype=F32) / HEAD_SIZE)
    turned = position.astype(F32)[:, None] * inverse[None, :]
    cosine, sine = jnp.cos(turned), jnp.sin(turned)
    cos = jnp.concatenate([cosine, cosine], axis=1)
    sin = jnp.concatenate([-sine, sine], axis=1)
    block_starts = start_of(jnp.arange(blocks, dtype=jnp.int32) * BLOCK) // BLOCK
    info = jnp.concatenate(
        [block_starts, (me * (local_rows // BLOCK))[None], doc_starts]
    ).astype(jnp.int32)
    start = start_of_row[None, :]

    rows_float = tokens.astype(F32)
    tokens_across = flipped(tokens, "tensor", 2, "tokens_across")
    tokens_all = jnp.concatenate(
        [tokens, flipped(tokens, "tensor", 1), tokens_across, flipped(tokens_across, "tensor", 1)],
        axis=0,
    )
    normed_turned, raw_q, raw_k, q, k, v, k_turned = project(
        tokens_all, gain_attn, full_one if cubic else qkv_matrix[None], cos, sin, gain_query, gain_key
    )
    grad_across = flipped(cotangent, "tensor", 2, "grad_across")
    heads_other, heads_other_turned, logs_other = attend(1, info, q, k_turned, v)
    heads_other, grad_across = together(heads_other, grad_across)
    beside = nn(heads_other[local_rows:], out_matrix).astype(BF16)
    near = near_sum(nn(heads_other[:local_rows], out_matrix), beside).astype(BF16)
    near, q_own = together(near, q)
    attn_across = flipped(near, "tensor", 2, "attn_across")
    heads_own, heads_own_turned, logs_own = attend(0, info, q_own, k_turned, v)
    heads_own, attn_across = together(heads_own, attn_across)
    beside = nn(heads_own[local_rows:], out_matrix).astype(BF16)
    own_sum = near_sum(nn(heads_own[:local_rows], out_matrix), beside)
    own_sum, full_two = together(own_sum, full_two)
    middle = rows_float + own_sum + attn_across.astype(F32)
    grad_own = jnp.concatenate([cotangent, flipped(cotangent, "tensor", 1)], axis=0)
    grad_other = jnp.concatenate([grad_across, flipped(grad_across, "tensor", 1)], axis=0)
    normed_two = norm_rows(middle, gain_mlp).astype(BF16)
    normed_across = flipped(normed_two, "tensor", 2, "normed_across")
    normed_own = jnp.concatenate([normed_two, flipped(normed_two, "tensor", 1)], axis=0)
    if cubic:
        feed_matrices = (full_two,)
    else:
        feed_matrices = (
            full_two[:, :gate_rows]
            .reshape(spread, pieces, depth, half)
            .swapaxes(1, 2)
            .reshape(MODEL_WIDTH, -1),
            full_two[:, gate_rows:]
            .reshape(spread, 2, down_blocks, down_depth, half)
            .transpose(2, 0, 3, 1, 4)
            .reshape(-1, MODEL_WIDTH),
        )
    h_own, hidden_own, feed_grad_own, back_0, back_1, sum_0, sum_1 = feed(
        normed_own, grad_own, feed_matrices, hidden_local
    )
    normed_across, back_0 = together(normed_across, back_0)
    normed_other = jnp.concatenate([normed_across, flipped(normed_across, "tensor", 1)], axis=0)
    h_other, hidden_other, feed_grad_other, back_2, back_3, sum_2, sum_3 = feed(
        normed_other, grad_other, feed_matrices, hidden_local
    )
    near = near_sum(back_2, back_3).astype(BF16)
    back_beside = flipped(back_1, "tensor", 1)
    near, h_own = together(near, h_own)
    back_across = flipped(near, "tensor", 2, "back_across")

    feed_grads = feed_weights(
        full_two.shape if cubic else None, (h_own, h_other), (feed_grad_own, feed_grad_other),
        (hidden_own, hidden_other), (grad_own, grad_other),
    )
    back_across, _ = together(back_across, feed_grads[0])
    if cubic:
        feed_pack = feed_grads[0]
    else:
        feed_pack = jnp.concatenate(
            [
                feed_grads[0].reshape(spread, depth, pieces, half)
                .swapaxes(1, 2)
                .reshape(spread, -1, half),
                feed_grads[1].reshape(down_blocks, spread, down_depth, 2, half)
                .transpose(1, 3, 0, 2, 4)
                .reshape(spread, -1, half),
            ],
            axis=1,
        )
    feed_sum = lax.psum_scatter(feed_pack, "dp", scatter_dimension=0, tiled=True)[0].astype(F32)
    grad_middle, grad_middle_low, grad_gain_mlp = middle_back(
        back_0, back_beside, back_across, middle, cotangent, gain_mlp[None, :]
    )
    grad_gain_mlp = grad_gain_mlp[0]
    grad_middle_across = flipped(grad_middle_low, "tensor", 2, "grad_middle_across")

    grad_middle_own = jnp.concatenate(
        [grad_middle_low, flipped(grad_middle_low, "tensor", 1)], axis=0
    )
    grad_heads_own = nt(grad_middle_own, out_matrix).astype(BF16)
    grad_q, grad_k, grad_v, gain_own = attend_back_own(
        info, q, k, v, k_turned, start, logs_own, heads_own, grad_heads_own, raw_q, cos, sin,
        gain_query,
    )
    grad_middle_across, grad_q = together(grad_middle_across, grad_q)
    grad_middle_other = jnp.concatenate(
        [grad_middle_across, flipped(grad_middle_across, "tensor", 1)], axis=0
    )
    grad_heads_other = nt(grad_middle_other, out_matrix).astype(BF16)
    grad_qkv, gain_other = attend_back_other(
        info, q, k, v, k_turned, start, logs_other, heads_other, grad_heads_other,
        raw_q, cos, sin, gain_query, raw_k, gain_key, grad_q, grad_k, grad_v,
    )
    back_2, back_3 = unproject(1, grad_qkv, qkv_matrix)
    back_2, back_3, grad_qkv = together(back_2, back_3, grad_qkv)
    grad_qkv_w = nn(normed_turned, grad_qkv)
    near = near_sum(back_2, back_3).astype(BF16)
    near, grad_qkv, grad_qkv_w, sum_2, sum_3 = together(near, grad_qkv, grad_qkv_w, sum_2, sum_3)
    near_mlp = near_sum(sum_2, sum_3).astype(BF16)
    back_across = flipped(near, "tensor", 2, "back_across")
    grad_gain_attn = jnp.sum(qkv_matrix.astype(F32) * grad_qkv_w, axis=1) / gain_attn[0]
    grad_gain_heads = jnp.sum(gain_other, axis=0) + jnp.pad(
        jnp.sum(gain_own, axis=0), ((0, 1), (0, 0))
    )
    gain_sums = jnp.concatenate([grad_gain_attn, grad_gain_mlp, grad_gain_heads.reshape(-1)])
    back_0, back_1 = unproject(0, grad_qkv, qkv_matrix)

    def out_gradient(own_turned, other_turned):
        return (nn(own_turned, grad_middle_own) + nn(other_turned, grad_middle_other)).astype(BF16)

    if cubic:
        cube = (2, 2, 2)
        columns = grad_qkv_w.shape[1] // 2
        gain_rows = jnp.pad(
            gain_sums.reshape(cube + (1, gain_count)),
            ((0, 0),) * 3 + ((0, 15), (0, columns - gain_count)),
        )
        sum_one = jnp.concatenate(
            [grad_qkv_w[:, :columns].reshape(cube + (depth, -1)), gain_rows], axis=3
        )
        sum_two = grad_qkv_w[:, columns:].reshape(cube + (depth, -1))
        sum_one, sum_two = halved(sum_one, 1, 2), halved(sum_two, 2, 1)
        sum_one, sum_two, back_across, sum_0, sum_1, near_mlp, *heads_turned = together(
            sum_one, sum_two, back_across, sum_0, sum_1, near_mlp,
            heads_own_turned, heads_other_turned,
        )
        mlp_across = flipped(near_mlp, "tensor", 2, "mlp_across")
        sum_one, sum_two = halved(sum_one, 1, 1), halved(sum_two, 1, 2)
        sum_one, sum_two, feed_sum = together(sum_one, sum_two, feed_sum)
        grad_out_w = out_gradient(*heads_turned)
        sum_out = grad_out_w.reshape((out_heads,) + cube + (out_depth, MODEL_WIDTH))
        sum_out = halved(halved(sum_out, 3, 1), 2, 2)
        sum_one, sum_two = halved(sum_one, 0, 4), halved(sum_two, 0, 4)
        sum_out = halved(sum_out, 1, 4)
        block_out = (middle + near_sum(sum_0, sum_1) + mlp_across.astype(F32)).astype(BF16)
        sum_one, sum_two, block_out = together(sum_one, sum_two, block_out)
        sum_qkv = jnp.concatenate([sum_one[:depth], sum_two], axis=1)
        sum_qkv = sum_qkv.reshape(projection_weight.shape)
        sum_gains = sum_one[depth, :gain_count]
    else:
        mlp_across = flipped(near_mlp, "tensor", 2, "mlp_across")
        block_out = (middle + near_sum(sum_0, sum_1) + mlp_across.astype(F32)).astype(BF16)
        sum_qkv = (
            lax.psum_scatter(grad_qkv_w.astype(BF16), "dp", scatter_dimension=0, tiled=True)
            .astype(F32)
            .reshape(projection_weight.shape)
        )
        sum_out = lax.psum_scatter(
            out_gradient(heads_own_turned, heads_other_turned).reshape(out_heads, -1, MODEL_WIDTH), "dp",
            scatter_dimension=1, tiled=True,
        ).astype(F32)
        sum_gains = lax.psum_scatter(gain_sums, "dp", scatter_dimension=0, tiled=True)
    sum_gains = sum_gains + sum(flipped(sum_gains, "tensor", bit) for bit in range(1, shards))

    grad_normed_one = near_sum(back_0, back_1) + back_across.astype(F32)
    grad_rows_part, _ = norm_back(rows_float, gain_attn, grad_normed_one)
    grad_tokens = grad_middle + grad_rows_part

    sum_gate_up = (
        feed_sum[:gate_rows].reshape(pieces, depth, half).swapaxes(0, 1).reshape(w_gate_up.shape)
    )
    sum_down = feed_sum[gate_rows:].reshape(2, -1, half).swapaxes(0, 1).reshape(w_down.shape)

    upd_qkv = adamw_update(
        projection_weight, first_moment_projection, second_moment_projection,
        row_major(sum_qkv), 2.0 * MODEL_WIDTH ** (-0.5), DECAY,
    )
    upd_out = adamw_update(
        w_out, first_out, second_out, sum_out,
        2.0 * (QUERY_HEADS * HEAD_SIZE // 64) ** (-0.5), DECAY,
    )
    upd_gate_up = adamw_update(
        w_gate_up, first_gate_up, second_gate_up, row_major(sum_gate_up),
        2.0 * MODEL_WIDTH ** (-0.5), DECAY,
    )
    upd_down = adamw_update(w_down, first_down, second_down, sum_down, 2.0 * FF ** (-0.5), DECAY)
    upd_gains = adamw_update(gains, first_gains, second_gains, sum_gains, 0.5, 0.0)
    updates = (upd_qkv, upd_out, upd_gate_up, upd_down, upd_gains)
    return (
        block_out,
        grad_tokens,
        *(update[2] for update in updates),
        *(update[0] for update in updates),
        *(update[1] for update in updates),
    )


def solution(mesh):
    weights = (
        P("dp", "tensor", None),
        P("tensor", "dp", None),
        P("dp", None, "tensor"),
        P("tensor", "dp", None),
        P("dp"),
    )
    batch = P(("dp", "tensor"), None)
    return jax.shard_map(
        per_device,
        mesh=mesh,
        in_specs=(batch, batch, P("dp", None), *weights, *weights, *weights),
        out_specs=(batch, batch, *weights, *weights, *weights),
        check_vma=False,
    )
```

```python
import jax
import jax.numpy as jnp
from jax import lax
from jax.experimental import pallas as pl
from jax.experimental.layout import Layout, with_layout_constraint
from jax.experimental.pallas import tpu as pltpu
from jax.sharding import PartitionSpec as P

MODEL_WIDTH = 1024
QUERY_HEADS = 16
KEY_VALUE_HEADS = 8
HEAD_SIZE = 128
FF = 3072
STEP = 10

EPS = 1e-06
THETA = 1000000.0
BETA_ONE = 0.9
BETA_TWO = 0.95
ADAM_EPS = 1e-08
DECAY = 0.1

GROUP = QUERY_HEADS // KEY_VALUE_HEADS
SLOTS = GROUP + 2
SCALE = HEAD_SIZE ** (-0.5)
LOG2E = 1.4426950408889634
BLOCK = 256
VMEM_LIMIT = 48 * 1024 * 1024
F32 = jnp.float32
BF16 = jnp.bfloat16


def norm_rows(values, scales):
    return values * lax.rsqrt(jnp.mean(values * values, axis=-1, keepdims=True) + EPS) * scales


def norm_back(values, scales, grad):
    r = lax.rsqrt(jnp.mean(values * values, axis=-1, keepdims=True) + EPS)
    u = grad * scales
    back = r * u - values * (r * r * r) * jnp.mean(u * values, axis=-1, keepdims=True)
    return back, jnp.sum(grad * values * r, axis=0)


def row_major(value):
    return with_layout_constraint(value, Layout(major_to_minor=tuple(range(value.ndim))))


def adamw_update(master, moment_one, moment_two, gradient, step_rate, decay_rate):
    next_one = BETA_ONE * moment_one + (1.0 - BETA_ONE) * gradient
    next_two = BETA_TWO * moment_two + (1.0 - BETA_TWO) * gradient * gradient
    one_hat = next_one / (1.0 - BETA_ONE**STEP)
    two_hat = next_two / (1.0 - BETA_TWO**STEP)
    next_master = master - step_rate * (
        one_hat / (jnp.sqrt(two_hat) + ADAM_EPS) + decay_rate * master
    )
    return (next_one, next_two, next_master)


def nt(a, b):
    return lax.dot_general(a, b, (((1,), (1,)), ((), ())), preferred_element_type=F32)


def nn(a, b):
    return jnp.dot(a, b, preferred_element_type=F32)


def head_rotated(x, gain, cos, sin):
    r = lax.rsqrt(jnp.mean(x * x, axis=-1, keepdims=True) + EPS)
    y = x * r * gain
    return y * cos + pltpu.roll(y, HEAD_SIZE // 2, 1) * sin


def head_back(x, gain, cos, sin, grad):
    r = lax.rsqrt(jnp.mean(x * x, axis=-1, keepdims=True) + EPS)
    turned = grad * cos - pltpu.roll(grad, HEAD_SIZE // 2, 1) * sin
    u = turned * gain
    back = r * u - x * (r * r * r) * jnp.mean(u * x, axis=-1, keepdims=True)
    return back, jnp.sum(turned * x * r, axis=0, keepdims=True)


def at_block(index):
    return pl.ds(pl.multiple_of(index * BLOCK, BLOCK), BLOCK)


def allowed_block(key_block, query_block, start):
    keys = key_block * BLOCK + lax.broadcasted_iota(jnp.int32, (BLOCK, BLOCK), 0)
    queries = query_block * BLOCK + lax.broadcasted_iota(jnp.int32, (BLOCK, BLOCK), 1)
    return (keys >= start) & (keys <= queries)


def lanes_of(h):
    return slice(h * HEAD_SIZE, (h + 1) * HEAD_SIZE)


def project_kernel(
    x, gain, matrix, cos, sin, gain_q, gain_k, normed_turned, raw_q, raw_k, q, k, v, k_turned
):
    normed = norm_rows(x[...].astype(F32), gain[...])
    normed_turned[...] = normed.T.astype(BF16)
    h = normed.astype(BF16)
    c, s = cos[...], sin[...]
    for j in range(matrix.shape[2] // (SLOTS * HEAD_SIZE)):
        base = j * SLOTS * HEAD_SIZE
        columns = matrix[:, :, base : base + SLOTS * HEAD_SIZE]
        part = nn(h, columns.reshape(-1, SLOTS * HEAD_SIZE))
        for g in range(GROUP):
            value = part[:, lanes_of(g)]
            raw_q[:, lanes_of(j * GROUP + g)] = value
            q[:, lanes_of(j * GROUP + g)] = head_rotated(value, gain_q[...], c, s).astype(BF16)
        value = part[:, lanes_of(GROUP)]
        raw_k[:, lanes_of(j)] = value
        turned = head_rotated(value, gain_k[...], c, s)
        k[:, lanes_of(j)] = turned.astype(BF16)
        k_turned[lanes_of(j), :] = turned.T.astype(BF16)
        v[:, lanes_of(j)] = part[:, lanes_of(GROUP + 1)].astype(BF16)


def stacked(value):
    return jnp.concatenate([value[:, lanes_of(h)] for h in range(GROUP)], axis=0)


def stacked_turned(value):
    return jnp.concatenate(
        [value[:, lanes_of(h)].astype(F32).T.astype(BF16) for h in range(GROUP)], axis=1
    )


def attend_kernel(offset, info, q, k_turned, v, out, out_turned, logs):
    blocks = v.shape[0] // BLOCK
    flip = info[blocks]
    documents = info.shape[0] - blocks - 1

    def one_block(i, _):
        here = at_block(i)
        b = (i + offset) ^ flip
        index = b * BLOCK + lax.broadcasted_iota(jnp.int32, (BLOCK, 1), 0)
        first = jnp.zeros((BLOCK, 1), jnp.int32)
        for d in range(documents):
            begin = info[blocks + 1 + d]
            first = jnp.maximum(first, jnp.where(index >= begin, begin, 0))
        query = stacked(q[here, :])

        def keys_step(kb, carry):
            total, blend = carry
            there = at_block(kb ^ flip)
            keys = kb * BLOCK + lax.broadcasted_iota(jnp.int32, (BLOCK, BLOCK), 1)
            allowed = (keys >= first) & (keys <= index)
            score = nn(query, k_turned[:, there]).reshape(GROUP, BLOCK, BLOCK)
            p = jnp.where(allowed[None], jnp.exp2(score * (SCALE * LOG2E)), 0.0)
            p = p.reshape(GROUP * BLOCK, BLOCK)
            for lane in range(0, BLOCK, HEAD_SIZE):
                total = total + p[:, lane : lane + HEAD_SIZE]
            return total, blend + nn(p.astype(BF16), v[there, :])

        zero = jnp.zeros((GROUP * BLOCK, HEAD_SIZE), F32)
        total, blend = lax.fori_loop(info[b], b + 1, keys_step, (zero, zero))
        total = jnp.sum(total, axis=1, keepdims=True)
        result = blend / total
        log = jnp.broadcast_to(jnp.log2(total), result.shape)
        for h in range(GROUP):
            rows = slice(h * BLOCK, (h + 1) * BLOCK)
            out[here, lanes_of(h)] = result[rows].astype(BF16)
            out_turned[lanes_of(h), here] = result[rows].T.astype(BF16)
            logs[0, h : h + 1, here] = log[rows].T[0:1, :]
        return 0

    lax.fori_loop(0, q.shape[0] // BLOCK, one_block, 0)


def back_blocks(
    offset, info, q, k, v, k_turned, start, logs, out, grad_out, raw_q, cos, sin, gain_q,
    grad_k, grad_v, store,
):
    flip = info[k.shape[0] // BLOCK]

    def twice(row):
        return jnp.concatenate([row] * GROUP, axis=1)

    def one_block(i, total_gain):
        here = at_block(i)
        b = (i + offset) ^ flip
        first = start[:, here]
        gradients = grad_out[here, :]
        both = gradients.astype(F32) * out[here, :].astype(F32)
        query, gradient = stacked(q[here, :]), stacked(gradients)
        query_turned, gradient_turned = stacked_turned(q[here, :]), stacked_turned(gradients)
        across, log = [], []
        for h in range(GROUP):
            across.append(jnp.sum(both[:, lanes_of(h)].T, axis=0, keepdims=True))
            log.append(logs[0, h : h + 1, here])
        across, log = jnp.concatenate(across, axis=1), jnp.concatenate(log, axis=1)

        def keys_step(kb, grad_query):
            there = at_block(kb ^ flip)
            allowed = twice(allowed_block(kb, b, first).astype(jnp.int32)) > 0
            s = nn(k[there, :], query_turned)
            p = jnp.where(allowed, jnp.exp2(s * (SCALE * LOG2E) - log), 0.0)
            d = (p * (nn(v[there, :], gradient_turned) - across)).astype(BF16)
            grad_v[there, :] += nn(p.astype(BF16), gradient)
            grad_k[there, :] += nn(d, query)
            return grad_query + nn(k_turned[:, there], d)

        done = lax.fori_loop(
            info[b], b + 1, keys_step, jnp.zeros((HEAD_SIZE, GROUP * BLOCK), F32)
        )
        c, s = cos[here, :], sin[here, :]
        for h in range(GROUP):
            grad = done[:, h * BLOCK : (h + 1) * BLOCK].T * SCALE
            back, gain = head_back(raw_q[here, lanes_of(h)], gain_q[...], c, s, grad)
            store(i, h, back.astype(BF16))
            total_gain = total_gain + gain
        return total_gain

    return lax.fori_loop(0, q.shape[0] // BLOCK, one_block, jnp.zeros((1, HEAD_SIZE), F32))


def back_own_kernel(
    info, q, k, v, k_turned, start, logs, out, grad_out, raw_q, cos, sin, gain_q,
    grad_q, grad_k, grad_v, grad_gain,
):
    grad_k[...] = jnp.zeros(grad_k.shape, F32)
    grad_v[...] = jnp.zeros(grad_v.shape, F32)

    def store(i, h, value):
        grad_q[at_block(i), lanes_of(h)] = value

    grad_gain[0, :, :] = back_blocks(
        0, info, q, k, v, k_turned, start, logs, out, grad_out, raw_q, cos, sin, gain_q,
        grad_k, grad_v, store,
    )


def back_other_kernel(
    info, q, k, v, k_turned, start, logs, out, grad_out, raw_q, cos, sin, gain_q,
    cos_all, sin_all, raw_k, gain_k, grad_q_own, grad_k_own, grad_v_own,
    grad_qkv, grad_gains, grad_k, grad_v,
):
    half = q.shape[0] // BLOCK
    blocks = k.shape[0] // BLOCK
    queries = GROUP * HEAD_SIZE
    grad_k[...] = grad_k_own[...]
    grad_v[...] = grad_v_own[...]
    grad_qkv[: half * BLOCK, :queries] = grad_q_own[...]

    def store(i, h, value):
        grad_qkv[at_block(i + half), lanes_of(h)] = value

    grad_gains[0, 0:1, :] = back_blocks(
        half, info, q, k, v, k_turned, start, logs, out, grad_out, raw_q, cos, sin, gain_q,
        grad_k, grad_v, store,
    )

    def finish(i, total_gain):
        rows = at_block(i)
        back, gain = head_back(
            raw_k[rows, :], gain_k[...], cos_all[rows, :], sin_all[rows, :], grad_k[rows, :] * SCALE
        )
        grad_qkv[rows, lanes_of(GROUP)] = back.astype(BF16)
        grad_qkv[rows, lanes_of(GROUP + 1)] = grad_v[rows, :].astype(BF16)
        return total_gain + gain

    grad_gains[0, 1:2, :] = lax.fori_loop(0, blocks, finish, jnp.zeros((1, HEAD_SIZE), F32))


def unpack(packed, gate_up, down):
    n, _, half = packed.shape
    depth = gate_up.shape[0] // n
    pieces = gate_up.shape[1] // half
    blocks = down.shape[0] // HEAD_SIZE
    deep = HEAD_SIZE // n
    for d in range(n):
        for b in range(pieces):
            gate_up[d * depth : (d + 1) * depth, b * half : (b + 1) * half] = packed[
                d, b * depth : (b + 1) * depth, :
            ]
        for c in range(2):
            for i in range(blocks):
                at = pieces * depth + (c * blocks + i) * deep
                to = i * HEAD_SIZE + d * deep
                down[to : to + deep, c * half : (c + 1) * half] = packed[d, at : at + deep, :]


def feed_kernel(packs, h, grad, *refs):
    step = pl.program_id(0)
    if packs:
        packed, *refs = refs
        *refs, gate_up, down = refs

        @pl.when(step == 0)
        def _():
            unpack(packed, gate_up, down)
    else:
        gate_up, down, *refs = refs
    h_turned, hidden_turned, grad_gate_up, back_a, back_b, sum_a, sum_b = refs
    width = down.shape[0]
    rows = h[...]
    both = nn(rows, gate_up[...])
    gate, up = both[:, :width], both[:, width:]
    sig = jax.nn.sigmoid(gate)
    gated = gate * sig
    value = gated * up
    hidden_turned[...] = value.T.astype(BF16)
    h_turned[...] = rows.astype(F32).T.astype(BF16)
    grad_hidden = nt(grad[...], down[...])
    grad_gate_up[:, :width] = (grad_hidden * up * (sig + gated * (1.0 - sig))).astype(BF16)
    grad_gate_up[:, width:] = (grad_hidden * gated).astype(BF16)
    back = nt(grad_gate_up[...], gate_up[...]).astype(BF16)
    total = nn(value.astype(BF16), down[...]).astype(BF16)
    first = step < pl.num_programs(0) // 2

    @pl.when(first)
    def _():
        back_a[...] = back
        sum_a[...] = total

    @pl.when(jnp.logical_not(first))
    def _():
        back_b[...] = back
        sum_b[...] = total


def feed_weights_kernel(
    packs, pieces, h_own, h_other, grad_own, grad_other, hidden_own, hidden_other, dy_own, dy_other,
    *out
):
    step = pl.program_id(0)
    half = dy_own.shape[1]

    for b in range(pieces):
        @pl.when(step == b)
        def _():
            value = nn(h_own[...], grad_own[...]) + nn(h_other[...], grad_other[...])
            value = value.astype(BF16)
            if packs:
                n = out[0].shape[0]
                depth = value.shape[0] // n
                for d in range(n):
                    out[0][d, b * depth : (b + 1) * depth, :] = value[d * depth : (d + 1) * depth]
            else:
                out[0][:, b * half : (b + 1) * half] = value

    for c in range(2):
        @pl.when(step == pieces + c)
        def _():
            value = nn(hidden_own[...], dy_own[...]) + nn(hidden_other[...], dy_other[...])
            value = value.astype(BF16)
            if packs:
                n = out[0].shape[0]
                depth, deep = h_own.shape[0] // n, HEAD_SIZE // n
                blocks = value.shape[0] // HEAD_SIZE
                for d in range(n):
                    for i in range(blocks):
                        at = pieces * depth + (c * blocks + i) * deep
                        of = i * HEAD_SIZE + d * deep
                        out[0][d, at : at + deep, :] = value[of : of + deep]
            else:
                out[1][:, c * half : (c + 1) * half] = value


def unproject_kernel(grad, matrix, out_a, out_b):
    value = nt(grad[...], matrix[...]).astype(BF16)
    first = pl.program_id(0) < pl.num_programs(0) // 2

    @pl.when(first)
    def _():
        out_a[...] = value

    @pl.when(jnp.logical_not(first))
    def _():
        out_b[...] = value


def params(name, flops):
    return dict(
        compiler_params=pltpu.CompilerParams(
            dimension_semantics=("arbitrary",), vmem_limit_bytes=VMEM_LIMIT
        ),
        cost_estimate=pl.CostEstimate(flops=flops // 64, bytes_accessed=1_000, transcendentals=0),
        name=name,
    )


def fixed(shape, index=None):
    index = (0,) * len(shape) if index is None else index
    return pl.BlockSpec(shape, lambda i, *_: index)


def shaped(shape, kind):
    return jax.ShapeDtypeStruct(shape, kind)


def project(x, gain, matrix, cos, sin, gain_q, gain_k):
    rows, width = x.shape
    heads = matrix.shape[2] // (SLOTS * HEAD_SIZE)
    by_rows = lambda n: pl.BlockSpec((BLOCK, n), lambda i: (i, 0))
    by_lanes = lambda n: pl.BlockSpec((n, BLOCK), lambda i: (0, i))
    q_width, k_width = heads * GROUP * HEAD_SIZE, heads * HEAD_SIZE
    return pl.pallas_call(
        project_kernel,
        grid=(rows // BLOCK,),
        in_specs=[
            by_rows(width), fixed((1, width)),
            fixed((matrix.shape[0], width // matrix.shape[0], matrix.shape[2])), by_rows(HEAD_SIZE),
            by_rows(HEAD_SIZE), fixed((1, HEAD_SIZE)), fixed((1, HEAD_SIZE)),
        ],
        out_specs=[
            by_lanes(width), by_rows(q_width), by_rows(k_width), by_rows(q_width),
            by_rows(k_width), by_rows(k_width), by_lanes(k_width),
        ],
        out_shape=[
            shaped((width, rows), BF16), shaped((rows, q_width), F32),
            shaped((rows, k_width), F32), shaped((rows, q_width), BF16),
            shaped((rows, k_width), BF16), shaped((rows, k_width), BF16),
            shaped((k_width, rows), BF16),
        ],
        **params("project", 10_000_000_000),
    )(x, gain, matrix, cos, sin, gain_q, gain_k)


def head_specs(half, rows):
    n = rows // 2
    queries = GROUP * HEAD_SIZE
    return dict(
        q=pl.BlockSpec((n, queries), lambda j, info: (half, j)),
        k=pl.BlockSpec((rows, HEAD_SIZE), lambda j, info: (0, j)),
        turned=pl.BlockSpec((HEAD_SIZE, rows), lambda j, info: (j, 0)),
        start=pl.BlockSpec((1, n), lambda j, info: (0, half)),
        out=pl.BlockSpec((n, queries), lambda j, info: (0, j)),
        out_turned=pl.BlockSpec((queries, n), lambda j, info: (j, 0)),
        logs=pl.BlockSpec((1, GROUP, n), lambda j, info: (j, 0, 0)),
        angle=pl.BlockSpec((n, HEAD_SIZE), lambda j, info: (half, 0)),
        row=fixed((1, HEAD_SIZE)),
    )


def attend(half, info, q, k_turned, v):
    rows = v.shape[0]
    n, heads = rows // 2, v.shape[1] // HEAD_SIZE
    s = head_specs(half, rows)
    return pl.pallas_call(
        lambda *refs: attend_kernel(half * n // BLOCK, *refs),
        grid_spec=pltpu.PrefetchScalarGridSpec(
            num_scalar_prefetch=1,
            grid=(heads,),
            in_specs=[s["q"], s["turned"], s["k"]],
            out_specs=[s["out"], s["out_turned"], s["logs"]],
        ),
        out_shape=[
            shaped((n, q.shape[1]), BF16), shaped((q.shape[1], n), BF16),
            shaped((heads, GROUP, n), F32),
        ],
        **params("attend", 18_000_000_000),
    )(info, q, k_turned, v)


def attend_back_own(info, q, k, v, k_turned, start, logs, out, grad_out, raw_q, cos, sin, gain_q):
    rows = k.shape[0]
    n, heads = rows // 2, k.shape[1] // HEAD_SIZE
    s = head_specs(0, rows)
    return pl.pallas_call(
        back_own_kernel,
        grid_spec=pltpu.PrefetchScalarGridSpec(
            num_scalar_prefetch=1,
            grid=(heads,),
            in_specs=[
                s["q"], s["k"], s["k"], s["turned"], s["start"], s["logs"], s["out"], s["out"],
                s["q"], s["angle"], s["angle"], s["row"],
            ],
            out_specs=[
                s["out"], s["k"], s["k"],
                pl.BlockSpec((1, 1, HEAD_SIZE), lambda j, info: (j, 0, 0)),
            ],
        ),
        out_shape=[
            shaped((n, q.shape[1]), BF16), shaped(k.shape, F32), shaped(k.shape, F32),
            shaped((heads, 1, HEAD_SIZE), F32),
        ],
        **params("attend_back_own", 25_000_000_000),
    )(info, q, k, v, k_turned, start, logs, out, grad_out, raw_q, cos, sin, gain_q)


def attend_back_other(
    info, q, k, v, k_turned, start, logs, out, grad_out, raw_q, cos, sin, gain_q,
    raw_k, gain_k, grad_q, grad_k, grad_v,
):
    rows = k.shape[0]
    heads = k.shape[1] // HEAD_SIZE
    width = SLOTS * HEAD_SIZE
    s = head_specs(1, rows)
    whole = fixed((rows, HEAD_SIZE))
    return pl.pallas_call(
        back_other_kernel,
        grid_spec=pltpu.PrefetchScalarGridSpec(
            num_scalar_prefetch=1,
            grid=(heads,),
            in_specs=[
                s["q"], s["k"], s["k"], s["turned"], s["start"], s["logs"], s["out"], s["out"],
                s["q"], s["angle"], s["angle"], s["row"],
                whole, whole, s["k"], s["row"], s["out"], s["k"], s["k"],
            ],
            out_specs=[
                pl.BlockSpec((rows, width), lambda j, info: (0, j)),
                pl.BlockSpec((1, 2, HEAD_SIZE), lambda j, info: (j, 0, 0)),
            ],
            scratch_shapes=[pltpu.VMEM((rows, HEAD_SIZE), F32)] * 2,
        ),
        out_shape=[shaped((rows, heads * width), BF16), shaped((heads, 2, HEAD_SIZE), F32)],
        **params("attend_back_other", 28_000_000_000),
    )(
        info, q, k, v, k_turned, start, logs, out, grad_out, raw_q, cos, sin, gain_q,
        cos, sin, raw_k, gain_k, grad_q, grad_k, grad_v,
    )


def two_parts(rows, width):
    steps = rows // BLOCK // 2
    return (
        [
            pl.BlockSpec((BLOCK, width), lambda i: (jnp.minimum(i, steps - 1), 0)),
            pl.BlockSpec((BLOCK, width), lambda i: (jnp.maximum(i - steps, 0), 0)),
        ],
        [shaped((rows // 2, width), BF16)] * 2,
    )


def feed(h, grad, weights, hidden_count):
    rows, width = h.shape
    packs = len(weights) == 1
    by_rows = lambda n: pl.BlockSpec((BLOCK, n), lambda i: (i, 0))
    by_lanes = lambda n: pl.BlockSpec((n, BLOCK), lambda i: (0, i))
    specs, shapes = two_parts(rows, width)
    scratch = [
        pltpu.VMEM((width, 2 * hidden_count), BF16), pltpu.VMEM((hidden_count, width), BF16)
    ]
    return pl.pallas_call(
        lambda *refs: feed_kernel(packs, *refs),
        grid=(rows // BLOCK,),
        in_specs=[by_rows(width), by_rows(width), *(fixed(w.shape) for w in weights)],
        out_specs=[
            by_lanes(width), by_lanes(hidden_count), by_rows(2 * hidden_count), *specs, *specs
        ],
        out_shape=[
            shaped((width, rows), BF16), shaped((hidden_count, rows), BF16),
            shaped((rows, 2 * hidden_count), BF16), *shapes, *shapes,
        ],
        scratch_shapes=scratch if packs else [],
        **params("feed", 16_000_000_000),
    )(h, grad, *weights)


def feed_weights(packed_shape, h, grads, hidden, dy):
    width, n = h[0].shape
    half = width // 2
    pieces = grads[0].shape[1] // half
    count = hidden[0].shape[0]
    packs = packed_shape is not None
    gate_block = pl.BlockSpec((n, half), lambda i: (0, jnp.minimum(i, pieces - 1)))
    down_block = pl.BlockSpec((n, half), lambda i: (0, jnp.maximum(i - pieces, 0)))
    shapes = [packed_shape] if packs else [(width, 2 * count), (count, width)]
    return pl.pallas_call(
        lambda *refs: feed_weights_kernel(packs, pieces, *refs),
        grid=(pieces + 2,),
        in_specs=[
            fixed((width, n)), fixed((width, n)), gate_block, gate_block,
            fixed((count, n)), fixed((count, n)), down_block, down_block,
        ],
        out_specs=[fixed(shape) for shape in shapes],
        out_shape=[shaped(shape, BF16) for shape in shapes],
        **params("feed_weights", 16_000_000_000),
    )(*h, *grads, *hidden, *dy)


def unproject(half, grad, matrix):
    rows, width = grad.shape
    n = rows // 2
    steps = n // BLOCK
    specs, shapes = two_parts(n, matrix.shape[0])
    return pl.pallas_call(
        unproject_kernel,
        grid=(steps,),
        in_specs=[pl.BlockSpec((BLOCK, width), lambda i: (i + half * steps, 0)), fixed(matrix.shape)],
        out_specs=specs,
        out_shape=shapes,
        **params("unproject", 4_000_000_000),
    )(grad, matrix)


def middle_back_kernel(own, beside, across, value, grad, gain, out, out_low, grad_gain):
    total = own[...].astype(F32) + beside[...].astype(F32) + across[...].astype(F32)
    x = value[...]
    r = lax.rsqrt(jnp.mean(x * x, axis=-1, keepdims=True) + EPS)
    u = total * gain[...]
    back = r * u - x * (r * r * r) * jnp.mean(u * x, axis=-1, keepdims=True)
    result = grad[...].astype(F32) + back
    out[...] = result
    out_low[...] = result.astype(BF16)
    part = jnp.sum(total * x * r, axis=0, keepdims=True)

    @pl.when(pl.program_id(0) == 0)
    def _():
        grad_gain[...] = part

    @pl.when(pl.program_id(0) > 0)
    def _():
        grad_gain[...] += part


def middle_back(own, beside, across, value, grad, gain):
    rows, width = value.shape
    block = pl.BlockSpec((BLOCK // 2, width), lambda i: (i, 0))
    row = fixed((1, width))
    return pl.pallas_call(
        middle_back_kernel,
        grid=(rows // (BLOCK // 2),),
        in_specs=[block] * 5 + [row],
        out_specs=[block, block, row],
        out_shape=[shaped((rows, width), F32), shaped((rows, width), BF16), shaped((1, width), F32)],
        **params("middle_back", 2_000_000_000),
    )(own, beside, across, value, grad, gain)


def flipped(value, axis, bit, name="part"):
    with jax.named_scope(name):
        return lax.ppermute(value, axis, [(i, i ^ bit) for i in range(lax.axis_size(axis))])


def together(*values):
    return lax.optimization_barrier(values)


def near_sum(part, beside):
    return part.astype(F32) + flipped(beside, "tensor", 1).astype(F32)


def halved(parts, axis, bit):
    mine = (lax.axis_index("dp") // bit) % 2
    send = lax.dynamic_index_in_dim(parts, 1 - mine, axis, keepdims=False).astype(BF16)
    keep = lax.dynamic_index_in_dim(parts, mine, axis, keepdims=False)
    return keep.astype(F32) + flipped(send, "dp", bit).astype(F32)


def per_device(
    tokens, cotangent, lengths,
    projection_weight, w_out, w_gate_up, w_down, gains,
    first_moment_projection, first_out, first_gate_up, first_down, first_gains,
    second_moment_projection, second_out, second_gate_up, second_down, second_gains,
):
    shards = lax.axis_size("tensor")
    spread = lax.axis_size("dp")
    me = lax.axis_index("tensor")
    local_rows = tokens.shape[0]
    rows = local_rows * shards
    blocks = rows // BLOCK
    kv_local = projection_weight.shape[1]
    hidden_local = w_gate_up.shape[2]
    out_heads, out_depth = w_out.shape[0], w_out.shape[1]
    down_blocks, down_depth = w_down.shape[0], w_down.shape[1]
    depth = projection_weight.shape[0]
    gain_count = gains.shape[0]

    half = MODEL_WIDTH // 2
    pieces = 2 * hidden_local // half
    gate_rows = pieces * depth
    out_rows = out_heads * out_depth
    cubic = spread == 8

    pack_one = jnp.concatenate(
        [
            projection_weight.astype(BF16).reshape(depth, -1),
            w_out.astype(BF16).reshape(-1, MODEL_WIDTH),
            jnp.pad(gains.astype(BF16)[None, :], ((0, 15), (0, MODEL_WIDTH - gain_count))),
        ],
        axis=0,
    )
    pack_two = jnp.concatenate(
        [
            w_gate_up.astype(BF16).reshape(depth, pieces, half).swapaxes(0, 1).reshape(-1, half),
            w_down.astype(BF16).reshape(-1, 2, half).swapaxes(0, 1).reshape(-1, half),
        ],
        axis=0,
    )

    def split_one(value):
        return (
            value[..., :depth, :],
            value[..., depth : depth + out_rows, :],
            value[..., depth + out_rows, :gain_count],
        )

    full_one = lax.all_gather(pack_one, "dp", axis=0, tiled=False)
    full_qkv, full_out, full_gains = split_one(full_one)
    full_out = full_out.reshape(spread, out_heads, out_depth, MODEL_WIDTH).swapaxes(0, 1)
    full_two = lax.all_gather(pack_two, "dp", axis=0, tiled=False)
    qkv_matrix = full_qkv.reshape(MODEL_WIDTH, -1)
    out_matrix = full_out.reshape(-1, MODEL_WIDTH)
    gains_all = full_gains.reshape(-1).astype(F32)
    gain_attn = gains_all[None, :MODEL_WIDTH]
    gain_mlp = gains_all[MODEL_WIDTH : 2 * MODEL_WIDTH]
    gain_query = gains_all[None, 2 * MODEL_WIDTH : 2 * MODEL_WIDTH + HEAD_SIZE]
    gain_key = gains_all[None, 2 * MODEL_WIDTH + HEAD_SIZE :]

    doc_ends = jnp.cumsum(lengths[0])
    doc_starts = doc_ends - lengths[0]

    def start_of(index):
        return jnp.max(
            jnp.where(index[:, None] >= doc_starts[None, :], doc_starts[None, :], 0), axis=1
        )

    order = me ^ jnp.arange(shards, dtype=jnp.int32)
    index_of_row = (
        order[:, None] * local_rows + jnp.arange(local_rows, dtype=jnp.int32)[None, :]
    ).reshape(-1)
    start_of_row = start_of(index_of_row)
    position = index_of_row - start_of_row
    inverse = THETA ** (-2.0 * jnp.arange(HEAD_SIZE // 2, dtype=F32) / HEAD_SIZE)
    turned = position.astype(F32)[:, None] * inverse[None, :]
    cosine, sine = jnp.cos(turned), jnp.sin(turned)
    cos = jnp.concatenate([cosine, cosine], axis=1)
    sin = jnp.concatenate([-sine, sine], axis=1)
    block_starts = start_of(jnp.arange(blocks, dtype=jnp.int32) * BLOCK) // BLOCK
    info = jnp.concatenate(
        [block_starts, (me * (local_rows // BLOCK))[None], doc_starts]
    ).astype(jnp.int32)
    start = start_of_row[None, :]

    rows_float = tokens.astype(F32)
    tokens_across = flipped(tokens, "tensor", 2, "tokens_across")
    tokens_all = jnp.concatenate(
        [tokens, flipped(tokens, "tensor", 1), tokens_across, flipped(tokens_across, "tensor", 1)],
        axis=0,
    )
    normed_turned, raw_q, raw_k, q, k, v, k_turned = project(
        tokens_all, gain_attn, full_one if cubic else qkv_matrix[None], cos, sin, gain_query, gain_key
    )
    grad_across = flipped(cotangent, "tensor", 2, "grad_across")
    heads_other, heads_other_turned, logs_other = attend(1, info, q, k_turned, v)
    heads_other, grad_across = together(heads_other, grad_across)
    beside = nn(heads_other[local_rows:], out_matrix).astype(BF16)
    near = near_sum(nn(heads_other[:local_rows], out_matrix), beside).astype(BF16)
    near, q_own = together(near, q)
    attn_across = flipped(near, "tensor", 2, "attn_across")
    heads_own, heads_own_turned, logs_own = attend(0, info, q_own, k_turned, v)
    heads_own, attn_across = together(heads_own, attn_across)
    beside = nn(heads_own[local_rows:], out_matrix).astype(BF16)
    own_sum = near_sum(nn(heads_own[:local_rows], out_matrix), beside)
    own_sum, full_two = together(own_sum, full_two)
    middle = rows_float + own_sum + attn_across.astype(F32)
    grad_own = jnp.concatenate([cotangent, flipped(cotangent, "tensor", 1)], axis=0)
    grad_other = jnp.concatenate([grad_across, flipped(grad_across, "tensor", 1)], axis=0)
    normed_two = norm_rows(middle, gain_mlp).astype(BF16)
    normed_across = flipped(normed_two, "tensor", 2, "normed_across")
    normed_own = jnp.concatenate([normed_two, flipped(normed_two, "tensor", 1)], axis=0)
    if cubic:
        feed_matrices = (full_two,)
    else:
        feed_matrices = (
            full_two[:, :gate_rows]
            .reshape(spread, pieces, depth, half)
            .swapaxes(1, 2)
            .reshape(MODEL_WIDTH, -1),
            full_two[:, gate_rows:]
            .reshape(spread, 2, down_blocks, down_depth, half)
            .transpose(2, 0, 3, 1, 4)
            .reshape(-1, MODEL_WIDTH),
        )
    h_own, hidden_own, feed_grad_own, back_0, back_1, sum_0, sum_1 = feed(
        normed_own, grad_own, feed_matrices, hidden_local
    )
    normed_across, back_0 = together(normed_across, back_0)
    normed_other = jnp.concatenate([normed_across, flipped(normed_across, "tensor", 1)], axis=0)
    h_other, hidden_other, feed_grad_other, back_2, back_3, sum_2, sum_3 = feed(
        normed_other, grad_other, feed_matrices, hidden_local
    )
    near = near_sum(back_2, back_3).astype(BF16)
    back_beside = flipped(back_1, "tensor", 1)
    near, h_own = together(near, h_own)
    back_across = flipped(near, "tensor", 2, "back_across")

    feed_grads = feed_weights(
        full_two.shape if cubic else None, (h_own, h_other), (feed_grad_own, feed_grad_other),
        (hidden_own, hidden_other), (grad_own, grad_other),
    )
    back_across, *feed_grads = together(back_across, *feed_grads)
    if cubic:
        feed_pack = feed_grads[0]
    else:
        feed_pack = jnp.concatenate(
            [
                feed_grads[0].reshape(spread, depth, pieces, half)
                .swapaxes(1, 2)
                .reshape(spread, -1, half),
                feed_grads[1].reshape(down_blocks, spread, down_depth, 2, half)
                .transpose(1, 3, 0, 2, 4)
                .reshape(spread, -1, half),
            ],
            axis=1,
        )
    feed_sum = lax.psum_scatter(feed_pack, "dp", scatter_dimension=0, tiled=True)[0].astype(F32)
    grad_middle, grad_middle_low, grad_gain_mlp = middle_back(
        back_0, back_beside, back_across, middle, cotangent, gain_mlp[None, :]
    )
    grad_gain_mlp = grad_gain_mlp[0]
    grad_middle_across = flipped(grad_middle_low, "tensor", 2, "grad_middle_across")

    grad_middle_own = jnp.concatenate(
        [grad_middle_low, flipped(grad_middle_low, "tensor", 1)], axis=0
    )
    grad_heads_own = nt(grad_middle_own, out_matrix).astype(BF16)
    grad_q, grad_k, grad_v, gain_own = attend_back_own(
        info, q, k, v, k_turned, start, logs_own, heads_own, grad_heads_own, raw_q, cos, sin,
        gain_query,
    )
    grad_middle_across, grad_q = together(grad_middle_across, grad_q)
    grad_middle_other = jnp.concatenate(
        [grad_middle_across, flipped(grad_middle_across, "tensor", 1)], axis=0
    )
    grad_heads_other = nt(grad_middle_other, out_matrix).astype(BF16)
    grad_out_w = (
        nn(heads_own_turned, grad_middle_own) + nn(heads_other_turned, grad_middle_other)
    ).astype(BF16)
    grad_out_w, grad_heads_other = together(grad_out_w, grad_heads_other)
    grad_qkv, gain_other = attend_back_other(
        info, q, k, v, k_turned, start, logs_other, heads_other, grad_heads_other,
        raw_q, cos, sin, gain_query, raw_k, gain_key, grad_q, grad_k, grad_v,
    )
    back_2, back_3 = unproject(1, grad_qkv, qkv_matrix)
    back_2, back_3, grad_qkv = together(back_2, back_3, grad_qkv)
    grad_qkv_w = nn(normed_turned, grad_qkv).astype(BF16)
    near = near_sum(back_2, back_3).astype(BF16)
    near, grad_qkv, grad_qkv_w, grad_out_w, sum_2, sum_3 = together(
        near, grad_qkv, grad_qkv_w, grad_out_w, sum_2, sum_3
    )
    near_mlp = near_sum(sum_2, sum_3).astype(BF16)
    back_across = flipped(near, "tensor", 2, "back_across")
    grad_gain_attn = jnp.sum(
        qkv_matrix.astype(F32) * grad_qkv_w.astype(F32), axis=1
    ) / gain_attn[0]
    grad_gain_heads = jnp.sum(gain_other, axis=0) + jnp.pad(
        jnp.sum(gain_own, axis=0), ((0, 1), (0, 0))
    )
    gain_sums = jnp.concatenate([grad_gain_attn, grad_gain_mlp, grad_gain_heads.reshape(-1)])
    back_0, back_1 = unproject(0, grad_qkv, qkv_matrix)

    if cubic:
        cube = (2, 2, 2)
        columns = grad_qkv_w.shape[1] // 2
        gain_rows = jnp.pad(
            gain_sums.astype(BF16).reshape(cube + (1, gain_count)),
            ((0, 0),) * 3 + ((0, 15), (0, columns - gain_count)),
        )
        sum_one = jnp.concatenate(
            [grad_qkv_w[:, :columns].reshape(cube + (depth, -1)), gain_rows], axis=3
        )
        sum_two = grad_qkv_w[:, columns:].reshape(cube + (depth, -1))
        sum_one, sum_two = halved(sum_one, 1, 2), halved(sum_two, 2, 1)
        sum_out = grad_out_w.reshape((out_heads,) + cube + (out_depth, MODEL_WIDTH))
        sum_out = halved(sum_out, 3, 1)
        sum_one, sum_two, back_across, sum_0, sum_1, near_mlp = together(
            sum_one, sum_two, back_across, sum_0, sum_1, near_mlp
        )
        mlp_across = flipped(near_mlp, "tensor", 2, "mlp_across")
        sum_one, sum_two = halved(sum_one, 1, 1), halved(sum_two, 1, 2)
        sum_out = halved(sum_out, 2, 2)
        sum_one, sum_two, sum_out, feed_sum = together(sum_one, sum_two, sum_out, feed_sum)
        sum_one, sum_two = halved(sum_one, 0, 4), halved(sum_two, 0, 4)
        sum_out = halved(sum_out, 1, 4)
        block_out = (middle + near_sum(sum_0, sum_1) + mlp_across.astype(F32)).astype(BF16)
        sum_one, sum_two, sum_out, block_out = together(sum_one, sum_two, sum_out, block_out)
        sum_qkv = jnp.concatenate([sum_one[:depth], sum_two], axis=1)
        sum_qkv = sum_qkv.reshape(projection_weight.shape)
        sum_gains = sum_one[depth, :gain_count]
    else:
        mlp_across = flipped(near_mlp, "tensor", 2, "mlp_across")
        block_out = (middle + near_sum(sum_0, sum_1) + mlp_across.astype(F32)).astype(BF16)
        sum_qkv = (
            lax.psum_scatter(grad_qkv_w.astype(BF16), "dp", scatter_dimension=0, tiled=True)
            .astype(F32)
            .reshape(projection_weight.shape)
        )
        sum_out = lax.psum_scatter(
            grad_out_w.reshape(out_heads, -1, MODEL_WIDTH), "dp",
            scatter_dimension=1, tiled=True,
        ).astype(F32)
        sum_gains = lax.psum_scatter(gain_sums, "dp", scatter_dimension=0, tiled=True)
    sum_gains = sum_gains + sum(flipped(sum_gains, "tensor", bit) for bit in range(1, shards))

    grad_normed_one = near_sum(back_0, back_1) + back_across.astype(F32)
    grad_rows_part, _ = norm_back(rows_float, gain_attn, grad_normed_one)
    grad_tokens = grad_middle + grad_rows_part

    sum_gate_up = (
        feed_sum[:gate_rows].reshape(pieces, depth, half).swapaxes(0, 1).reshape(w_gate_up.shape)
    )
    sum_down = feed_sum[gate_rows:].reshape(2, -1, half).swapaxes(0, 1).reshape(w_down.shape)

    upd_qkv = adamw_update(
        projection_weight, first_moment_projection, second_moment_projection,
        row_major(sum_qkv), 2.0 * MODEL_WIDTH ** (-0.5), DECAY,
    )
    upd_out = adamw_update(
        w_out, first_out, second_out, sum_out,
        2.0 * (QUERY_HEADS * HEAD_SIZE // 64) ** (-0.5), DECAY,
    )
    upd_gate_up = adamw_update(
        w_gate_up, first_gate_up, second_gate_up, row_major(sum_gate_up),
        2.0 * MODEL_WIDTH ** (-0.5), DECAY,
    )
    upd_down = adamw_update(w_down, first_down, second_down, sum_down, 2.0 * FF ** (-0.5), DECAY)
    upd_gains = adamw_update(gains, first_gains, second_gains, sum_gains, 0.5, 0.0)
    updates = (upd_qkv, upd_out, upd_gate_up, upd_down, upd_gains)
    return (
        block_out,
        grad_tokens,
        *(update[2] for update in updates),
        *(update[0] for update in updates),
        *(update[1] for update in updates),
    )


def solution(mesh):
    weights = (
        P("dp", "tensor", None),
        P("tensor", "dp", None),
        P("dp", None, "tensor"),
        P("tensor", "dp", None),
        P("dp"),
    )
    batch = P(("dp", "tensor"), None)
    return jax.shard_map(
        per_device,
        mesh=mesh,
        in_specs=(batch, batch, P("dp", None), *weights, *weights, *weights),
        out_specs=(batch, batch, *weights, *weights, *weights),
        check_vma=False,
    )
```

```python
import jax
import jax.numpy as jnp
from jax import lax
from jax.experimental import pallas as pl
from jax.experimental.layout import Layout, with_layout_constraint
from jax.experimental.pallas import tpu as pltpu
from jax.sharding import PartitionSpec as P

MODEL_WIDTH = 1024
QUERY_HEADS = 16
KEY_VALUE_HEADS = 8
HEAD_SIZE = 128
FF = 3072
STEP = 10

EPS = 1e-06
THETA = 1000000.0
BETA_ONE = 0.9
BETA_TWO = 0.95
ADAM_EPS = 1e-08
DECAY = 0.1

GROUP = QUERY_HEADS // KEY_VALUE_HEADS
SLOTS = GROUP + 2
SCALE = HEAD_SIZE ** (-0.5)
LOG2E = 1.4426950408889634
BLOCK = 256
VMEM_LIMIT = 48 * 1024 * 1024
F32 = jnp.float32
BF16 = jnp.bfloat16


def norm_rows(values, scales):
    return values * lax.rsqrt(jnp.mean(values * values, axis=-1, keepdims=True) + EPS) * scales


def norm_back(values, scales, grad):
    r = lax.rsqrt(jnp.mean(values * values, axis=-1, keepdims=True) + EPS)
    u = grad * scales
    back = r * u - values * (r * r * r) * jnp.mean(u * values, axis=-1, keepdims=True)
    return back, jnp.sum(grad * values * r, axis=0)


def row_major(value):
    return with_layout_constraint(value, Layout(major_to_minor=tuple(range(value.ndim))))


def adamw_update(master, moment_one, moment_two, gradient, step_rate, decay_rate):
    next_one = BETA_ONE * moment_one + (1.0 - BETA_ONE) * gradient
    next_two = BETA_TWO * moment_two + (1.0 - BETA_TWO) * gradient * gradient
    one_hat = next_one / (1.0 - BETA_ONE**STEP)
    two_hat = next_two / (1.0 - BETA_TWO**STEP)
    next_master = master - step_rate * (
        one_hat / (jnp.sqrt(two_hat) + ADAM_EPS) + decay_rate * master
    )
    return (next_one, next_two, next_master)


def nt(a, b):
    return lax.dot_general(a, b, (((1,), (1,)), ((), ())), preferred_element_type=F32)


def nn(a, b):
    return jnp.dot(a, b, preferred_element_type=F32)


def head_rotated(x, gain, cos, sin):
    r = lax.rsqrt(jnp.mean(x * x, axis=-1, keepdims=True) + EPS)
    y = x * r * gain
    return y * cos + pltpu.roll(y, HEAD_SIZE // 2, 1) * sin


def head_back(x, gain, cos, sin, grad):
    r = lax.rsqrt(jnp.mean(x * x, axis=-1, keepdims=True) + EPS)
    turned = grad * cos - pltpu.roll(grad, HEAD_SIZE // 2, 1) * sin
    u = turned * gain
    back = r * u - x * (r * r * r) * jnp.mean(u * x, axis=-1, keepdims=True)
    return back, jnp.sum(turned * x * r, axis=0, keepdims=True)


def at_block(index):
    return pl.ds(pl.multiple_of(index * BLOCK, BLOCK), BLOCK)


def allowed_block(key_block, query_block, start):
    keys = key_block * BLOCK + lax.broadcasted_iota(jnp.int32, (BLOCK, BLOCK), 0)
    queries = query_block * BLOCK + lax.broadcasted_iota(jnp.int32, (BLOCK, BLOCK), 1)
    return (keys >= start) & (keys <= queries)


def lanes_of(h):
    return slice(h * HEAD_SIZE, (h + 1) * HEAD_SIZE)


def project_kernel(
    x, gain, matrix, cos, sin, gain_q, gain_k, normed_turned, raw_q, raw_k, q, k, v, k_turned
):
    normed = norm_rows(x[...].astype(F32), gain[...])
    normed_turned[...] = normed.T.astype(BF16)
    h = normed.astype(BF16)
    c, s = cos[...], sin[...]
    for j in range(matrix.shape[1] // (SLOTS * HEAD_SIZE)):
        base = j * SLOTS * HEAD_SIZE
        part = nn(h, matrix[:, base : base + SLOTS * HEAD_SIZE])
        for g in range(GROUP):
            value = part[:, lanes_of(g)]
            raw_q[:, lanes_of(j * GROUP + g)] = value
            q[:, lanes_of(j * GROUP + g)] = head_rotated(value, gain_q[...], c, s).astype(BF16)
        value = part[:, lanes_of(GROUP)]
        raw_k[:, lanes_of(j)] = value
        turned = head_rotated(value, gain_k[...], c, s)
        k[:, lanes_of(j)] = turned.astype(BF16)
        k_turned[lanes_of(j), :] = turned.T.astype(BF16)
        v[:, lanes_of(j)] = part[:, lanes_of(GROUP + 1)].astype(BF16)


def stacked(value):
    return jnp.concatenate([value[:, lanes_of(h)] for h in range(GROUP)], axis=0)


def stacked_turned(value):
    return jnp.concatenate(
        [value[:, lanes_of(h)].astype(F32).T.astype(BF16) for h in range(GROUP)], axis=1
    )


def attend_kernel(offset, info, q, k_turned, v, out, out_turned, logs):
    blocks = v.shape[0] // BLOCK
    flip = info[blocks]
    documents = info.shape[0] - blocks - 1

    def one_block(i, _):
        here = at_block(i)
        b = (i + offset) ^ flip
        index = b * BLOCK + lax.broadcasted_iota(jnp.int32, (BLOCK, 1), 0)
        first = jnp.zeros((BLOCK, 1), jnp.int32)
        for d in range(documents):
            begin = info[blocks + 1 + d]
            first = jnp.maximum(first, jnp.where(index >= begin, begin, 0))
        query = stacked(q[here, :])

        def keys_step(kb, carry):
            total, blend = carry
            there = at_block(kb ^ flip)
            keys = kb * BLOCK + lax.broadcasted_iota(jnp.int32, (BLOCK, BLOCK), 1)
            allowed = (keys >= first) & (keys <= index)
            score = nn(query, k_turned[:, there]).reshape(GROUP, BLOCK, BLOCK)
            p = jnp.where(allowed[None], jnp.exp2(score * (SCALE * LOG2E)), 0.0)
            p = p.reshape(GROUP * BLOCK, BLOCK)
            for lane in range(0, BLOCK, HEAD_SIZE):
                total = total + p[:, lane : lane + HEAD_SIZE]
            return total, blend + nn(p.astype(BF16), v[there, :])

        zero = jnp.zeros((GROUP * BLOCK, HEAD_SIZE), F32)
        total, blend = lax.fori_loop(info[b], b + 1, keys_step, (zero, zero))
        total = jnp.sum(total, axis=1, keepdims=True)
        result = blend / total
        log = jnp.broadcast_to(jnp.log2(total), result.shape)
        for h in range(GROUP):
            rows = slice(h * BLOCK, (h + 1) * BLOCK)
            out[here, lanes_of(h)] = result[rows].astype(BF16)
            out_turned[lanes_of(h), here] = result[rows].T.astype(BF16)
            logs[0, h : h + 1, here] = log[rows].T[0:1, :]
        return 0

    lax.fori_loop(0, q.shape[0] // BLOCK, one_block, 0)


def back_blocks(
    offset, info, q, k, v, k_turned, start, logs, out, grad_out, raw_q, cos, sin, gain_q,
    grad_k, grad_v, store,
):
    flip = info[k.shape[0] // BLOCK]

    def twice(row):
        return jnp.concatenate([row] * GROUP, axis=1)

    def one_block(i, total_gain):
        here = at_block(i)
        b = (i + offset) ^ flip
        first = start[:, here]
        gradients = grad_out[here, :]
        both = gradients.astype(F32) * out[here, :].astype(F32)
        query, gradient = stacked(q[here, :]), stacked(gradients)
        query_turned, gradient_turned = stacked_turned(q[here, :]), stacked_turned(gradients)
        across, log = [], []
        for h in range(GROUP):
            across.append(jnp.sum(both[:, lanes_of(h)].T, axis=0, keepdims=True))
            log.append(logs[0, h : h + 1, here])
        across, log = jnp.concatenate(across, axis=1), jnp.concatenate(log, axis=1)

        def keys_step(kb, grad_query):
            there = at_block(kb ^ flip)
            allowed = twice(allowed_block(kb, b, first).astype(jnp.int32)) > 0
            s = nn(k[there, :], query_turned)
            p = jnp.where(allowed, jnp.exp2(s * (SCALE * LOG2E) - log), 0.0)
            d = (p * (nn(v[there, :], gradient_turned) - across)).astype(BF16)
            grad_v[there, :] += nn(p.astype(BF16), gradient)
            grad_k[there, :] += nn(d, query)
            return grad_query + nn(k_turned[:, there], d)

        done = lax.fori_loop(
            info[b], b + 1, keys_step, jnp.zeros((HEAD_SIZE, GROUP * BLOCK), F32)
        )
        c, s = cos[here, :], sin[here, :]
        for h in range(GROUP):
            grad = done[:, h * BLOCK : (h + 1) * BLOCK].T * SCALE
            back, gain = head_back(raw_q[here, lanes_of(h)], gain_q[...], c, s, grad)
            store(i, h, back.astype(BF16))
            total_gain = total_gain + gain
        return total_gain

    return lax.fori_loop(0, q.shape[0] // BLOCK, one_block, jnp.zeros((1, HEAD_SIZE), F32))


def back_own_kernel(
    info, q, k, v, k_turned, start, logs, out, grad_out, raw_q, cos, sin, gain_q,
    grad_q, grad_k, grad_v, grad_gain,
):
    grad_k[...] = jnp.zeros(grad_k.shape, F32)
    grad_v[...] = jnp.zeros(grad_v.shape, F32)

    def store(i, h, value):
        grad_q[at_block(i), lanes_of(h)] = value

    grad_gain[0, :, :] = back_blocks(
        0, info, q, k, v, k_turned, start, logs, out, grad_out, raw_q, cos, sin, gain_q,
        grad_k, grad_v, store,
    )


def back_other_kernel(
    info, q, k, v, k_turned, start, logs, out, grad_out, raw_q, cos, sin, gain_q,
    cos_all, sin_all, raw_k, gain_k, grad_q_own, grad_k_own, grad_v_own,
    grad_qkv, grad_gains, grad_k, grad_v,
):
    half = q.shape[0] // BLOCK
    blocks = k.shape[0] // BLOCK
    queries = GROUP * HEAD_SIZE
    grad_k[...] = grad_k_own[...]
    grad_v[...] = grad_v_own[...]
    grad_qkv[: half * BLOCK, :queries] = grad_q_own[...]

    def store(i, h, value):
        grad_qkv[at_block(i + half), lanes_of(h)] = value

    grad_gains[0, 0:1, :] = back_blocks(
        half, info, q, k, v, k_turned, start, logs, out, grad_out, raw_q, cos, sin, gain_q,
        grad_k, grad_v, store,
    )

    def finish(i, total_gain):
        rows = at_block(i)
        back, gain = head_back(
            raw_k[rows, :], gain_k[...], cos_all[rows, :], sin_all[rows, :], grad_k[rows, :] * SCALE
        )
        grad_qkv[rows, lanes_of(GROUP)] = back.astype(BF16)
        grad_qkv[rows, lanes_of(GROUP + 1)] = grad_v[rows, :].astype(BF16)
        return total_gain + gain

    grad_gains[0, 1:2, :] = lax.fori_loop(0, blocks, finish, jnp.zeros((1, HEAD_SIZE), F32))


def unpack(packed, gate_up, down):
    n, _, half = packed.shape
    depth = gate_up.shape[0] // n
    pieces = gate_up.shape[1] // half
    blocks = down.shape[0] // HEAD_SIZE
    deep = HEAD_SIZE // n
    for d in range(n):
        for b in range(pieces):
            gate_up[d * depth : (d + 1) * depth, b * half : (b + 1) * half] = packed[
                d, b * depth : (b + 1) * depth, :
            ]
        for c in range(2):
            for i in range(blocks):
                at = pieces * depth + (c * blocks + i) * deep
                to = i * HEAD_SIZE + d * deep
                down[to : to + deep, c * half : (c + 1) * half] = packed[d, at : at + deep, :]


def feed_kernel(packs, h, grad, *refs):
    step = pl.program_id(0)
    if packs:
        packed, *refs = refs
        *refs, gate_up, down = refs

        @pl.when(step == 0)
        def _():
            unpack(packed, gate_up, down)
    else:
        gate_up, down, *refs = refs
    h_turned, hidden_turned, grad_gate_up, back_a, back_b, sum_a, sum_b = refs
    width = down.shape[0]
    rows = h[...]
    both = nn(rows, gate_up[...])
    gate, up = both[:, :width], both[:, width:]
    sig = jax.nn.sigmoid(gate)
    gated = gate * sig
    value = gated * up
    hidden_turned[...] = value.T.astype(BF16)
    h_turned[...] = rows.astype(F32).T.astype(BF16)
    grad_hidden = nt(grad[...], down[...])
    grad_gate_up[:, :width] = (grad_hidden * up * (sig + gated * (1.0 - sig))).astype(BF16)
    grad_gate_up[:, width:] = (grad_hidden * gated).astype(BF16)
    back = nt(grad_gate_up[...], gate_up[...]).astype(BF16)
    total = nn(value.astype(BF16), down[...]).astype(BF16)
    first = step < pl.num_programs(0) // 2

    @pl.when(first)
    def _():
        back_a[...] = back
        sum_a[...] = total

    @pl.when(jnp.logical_not(first))
    def _():
        back_b[...] = back
        sum_b[...] = total


def feed_weights_kernel(
    packs, pieces, h_own, h_other, grad_own, grad_other, hidden_own, hidden_other, dy_own, dy_other,
    *out
):
    step = pl.program_id(0)
    half = dy_own.shape[1]

    for b in range(pieces):
        @pl.when(step == b)
        def _():
            value = nn(h_own[...], grad_own[...]) + nn(h_other[...], grad_other[...])
            value = value.astype(BF16)
            if packs:
                n = out[0].shape[0]
                depth = value.shape[0] // n
                for d in range(n):
                    out[0][d, b * depth : (b + 1) * depth, :] = value[d * depth : (d + 1) * depth]
            else:
                out[0][:, b * half : (b + 1) * half] = value

    for c in range(2):
        @pl.when(step == pieces + c)
        def _():
            value = nn(hidden_own[...], dy_own[...]) + nn(hidden_other[...], dy_other[...])
            value = value.astype(BF16)
            if packs:
                n = out[0].shape[0]
                depth, deep = h_own.shape[0] // n, HEAD_SIZE // n
                blocks = value.shape[0] // HEAD_SIZE
                for d in range(n):
                    for i in range(blocks):
                        at = pieces * depth + (c * blocks + i) * deep
                        of = i * HEAD_SIZE + d * deep
                        out[0][d, at : at + deep, :] = value[of : of + deep]
            else:
                out[1][:, c * half : (c + 1) * half] = value


def unproject_kernel(grad, matrix, out_a, out_b):
    value = nt(grad[...], matrix[...]).astype(BF16)
    first = pl.program_id(0) < pl.num_programs(0) // 2

    @pl.when(first)
    def _():
        out_a[...] = value

    @pl.when(jnp.logical_not(first))
    def _():
        out_b[...] = value


def params(name, flops):
    return dict(
        compiler_params=pltpu.CompilerParams(
            dimension_semantics=("arbitrary",), vmem_limit_bytes=VMEM_LIMIT
        ),
        cost_estimate=pl.CostEstimate(flops=flops // 64, bytes_accessed=1_000, transcendentals=0),
        name=name,
    )


def fixed(shape, index=None):
    index = (0,) * len(shape) if index is None else index
    return pl.BlockSpec(shape, lambda i, *_: index)


def shaped(shape, kind):
    return jax.ShapeDtypeStruct(shape, kind)


def project(x, gain, matrix, cos, sin, gain_q, gain_k):
    rows, width = x.shape
    heads = matrix.shape[1] // (SLOTS * HEAD_SIZE)
    by_rows = lambda n: pl.BlockSpec((BLOCK, n), lambda i: (i, 0))
    by_lanes = lambda n: pl.BlockSpec((n, BLOCK), lambda i: (0, i))
    q_width, k_width = heads * GROUP * HEAD_SIZE, heads * HEAD_SIZE
    return pl.pallas_call(
        project_kernel,
        grid=(rows // BLOCK,),
        in_specs=[
            by_rows(width), fixed((1, width)), fixed(matrix.shape), by_rows(HEAD_SIZE),
            by_rows(HEAD_SIZE), fixed((1, HEAD_SIZE)), fixed((1, HEAD_SIZE)),
        ],
        out_specs=[
            by_lanes(width), by_rows(q_width), by_rows(k_width), by_rows(q_width),
            by_rows(k_width), by_rows(k_width), by_lanes(k_width),
        ],
        out_shape=[
            shaped((width, rows), BF16), shaped((rows, q_width), F32),
            shaped((rows, k_width), F32), shaped((rows, q_width), BF16),
            shaped((rows, k_width), BF16), shaped((rows, k_width), BF16),
            shaped((k_width, rows), BF16),
        ],
        **params("project", 10_000_000_000),
    )(x, gain, matrix, cos, sin, gain_q, gain_k)


def head_specs(half, rows):
    n = rows // 2
    queries = GROUP * HEAD_SIZE
    return dict(
        q=pl.BlockSpec((n, queries), lambda j, info: (half, j)),
        k=pl.BlockSpec((rows, HEAD_SIZE), lambda j, info: (0, j)),
        turned=pl.BlockSpec((HEAD_SIZE, rows), lambda j, info: (j, 0)),
        start=pl.BlockSpec((1, n), lambda j, info: (0, half)),
        out=pl.BlockSpec((n, queries), lambda j, info: (0, j)),
        out_turned=pl.BlockSpec((queries, n), lambda j, info: (j, 0)),
        logs=pl.BlockSpec((1, GROUP, n), lambda j, info: (j, 0, 0)),
        angle=pl.BlockSpec((n, HEAD_SIZE), lambda j, info: (half, 0)),
        row=fixed((1, HEAD_SIZE)),
    )


def attend(half, info, q, k_turned, v):
    rows = v.shape[0]
    n, heads = rows // 2, v.shape[1] // HEAD_SIZE
    s = head_specs(half, rows)
    return pl.pallas_call(
        lambda *refs: attend_kernel(half * n // BLOCK, *refs),
        grid_spec=pltpu.PrefetchScalarGridSpec(
            num_scalar_prefetch=1,
            grid=(heads,),
            in_specs=[s["q"], s["turned"], s["k"]],
            out_specs=[s["out"], s["out_turned"], s["logs"]],
        ),
        out_shape=[
            shaped((n, q.shape[1]), BF16), shaped((q.shape[1], n), BF16),
            shaped((heads, GROUP, n), F32),
        ],
        **params("attend", 18_000_000_000),
    )(info, q, k_turned, v)


def attend_back_own(info, q, k, v, k_turned, start, logs, out, grad_out, raw_q, cos, sin, gain_q):
    rows = k.shape[0]
    n, heads = rows // 2, k.shape[1] // HEAD_SIZE
    s = head_specs(0, rows)
    return pl.pallas_call(
        back_own_kernel,
        grid_spec=pltpu.PrefetchScalarGridSpec(
            num_scalar_prefetch=1,
            grid=(heads,),
            in_specs=[
                s["q"], s["k"], s["k"], s["turned"], s["start"], s["logs"], s["out"], s["out"],
                s["q"], s["angle"], s["angle"], s["row"],
            ],
            out_specs=[
                s["out"], s["k"], s["k"],
                pl.BlockSpec((1, 1, HEAD_SIZE), lambda j, info: (j, 0, 0)),
            ],
        ),
        out_shape=[
            shaped((n, q.shape[1]), BF16), shaped(k.shape, F32), shaped(k.shape, F32),
            shaped((heads, 1, HEAD_SIZE), F32),
        ],
        **params("attend_back_own", 25_000_000_000),
    )(info, q, k, v, k_turned, start, logs, out, grad_out, raw_q, cos, sin, gain_q)


def attend_back_other(
    info, q, k, v, k_turned, start, logs, out, grad_out, raw_q, cos, sin, gain_q,
    raw_k, gain_k, grad_q, grad_k, grad_v,
):
    rows = k.shape[0]
    heads = k.shape[1] // HEAD_SIZE
    width = SLOTS * HEAD_SIZE
    s = head_specs(1, rows)
    whole = fixed((rows, HEAD_SIZE))
    return pl.pallas_call(
        back_other_kernel,
        grid_spec=pltpu.PrefetchScalarGridSpec(
            num_scalar_prefetch=1,
            grid=(heads,),
            in_specs=[
                s["q"], s["k"], s["k"], s["turned"], s["start"], s["logs"], s["out"], s["out"],
                s["q"], s["angle"], s["angle"], s["row"],
                whole, whole, s["k"], s["row"], s["out"], s["k"], s["k"],
            ],
            out_specs=[
                pl.BlockSpec((rows, width), lambda j, info: (0, j)),
                pl.BlockSpec((1, 2, HEAD_SIZE), lambda j, info: (j, 0, 0)),
            ],
            scratch_shapes=[pltpu.VMEM((rows, HEAD_SIZE), F32)] * 2,
        ),
        out_shape=[shaped((rows, heads * width), BF16), shaped((heads, 2, HEAD_SIZE), F32)],
        **params("attend_back_other", 28_000_000_000),
    )(
        info, q, k, v, k_turned, start, logs, out, grad_out, raw_q, cos, sin, gain_q,
        cos, sin, raw_k, gain_k, grad_q, grad_k, grad_v,
    )


def two_parts(rows, width):
    steps = rows // BLOCK // 2
    return (
        [
            pl.BlockSpec((BLOCK, width), lambda i: (jnp.minimum(i, steps - 1), 0)),
            pl.BlockSpec((BLOCK, width), lambda i: (jnp.maximum(i - steps, 0), 0)),
        ],
        [shaped((rows // 2, width), BF16)] * 2,
    )


def feed(h, grad, weights, hidden_count):
    rows, width = h.shape
    packs = len(weights) == 1
    by_rows = lambda n: pl.BlockSpec((BLOCK, n), lambda i: (i, 0))
    by_lanes = lambda n: pl.BlockSpec((n, BLOCK), lambda i: (0, i))
    specs, shapes = two_parts(rows, width)
    scratch = [
        pltpu.VMEM((width, 2 * hidden_count), BF16), pltpu.VMEM((hidden_count, width), BF16)
    ]
    return pl.pallas_call(
        lambda *refs: feed_kernel(packs, *refs),
        grid=(rows // BLOCK,),
        in_specs=[by_rows(width), by_rows(width), *(fixed(w.shape) for w in weights)],
        out_specs=[
            by_lanes(width), by_lanes(hidden_count), by_rows(2 * hidden_count), *specs, *specs
        ],
        out_shape=[
            shaped((width, rows), BF16), shaped((hidden_count, rows), BF16),
            shaped((rows, 2 * hidden_count), BF16), *shapes, *shapes,
        ],
        scratch_shapes=scratch if packs else [],
        **params("feed", 16_000_000_000),
    )(h, grad, *weights)


def feed_weights(packed_shape, h, grads, hidden, dy):
    width, n = h[0].shape
    half = width // 2
    pieces = grads[0].shape[1] // half
    count = hidden[0].shape[0]
    packs = packed_shape is not None
    gate_block = pl.BlockSpec((n, half), lambda i: (0, jnp.minimum(i, pieces - 1)))
    down_block = pl.BlockSpec((n, half), lambda i: (0, jnp.maximum(i - pieces, 0)))
    shapes = [packed_shape] if packs else [(width, 2 * count), (count, width)]
    return pl.pallas_call(
        lambda *refs: feed_weights_kernel(packs, pieces, *refs),
        grid=(pieces + 2,),
        in_specs=[
            fixed((width, n)), fixed((width, n)), gate_block, gate_block,
            fixed((count, n)), fixed((count, n)), down_block, down_block,
        ],
        out_specs=[fixed(shape) for shape in shapes],
        out_shape=[shaped(shape, BF16) for shape in shapes],
        **params("feed_weights", 16_000_000_000),
    )(*h, *grads, *hidden, *dy)


def unproject(half, grad, matrix):
    rows, width = grad.shape
    n = rows // 2
    steps = n // BLOCK
    specs, shapes = two_parts(n, matrix.shape[0])
    return pl.pallas_call(
        unproject_kernel,
        grid=(steps,),
        in_specs=[pl.BlockSpec((BLOCK, width), lambda i: (i + half * steps, 0)), fixed(matrix.shape)],
        out_specs=specs,
        out_shape=shapes,
        **params("unproject", 4_000_000_000),
    )(grad, matrix)


def flipped(value, axis, bit, name="part"):
    with jax.named_scope(name):
        return lax.ppermute(value, axis, [(i, i ^ bit) for i in range(lax.axis_size(axis))])


def together(*values):
    return lax.optimization_barrier(values)


def near_sum(part, beside):
    return part.astype(F32) + flipped(beside, "tensor", 1).astype(F32)


def halved(parts, axis, bit):
    mine = (lax.axis_index("dp") // bit) % 2
    send = lax.dynamic_index_in_dim(parts, 1 - mine, axis, keepdims=False).astype(BF16)
    keep = lax.dynamic_index_in_dim(parts, mine, axis, keepdims=False)
    return keep + flipped(send, "dp", bit).astype(F32)


def per_device(
    tokens, cotangent, lengths,
    projection_weight, w_out, w_gate_up, w_down, gains,
    first_moment_projection, first_out, first_gate_up, first_down, first_gains,
    second_moment_projection, second_out, second_gate_up, second_down, second_gains,
):
    shards = lax.axis_size("tensor")
    spread = lax.axis_size("dp")
    me = lax.axis_index("tensor")
    local_rows = tokens.shape[0]
    rows = local_rows * shards
    blocks = rows // BLOCK
    kv_local = projection_weight.shape[1]
    hidden_local = w_gate_up.shape[2]
    out_heads, out_depth = w_out.shape[0], w_out.shape[1]
    down_blocks, down_depth = w_down.shape[0], w_down.shape[1]
    depth = projection_weight.shape[0]
    gain_count = gains.shape[0]

    half = MODEL_WIDTH // 2
    pieces = 2 * hidden_local // half
    gate_rows = pieces * depth
    out_rows = out_heads * out_depth
    cubic = spread == 8

    pack_one = jnp.concatenate(
        [
            projection_weight.astype(BF16).reshape(depth, -1),
            w_out.astype(BF16).reshape(-1, MODEL_WIDTH),
            jnp.pad(gains.astype(BF16)[None, :], ((0, 15), (0, MODEL_WIDTH - gain_count))),
        ],
        axis=0,
    )
    pack_two = jnp.concatenate(
        [
            w_gate_up.astype(BF16).reshape(depth, pieces, half).swapaxes(0, 1).reshape(-1, half),
            w_down.astype(BF16).reshape(-1, 2, half).swapaxes(0, 1).reshape(-1, half),
        ],
        axis=0,
    )

    def split_one(value):
        return (
            value[..., :depth, :],
            value[..., depth : depth + out_rows, :],
            value[..., depth + out_rows, :gain_count],
        )

    full_qkv, full_out, full_gains = split_one(lax.all_gather(pack_one, "dp", axis=0, tiled=False))
    full_out = full_out.reshape(spread, out_heads, out_depth, MODEL_WIDTH).swapaxes(0, 1)
    full_two = lax.all_gather(pack_two, "dp", axis=0, tiled=False)
    qkv_matrix = full_qkv.reshape(MODEL_WIDTH, -1)
    out_matrix = full_out.reshape(-1, MODEL_WIDTH)
    gains_all = full_gains.reshape(-1).astype(F32)
    gain_attn = gains_all[None, :MODEL_WIDTH]
    gain_mlp = gains_all[MODEL_WIDTH : 2 * MODEL_WIDTH]
    gain_query = gains_all[None, 2 * MODEL_WIDTH : 2 * MODEL_WIDTH + HEAD_SIZE]
    gain_key = gains_all[None, 2 * MODEL_WIDTH + HEAD_SIZE :]

    doc_ends = jnp.cumsum(lengths[0])
    doc_starts = doc_ends - lengths[0]

    def start_of(index):
        return jnp.max(
            jnp.where(index[:, None] >= doc_starts[None, :], doc_starts[None, :], 0), axis=1
        )

    order = me ^ jnp.arange(shards, dtype=jnp.int32)
    index_of_row = (
        order[:, None] * local_rows + jnp.arange(local_rows, dtype=jnp.int32)[None, :]
    ).reshape(-1)
    start_of_row = start_of(index_of_row)
    position = index_of_row - start_of_row
    inverse = THETA ** (-2.0 * jnp.arange(HEAD_SIZE // 2, dtype=F32) / HEAD_SIZE)
    turned = position.astype(F32)[:, None] * inverse[None, :]
    cosine, sine = jnp.cos(turned), jnp.sin(turned)
    cos = jnp.concatenate([cosine, cosine], axis=1)
    sin = jnp.concatenate([-sine, sine], axis=1)
    block_starts = start_of(jnp.arange(blocks, dtype=jnp.int32) * BLOCK) // BLOCK
    info = jnp.concatenate(
        [block_starts, (me * (local_rows // BLOCK))[None], doc_starts]
    ).astype(jnp.int32)
    start = start_of_row[None, :]

    rows_float = tokens.astype(F32)
    tokens_across = flipped(tokens, "tensor", 2, "tokens_across")
    tokens_all = jnp.concatenate(
        [tokens, flipped(tokens, "tensor", 1), tokens_across, flipped(tokens_across, "tensor", 1)],
        axis=0,
    )
    normed_turned, raw_q, raw_k, q, k, v, k_turned = project(
        tokens_all, gain_attn, qkv_matrix, cos, sin, gain_query, gain_key
    )
    grad_across = flipped(cotangent, "tensor", 2, "grad_across")
    heads_other, heads_other_turned, logs_other = attend(1, info, q, k_turned, v)
    heads_other, grad_across = together(heads_other, grad_across)
    beside = nn(heads_other[local_rows:], out_matrix).astype(BF16)
    near = near_sum(nn(heads_other[:local_rows], out_matrix), beside).astype(BF16)
    near, q_own = together(near, q)
    attn_across = flipped(near, "tensor", 2, "attn_across")
    heads_own, heads_own_turned, logs_own = attend(0, info, q_own, k_turned, v)
    heads_own, attn_across = together(heads_own, attn_across)
    beside = nn(heads_own[local_rows:], out_matrix).astype(BF16)
    own_sum = near_sum(nn(heads_own[:local_rows], out_matrix), beside)
    own_sum, full_two = together(own_sum, full_two)
    middle = rows_float + own_sum + attn_across.astype(F32)
    grad_own = jnp.concatenate([cotangent, flipped(cotangent, "tensor", 1)], axis=0)
    grad_other = jnp.concatenate([grad_across, flipped(grad_across, "tensor", 1)], axis=0)
    normed_two = norm_rows(middle, gain_mlp).astype(BF16)
    normed_across = flipped(normed_two, "tensor", 2, "normed_across")
    normed_own = jnp.concatenate([normed_two, flipped(normed_two, "tensor", 1)], axis=0)
    if cubic:
        feed_matrices = (full_two,)
    else:
        feed_matrices = (
            full_two[:, :gate_rows]
            .reshape(spread, pieces, depth, half)
            .swapaxes(1, 2)
            .reshape(MODEL_WIDTH, -1),
            full_two[:, gate_rows:]
            .reshape(spread, 2, down_blocks, down_depth, half)
            .transpose(2, 0, 3, 1, 4)
            .reshape(-1, MODEL_WIDTH),
        )
    h_own, hidden_own, feed_grad_own, back_0, back_1, sum_0, sum_1 = feed(
        normed_own, grad_own, feed_matrices, hidden_local
    )
    normed_across, back_0 = together(normed_across, back_0)
    normed_other = jnp.concatenate([normed_across, flipped(normed_across, "tensor", 1)], axis=0)
    h_other, hidden_other, feed_grad_other, back_2, back_3, sum_2, sum_3 = feed(
        normed_other, grad_other, feed_matrices, hidden_local
    )
    near = near_sum(back_2, back_3).astype(BF16)
    back_near = near_sum(back_0, back_1)
    near, h_own = together(near, h_own)
    back_across = flipped(near, "tensor", 2, "back_across")

    feed_grads = feed_weights(
        full_two.shape if cubic else None, (h_own, h_other), (feed_grad_own, feed_grad_other),
        (hidden_own, hidden_other), (grad_own, grad_other),
    )
    back_across, *feed_grads = together(back_across, *feed_grads)
    if cubic:
        feed_pack = feed_grads[0]
    else:
        feed_pack = jnp.concatenate(
            [
                feed_grads[0].reshape(spread, depth, pieces, half)
                .swapaxes(1, 2)
                .reshape(spread, -1, half),
                feed_grads[1].reshape(down_blocks, spread, down_depth, 2, half)
                .transpose(1, 3, 0, 2, 4)
                .reshape(spread, -1, half),
            ],
            axis=1,
        )
    feed_sum = lax.psum_scatter(feed_pack, "dp", scatter_dimension=0, tiled=True)[0].astype(F32)
    grad_middle_part, grad_gain_mlp = norm_back(
        middle, gain_mlp, back_near + back_across.astype(F32)
    )
    grad_middle = cotangent.astype(F32) + grad_middle_part
    grad_middle_low = grad_middle.astype(BF16)
    grad_middle_across = flipped(grad_middle_low, "tensor", 2, "grad_middle_across")

    grad_middle_own = jnp.concatenate(
        [grad_middle_low, flipped(grad_middle_low, "tensor", 1)], axis=0
    )
    grad_heads_own = nt(grad_middle_own, out_matrix).astype(BF16)
    grad_q, grad_k, grad_v, gain_own = attend_back_own(
        info, q, k, v, k_turned, start, logs_own, heads_own, grad_heads_own, raw_q, cos, sin,
        gain_query,
    )
    grad_middle_across, grad_q = together(grad_middle_across, grad_q)
    grad_middle_other = jnp.concatenate(
        [grad_middle_across, flipped(grad_middle_across, "tensor", 1)], axis=0
    )
    grad_heads_other = nt(grad_middle_other, out_matrix).astype(BF16)
    grad_out_w = (
        nn(heads_own_turned, grad_middle_own) + nn(heads_other_turned, grad_middle_other)
    ).astype(BF16)
    grad_out_w, grad_heads_other = together(grad_out_w, grad_heads_other)
    grad_qkv, gain_other = attend_back_other(
        info, q, k, v, k_turned, start, logs_other, heads_other, grad_heads_other,
        raw_q, cos, sin, gain_query, raw_k, gain_key, grad_q, grad_k, grad_v,
    )
    back_2, back_3 = unproject(1, grad_qkv, qkv_matrix)
    back_2, back_3, grad_qkv = together(back_2, back_3, grad_qkv)
    grad_qkv_w = nn(normed_turned, grad_qkv)
    near = near_sum(back_2, back_3).astype(BF16)
    near, grad_qkv, grad_qkv_w, grad_out_w, sum_2, sum_3 = together(
        near, grad_qkv, grad_qkv_w, grad_out_w, sum_2, sum_3
    )
    near_mlp = near_sum(sum_2, sum_3).astype(BF16)
    back_across = flipped(near, "tensor", 2, "back_across")
    grad_gain_attn = jnp.sum(qkv_matrix.astype(F32) * grad_qkv_w, axis=1) / gain_attn[0]
    grad_gain_heads = jnp.sum(gain_other, axis=0) + jnp.pad(
        jnp.sum(gain_own, axis=0), ((0, 1), (0, 0))
    )
    gain_sums = jnp.concatenate([grad_gain_attn, grad_gain_mlp, grad_gain_heads.reshape(-1)])
    back_0, back_1 = unproject(0, grad_qkv, qkv_matrix)
    if cubic:
        cube = (2, 2, 2)
        columns = grad_qkv_w.shape[1] // 2
        gain_rows = jnp.pad(
            gain_sums.reshape(cube + (1, gain_count)),
            ((0, 0),) * 3 + ((0, 15), (0, columns - gain_count)),
        )
        sum_one = jnp.concatenate(
            [grad_qkv_w[:, :columns].reshape(cube + (depth, -1)), gain_rows], axis=3
        )
        sum_two = grad_qkv_w[:, columns:].reshape(cube + (depth, -1))
        sum_one, sum_two = halved(sum_one, 1, 2), halved(sum_two, 2, 1)
        sum_out = grad_out_w.reshape((out_heads,) + cube + (out_depth, MODEL_WIDTH))
        sum_out = halved(sum_out, 3, 1)
        sum_one, sum_two, back_across, sum_0, sum_1, near_mlp, feed_sum = together(
            sum_one, sum_two, back_across, sum_0, sum_1, near_mlp, feed_sum
        )
        mlp_across = flipped(near_mlp, "tensor", 2, "mlp_across")
        sum_one, sum_two = halved(sum_one, 1, 1), halved(sum_two, 1, 2)
        sum_out = halved(sum_out, 2, 2)
        sum_one, sum_two, sum_out = together(sum_one, sum_two, sum_out)
        sum_one, sum_two = halved(sum_one, 0, 4), halved(sum_two, 0, 4)
        sum_out = halved(sum_out, 1, 4)
        sum_one, sum_two, sum_out, mlp_across = together(sum_one, sum_two, sum_out, mlp_across)
        sum_qkv = jnp.concatenate([sum_one[:depth], sum_two], axis=1)
        sum_qkv = sum_qkv.reshape(projection_weight.shape)
        sum_gains = sum_one[depth, :gain_count]
    else:
        mlp_across = flipped(near_mlp, "tensor", 2, "mlp_across")
        sum_qkv = (
            lax.psum_scatter(grad_qkv_w.astype(BF16), "dp", scatter_dimension=0, tiled=True)
            .astype(F32)
            .reshape(projection_weight.shape)
        )
        sum_out = lax.psum_scatter(
            grad_out_w.reshape(out_heads, -1, MODEL_WIDTH), "dp", scatter_dimension=1, tiled=True
        ).astype(F32)
        sum_gains = lax.psum_scatter(gain_sums, "dp", scatter_dimension=0, tiled=True)
    sum_gains = sum_gains + sum(flipped(sum_gains, "tensor", bit) for bit in range(1, shards))

    grad_normed_one = near_sum(back_0, back_1) + back_across.astype(F32)
    grad_rows_part, _ = norm_back(rows_float, gain_attn, grad_normed_one)
    grad_tokens = grad_middle + grad_rows_part
    mlp_rows = near_sum(sum_0, sum_1) + mlp_across.astype(F32)
    block_out = (middle + mlp_rows).astype(BF16)

    sum_gate_up = (
        feed_sum[:gate_rows].reshape(pieces, depth, half).swapaxes(0, 1).reshape(w_gate_up.shape)
    )
    sum_down = feed_sum[gate_rows:].reshape(2, -1, half).swapaxes(0, 1).reshape(w_down.shape)

    upd_qkv = adamw_update(
        projection_weight, first_moment_projection, second_moment_projection,
        row_major(sum_qkv), 2.0 * MODEL_WIDTH ** (-0.5), DECAY,
    )
    upd_out = adamw_update(
        w_out, first_out, second_out, sum_out,
        2.0 * (QUERY_HEADS * HEAD_SIZE // 64) ** (-0.5), DECAY,
    )
    upd_gate_up = adamw_update(
        w_gate_up, first_gate_up, second_gate_up, row_major(sum_gate_up),
        2.0 * MODEL_WIDTH ** (-0.5), DECAY,
    )
    upd_down = adamw_update(w_down, first_down, second_down, sum_down, 2.0 * FF ** (-0.5), DECAY)
    upd_gains = adamw_update(gains, first_gains, second_gains, sum_gains, 0.5, 0.0)
    updates = (upd_qkv, upd_out, upd_gate_up, upd_down, upd_gains)
    return (
        block_out,
        grad_tokens,
        *(update[2] for update in updates),
        *(update[0] for update in updates),
        *(update[1] for update in updates),
    )


def solution(mesh):
    weights = (
        P("dp", "tensor", None),
        P("tensor", "dp", None),
        P("dp", None, "tensor"),
        P("tensor", "dp", None),
        P("dp"),
    )
    batch = P(("dp", "tensor"), None)
    return jax.shard_map(
        per_device,
        mesh=mesh,
        in_specs=(batch, batch, P("dp", None), *weights, *weights, *weights),
        out_specs=(batch, batch, *weights, *weights, *weights),
        check_vma=False,
    )
```

```python
import jax
import jax.numpy as jnp
from jax import lax
from jax.experimental import pallas as pl
from jax.experimental.layout import Layout, with_layout_constraint
from jax.experimental.pallas import tpu as pltpu
from jax.sharding import PartitionSpec as P

MODEL_WIDTH = 1024
QUERY_HEADS = 16
KEY_VALUE_HEADS = 8
HEAD_SIZE = 128
FF = 3072
STEP = 10

EPS = 1e-06
THETA = 1000000.0
BETA_ONE = 0.9
BETA_TWO = 0.95
ADAM_EPS = 1e-08
DECAY = 0.1

GROUP = QUERY_HEADS // KEY_VALUE_HEADS
SLOTS = GROUP + 2
SCALE = HEAD_SIZE ** (-0.5)
LOG2E = 1.4426950408889634
BLOCK = 256
VMEM_LIMIT = 48 * 1024 * 1024
F32 = jnp.float32
BF16 = jnp.bfloat16


def norm_rows(values, scales):
    return values * lax.rsqrt(jnp.mean(values * values, axis=-1, keepdims=True) + EPS) * scales


def norm_back(values, scales, grad):
    r = lax.rsqrt(jnp.mean(values * values, axis=-1, keepdims=True) + EPS)
    u = grad * scales
    back = r * u - values * (r * r * r) * jnp.mean(u * values, axis=-1, keepdims=True)
    return back, jnp.sum(grad * values * r, axis=0)


def row_major(value):
    return with_layout_constraint(value, Layout(major_to_minor=tuple(range(value.ndim))))


def adamw_update(master, moment_one, moment_two, gradient, step_rate, decay_rate):
    next_one = BETA_ONE * moment_one + (1.0 - BETA_ONE) * gradient
    next_two = BETA_TWO * moment_two + (1.0 - BETA_TWO) * gradient * gradient
    one_hat = next_one / (1.0 - BETA_ONE**STEP)
    two_hat = next_two / (1.0 - BETA_TWO**STEP)
    next_master = master - step_rate * (
        one_hat / (jnp.sqrt(two_hat) + ADAM_EPS) + decay_rate * master
    )
    return (next_one, next_two, next_master)


def nt(a, b):
    return lax.dot_general(a, b, (((1,), (1,)), ((), ())), preferred_element_type=F32)


def nn(a, b):
    return jnp.dot(a, b, preferred_element_type=F32)


def head_rotated(x, gain, cos, sin):
    r = lax.rsqrt(jnp.mean(x * x, axis=-1, keepdims=True) + EPS)
    y = x * r * gain
    return y * cos + pltpu.roll(y, HEAD_SIZE // 2, 1) * sin


def head_back(x, gain, cos, sin, grad):
    r = lax.rsqrt(jnp.mean(x * x, axis=-1, keepdims=True) + EPS)
    turned = grad * cos - pltpu.roll(grad, HEAD_SIZE // 2, 1) * sin
    u = turned * gain
    back = r * u - x * (r * r * r) * jnp.mean(u * x, axis=-1, keepdims=True)
    return back, jnp.sum(turned * x * r, axis=0, keepdims=True)


def at_block(index):
    return pl.ds(pl.multiple_of(index * BLOCK, BLOCK), BLOCK)


def allowed_block(key_block, query_block, start):
    keys = key_block * BLOCK + lax.broadcasted_iota(jnp.int32, (BLOCK, BLOCK), 0)
    queries = query_block * BLOCK + lax.broadcasted_iota(jnp.int32, (BLOCK, BLOCK), 1)
    return (keys >= start) & (keys <= queries)


def lanes_of(h):
    return slice(h * HEAD_SIZE, (h + 1) * HEAD_SIZE)


def project_kernel(
    x, gain, matrix, cos, sin, gain_q, gain_k, normed_turned, raw_q, raw_k, q, k, v, k_turned
):
    normed = norm_rows(x[...].astype(F32), gain[...])
    normed_turned[...] = normed.T.astype(BF16)
    h = normed.astype(BF16)
    c, s = cos[...], sin[...]
    for j in range(matrix.shape[1] // (SLOTS * HEAD_SIZE)):
        base = j * SLOTS * HEAD_SIZE
        part = nn(h, matrix[:, base : base + SLOTS * HEAD_SIZE])
        for g in range(GROUP):
            value = part[:, lanes_of(g)]
            raw_q[:, lanes_of(j * GROUP + g)] = value
            q[:, lanes_of(j * GROUP + g)] = head_rotated(value, gain_q[...], c, s).astype(BF16)
        value = part[:, lanes_of(GROUP)]
        raw_k[:, lanes_of(j)] = value
        turned = head_rotated(value, gain_k[...], c, s)
        k[:, lanes_of(j)] = turned.astype(BF16)
        k_turned[lanes_of(j), :] = turned.T.astype(BF16)
        v[:, lanes_of(j)] = part[:, lanes_of(GROUP + 1)].astype(BF16)


def stacked(value):
    return jnp.concatenate([value[:, lanes_of(h)] for h in range(GROUP)], axis=0)


def stacked_turned(value):
    return jnp.concatenate(
        [value[:, lanes_of(h)].astype(F32).T.astype(BF16) for h in range(GROUP)], axis=1
    )


def attend_kernel(offset, info, q, k_turned, v, out, out_turned, logs):
    blocks = v.shape[0] // BLOCK
    flip = info[blocks]
    documents = info.shape[0] - blocks - 1

    def one_block(i, _):
        here = at_block(i)
        b = (i + offset) ^ flip
        index = b * BLOCK + lax.broadcasted_iota(jnp.int32, (BLOCK, 1), 0)
        first = jnp.zeros((BLOCK, 1), jnp.int32)
        for d in range(documents):
            begin = info[blocks + 1 + d]
            first = jnp.maximum(first, jnp.where(index >= begin, begin, 0))
        query = stacked(q[here, :])

        def keys_step(kb, carry):
            total, blend = carry
            there = at_block(kb ^ flip)
            keys = kb * BLOCK + lax.broadcasted_iota(jnp.int32, (BLOCK, BLOCK), 1)
            allowed = (keys >= first) & (keys <= index)
            score = nn(query, k_turned[:, there]).reshape(GROUP, BLOCK, BLOCK)
            p = jnp.where(allowed[None], jnp.exp2(score * (SCALE * LOG2E)), 0.0)
            p = p.reshape(GROUP * BLOCK, BLOCK)
            for lane in range(0, BLOCK, HEAD_SIZE):
                total = total + p[:, lane : lane + HEAD_SIZE]
            return total, blend + nn(p.astype(BF16), v[there, :])

        zero = jnp.zeros((GROUP * BLOCK, HEAD_SIZE), F32)
        total, blend = lax.fori_loop(info[b], b + 1, keys_step, (zero, zero))
        total = jnp.sum(total, axis=1, keepdims=True)
        result = blend / total
        log = jnp.broadcast_to(jnp.log2(total), result.shape)
        for h in range(GROUP):
            rows = slice(h * BLOCK, (h + 1) * BLOCK)
            out[here, lanes_of(h)] = result[rows].astype(BF16)
            out_turned[lanes_of(h), here] = result[rows].T.astype(BF16)
            logs[0, h : h + 1, here] = log[rows].T[0:1, :]
        return 0

    lax.fori_loop(0, q.shape[0] // BLOCK, one_block, 0)


def back_blocks(
    offset, info, q, k, v, k_turned, start, logs, out, grad_out, raw_q, cos, sin, gain_q,
    grad_k, grad_v, store,
):
    flip = info[k.shape[0] // BLOCK]

    def twice(row):
        return jnp.concatenate([row] * GROUP, axis=1)

    def one_block(i, total_gain):
        here = at_block(i)
        b = (i + offset) ^ flip
        first = start[:, here]
        gradients = grad_out[here, :]
        both = gradients.astype(F32) * out[here, :].astype(F32)
        query, gradient = stacked(q[here, :]), stacked(gradients)
        query_turned, gradient_turned = stacked_turned(q[here, :]), stacked_turned(gradients)
        across, log = [], []
        for h in range(GROUP):
            across.append(jnp.sum(both[:, lanes_of(h)].T, axis=0, keepdims=True))
            log.append(logs[0, h : h + 1, here])
        across, log = jnp.concatenate(across, axis=1), jnp.concatenate(log, axis=1)

        def keys_step(kb, grad_query):
            there = at_block(kb ^ flip)
            allowed = twice(allowed_block(kb, b, first).astype(jnp.int32)) > 0
            s = nn(k[there, :], query_turned)
            p = jnp.where(allowed, jnp.exp2(s * (SCALE * LOG2E) - log), 0.0)
            d = (p * (nn(v[there, :], gradient_turned) - across)).astype(BF16)
            grad_v[there, :] += nn(p.astype(BF16), gradient)
            grad_k[there, :] += nn(d, query)
            return grad_query + nn(k_turned[:, there], d)

        done = lax.fori_loop(
            info[b], b + 1, keys_step, jnp.zeros((HEAD_SIZE, GROUP * BLOCK), F32)
        )
        c, s = cos[here, :], sin[here, :]
        for h in range(GROUP):
            grad = done[:, h * BLOCK : (h + 1) * BLOCK].T * SCALE
            back, gain = head_back(raw_q[here, lanes_of(h)], gain_q[...], c, s, grad)
            store(i, h, back.astype(BF16))
            total_gain = total_gain + gain
        return total_gain

    return lax.fori_loop(0, q.shape[0] // BLOCK, one_block, jnp.zeros((1, HEAD_SIZE), F32))


def back_own_kernel(
    info, q, k, v, k_turned, start, logs, out, grad_out, raw_q, cos, sin, gain_q,
    grad_q, grad_k, grad_v, grad_gain,
):
    grad_k[...] = jnp.zeros(grad_k.shape, F32)
    grad_v[...] = jnp.zeros(grad_v.shape, F32)

    def store(i, h, value):
        grad_q[at_block(i), lanes_of(h)] = value

    grad_gain[0, :, :] = back_blocks(
        0, info, q, k, v, k_turned, start, logs, out, grad_out, raw_q, cos, sin, gain_q,
        grad_k, grad_v, store,
    )


def back_other_kernel(
    info, q, k, v, k_turned, start, logs, out, grad_out, raw_q, cos, sin, gain_q,
    cos_all, sin_all, raw_k, gain_k, grad_q_own, grad_k_own, grad_v_own,
    grad_qkv, grad_gains, grad_k, grad_v,
):
    half = q.shape[0] // BLOCK
    blocks = k.shape[0] // BLOCK
    queries = GROUP * HEAD_SIZE
    grad_k[...] = grad_k_own[...]
    grad_v[...] = grad_v_own[...]
    grad_qkv[: half * BLOCK, :queries] = grad_q_own[...]

    def store(i, h, value):
        grad_qkv[at_block(i + half), lanes_of(h)] = value

    grad_gains[0, 0:1, :] = back_blocks(
        half, info, q, k, v, k_turned, start, logs, out, grad_out, raw_q, cos, sin, gain_q,
        grad_k, grad_v, store,
    )

    def finish(i, total_gain):
        rows = at_block(i)
        back, gain = head_back(
            raw_k[rows, :], gain_k[...], cos_all[rows, :], sin_all[rows, :], grad_k[rows, :] * SCALE
        )
        grad_qkv[rows, lanes_of(GROUP)] = back.astype(BF16)
        grad_qkv[rows, lanes_of(GROUP + 1)] = grad_v[rows, :].astype(BF16)
        return total_gain + gain

    grad_gains[0, 1:2, :] = lax.fori_loop(0, blocks, finish, jnp.zeros((1, HEAD_SIZE), F32))


def unpack(packed, gate_up, down):
    n, _, half = packed.shape
    depth = gate_up.shape[0] // n
    pieces = gate_up.shape[1] // half
    blocks = down.shape[0] // HEAD_SIZE
    deep = HEAD_SIZE // n
    for d in range(n):
        for b in range(pieces):
            gate_up[d * depth : (d + 1) * depth, b * half : (b + 1) * half] = packed[
                d, b * depth : (b + 1) * depth, :
            ]
        for c in range(2):
            for i in range(blocks):
                at = pieces * depth + (c * blocks + i) * deep
                to = i * HEAD_SIZE + d * deep
                down[to : to + deep, c * half : (c + 1) * half] = packed[d, at : at + deep, :]


def feed_kernel(packs, h, grad, *refs):
    step = pl.program_id(0)
    if packs:
        packed, *refs = refs
        *refs, gate_up, down = refs

        @pl.when(step == 0)
        def _():
            unpack(packed, gate_up, down)
    else:
        gate_up, down, *refs = refs
    h_turned, hidden_turned, grad_gate_up, back_a, back_b, sum_a, sum_b = refs
    width = down.shape[0]
    rows = h[...]
    both = nn(rows, gate_up[...])
    gate, up = both[:, :width], both[:, width:]
    sig = jax.nn.sigmoid(gate)
    gated = gate * sig
    value = gated * up
    hidden_turned[...] = value.T.astype(BF16)
    h_turned[...] = rows.astype(F32).T.astype(BF16)
    grad_hidden = nt(grad[...], down[...])
    grad_gate_up[:, :width] = (grad_hidden * up * (sig + gated * (1.0 - sig))).astype(BF16)
    grad_gate_up[:, width:] = (grad_hidden * gated).astype(BF16)
    back = nt(grad_gate_up[...], gate_up[...]).astype(BF16)
    total = nn(value.astype(BF16), down[...]).astype(BF16)
    first = step < pl.num_programs(0) // 2

    @pl.when(first)
    def _():
        back_a[...] = back
        sum_a[...] = total

    @pl.when(jnp.logical_not(first))
    def _():
        back_b[...] = back
        sum_b[...] = total


def feed_weights_kernel(
    packs, pieces, h_own, h_other, grad_own, grad_other, hidden_own, hidden_other, dy_own, dy_other,
    *out
):
    step = pl.program_id(0)
    half = dy_own.shape[1]

    for b in range(pieces):
        @pl.when(step == b)
        def _():
            value = nn(h_own[...], grad_own[...]) + nn(h_other[...], grad_other[...])
            value = value.astype(BF16)
            if packs:
                n = out[0].shape[0]
                depth = value.shape[0] // n
                for d in range(n):
                    out[0][d, b * depth : (b + 1) * depth, :] = value[d * depth : (d + 1) * depth]
            else:
                out[0][:, b * half : (b + 1) * half] = value

    for c in range(2):
        @pl.when(step == pieces + c)
        def _():
            value = nn(hidden_own[...], dy_own[...]) + nn(hidden_other[...], dy_other[...])
            value = value.astype(BF16)
            if packs:
                n = out[0].shape[0]
                depth, deep = h_own.shape[0] // n, HEAD_SIZE // n
                blocks = value.shape[0] // HEAD_SIZE
                for d in range(n):
                    for i in range(blocks):
                        at = pieces * depth + (c * blocks + i) * deep
                        of = i * HEAD_SIZE + d * deep
                        out[0][d, at : at + deep, :] = value[of : of + deep]
            else:
                out[1][:, c * half : (c + 1) * half] = value


def unproject_kernel(grad, matrix, out_a, out_b):
    value = nt(grad[...], matrix[...]).astype(BF16)
    first = pl.program_id(0) < pl.num_programs(0) // 2

    @pl.when(first)
    def _():
        out_a[...] = value

    @pl.when(jnp.logical_not(first))
    def _():
        out_b[...] = value


def params(name, flops):
    return dict(
        compiler_params=pltpu.CompilerParams(
            dimension_semantics=("arbitrary",), vmem_limit_bytes=VMEM_LIMIT
        ),
        cost_estimate=pl.CostEstimate(flops=flops // 64, bytes_accessed=1_000, transcendentals=0),
        name=name,
    )


def fixed(shape, index=None):
    index = (0,) * len(shape) if index is None else index
    return pl.BlockSpec(shape, lambda i, *_: index)


def shaped(shape, kind):
    return jax.ShapeDtypeStruct(shape, kind)


def project(x, gain, matrix, cos, sin, gain_q, gain_k):
    rows, width = x.shape
    heads = matrix.shape[1] // (SLOTS * HEAD_SIZE)
    by_rows = lambda n: pl.BlockSpec((BLOCK, n), lambda i: (i, 0))
    by_lanes = lambda n: pl.BlockSpec((n, BLOCK), lambda i: (0, i))
    q_width, k_width = heads * GROUP * HEAD_SIZE, heads * HEAD_SIZE
    return pl.pallas_call(
        project_kernel,
        grid=(rows // BLOCK,),
        in_specs=[
            by_rows(width), fixed((1, width)), fixed(matrix.shape), by_rows(HEAD_SIZE),
            by_rows(HEAD_SIZE), fixed((1, HEAD_SIZE)), fixed((1, HEAD_SIZE)),
        ],
        out_specs=[
            by_lanes(width), by_rows(q_width), by_rows(k_width), by_rows(q_width),
            by_rows(k_width), by_rows(k_width), by_lanes(k_width),
        ],
        out_shape=[
            shaped((width, rows), BF16), shaped((rows, q_width), F32),
            shaped((rows, k_width), F32), shaped((rows, q_width), BF16),
            shaped((rows, k_width), BF16), shaped((rows, k_width), BF16),
            shaped((k_width, rows), BF16),
        ],
        **params("project", 10_000_000_000),
    )(x, gain, matrix, cos, sin, gain_q, gain_k)


def head_specs(half, rows):
    n = rows // 2
    queries = GROUP * HEAD_SIZE
    return dict(
        q=pl.BlockSpec((n, queries), lambda j, info: (half, j)),
        k=pl.BlockSpec((rows, HEAD_SIZE), lambda j, info: (0, j)),
        turned=pl.BlockSpec((HEAD_SIZE, rows), lambda j, info: (j, 0)),
        start=pl.BlockSpec((1, n), lambda j, info: (0, half)),
        out=pl.BlockSpec((n, queries), lambda j, info: (0, j)),
        out_turned=pl.BlockSpec((queries, n), lambda j, info: (j, 0)),
        logs=pl.BlockSpec((1, GROUP, n), lambda j, info: (j, 0, 0)),
        angle=pl.BlockSpec((n, HEAD_SIZE), lambda j, info: (half, 0)),
        row=fixed((1, HEAD_SIZE)),
    )


def attend(half, info, q, k_turned, v):
    rows = v.shape[0]
    n, heads = rows // 2, v.shape[1] // HEAD_SIZE
    s = head_specs(half, rows)
    return pl.pallas_call(
        lambda *refs: attend_kernel(half * n // BLOCK, *refs),
        grid_spec=pltpu.PrefetchScalarGridSpec(
            num_scalar_prefetch=1,
            grid=(heads,),
            in_specs=[s["q"], s["turned"], s["k"]],
            out_specs=[s["out"], s["out_turned"], s["logs"]],
        ),
        out_shape=[
            shaped((n, q.shape[1]), BF16), shaped((q.shape[1], n), BF16),
            shaped((heads, GROUP, n), F32),
        ],
        **params("attend", 18_000_000_000),
    )(info, q, k_turned, v)


def attend_back_own(info, q, k, v, k_turned, start, logs, out, grad_out, raw_q, cos, sin, gain_q):
    rows = k.shape[0]
    n, heads = rows // 2, k.shape[1] // HEAD_SIZE
    s = head_specs(0, rows)
    return pl.pallas_call(
        back_own_kernel,
        grid_spec=pltpu.PrefetchScalarGridSpec(
            num_scalar_prefetch=1,
            grid=(heads,),
            in_specs=[
                s["q"], s["k"], s["k"], s["turned"], s["start"], s["logs"], s["out"], s["out"],
                s["q"], s["angle"], s["angle"], s["row"],
            ],
            out_specs=[
                s["out"], s["k"], s["k"],
                pl.BlockSpec((1, 1, HEAD_SIZE), lambda j, info: (j, 0, 0)),
            ],
        ),
        out_shape=[
            shaped((n, q.shape[1]), BF16), shaped(k.shape, F32), shaped(k.shape, F32),
            shaped((heads, 1, HEAD_SIZE), F32),
        ],
        **params("attend_back_own", 25_000_000_000),
    )(info, q, k, v, k_turned, start, logs, out, grad_out, raw_q, cos, sin, gain_q)


def attend_back_other(
    info, q, k, v, k_turned, start, logs, out, grad_out, raw_q, cos, sin, gain_q,
    raw_k, gain_k, grad_q, grad_k, grad_v,
):
    rows = k.shape[0]
    heads = k.shape[1] // HEAD_SIZE
    width = SLOTS * HEAD_SIZE
    s = head_specs(1, rows)
    whole = fixed((rows, HEAD_SIZE))
    return pl.pallas_call(
        back_other_kernel,
        grid_spec=pltpu.PrefetchScalarGridSpec(
            num_scalar_prefetch=1,
            grid=(heads,),
            in_specs=[
                s["q"], s["k"], s["k"], s["turned"], s["start"], s["logs"], s["out"], s["out"],
                s["q"], s["angle"], s["angle"], s["row"],
                whole, whole, s["k"], s["row"], s["out"], s["k"], s["k"],
            ],
            out_specs=[
                pl.BlockSpec((rows, width), lambda j, info: (0, j)),
                pl.BlockSpec((1, 2, HEAD_SIZE), lambda j, info: (j, 0, 0)),
            ],
            scratch_shapes=[pltpu.VMEM((rows, HEAD_SIZE), F32)] * 2,
        ),
        out_shape=[shaped((rows, heads * width), BF16), shaped((heads, 2, HEAD_SIZE), F32)],
        **params("attend_back_other", 28_000_000_000),
    )(
        info, q, k, v, k_turned, start, logs, out, grad_out, raw_q, cos, sin, gain_q,
        cos, sin, raw_k, gain_k, grad_q, grad_k, grad_v,
    )


def two_parts(rows, width):
    steps = rows // BLOCK // 2
    return (
        [
            pl.BlockSpec((BLOCK, width), lambda i: (jnp.minimum(i, steps - 1), 0)),
            pl.BlockSpec((BLOCK, width), lambda i: (jnp.maximum(i - steps, 0), 0)),
        ],
        [shaped((rows // 2, width), BF16)] * 2,
    )


def feed(h, grad, weights, hidden_count):
    rows, width = h.shape
    packs = len(weights) == 1
    by_rows = lambda n: pl.BlockSpec((BLOCK, n), lambda i: (i, 0))
    by_lanes = lambda n: pl.BlockSpec((n, BLOCK), lambda i: (0, i))
    specs, shapes = two_parts(rows, width)
    scratch = [
        pltpu.VMEM((width, 2 * hidden_count), BF16), pltpu.VMEM((hidden_count, width), BF16)
    ]
    return pl.pallas_call(
        lambda *refs: feed_kernel(packs, *refs),
        grid=(rows // BLOCK,),
        in_specs=[by_rows(width), by_rows(width), *(fixed(w.shape) for w in weights)],
        out_specs=[
            by_lanes(width), by_lanes(hidden_count), by_rows(2 * hidden_count), *specs, *specs
        ],
        out_shape=[
            shaped((width, rows), BF16), shaped((hidden_count, rows), BF16),
            shaped((rows, 2 * hidden_count), BF16), *shapes, *shapes,
        ],
        scratch_shapes=scratch if packs else [],
        **params("feed", 16_000_000_000),
    )(h, grad, *weights)


def feed_weights(packed_shape, h, grads, hidden, dy):
    width, n = h[0].shape
    half = width // 2
    pieces = grads[0].shape[1] // half
    count = hidden[0].shape[0]
    packs = packed_shape is not None
    gate_block = pl.BlockSpec((n, half), lambda i: (0, jnp.minimum(i, pieces - 1)))
    down_block = pl.BlockSpec((n, half), lambda i: (0, jnp.maximum(i - pieces, 0)))
    shapes = [packed_shape] if packs else [(width, 2 * count), (count, width)]
    return pl.pallas_call(
        lambda *refs: feed_weights_kernel(packs, pieces, *refs),
        grid=(pieces + 2,),
        in_specs=[
            fixed((width, n)), fixed((width, n)), gate_block, gate_block,
            fixed((count, n)), fixed((count, n)), down_block, down_block,
        ],
        out_specs=[fixed(shape) for shape in shapes],
        out_shape=[shaped(shape, BF16) for shape in shapes],
        **params("feed_weights", 16_000_000_000),
    )(*h, *grads, *hidden, *dy)


def unproject(half, grad, matrix):
    rows, width = grad.shape
    n = rows // 2
    steps = n // BLOCK
    specs, shapes = two_parts(n, matrix.shape[0])
    return pl.pallas_call(
        unproject_kernel,
        grid=(steps,),
        in_specs=[pl.BlockSpec((BLOCK, width), lambda i: (i + half * steps, 0)), fixed(matrix.shape)],
        out_specs=specs,
        out_shape=shapes,
        **params("unproject", 4_000_000_000),
    )(grad, matrix)


def flipped(value, axis, bit, name="part"):
    with jax.named_scope(name):
        return lax.ppermute(value, axis, [(i, i ^ bit) for i in range(lax.axis_size(axis))])


def together(*values):
    return lax.optimization_barrier(values)


def near_sum(part, beside):
    return part.astype(F32) + flipped(beside, "tensor", 1).astype(F32)


def halved(parts, axis, bit):
    mine = (lax.axis_index("dp") // bit) % 2
    send = lax.dynamic_index_in_dim(parts, 1 - mine, axis, keepdims=False).astype(BF16)
    keep = lax.dynamic_index_in_dim(parts, mine, axis, keepdims=False)
    return keep + flipped(send, "dp", bit).astype(F32)


def per_device(
    tokens, cotangent, lengths,
    projection_weight, w_out, w_gate_up, w_down, gains,
    first_moment_projection, first_out, first_gate_up, first_down, first_gains,
    second_moment_projection, second_out, second_gate_up, second_down, second_gains,
):
    shards = lax.axis_size("tensor")
    spread = lax.axis_size("dp")
    me = lax.axis_index("tensor")
    local_rows = tokens.shape[0]
    rows = local_rows * shards
    blocks = rows // BLOCK
    kv_local = projection_weight.shape[1]
    hidden_local = w_gate_up.shape[2]
    out_heads, out_depth = w_out.shape[0], w_out.shape[1]
    down_blocks, down_depth = w_down.shape[0], w_down.shape[1]
    depth = projection_weight.shape[0]
    gain_count = gains.shape[0]

    half = MODEL_WIDTH // 2
    pieces = 2 * hidden_local // half
    gate_rows = pieces * depth
    out_rows = out_heads * out_depth
    cubic = spread == 8

    pack_one = jnp.concatenate(
        [
            projection_weight.astype(BF16).reshape(depth, -1),
            w_out.astype(BF16).reshape(-1, MODEL_WIDTH),
            jnp.pad(gains.astype(BF16)[None, :], ((0, 15), (0, MODEL_WIDTH - gain_count))),
        ],
        axis=0,
    )
    pack_two = jnp.concatenate(
        [
            w_gate_up.astype(BF16).reshape(depth, pieces, half).swapaxes(0, 1).reshape(-1, half),
            w_down.astype(BF16).reshape(-1, 2, half).swapaxes(0, 1).reshape(-1, half),
        ],
        axis=0,
    )

    def split_one(value):
        return (
            value[..., :depth, :],
            value[..., depth : depth + out_rows, :],
            value[..., depth + out_rows, :gain_count],
        )

    full_qkv, full_out, full_gains = split_one(lax.all_gather(pack_one, "dp", axis=0, tiled=False))
    full_out = full_out.reshape(spread, out_heads, out_depth, MODEL_WIDTH).swapaxes(0, 1)
    full_two = lax.all_gather(pack_two, "dp", axis=0, tiled=False)
    qkv_matrix = full_qkv.reshape(MODEL_WIDTH, -1)
    out_matrix = full_out.reshape(-1, MODEL_WIDTH)
    gains_all = full_gains.reshape(-1).astype(F32)
    gain_attn = gains_all[None, :MODEL_WIDTH]
    gain_mlp = gains_all[MODEL_WIDTH : 2 * MODEL_WIDTH]
    gain_query = gains_all[None, 2 * MODEL_WIDTH : 2 * MODEL_WIDTH + HEAD_SIZE]
    gain_key = gains_all[None, 2 * MODEL_WIDTH + HEAD_SIZE :]

    doc_ends = jnp.cumsum(lengths[0])
    doc_starts = doc_ends - lengths[0]

    def start_of(index):
        return jnp.max(
            jnp.where(index[:, None] >= doc_starts[None, :], doc_starts[None, :], 0), axis=1
        )

    order = me ^ jnp.arange(shards, dtype=jnp.int32)
    index_of_row = (
        order[:, None] * local_rows + jnp.arange(local_rows, dtype=jnp.int32)[None, :]
    ).reshape(-1)
    start_of_row = start_of(index_of_row)
    position = index_of_row - start_of_row
    inverse = THETA ** (-2.0 * jnp.arange(HEAD_SIZE // 2, dtype=F32) / HEAD_SIZE)
    turned = position.astype(F32)[:, None] * inverse[None, :]
    cosine, sine = jnp.cos(turned), jnp.sin(turned)
    cos = jnp.concatenate([cosine, cosine], axis=1)
    sin = jnp.concatenate([-sine, sine], axis=1)
    block_starts = start_of(jnp.arange(blocks, dtype=jnp.int32) * BLOCK) // BLOCK
    info = jnp.concatenate(
        [block_starts, (me * (local_rows // BLOCK))[None], doc_starts]
    ).astype(jnp.int32)
    start = start_of_row[None, :]

    rows_float = tokens.astype(F32)
    tokens_across = flipped(tokens, "tensor", 2, "tokens_across")
    tokens_all = jnp.concatenate(
        [tokens, flipped(tokens, "tensor", 1), tokens_across, flipped(tokens_across, "tensor", 1)],
        axis=0,
    )
    normed_turned, raw_q, raw_k, q, k, v, k_turned = project(
        tokens_all, gain_attn, qkv_matrix, cos, sin, gain_query, gain_key
    )
    grad_across = flipped(cotangent, "tensor", 2, "grad_across")
    heads_other, heads_other_turned, logs_other = attend(1, info, q, k_turned, v)
    heads_other, grad_across = together(heads_other, grad_across)
    beside = nn(heads_other[local_rows:], out_matrix).astype(BF16)
    near = near_sum(nn(heads_other[:local_rows], out_matrix), beside).astype(BF16)
    near, q_own = together(near, q)
    attn_across = flipped(near, "tensor", 2, "attn_across")
    heads_own, heads_own_turned, logs_own = attend(0, info, q_own, k_turned, v)
    heads_own, attn_across = together(heads_own, attn_across)
    beside = nn(heads_own[local_rows:], out_matrix).astype(BF16)
    own_sum = near_sum(nn(heads_own[:local_rows], out_matrix), beside)
    own_sum, full_two = together(own_sum, full_two)
    middle = rows_float + own_sum + attn_across.astype(F32)
    grad_own = jnp.concatenate([cotangent, flipped(cotangent, "tensor", 1)], axis=0)
    grad_other = jnp.concatenate([grad_across, flipped(grad_across, "tensor", 1)], axis=0)
    normed_two = norm_rows(middle, gain_mlp).astype(BF16)
    normed_across = flipped(normed_two, "tensor", 2, "normed_across")
    normed_own = jnp.concatenate([normed_two, flipped(normed_two, "tensor", 1)], axis=0)
    if cubic:
        feed_matrices = (full_two,)
    else:
        feed_matrices = (
            full_two[:, :gate_rows]
            .reshape(spread, pieces, depth, half)
            .swapaxes(1, 2)
            .reshape(MODEL_WIDTH, -1),
            full_two[:, gate_rows:]
            .reshape(spread, 2, down_blocks, down_depth, half)
            .transpose(2, 0, 3, 1, 4)
            .reshape(-1, MODEL_WIDTH),
        )
    h_own, hidden_own, feed_grad_own, back_0, back_1, sum_0, sum_1 = feed(
        normed_own, grad_own, feed_matrices, hidden_local
    )
    normed_across, back_0 = together(normed_across, back_0)
    normed_other = jnp.concatenate([normed_across, flipped(normed_across, "tensor", 1)], axis=0)
    h_other, hidden_other, feed_grad_other, back_2, back_3, sum_2, sum_3 = feed(
        normed_other, grad_other, feed_matrices, hidden_local
    )
    near = near_sum(back_2, back_3).astype(BF16)
    back_near = near_sum(back_0, back_1)
    near, h_own = together(near, h_own)
    back_across = flipped(near, "tensor", 2, "back_across")

    feed_grads = feed_weights(
        full_two.shape if cubic else None, (h_own, h_other), (feed_grad_own, feed_grad_other),
        (hidden_own, hidden_other), (grad_own, grad_other),
    )
    back_across, *feed_grads = together(back_across, *feed_grads)
    if cubic:
        feed_pack = feed_grads[0]
    else:
        feed_pack = jnp.concatenate(
            [
                feed_grads[0].reshape(spread, depth, pieces, half)
                .swapaxes(1, 2)
                .reshape(spread, -1, half),
                feed_grads[1].reshape(down_blocks, spread, down_depth, 2, half)
                .transpose(1, 3, 0, 2, 4)
                .reshape(spread, -1, half),
            ],
            axis=1,
        )
    feed_sum = lax.psum_scatter(feed_pack, "dp", scatter_dimension=0, tiled=True)[0].astype(F32)
    grad_middle_part, grad_gain_mlp = norm_back(
        middle, gain_mlp, back_near + back_across.astype(F32)
    )
    grad_middle = cotangent.astype(F32) + grad_middle_part
    grad_middle_low = grad_middle.astype(BF16)
    grad_middle_across = flipped(grad_middle_low, "tensor", 2, "grad_middle_across")

    grad_middle_own = jnp.concatenate(
        [grad_middle_low, flipped(grad_middle_low, "tensor", 1)], axis=0
    )
    grad_heads_own = nt(grad_middle_own, out_matrix).astype(BF16)
    grad_q, grad_k, grad_v, gain_own = attend_back_own(
        info, q, k, v, k_turned, start, logs_own, heads_own, grad_heads_own, raw_q, cos, sin,
        gain_query,
    )
    grad_middle_across, grad_q = together(grad_middle_across, grad_q)
    grad_middle_other = jnp.concatenate(
        [grad_middle_across, flipped(grad_middle_across, "tensor", 1)], axis=0
    )
    grad_heads_other = nt(grad_middle_other, out_matrix).astype(BF16)
    grad_out_w = (
        nn(heads_own_turned, grad_middle_own) + nn(heads_other_turned, grad_middle_other)
    ).astype(BF16)
    grad_out_w, grad_heads_other = together(grad_out_w, grad_heads_other)
    grad_qkv, gain_other = attend_back_other(
        info, q, k, v, k_turned, start, logs_other, heads_other, grad_heads_other,
        raw_q, cos, sin, gain_query, raw_k, gain_key, grad_q, grad_k, grad_v,
    )
    back_2, back_3 = unproject(1, grad_qkv, qkv_matrix)
    back_2, back_3, grad_qkv = together(back_2, back_3, grad_qkv)
    grad_qkv_w = nn(normed_turned, grad_qkv)
    near = near_sum(back_2, back_3).astype(BF16)
    near, grad_qkv, grad_qkv_w, grad_out_w, sum_2, sum_3 = together(
        near, grad_qkv, grad_qkv_w, grad_out_w, sum_2, sum_3
    )
    near_mlp = near_sum(sum_2, sum_3).astype(BF16)
    back_across = flipped(near, "tensor", 2, "back_across")
    grad_gain_attn = jnp.sum(qkv_matrix.astype(F32) * grad_qkv_w, axis=1) / gain_attn[0]
    grad_gain_heads = jnp.sum(gain_other, axis=0) + jnp.pad(
        jnp.sum(gain_own, axis=0), ((0, 1), (0, 0))
    )
    gain_sums = jnp.concatenate([grad_gain_attn, grad_gain_mlp, grad_gain_heads.reshape(-1)])
    back_0, back_1 = unproject(0, grad_qkv, qkv_matrix)
    if cubic:
        cube = (2, 2, 2)
        columns = grad_qkv_w.shape[1] // 2
        gain_rows = jnp.pad(
            gain_sums.reshape(cube + (1, gain_count)),
            ((0, 0),) * 3 + ((0, 15), (0, columns - gain_count)),
        )
        sum_one = jnp.concatenate(
            [grad_qkv_w[:, :columns].reshape(cube + (depth, -1)), gain_rows], axis=3
        )
        sum_two = grad_qkv_w[:, columns:].reshape(cube + (depth, -1))
        sum_one, sum_two = halved(sum_one, 1, 2), halved(sum_two, 2, 1)
        sum_out = grad_out_w.reshape((out_heads,) + cube + (out_depth, MODEL_WIDTH))
        sum_out = halved(sum_out, 3, 1)
        sum_one, sum_two, back_across, sum_0, sum_1, near_mlp, feed_sum = together(
            sum_one, sum_two, back_across, sum_0, sum_1, near_mlp, feed_sum
        )
        mlp_across = flipped(near_mlp, "tensor", 2, "mlp_across")
        sum_one, sum_two = halved(sum_one, 1, 1), halved(sum_two, 1, 2)
        sum_out = halved(sum_out, 2, 2)
        sum_one, sum_two, sum_out, feed_sum = together(sum_one, sum_two, sum_out, feed_sum)
        sum_one, sum_two = halved(sum_one, 0, 4), halved(sum_two, 0, 4)
        sum_out = halved(sum_out, 1, 4)
        sum_one, sum_two, sum_out, mlp_across = together(sum_one, sum_two, sum_out, mlp_across)
        sum_qkv = jnp.concatenate([sum_one[:depth], sum_two], axis=1)
        sum_qkv = sum_qkv.reshape(projection_weight.shape)
        sum_gains = sum_one[depth, :gain_count]
    else:
        mlp_across = flipped(near_mlp, "tensor", 2, "mlp_across")
        sum_qkv = (
            lax.psum_scatter(grad_qkv_w.astype(BF16), "dp", scatter_dimension=0, tiled=True)
            .astype(F32)
            .reshape(projection_weight.shape)
        )
        sum_out = lax.psum_scatter(
            grad_out_w.reshape(out_heads, -1, MODEL_WIDTH), "dp", scatter_dimension=1, tiled=True
        ).astype(F32)
        sum_gains = lax.psum_scatter(gain_sums, "dp", scatter_dimension=0, tiled=True)
    sum_gains = sum_gains + sum(flipped(sum_gains, "tensor", bit) for bit in range(1, shards))

    grad_normed_one = near_sum(back_0, back_1) + back_across.astype(F32)
    grad_rows_part, _ = norm_back(rows_float, gain_attn, grad_normed_one)
    grad_tokens = grad_middle + grad_rows_part
    mlp_rows = near_sum(sum_0, sum_1) + mlp_across.astype(F32)
    block_out = (middle + mlp_rows).astype(BF16)

    sum_gate_up = (
        feed_sum[:gate_rows].reshape(pieces, depth, half).swapaxes(0, 1).reshape(w_gate_up.shape)
    )
    sum_down = feed_sum[gate_rows:].reshape(2, -1, half).swapaxes(0, 1).reshape(w_down.shape)

    upd_qkv = adamw_update(
        projection_weight, first_moment_projection, second_moment_projection,
        row_major(sum_qkv), 2.0 * MODEL_WIDTH ** (-0.5), DECAY,
    )
    upd_out = adamw_update(
        w_out, first_out, second_out, sum_out,
        2.0 * (QUERY_HEADS * HEAD_SIZE // 64) ** (-0.5), DECAY,
    )
    upd_gate_up = adamw_update(
        w_gate_up, first_gate_up, second_gate_up, row_major(sum_gate_up),
        2.0 * MODEL_WIDTH ** (-0.5), DECAY,
    )
    upd_down = adamw_update(w_down, first_down, second_down, sum_down, 2.0 * FF ** (-0.5), DECAY)
    upd_gains = adamw_update(gains, first_gains, second_gains, sum_gains, 0.5, 0.0)
    updates = (upd_qkv, upd_out, upd_gate_up, upd_down, upd_gains)
    return (
        block_out,
        grad_tokens,
        *(update[2] for update in updates),
        *(update[0] for update in updates),
        *(update[1] for update in updates),
    )


def solution(mesh):
    weights = (
        P("dp", "tensor", None),
        P("tensor", "dp", None),
        P("dp", None, "tensor"),
        P("tensor", "dp", None),
        P("dp"),
    )
    batch = P(("dp", "tensor"), None)
    return jax.shard_map(
        per_device,
        mesh=mesh,
        in_specs=(batch, batch, P("dp", None), *weights, *weights, *weights),
        out_specs=(batch, batch, *weights, *weights, *weights),
        check_vma=False,
    )
```
